32 devices in a mesh: ctx: 4 (over y, x), fsdp: 8 (over z, core).
Axes of the slice: x: 2, y: 2, z: 4, core: 2. Of those that a mesh axis runs over, the one named last changes fastest.
Arguments:
- tokens: bfloat16 [4096, 2048], P(('ctx', 'fsdp')), may hold values from -6 to 6
- per_layer: bfloat16 [4096, 256], P(('ctx', 'fsdp')), may hold values from -6 to 6
- cotangent: bfloat16 [4096, 2048], P(('ctx', 'fsdp')), may hold values from -6 to 6
- doc_lengths: int32 [7], replicated, may hold values from 1 to 4090, as said below
- positions: int32 [4096], P(('ctx', 'fsdp')), may hold values from 0 to 4095, as said below
- w_query: float32 [2048, 2048], P('fsdp'), may hold values from -0.125 to 0.125
- w_key: float32 [2048, 512], P('fsdp'), may hold values from -0.125 to 0.125
- w_value: float32 [2048, 512], P('fsdp'), may hold values from -0.125 to 0.125
- w_out: float32 [2048, 2048], P('fsdp'), may hold values from -0.125 to 0.125
- laurel_left: float32 [2048, 64], P('fsdp'), may hold values from -0.125 to 0.125
- laurel_right: float32 [64, 2048], P('fsdp'), may hold values from -0.75 to 0.75
- w_gate: float32 [2048, 8192], P('fsdp'), may hold values from -0.125 to 0.125
- w_up: float32 [2048, 8192], P('fsdp'), may hold values from -0.125 to 0.125
- w_down: float32 [8192, 2048], P('fsdp'), may hold values from -0.0625 to 0.0625
- ple_gate: float32 [2048, 256], P('fsdp'), may hold values from -0.125 to 0.125
- ple_proj: float32 [256, 2048], P('fsdp'), may hold values from -0.375 to 0.375
- attn_in_gain: float32 [2048], P('fsdp'), may hold values from 0.25 to 1.75
- query_gain: float32 [256], P('fsdp'), may hold values from 0.25 to 1.75
- key_gain: float32 [256], P('fsdp'), may hold values from 0.25 to 1.75
- attn_out_gain: float32 [2048], P('fsdp'), may hold values from 0.25 to 1.75
- laurel_gain: float32 [2048], P('fsdp'), may hold values from 0.25 to 1.75
- ffn_in_gain: float32 [2048], P('fsdp'), may hold values from 0.25 to 1.75
- ffn_out_gain: float32 [2048], P('fsdp'), may hold values from 0.25 to 1.75
- ple_gain: float32 [2048], P('fsdp'), may hold values from 0.25 to 1.75
Outputs:
- layer_out: bfloat16 [4096, 2048], P(('ctx', 'fsdp'))
- grad_tokens: float32 [4096, 2048], P(('ctx', 'fsdp'))
- grad_per_layer: float32 [4096, 256], P(('ctx', 'fsdp'))
- grad_w_query: float32 [2048, 2048], P('fsdp')
- grad_w_key: float32 [2048, 512], P('fsdp')
- grad_w_value: float32 [2048, 512], P('fsdp')
- grad_w_out: float32 [2048, 2048], P('fsdp')
- grad_laurel_left: float32 [2048, 64], P('fsdp')
- grad_laurel_right: float32 [64, 2048], P('fsdp')
- grad_w_gate: float32 [2048, 8192], P('fsdp')
- grad_w_up: float32 [2048, 8192], P('fsdp')
- grad_w_down: float32 [8192, 2048], P('fsdp')
- grad_ple_gate: float32 [2048, 256], P('fsdp')
- grad_ple_proj: float32 [256, 2048], P('fsdp')
- grad_attn_in_gain: float32 [2048], P('fsdp')
- grad_query_gain: float32 [256], P('fsdp')
- grad_key_gain: float32 [256], P('fsdp')
- grad_attn_out_gain: float32 [2048], P('fsdp')
- grad_laurel_gain: float32 [2048], P('fsdp')
- grad_ffn_in_gain: float32 [2048], P('fsdp')
- grad_ffn_out_gain: float32 [2048], P('fsdp')
- grad_ple_gain: float32 [2048], P('fsdp')
The draws below stay inside these ranges and needn't reach their ends.
Inputs may be any that keep to these rules, and one draw needn't show every extreme that they name: `doc_lengths`: the 7 lengths are in token order and sum to 4096; the first (6) // 2 and the last (6) // 2 are each at most 21. Each document's positions start at 0 at its first token and rise by 1 or 2 from one token to the next.
All inputs are finite; a program needn't handle non-finite values.
Results may differ from the reference program's by a relative error of at most 0.025.
Values may be sent and summed in bfloat16 or wider, within the bound.
A program may use at most 256 MiB of HBM per device.

```python
import math
import jax
import jax.numpy as jnp
from jax import lax

D = 2048
HQ = 8
KV = 2
HD = 256
FF = 8192
LAUREL = 64
PLE = 256
TOK_DEV = 128
WINDOW = 1024
NDOC = 7
TOKENS = 4096


def doc_layout(key):
    side_count = (NDOC - 1) // 2
    head_docs = jax.random.randint(jax.random.fold_in(key, 11), (side_count,), 1, TOK_DEV // 6 + 1)
    tail_docs = jax.random.randint(jax.random.fold_in(key, 12), (side_count,), 1, TOK_DEV // 6 + 1)
    middle_doc = TOKENS - jnp.sum(head_docs) - jnp.sum(tail_docs)
    return jnp.concatenate([head_docs, middle_doc[None], tail_docs]).astype(jnp.int32)


def draw_doc_lengths(key, part):
    lengths = doc_layout(key)
    return lengths


def draw_positions(key, part):
    lengths = doc_layout(key)
    key = jax.random.fold_in(key, 2)
    steps_up = jax.random.randint(key, (TOKENS,), 1, 3).astype(jnp.int32)
    doc_ends = jnp.cumsum(lengths).astype(jnp.int32)
    places = jnp.arange(TOKENS, dtype=jnp.int32)
    doc_ids = jnp.sum((places[:, None] >= doc_ends[None, :-1]).astype(jnp.int32), axis=1)
    doc_starts = (doc_ends - lengths)[doc_ids]
    middle_index = (NDOC - 1) // 2
    in_middle = (doc_ids == middle_index) & (places != doc_starts)
    shuffled = jax.random.permutation(jax.random.fold_in(key, 5), TOKENS).astype(jnp.int32)
    sort_keys = jnp.where(in_middle, shuffled, TOKENS + shuffled).astype(jnp.int32)
    order = jnp.argsort(sort_keys, stable=True).astype(jnp.int32)
    doubled = TOKENS - lengths[middle_index]
    rank_steps = jnp.where(places < doubled, 2, 1).astype(jnp.int32)
    middle_steps = jnp.zeros((TOKENS,), jnp.int32).at[order].set(rank_steps)
    steps_up = jnp.where(in_middle, middle_steps, steps_up).astype(jnp.int32)
    climbed = jnp.cumsum(steps_up).astype(jnp.int32)
    return (climbed - climbed[doc_starts]).astype(jnp.int32)


def raised(values, own_key, source, target, parts, factor):
    def block_of(dim):
        return (jnp.arange(values.shape[dim]) // (values.shape[dim] // parts)).reshape((-1,) + (1,) * (values.ndim - 1 - dim))

    first = jax.random.permutation(own_key, parts)[block_of(target)]
    other_side = (block_of(target) + parts // 2) % parts
    return jnp.where((block_of(source) == first) | (block_of(source) == other_side), factor * values, values)


def block_levels(key, shape, split, least, largest):
    loudness, own = 1.0, jax.random.fold_in(key, 6)
    for axis_at, parts in split:
        draws = jnp.exp(jax.random.uniform(jax.random.fold_in(own, axis_at), (parts,), jnp.float32, least / len(split), largest / len(split)))
        loudness = loudness * jnp.repeat(draws, shape[axis_at] // parts).reshape([-1 if axis == axis_at else 1 for axis in range(len(shape))])
    return loudness


def noise(key, dims, scale, most, pieces=(), kind=jnp.bfloat16):
    values = scale * jax.random.normal(key, dims, jnp.float32)
    if pieces:
        values = values * block_levels(key, dims, pieces, -0.22, 0.18)
    return jnp.clip(values, -most, most).astype(kind)


def gaussian_with(rng, shape, deviation, limit, cuts, heavy, kind=jnp.bfloat16):
    result = deviation * jax.random.normal(rng, shape, jnp.float32)
    if cuts:
        result = result * block_levels(rng, shape, cuts, -0.22, 0.18)
    return jnp.clip(raised(result, jax.random.fold_in(rng, 3), *heavy), -limit, limit).astype(kind)


def setup_inputs(seed: int = 0) -> dict:
    keys = jax.random.split(jax.random.key(seed), 25)
    return {
        "tokens": gaussian_with(keys[0], (TOKENS, D), 1.0, 6.0, ((0, 32),), (0, 1, 32, 2.75)),
        "per_layer": noise(keys[1], (TOKENS, PLE), 1.0, 6.0, ((0, 32),)),
        "cotangent": noise(keys[2], (TOKENS, D), 1.0, 6.0, ((0, 32),)),
        "doc_lengths": draw_doc_lengths(jax.random.fold_in(keys[24], 71), 0),
        "positions": draw_positions(jax.random.fold_in(keys[24], 71), 0),
        "w_query": noise(keys[5], (D, HQ * HD), D ** -0.5, 0.125, ((0, 8),), jnp.float32),
        "w_key": noise(keys[6], (D, KV * HD), D ** -0.5, 0.125, ((0, 8),), jnp.float32),
        "w_value": noise(keys[7], (D, KV * HD), D ** -0.5, 0.125, ((0, 8),), jnp.float32),
        "w_out": noise(keys[8], (HQ * HD, D), (HQ * HD) ** -0.5, 0.125, ((0, 8),), jnp.float32),
        "laurel_left": noise(keys[9], (D, LAUREL), D ** -0.5, 0.125, ((0, 8),), jnp.float32),
        "laurel_right": noise(keys[10], (LAUREL, D), LAUREL ** -0.5, 0.75, ((0, 8),), jnp.float32),
        "w_gate": noise(keys[11], (D, FF), D ** -0.5, 0.125, ((0, 8),), jnp.float32),
        "w_up": noise(keys[12], (D, FF), D ** -0.5, 0.125, ((0, 8),), jnp.float32),
        "w_down": noise(keys[13], (FF, D), FF ** -0.5, 0.0625, ((0, 8),), jnp.float32),
        "ple_gate": noise(keys[14], (D, PLE), D ** -0.5, 0.125, ((0, 8),), jnp.float32),
        "ple_proj": noise(keys[15], (PLE, D), PLE ** -0.5, 0.375, ((0, 8),), jnp.float32),
        "attn_in_gain": jnp.clip(1.0 + 0.15 * jax.random.normal(keys[16], (D,), jnp.float32), 0.25, 1.75),
        "query_gain": jnp.clip(1.0 + 0.15 * jax.random.normal(keys[17], (HD,), jnp.float32), 0.25, 1.75),
        "key_gain": jnp.clip(1.0 + 0.15 * jax.random.normal(keys[18], (HD,), jnp.float32), 0.25, 1.75),
        "attn_out_gain": jnp.clip(1.0 + 0.15 * jax.random.normal(keys[19], (D,), jnp.float32), 0.25, 1.75),
        "laurel_gain": jnp.clip(1.0 + 0.15 * jax.random.normal(keys[20], (D,), jnp.float32), 0.25, 1.75),
        "ffn_in_gain": jnp.clip(1.0 + 0.15 * jax.random.normal(keys[21], (D,), jnp.float32), 0.25, 1.75),
        "ffn_out_gain": jnp.clip(1.0 + 0.15 * jax.random.normal(keys[22], (D,), jnp.float32), 0.25, 1.75),
        "ple_gain": jnp.clip(1.0 + 0.15 * jax.random.normal(keys[23], (D,), jnp.float32), 0.25, 1.75),
    }


EPSILON = 1e-06
NEGATIVE = -1e+30
ROPE_BASE = 10000.0
HALF_ROOT = 1.0 / math.sqrt(2.0)
QUERY_BLOCK = 512

@jax.custom_vjp
def low(v):
    return lax.optimization_barrier(v.astype(jnp.bfloat16)).astype(jnp.float32)

@jax.custom_vjp
def low_back(v):
    return v

def low_keep(v):
    return (low(v), None)

def low_pass(kept, grad):
    return (grad,)

def back_keep(v):
    return (v, None)

def back_low(kept, grad):
    return (low(grad),)
low.defvjp(low_keep, low_pass)
low_back.defvjp(back_keep, back_low)

def hi_dot(left_mat, right_mat):
    return jnp.dot(left_mat, right_mat, precision=lax.Precision.HIGHEST, preferred_element_type=jnp.float32)

def rms_norm(values, gain_vec):
    return values * lax.rsqrt(lax.optimization_barrier(jnp.mean(values * values, axis=-1, keepdims=True)) + EPSILON) * gain_vec

def rope_tables(positions, width):
    half_width = width // 2
    frequency = jnp.exp(jnp.arange(half_width, dtype=jnp.float32) * (-2.0 * math.log(ROPE_BASE) / width))
    angles = positions.astype(jnp.float32)[:, None] * frequency[None, :]
    return (jnp.cos(angles)[:, None, :], jnp.sin(angles)[:, None, :])

def rotate(values, cosine, sine_part):
    half_width = values.shape[-1] // 2
    first_half = values[..., :half_width]
    second_half = values[..., half_width:]
    return jnp.concatenate([first_half * cosine - second_half * sine_part, second_half * cosine + first_half * sine_part], axis=-1)

def document_ids(doc_lengths, places):
    doc_ends = jnp.cumsum(doc_lengths).astype(jnp.int32)
    return lax.optimization_barrier(jnp.sum((places[:, None] >= doc_ends[None, :-1]).astype(jnp.int32), axis=1)).astype(jnp.int32)

def attention(query_use, key_use, value_use, doc_ids):
    tok_total = query_use.shape[0]
    span_len = WINDOW + QUERY_BLOCK
    key_pad = jnp.pad(key_use, ((WINDOW, 0), (0, 0), (0, 0)))
    value_pad = jnp.pad(value_use, ((WINDOW, 0), (0, 0), (0, 0)))
    doc_pad = jnp.pad(doc_ids, (WINDOW, 0), constant_values=-1)
    scale_factor = 1.0 / math.sqrt(HD)

    @jax.checkpoint
    def one_block(block_start):
        queries = lax.dynamic_slice_in_dim(query_use, block_start, QUERY_BLOCK, 0)
        keys_here = lax.dynamic_slice_in_dim(key_pad, block_start, span_len, 0)
        values_here = lax.dynamic_slice_in_dim(value_pad, block_start, span_len, 0)
        query_docs = lax.dynamic_slice_in_dim(doc_ids, block_start, QUERY_BLOCK, 0)
        key_docs = lax.dynamic_slice_in_dim(doc_pad, block_start, span_len, 0)
        query_places = block_start + jnp.arange(QUERY_BLOCK, dtype=jnp.int32)
        key_places = block_start - WINDOW + jnp.arange(span_len, dtype=jnp.int32)
        distance = query_places[:, None] - key_places[None, :]
        visible = (distance >= 0) & (distance < WINDOW) & (query_docs[:, None] == key_docs[None, :])
        scores = jnp.einsum('tkgh,skh->kgts', queries, keys_here, precision=lax.Precision.HIGHEST) * scale_factor
        scores = jnp.where(visible, low_back(scores), NEGATIVE)
        row_top = lax.optimization_barrier(jnp.max(scores, axis=-1, keepdims=True))
        shifted = jnp.exp(scores - row_top)
        attn_probs = shifted / lax.optimization_barrier(jnp.sum(shifted, axis=-1, keepdims=True))
        attended = jnp.einsum('kgts,skh->tkgh', low(attn_probs), values_here, precision=lax.Precision.HIGHEST)
        return attended.reshape(QUERY_BLOCK, -1)
    block_starts = jnp.arange(tok_total // QUERY_BLOCK, dtype=jnp.int32) * QUERY_BLOCK
    return lax.map(one_block, block_starts).reshape(tok_total, -1)

def layer(inputs, ple_input, w_query, w_key, w_value, w_out, laurel_left, laurel_right, w_gate, w_up, w_down, ple_gate, ple_proj, gain_in, gain_query, gain_key, gain_post, gain_laurel, gain_ffin, gain_ffout, gain_ple, cosine, sine_part, doc_ids):
    tok_total = inputs.shape[0]
    normed = rms_norm(inputs, gain_in)
    normed_low = low(normed)
    query_lin = low_back(hi_dot(normed_low, low(w_query)))
    key_lin = low_back(hi_dot(normed_low, low(w_key)))
    value_lin = low_back(hi_dot(normed_low, low(w_value)))
    query_rot = rotate(rms_norm(query_lin.reshape(tok_total, HQ, HD), gain_query), cosine, sine_part)
    key_rot = rotate(rms_norm(key_lin.reshape(tok_total, KV, HD), gain_key), cosine, sine_part)
    query_use = low(query_rot).reshape(tok_total, KV, HQ // KV, HD)
    key_use = low(key_rot)
    value_use = low(value_lin).reshape(tok_total, KV, HD)
    attended = low(low_back(attention(query_use, key_use, value_use, doc_ids)))
    projected = low_back(hi_dot(attended, low(w_out)))
    narrow = low(low_back(hi_dot(normed_low, low(laurel_left))))
    widened = low_back(hi_dot(narrow, low(laurel_right)))
    mixed = (inputs + rms_norm(projected, gain_post) + normed + rms_norm(widened, gain_laurel)) * HALF_ROOT
    ffn_low = low(rms_norm(mixed, gain_ffin))
    gate_lin = low_back(hi_dot(ffn_low, low(w_gate)))
    up_lin = low_back(hi_dot(ffn_low, low(w_up)))
    hidden = low(jax.nn.gelu(gate_lin, approximate=True) * up_lin)
    down_lin = low_back(hi_dot(hidden, low(w_down)))
    layer_mid = mixed + rms_norm(down_lin, gain_ffout)
    layer_low = low(layer_mid)
    ple_lin = low_back(hi_dot(layer_low, low(ple_gate)))
    ple_mid = low(jax.nn.gelu(ple_lin, approximate=True) * ple_input)
    ple_wide = low_back(hi_dot(ple_mid, low(ple_proj)))
    return layer_mid + rms_norm(ple_wide, gain_ple)

def reference(tokens, per_layer, cotangent, doc_lengths, positions, w_query, w_key, w_value, w_out, laurel_left, laurel_right, w_gate, w_up, w_down, ple_gate, ple_proj, attn_in_gain, query_gain, key_gain, attn_out_gain, laurel_gain, ffn_in_gain, ffn_out_gain, ple_gain):
    places = jnp.arange(tokens.shape[0], dtype=jnp.int32)
    doc_ids = document_ids(doc_lengths, places)
    cosine, sine_part = rope_tables(positions, HD)

    def forward(inputs, ple_input, *params):
        return layer(inputs, ple_input, *params, cosine, sine_part, doc_ids)
    out_full, pullback = jax.vjp(forward, tokens.astype(jnp.float32), per_layer.astype(jnp.float32), w_query, w_key, w_value, w_out, laurel_left, laurel_right, w_gate, w_up, w_down, ple_gate, ple_proj, attn_in_gain, query_gain, key_gain, attn_out_gain, laurel_gain, ffn_in_gain, ffn_out_gain, ple_gain)
    grads = pullback(cotangent.astype(jnp.float32))
    return (out_full.astype(jnp.bfloat16), grads[0], grads[1], grads[2], grads[3], grads[4], grads[5], grads[6], grads[7], grads[8], grads[9], grads[10], grads[11], grads[12], grads[13], grads[14], grads[15], grads[16], grads[17], grads[18], grads[19], grads[20])
```

```python
import functools
import math

import jax
import jax.numpy as jnp
from jax import lax
from jax.sharding import PartitionSpec as P

HQ = 8
KV = 2
HD = 256
WINDOW = 1024


EPSILON = 1e-06
NEGATIVE = -1e30
ROPE_BASE = 10000.0
HALF_ROOT = 1.0 / math.sqrt(2.0)


def passed_along(block, axis, distance):
    devices = range(lax.axis_size(axis))
    route = [(i - distance, i) for i in devices if i - distance in devices]
    return lax.ppermute(block, axis, route)


def matmul(left_mat, right_mat):
    return jnp.dot(left_mat, right_mat, preferred_element_type=jnp.float32)


def matmul_tn(left_mat, right_mat):
    return lax.dot_general(
        left_mat, right_mat, (((0,), (0,)), ((), ())), preferred_element_type=jnp.float32
    )


def matmul_nt(left_mat, right_mat):
    return lax.dot_general(
        left_mat, right_mat, (((1,), (1,)), ((), ())), preferred_element_type=jnp.float32
    )


def rms_norm(values, gain_vec):
    return (
        values * lax.rsqrt(jnp.mean(values * values, axis=-1, keepdims=True) + EPSILON) * gain_vec
    )


def rope_tables(positions, width):
    half_width = width // 2
    frequency = jnp.exp(
        jnp.arange(half_width, dtype=jnp.float32) * (-2.0 * math.log(ROPE_BASE) / width)
    )
    angles = positions.astype(jnp.float32)[:, None] * frequency[None, :]
    return (jnp.cos(angles)[:, None, :], jnp.sin(angles)[:, None, :])


def rotate(values, cosine, sine_part):
    half_width = values.shape[-1] // 2
    first_half = values[..., :half_width]
    second_half = values[..., half_width:]
    return jnp.concatenate(
        [
            first_half * cosine - second_half * sine_part,
            second_half * cosine + first_half * sine_part,
        ],
        axis=-1,
    )


def document_ids(doc_lengths, places):
    doc_ends = jnp.cumsum(doc_lengths)
    return jnp.sum((places[:, None] >= doc_ends[None, :-1]).astype(jnp.int32), axis=1)


def query_key(cosine, sine_part, query_lin, key_lin, gain_query, gain_key):
    tok_count = query_lin.shape[0]
    query_rot = rotate(
        rms_norm(query_lin.reshape(tok_count, HQ, HD), gain_query), cosine, sine_part
    )
    key_rot = rotate(rms_norm(key_lin.reshape(tok_count, KV, HD), gain_key), cosine, sine_part)
    return (query_rot, key_rot)


def mix_piece(inputs, normed, projected, widened, gain_post, gain_laurel):
    return (
        inputs + rms_norm(projected, gain_post) + normed + rms_norm(widened, gain_laurel)
    ) * HALF_ROOT


def geglu(gate_lin, up_lin):
    return jax.nn.gelu(gate_lin, approximate=True) * up_lin


def ffn_out_piece(mixed, down_lin, gain_ffout):
    return mixed + rms_norm(down_lin, gain_ffout)


def ple_act(ple_lin, ple_input):
    return jax.nn.gelu(ple_lin, approximate=True) * ple_input


def final_piece(layer_mid, ple_wide, gain_ple):
    return layer_mid + rms_norm(ple_wide, gain_ple)


def visibility(doc_lengths, query_start, key_start, tok_count, span_len):
    query_places = query_start + jnp.arange(tok_count, dtype=jnp.int32)
    key_places = key_start + jnp.arange(span_len, dtype=jnp.int32)
    distance = query_places[:, None] - key_places[None, :]
    query_docs = document_ids(doc_lengths, query_places)
    key_docs = document_ids(doc_lengths, key_places)
    return (
        (distance >= 0)
        & (distance < WINDOW)
        & (key_places[None, :] >= 0)
        & (query_docs[:, None] == key_docs[None, :])
    )


def attend_forward(query_low, span_kv, visible):
    tok_count = query_low.shape[0]
    scale_factor = 1.0 / math.sqrt(HD)
    scores = (
        jnp.einsum("tkgh,skh->kgts", query_low, span_kv[0], preferred_element_type=jnp.float32)
        * scale_factor
    )
    scores = jnp.where(visible, scores, NEGATIVE)
    row_top = jnp.max(scores, axis=-1, keepdims=True)
    shifted = jnp.exp(scores - row_top)
    row_total = jnp.sum(shifted, axis=-1, keepdims=True)
    attn_probs = shifted / row_total
    attended = jnp.einsum(
        "kgts,skh->tkgh",
        attn_probs.astype(jnp.bfloat16),
        span_kv[1],
        preferred_element_type=jnp.float32,
    )
    return (attended.reshape(tok_count, -1), row_top + jnp.log(row_total))


def attend_backward(query_low, span_kv, visible, log_total, grad_out_low):
    scale_factor = 1.0 / math.sqrt(HD)
    scores = (
        jnp.einsum("tkgh,skh->kgts", query_low, span_kv[0], preferred_element_type=jnp.float32)
        * scale_factor
    )
    attn_probs = jnp.where(visible, jnp.exp(jnp.where(visible, scores, NEGATIVE) - log_total), 0.0)
    grad_probs = jnp.einsum(
        "tkgh,skh->kgts", grad_out_low, span_kv[1], preferred_element_type=jnp.float32
    )
    inner_sum = jnp.sum(attn_probs * grad_probs, axis=-1, keepdims=True)
    grad_scores = (attn_probs * (grad_probs - inner_sum)).astype(jnp.bfloat16)
    grad_query = (
        jnp.einsum("kgts,skh->tkgh", grad_scores, span_kv[0], preferred_element_type=jnp.float32)
        * scale_factor
    )
    grad_keys = (
        jnp.einsum("kgts,tkgh->skh", grad_scores, query_low, preferred_element_type=jnp.float32)
        * scale_factor
    )
    grad_values = jnp.einsum(
        "kgts,tkgh->skh",
        attn_probs.astype(jnp.bfloat16),
        grad_out_low,
        preferred_element_type=jnp.float32,
    )
    return (grad_query, jnp.stack([grad_keys, grad_values]))


def settle(act_low, grad_low):
    act_cols = lax.all_to_all(act_low, "fsdp", split_axis=1, concat_axis=0, tiled=True)
    shard_rows = matmul_tn(act_cols, lax.all_gather(grad_low, "fsdp", axis=0, tiled=True))
    return lax.psum(shard_rows.astype(jnp.bfloat16), "ctx").astype(jnp.float32)


def local(
    tokens,
    per_layer,
    cotangent,
    doc_lengths,
    positions,
    w_query,
    w_key,
    w_value,
    w_out,
    laurel_left,
    laurel_right,
    w_gate,
    w_up,
    w_down,
    ple_gate,
    ple_proj,
    attn_in_gain,
    query_gain,
    key_gain,
    attn_out_gain,
    laurel_gain,
    ffn_in_gain,
    ffn_out_gain,
    ple_gain,
):
    bfloat = jnp.bfloat16
    tok_count = tokens.shape[0]
    span_len = WINDOW + tok_count
    groups = HQ // KV
    dev_index = lax.axis_index("ctx") * lax.axis_size("fsdp") + lax.axis_index("fsdp")
    query_start = dev_index * tok_count
    key_start = query_start - WINDOW
    visible = visibility(doc_lengths, query_start, key_start, tok_count, span_len)
    cosine, sine_part = rope_tables(positions, HD)
    gain_in, gain_query, gain_key, gain_post, gain_laurel, gain_ffin, gain_ffout, gain_ple = (
        lax.all_gather(attn_in_gain, "fsdp", axis=0, tiled=True),
        lax.all_gather(query_gain, "fsdp", axis=0, tiled=True),
        lax.all_gather(key_gain, "fsdp", axis=0, tiled=True),
        lax.all_gather(attn_out_gain, "fsdp", axis=0, tiled=True),
        lax.all_gather(laurel_gain, "fsdp", axis=0, tiled=True),
        lax.all_gather(ffn_in_gain, "fsdp", axis=0, tiled=True),
        lax.all_gather(ffn_out_gain, "fsdp", axis=0, tiled=True),
        lax.all_gather(ple_gain, "fsdp", axis=0, tiled=True),
    )
    full_query, full_key, full_value, full_out, full_left, full_right = (
        lax.all_gather(w_query.astype(bfloat), "fsdp", axis=0, tiled=True),
        lax.all_gather(w_key.astype(bfloat), "fsdp", axis=0, tiled=True),
        lax.all_gather(w_value.astype(bfloat), "fsdp", axis=0, tiled=True),
        lax.all_gather(w_out.astype(bfloat), "fsdp", axis=0, tiled=True),
        lax.all_gather(laurel_left.astype(bfloat), "fsdp", axis=0, tiled=True),
        lax.all_gather(laurel_right.astype(bfloat), "fsdp", axis=0, tiled=True),
    )
    inputs = tokens.astype(jnp.float32)
    ple_input = per_layer.astype(jnp.float32)
    normed, norm_back = jax.vjp(rms_norm, inputs, gain_in)
    normed_low = normed.astype(bfloat)
    query_lin = matmul(normed_low, full_query)
    key_lin = matmul(normed_low, full_key)
    value_lin = matmul(normed_low, full_value)
    (query_rot, key_rot), rope_back = jax.vjp(
        functools.partial(query_key, cosine, sine_part), query_lin, key_lin, gain_query, gain_key
    )
    query_low = query_rot.astype(bfloat).reshape(tok_count, KV, groups, HD)
    keys_values = jnp.stack(
        [key_rot.astype(bfloat), value_lin.astype(bfloat).reshape(tok_count, KV, HD)]
    )
    block_kv = lax.all_gather(keys_values, "fsdp", axis=1, tiled=True)
    block_len = block_kv.shape[1]
    before_kv = passed_along(block_kv, "ctx", 1)
    span_offset = block_len + lax.axis_index("fsdp") * tok_count - WINDOW
    span_kv = lax.dynamic_slice_in_dim(
        jnp.concatenate([before_kv, block_kv], axis=1), span_offset, span_len, 1
    )
    attended, log_total = attend_forward(query_low, span_kv, visible)
    attended_low = attended.astype(bfloat)
    projected = matmul(attended_low, full_out)
    narrow_low = matmul(normed_low, full_left).astype(bfloat)
    widened = matmul(narrow_low, full_right)
    mixed, mix_back = jax.vjp(mix_piece, inputs, normed, projected, widened, gain_post, gain_laurel)
    full_gate, full_up, full_down, full_pgate, full_pproj = (
        lax.all_gather(w_gate.astype(bfloat), "fsdp", axis=0, tiled=True),
        lax.all_gather(w_up.astype(bfloat), "fsdp", axis=0, tiled=True),
        lax.all_gather(w_down.astype(bfloat), "fsdp", axis=0, tiled=True),
        lax.all_gather(ple_gate.astype(bfloat), "fsdp", axis=0, tiled=True),
        lax.all_gather(ple_proj.astype(bfloat), "fsdp", axis=0, tiled=True),
    )
    ffn_normed, ffn_norm_back = jax.vjp(rms_norm, mixed, gain_ffin)
    ffn_low = ffn_normed.astype(bfloat)
    gate_lin = matmul(ffn_low, full_gate)
    up_lin = matmul(ffn_low, full_up)
    hidden, geglu_back = jax.vjp(geglu, gate_lin, up_lin)
    hidden_low = hidden.astype(bfloat)
    down_lin = matmul(hidden_low, full_down)
    layer_mid, ffn_out_back = jax.vjp(ffn_out_piece, mixed, down_lin, gain_ffout)
    layer_low = layer_mid.astype(bfloat)
    ple_lin = matmul(layer_low, full_pgate)
    ple_mid, ple_back = jax.vjp(ple_act, ple_lin, ple_input)
    ple_low = ple_mid.astype(bfloat)
    ple_wide = matmul(ple_low, full_pproj)
    out_full, final_back = jax.vjp(final_piece, layer_mid, ple_wide, gain_ple)
    full_gate, full_up, full_down, full_pgate, full_pproj = (
        lax.all_gather(w_gate.astype(bfloat), "fsdp", axis=0, tiled=True),
        lax.all_gather(w_up.astype(bfloat), "fsdp", axis=0, tiled=True),
        lax.all_gather(w_down.astype(bfloat), "fsdp", axis=0, tiled=True),
        lax.all_gather(ple_gate.astype(bfloat), "fsdp", axis=0, tiled=True),
        lax.all_gather(ple_proj.astype(bfloat), "fsdp", axis=0, tiled=True),
    )
    grad_layer, grad_pwide, grad_gple = final_back(cotangent.astype(jnp.float32))
    grad_pwide_low = grad_pwide.astype(bfloat)
    grad_pproj = settle(ple_low, grad_pwide_low)
    grad_plemid = matmul_nt(grad_pwide_low, full_pproj)
    grad_plelin, grad_pleinput = ple_back(grad_plemid)
    grad_plelin_low = grad_plelin.astype(bfloat)
    grad_pgate = settle(layer_low, grad_plelin_low)
    grad_layer = grad_layer + matmul_nt(grad_plelin_low, full_pgate)
    grad_mixed, grad_down, grad_gffout = ffn_out_back(grad_layer)
    grad_down_low = grad_down.astype(bfloat)
    grad_wdown = settle(hidden_low, grad_down_low)
    grad_hidden = matmul_nt(grad_down_low, full_down)
    grad_gate, grad_up = geglu_back(grad_hidden)
    grad_gate_low = grad_gate.astype(bfloat)
    grad_up_low = grad_up.astype(bfloat)
    grad_wgate = settle(ffn_low, grad_gate_low)
    grad_wup = settle(ffn_low, grad_up_low)
    grad_ffn = matmul_nt(grad_gate_low, full_gate) + matmul_nt(grad_up_low, full_up)
    grad_mixed_more, grad_gffin = ffn_norm_back(grad_ffn)
    grad_mixed = grad_mixed + grad_mixed_more
    full_query, full_key, full_value, full_out, full_left, full_right = (
        lax.all_gather(w_query.astype(bfloat), "fsdp", axis=0, tiled=True),
        lax.all_gather(w_key.astype(bfloat), "fsdp", axis=0, tiled=True),
        lax.all_gather(w_value.astype(bfloat), "fsdp", axis=0, tiled=True),
        lax.all_gather(w_out.astype(bfloat), "fsdp", axis=0, tiled=True),
        lax.all_gather(laurel_left.astype(bfloat), "fsdp", axis=0, tiled=True),
        lax.all_gather(laurel_right.astype(bfloat), "fsdp", axis=0, tiled=True),
    )
    grad_in_first, grad_normed, grad_proj, grad_lwide, grad_gpost, grad_glaurel = mix_back(
        grad_mixed
    )
    grad_proj_low = grad_proj.astype(bfloat)
    grad_wout = settle(attended_low, grad_proj_low)
    grad_att_low = matmul_nt(grad_proj_low, full_out).astype(bfloat)
    grad_lwide_low = grad_lwide.astype(bfloat)
    grad_wright = settle(narrow_low, grad_lwide_low)
    grad_narrow_low = matmul_nt(grad_lwide_low, full_right).astype(bfloat)
    grad_wleft = settle(normed_low, grad_narrow_low)
    grad_normed = grad_normed + matmul_nt(grad_narrow_low, full_left)
    grad_query_att, grad_span = attend_backward(
        query_low, span_kv, visible, log_total, grad_att_low.reshape(tok_count, KV, groups, HD)
    )
    whole_grad = jnp.zeros((2, 2 * block_len, KV, HD), jnp.float32)
    whole_grad = lax.dynamic_update_slice_in_dim(whole_grad, grad_span, span_offset, 1)
    returned = passed_along(whole_grad[:, :block_len].astype(jnp.bfloat16), "ctx", -1).astype(
        jnp.float32
    )
    own_grad = lax.psum_scatter(
        (whole_grad[:, block_len:] + returned).astype(jnp.bfloat16),
        "fsdp",
        scatter_dimension=1,
        tiled=True,
    ).astype(jnp.float32)
    grad_qlin, grad_klin, grad_gquery, grad_gkey = rope_back(
        (grad_query_att.reshape(tok_count, HQ, HD), own_grad[0])
    )
    grad_qlin_low = grad_qlin.astype(bfloat)
    grad_klin_low = grad_klin.astype(bfloat)
    grad_vlin_low = own_grad[1].reshape(tok_count, KV * HD).astype(bfloat)
    grad_wquery = settle(normed_low, grad_qlin_low)
    grad_wkey = settle(normed_low, grad_klin_low)
    grad_wvalue = settle(normed_low, grad_vlin_low)
    grad_normed = (
        grad_normed
        + matmul_nt(grad_qlin_low, full_query)
        + matmul_nt(grad_klin_low, full_key)
        + matmul_nt(grad_vlin_low, full_value)
    )
    grad_in_second, grad_gin = norm_back(grad_normed)
    grad_tokens = grad_in_first + grad_in_second
    sum_gin, sum_gquery, sum_gkey, sum_gpost, sum_glaurel, sum_gffin, sum_gffout, sum_gple = (
        lax.psum(
            (
                grad_gin,
                grad_gquery,
                grad_gkey,
                grad_gpost,
                grad_glaurel,
                grad_gffin,
                grad_gffout,
                grad_gple,
            ),
            ("ctx", "fsdp"),
        )
    )
    wide_rows = attn_in_gain.shape[0]
    head_rows = query_gain.shape[0]
    wide_start = lax.axis_index("fsdp") * wide_rows
    head_start = lax.axis_index("fsdp") * head_rows

    def wide_part(full_vec):
        return lax.dynamic_slice_in_dim(full_vec, wide_start, wide_rows, 0)

    def head_part(full_vec):
        return lax.dynamic_slice_in_dim(full_vec, head_start, head_rows, 0)

    return (
        out_full.astype(bfloat),
        grad_tokens,
        grad_pleinput,
        grad_wquery,
        grad_wkey,
        grad_wvalue,
        grad_wout,
        grad_wleft,
        grad_wright,
        grad_wgate,
        grad_wup,
        grad_wdown,
        grad_pgate,
        grad_pproj,
        wide_part(sum_gin),
        head_part(sum_gquery),
        head_part(sum_gkey),
        wide_part(sum_gpost),
        wide_part(sum_glaurel),
        wide_part(sum_gffin),
        wide_part(sum_gffout),
        wide_part(sum_gple),
    )

def to_columns(pieces, ctx_count):
    packed = jnp.concatenate(pieces, axis=2)
    quarter = packed.shape[0] // ctx_count
    start = lax.axis_index("ctx") * quarter
    mine = lax.dynamic_slice_in_dim(packed, start, quarter, 0).astype(jnp.bfloat16)
    spread = lax.all_to_all(mine, "fsdp", split_axis=1, concat_axis=0, tiled=False)
    whole = lax.all_gather(spread, "ctx", axis=1, tiled=True)
    return whole.reshape(-1, whole.shape[-1])


def to_rows(partial, fsdp_count):
    parts = partial.astype(jnp.bfloat16).reshape(fsdp_count, -1, partial.shape[-1])
    summed = lax.psum_scatter(parts, "ctx", scatter_dimension=1, tiled=True)
    swapped = lax.all_to_all(summed, "fsdp", split_axis=0, concat_axis=1, tiled=False)
    return swapped


def gather_rows(part):
    return lax.all_gather(part, "ctx", axis=0, tiled=True).astype(jnp.float32)


def scatter_tokens(partial):
    return lax.psum_scatter(
        partial.astype(jnp.bfloat16), "fsdp", scatter_dimension=0, tiled=True
    ).astype(jnp.float32)


def gather_tokens(part):
    return lax.all_gather(part, "fsdp", axis=0, tiled=True)


def small_sum(partial):
    rows = lax.psum_scatter(partial.astype(jnp.bfloat16), "fsdp", scatter_dimension=0, tiled=True)
    return lax.psum(rows, "ctx").astype(jnp.float32)


def row_sum(partial):
    return lax.psum(partial.astype(jnp.bfloat16), "ctx").astype(jnp.float32)


def head_rope(cosine, sine_part, lin, gain_vec):
    return rotate(rms_norm(lin, gain_vec), cosine, sine_part)


def by_heads(
    tokens,
    per_layer,
    cotangent,
    doc_lengths,
    positions,
    w_query,
    w_key,
    w_value,
    w_out,
    laurel_left,
    laurel_right,
    w_gate,
    w_up,
    w_down,
    ple_gate,
    ple_proj,
    attn_in_gain,
    query_gain,
    key_gain,
    attn_out_gain,
    laurel_gain,
    ffn_in_gain,
    ffn_out_gain,
    ple_gain,
):
    bfloat = jnp.bfloat16
    ctx_count = lax.axis_size("ctx")
    fsdp_count = lax.axis_size("fsdp")
    tok_count = tokens.shape[0]
    block_len = tok_count * fsdp_count
    rows = w_query.shape[0]
    ff_part = w_gate.shape[1] // fsdp_count
    scale_factor = 1.0 / math.sqrt(HD)
    ctx_at = lax.axis_index("ctx")
    fsdp_at = lax.axis_index("fsdp")

    gain_list = [
        attn_in_gain,
        query_gain,
        key_gain,
        attn_out_gain,
        laurel_gain,
        ffn_in_gain,
        ffn_out_gain,
        ple_gain,
    ]
    gain_sizes = [g.shape[0] for g in gain_list]
    gain_offsets = [sum(gain_sizes[:n]) for n in range(len(gain_sizes) + 1)]
    all_gains = lax.all_gather(jnp.concatenate(gain_list), "fsdp", axis=0, tiled=False)
    gain_in, gain_query, gain_key, gain_post, gain_laurel, gain_ffin, gain_ffout, gain_ple = (
        all_gains[:, gain_offsets[n] : gain_offsets[n + 1]].reshape(-1) for n in range(8)
    )
    block_positions = lax.all_gather(positions, "fsdp", axis=0, tiled=True)
    cosine, sine_part = rope_tables(block_positions, HD)
    cosine, sine_part = cosine[:, 0], sine_part[:, 0]

    query_parts = w_query.reshape(rows, fsdp_count, HD)
    group_size = HQ // KV
    key_parts = jnp.repeat(w_key.reshape(rows, KV, HD), group_size, axis=1)
    value_parts = jnp.repeat(w_value.reshape(rows, KV, HD), group_size, axis=1)
    col_qkv = to_columns([query_parts, key_parts, value_parts], ctx_count)
    col_gateup = to_columns(
        [w_gate.reshape(rows, fsdp_count, ff_part), w_up.reshape(rows, fsdp_count, ff_part)],
        ctx_count,
    )
    out_low = w_out.astype(bfloat)
    down_low = w_down.astype(bfloat)
    full_left, full_right, full_pgate, full_pproj = (
        lax.all_gather(w.astype(bfloat), "fsdp", axis=0, tiled=True)
        for w in (laurel_left, laurel_right, ple_gate, ple_proj)
    )

    inputs = tokens.astype(jnp.float32)
    ple_input = per_layer.astype(jnp.float32)
    normed, norm_back = jax.vjp(rms_norm, inputs, gain_in)
    normed_low = normed.astype(bfloat)
    normed_all = gather_tokens(normed_low)
    qkv_lin = matmul(normed_all, col_qkv)
    query_lin, key_lin, value_lin = qkv_lin[:, :HD], qkv_lin[:, HD : 2 * HD], qkv_lin[:, 2 * HD :]
    rope_here = functools.partial(head_rope, cosine, sine_part)
    query_rot, query_back = jax.vjp(rope_here, query_lin, gain_query)
    key_rot, key_back = jax.vjp(rope_here, key_lin, gain_key)
    query_low = query_rot.astype(bfloat)
    own_kv = jnp.stack([key_rot.astype(bfloat), value_lin.astype(bfloat)])
    before_kv = passed_along(own_kv[:, block_len - WINDOW :], "ctx", 1)
    span_kv = jnp.concatenate([before_kv, own_kv], axis=1)

    chunk = 256
    span_len = WINDOW + chunk
    block_start = ctx_at * block_len
    prob_list, attended_list = [], []
    for begin in range(0, block_len, chunk):
        visible = visibility(
            doc_lengths, block_start + begin, block_start + begin - WINDOW, chunk, span_len
        )
        keys = span_kv[0, begin : begin + span_len]
        values = span_kv[1, begin : begin + span_len]
        scores = matmul_nt(query_low[begin : begin + chunk], keys) * scale_factor
        scores = jnp.where(visible, scores, NEGATIVE)
        shifted = jnp.exp(scores - jnp.max(scores, axis=-1, keepdims=True))
        probs = shifted / jnp.sum(shifted, axis=-1, keepdims=True)
        prob_list.append(probs)
        attended_list.append(matmul(probs.astype(bfloat), values))
    attended_low = jnp.concatenate(attended_list, axis=0).astype(bfloat)
    projected = scatter_tokens(matmul(attended_low, out_low))
    narrow_low = matmul(normed_low, full_left).astype(bfloat)
    widened = matmul(narrow_low, full_right)
    mixed, mix_back = jax.vjp(mix_piece, inputs, normed, projected, widened, gain_post, gain_laurel)
    ffn_normed, ffn_norm_back = jax.vjp(rms_norm, mixed, gain_ffin)
    ffn_all = gather_tokens(ffn_normed.astype(bfloat))
    gateup = matmul(ffn_all, col_gateup)
    hidden, geglu_back = jax.vjp(geglu, gateup[:, :ff_part], gateup[:, ff_part:])
    hidden_low = hidden.astype(bfloat)
    down_lin = scatter_tokens(matmul(hidden_low, down_low))
    layer_mid, ffn_out_back = jax.vjp(ffn_out_piece, mixed, down_lin, gain_ffout)
    layer_low = layer_mid.astype(bfloat)
    ple_lin = matmul(layer_low, full_pgate)
    ple_mid, ple_back = jax.vjp(ple_act, ple_lin, ple_input)
    ple_low = ple_mid.astype(bfloat)
    ple_wide = matmul(ple_low, full_pproj)
    out_full, final_back = jax.vjp(final_piece, layer_mid, ple_wide, gain_ple)

    grad_layer, grad_pwide, grad_gple = final_back(cotangent.astype(jnp.float32))
    grad_pwide_low = grad_pwide.astype(bfloat)
    grad_pproj = small_sum(matmul_tn(ple_low, grad_pwide_low))
    grad_plemid = matmul_nt(grad_pwide_low, full_pproj)
    grad_plelin, grad_pleinput = ple_back(grad_plemid)
    grad_plelin_low = grad_plelin.astype(bfloat)
    grad_pgate = small_sum(matmul_tn(layer_low, grad_plelin_low))
    grad_layer = grad_layer + matmul_nt(grad_plelin_low, full_pgate)
    grad_mixed, grad_down, grad_gffout = ffn_out_back(grad_layer)
    grad_down_all = gather_tokens(grad_down.astype(bfloat))
    grad_wdown = row_sum(matmul_tn(hidden_low, grad_down_all))
    grad_hidden = matmul_nt(grad_down_all, down_low)
    grad_gate, grad_up = geglu_back(grad_hidden)
    grad_gateup_low = jnp.concatenate([grad_gate, grad_up], axis=1).astype(bfloat)
    gateup_rows = to_rows(matmul_tn(ffn_all, grad_gateup_low), fsdp_count)
    gateup_rows = gather_rows(gateup_rows)
    grad_wgate = gateup_rows[:, :, :ff_part].reshape(rows, -1)
    grad_wup = gateup_rows[:, :, ff_part:].reshape(rows, -1)
    grad_ffn = scatter_tokens(matmul_nt(grad_gateup_low, col_gateup))
    grad_mixed_more, grad_gffin = ffn_norm_back(grad_ffn)
    grad_mixed = grad_mixed + grad_mixed_more
    grad_in_first, grad_normed, grad_proj, grad_lwide, grad_gpost, grad_glaurel = mix_back(
        grad_mixed
    )
    grad_proj_all = gather_tokens(grad_proj.astype(bfloat))
    grad_wout = row_sum(matmul_tn(attended_low, grad_proj_all))
    grad_att_low = matmul_nt(grad_proj_all, out_low).astype(bfloat)
    grad_lwide_low = grad_lwide.astype(bfloat)
    grad_wright = small_sum(matmul_tn(narrow_low, grad_lwide_low))
    grad_narrow_low = matmul_nt(grad_lwide_low, full_right).astype(bfloat)
    grad_wleft = small_sum(matmul_tn(normed_low, grad_narrow_low))
    grad_normed = grad_normed + matmul_nt(grad_narrow_low, full_left)

    grad_query_list = []
    grad_keys = jnp.zeros((WINDOW + block_len, HD), jnp.float32)
    grad_values = jnp.zeros((WINDOW + block_len, HD), jnp.float32)
    for at, begin in enumerate(range(0, block_len, chunk)):
        keys = span_kv[0, begin : begin + span_len]
        values = span_kv[1, begin : begin + span_len]
        probs = prob_list[at]
        grad_rows = grad_att_low[begin : begin + chunk]
        grad_probs = matmul_nt(grad_rows, values)
        inner_sum = jnp.sum(probs * grad_probs, axis=-1, keepdims=True)
        grad_scores = (probs * (grad_probs - inner_sum)).astype(bfloat)
        grad_query_list.append(matmul(grad_scores, keys) * scale_factor)
        grad_keys = grad_keys.at[begin : begin + span_len].add(
            matmul_tn(grad_scores, query_low[begin : begin + chunk]) * scale_factor
        )
        grad_values = grad_values.at[begin : begin + span_len].add(
            matmul_tn(probs.astype(bfloat), grad_rows)
        )
    returned = passed_along(
        jnp.stack([grad_keys[:WINDOW], grad_values[:WINDOW]]).astype(bfloat), "ctx", -1
    ).astype(jnp.float32)
    returned = jnp.pad(returned, ((0, 0), (block_len - WINDOW, 0), (0, 0)))
    grad_qlin, grad_gquery = query_back(jnp.concatenate(grad_query_list, axis=0))
    grad_klin, grad_gkey = key_back(grad_keys[WINDOW:] + returned[0])
    grad_vlin = grad_values[WINDOW:] + returned[1]
    grad_qkv_low = jnp.concatenate([grad_qlin, grad_klin, grad_vlin], axis=1).astype(bfloat)
    qkv_rows = to_rows(matmul_tn(normed_all, grad_qkv_low), fsdp_count)
    kv_rows = qkv_rows[:, :, HD:].astype(jnp.float32)
    kv_rows = jnp.sum(kv_rows.reshape(kv_rows.shape[0], KV, group_size, 2 * HD), axis=2)
    quarter = rows // ctx_count
    qkv_rows = gather_rows(
        jnp.concatenate(
            [
                qkv_rows[:, :, :HD].reshape(quarter, HQ * HD),
                kv_rows[:, :, :HD].reshape(quarter, KV * HD).astype(bfloat),
                kv_rows[:, :, HD:].reshape(quarter, KV * HD).astype(bfloat),
            ],
            axis=1,
        )
    )
    grad_wquery = qkv_rows[:, : HQ * HD]
    grad_wkey = qkv_rows[:, HQ * HD : (HQ + KV) * HD]
    grad_wvalue = qkv_rows[:, (HQ + KV) * HD :]
    grad_normed = grad_normed + scatter_tokens(matmul_nt(grad_qkv_low, col_qkv))
    grad_in_second, grad_gin = norm_back(grad_normed)
    grad_tokens = grad_in_first + grad_in_second

    grad_gains = [
        grad_gin,
        grad_gquery,
        grad_gkey,
        grad_gpost,
        grad_glaurel,
        grad_gffin,
        grad_gffout,
        grad_gple,
    ]
    gain_rows = jnp.concatenate([g.reshape(fsdp_count, -1) for g in grad_gains], axis=1)
    gain_sums = lax.psum(gain_rows, ("ctx", "fsdp"))
    gain_sums = lax.dynamic_index_in_dim(gain_sums, fsdp_at, 0, keepdims=False)
    return (
        out_full.astype(bfloat),
        grad_tokens,
        grad_pleinput,
        grad_wquery,
        grad_wkey,
        grad_wvalue,
        grad_wout,
        grad_wleft,
        grad_wright,
        grad_wgate,
        grad_wup,
        grad_wdown,
        grad_pgate,
        grad_pproj,
        *(gain_sums[gain_offsets[n] : gain_offsets[n + 1]] for n in range(8)),
    )


def solution(mesh):
    in_specs = (
        P(("ctx", "fsdp"), None),
        P(("ctx", "fsdp"), None),
        P(("ctx", "fsdp"), None),
        P(),
        P(("ctx", "fsdp")),
        P("fsdp", None),
        P("fsdp", None),
        P("fsdp", None),
        P("fsdp", None),
        P("fsdp", None),
        P("fsdp", None),
        P("fsdp", None),
        P("fsdp", None),
        P("fsdp", None),
        P("fsdp", None),
        P("fsdp", None),
        P("fsdp"),
        P("fsdp"),
        P("fsdp"),
        P("fsdp"),
        P("fsdp"),
        P("fsdp"),
        P("fsdp"),
        P("fsdp"),
    )
    out_specs = (
        P(("ctx", "fsdp"), None),
        P(("ctx", "fsdp"), None),
        P(("ctx", "fsdp"), None),
        P("fsdp", None),
        P("fsdp", None),
        P("fsdp", None),
        P("fsdp", None),
        P("fsdp", None),
        P("fsdp", None),
        P("fsdp", None),
        P("fsdp", None),
        P("fsdp", None),
        P("fsdp", None),
        P("fsdp", None),
        P("fsdp"),
        P("fsdp"),
        P("fsdp"),
        P("fsdp"),
        P("fsdp"),
        P("fsdp"),
        P("fsdp"),
        P("fsdp"),
    )
    run = by_heads if mesh.shape["fsdp"] == HQ else local
    return jax.shard_map(run, mesh=mesh, in_specs=in_specs, out_specs=out_specs, check_vma=False)
```

```python
import functools
import math

import jax
import jax.numpy as jnp
from jax import lax
from jax.experimental import pallas as pl
from jax.experimental.pallas import tpu as pltpu
from jax.sharding import PartitionSpec as P

HQ = 8
KV = 2
HD = 256
WINDOW = 1024


EPSILON = 1e-06
NEGATIVE = -1e30
ROPE_BASE = 10000.0
HALF_ROOT = 1.0 / math.sqrt(2.0)
GELU_ROOT = math.sqrt(2.0 / math.pi)
GELU_CUBE = 0.044715
KERNEL_VMEM = 56 << 20


def passed_along(block, axis, distance):
    devices = range(lax.axis_size(axis))
    route = [(i - distance, i) for i in devices if i - distance in devices]
    return lax.ppermute(block, axis, route)


def matmul(left_mat, right_mat):
    return jnp.dot(left_mat, right_mat, preferred_element_type=jnp.float32)


def matmul_tn(left_mat, right_mat):
    return lax.dot_general(
        left_mat, right_mat, (((0,), (0,)), ((), ())), preferred_element_type=jnp.float32
    )


def matmul_nt(left_mat, right_mat):
    return lax.dot_general(
        left_mat, right_mat, (((1,), (1,)), ((), ())), preferred_element_type=jnp.float32
    )


def rms_norm(values, gain_vec):
    return (
        values * lax.rsqrt(jnp.mean(values * values, axis=-1, keepdims=True) + EPSILON) * gain_vec
    )


def rope_tables(positions, width):
    half_width = width // 2
    frequency = jnp.exp(
        jnp.arange(half_width, dtype=jnp.float32) * (-2.0 * math.log(ROPE_BASE) / width)
    )
    angles = positions.astype(jnp.float32)[:, None] * frequency[None, :]
    return (jnp.cos(angles)[:, None, :], jnp.sin(angles)[:, None, :])


def rotate(values, cosine, sine_part):
    half_width = values.shape[-1] // 2
    first_half = values[..., :half_width]
    second_half = values[..., half_width:]
    return jnp.concatenate(
        [
            first_half * cosine - second_half * sine_part,
            second_half * cosine + first_half * sine_part,
        ],
        axis=-1,
    )


def document_ids(doc_lengths, places):
    doc_ends = jnp.cumsum(doc_lengths)
    return jnp.sum((places[:, None] >= doc_ends[None, :-1]).astype(jnp.int32), axis=1)


def query_key(cosine, sine_part, query_lin, key_lin, gain_query, gain_key):
    tok_count = query_lin.shape[0]
    query_rot = rotate(
        rms_norm(query_lin.reshape(tok_count, HQ, HD), gain_query), cosine, sine_part
    )
    key_rot = rotate(rms_norm(key_lin.reshape(tok_count, KV, HD), gain_key), cosine, sine_part)
    return (query_rot, key_rot)


def mix_piece(inputs, normed, projected, widened, gain_post, gain_laurel):
    return (
        inputs + rms_norm(projected, gain_post) + normed + rms_norm(widened, gain_laurel)
    ) * HALF_ROOT


def geglu(gate_lin, up_lin):
    return jax.nn.gelu(gate_lin, approximate=True) * up_lin


def ffn_out_piece(mixed, down_lin, gain_ffout):
    return mixed + rms_norm(down_lin, gain_ffout)


def ple_act(ple_lin, ple_input):
    return jax.nn.gelu(ple_lin, approximate=True) * ple_input


def final_piece(layer_mid, ple_wide, gain_ple):
    return layer_mid + rms_norm(ple_wide, gain_ple)


def visibility(doc_lengths, query_start, key_start, tok_count, span_len):
    query_places = query_start + jnp.arange(tok_count, dtype=jnp.int32)
    key_places = key_start + jnp.arange(span_len, dtype=jnp.int32)
    distance = query_places[:, None] - key_places[None, :]
    query_docs = document_ids(doc_lengths, query_places)
    key_docs = document_ids(doc_lengths, key_places)
    return (
        (distance >= 0)
        & (distance < WINDOW)
        & (key_places[None, :] >= 0)
        & (query_docs[:, None] == key_docs[None, :])
    )


def attend_forward(query_low, span_kv, visible):
    tok_count = query_low.shape[0]
    scale_factor = 1.0 / math.sqrt(HD)
    scores = (
        jnp.einsum("tkgh,skh->kgts", query_low, span_kv[0], preferred_element_type=jnp.float32)
        * scale_factor
    )
    scores = jnp.where(visible, scores, NEGATIVE)
    row_top = jnp.max(scores, axis=-1, keepdims=True)
    shifted = jnp.exp(scores - row_top)
    row_total = jnp.sum(shifted, axis=-1, keepdims=True)
    attn_probs = shifted / row_total
    attended = jnp.einsum(
        "kgts,skh->tkgh",
        attn_probs.astype(jnp.bfloat16),
        span_kv[1],
        preferred_element_type=jnp.float32,
    )
    return (attended.reshape(tok_count, -1), row_top + jnp.log(row_total))


def attend_backward(query_low, span_kv, visible, log_total, grad_out_low):
    scale_factor = 1.0 / math.sqrt(HD)
    scores = (
        jnp.einsum("tkgh,skh->kgts", query_low, span_kv[0], preferred_element_type=jnp.float32)
        * scale_factor
    )
    attn_probs = jnp.where(visible, jnp.exp(jnp.where(visible, scores, NEGATIVE) - log_total), 0.0)
    grad_probs = jnp.einsum(
        "tkgh,skh->kgts", grad_out_low, span_kv[1], preferred_element_type=jnp.float32
    )
    inner_sum = jnp.sum(attn_probs * grad_probs, axis=-1, keepdims=True)
    grad_scores = (attn_probs * (grad_probs - inner_sum)).astype(jnp.bfloat16)
    grad_query = (
        jnp.einsum("kgts,skh->tkgh", grad_scores, span_kv[0], preferred_element_type=jnp.float32)
        * scale_factor
    )
    grad_keys = (
        jnp.einsum("kgts,tkgh->skh", grad_scores, query_low, preferred_element_type=jnp.float32)
        * scale_factor
    )
    grad_values = jnp.einsum(
        "kgts,tkgh->skh",
        attn_probs.astype(jnp.bfloat16),
        grad_out_low,
        preferred_element_type=jnp.float32,
    )
    return (grad_query, jnp.stack([grad_keys, grad_values]))


def settle(act_low, grad_low):
    act_cols = lax.all_to_all(act_low, "fsdp", split_axis=1, concat_axis=0, tiled=True)
    shard_rows = matmul_tn(act_cols, lax.all_gather(grad_low, "fsdp", axis=0, tiled=True))
    return lax.psum(shard_rows.astype(jnp.bfloat16), "ctx").astype(jnp.float32)


def local(
    tokens,
    per_layer,
    cotangent,
    doc_lengths,
    positions,
    w_query,
    w_key,
    w_value,
    w_out,
    laurel_left,
    laurel_right,
    w_gate,
    w_up,
    w_down,
    ple_gate,
    ple_proj,
    attn_in_gain,
    query_gain,
    key_gain,
    attn_out_gain,
    laurel_gain,
    ffn_in_gain,
    ffn_out_gain,
    ple_gain,
):
    bfloat = jnp.bfloat16
    tok_count = tokens.shape[0]
    span_len = WINDOW + tok_count
    groups = HQ // KV
    dev_index = lax.axis_index("ctx") * lax.axis_size("fsdp") + lax.axis_index("fsdp")
    query_start = dev_index * tok_count
    key_start = query_start - WINDOW
    visible = visibility(doc_lengths, query_start, key_start, tok_count, span_len)
    cosine, sine_part = rope_tables(positions, HD)
    gain_in, gain_query, gain_key, gain_post, gain_laurel, gain_ffin, gain_ffout, gain_ple = (
        lax.all_gather(attn_in_gain, "fsdp", axis=0, tiled=True),
        lax.all_gather(query_gain, "fsdp", axis=0, tiled=True),
        lax.all_gather(key_gain, "fsdp", axis=0, tiled=True),
        lax.all_gather(attn_out_gain, "fsdp", axis=0, tiled=True),
        lax.all_gather(laurel_gain, "fsdp", axis=0, tiled=True),
        lax.all_gather(ffn_in_gain, "fsdp", axis=0, tiled=True),
        lax.all_gather(ffn_out_gain, "fsdp", axis=0, tiled=True),
        lax.all_gather(ple_gain, "fsdp", axis=0, tiled=True),
    )
    full_query, full_key, full_value, full_out, full_left, full_right = (
        lax.all_gather(w_query.astype(bfloat), "fsdp", axis=0, tiled=True),
        lax.all_gather(w_key.astype(bfloat), "fsdp", axis=0, tiled=True),
        lax.all_gather(w_value.astype(bfloat), "fsdp", axis=0, tiled=True),
        lax.all_gather(w_out.astype(bfloat), "fsdp", axis=0, tiled=True),
        lax.all_gather(laurel_left.astype(bfloat), "fsdp", axis=0, tiled=True),
        lax.all_gather(laurel_right.astype(bfloat), "fsdp", axis=0, tiled=True),
    )
    inputs = tokens.astype(jnp.float32)
    ple_input = per_layer.astype(jnp.float32)
    normed, norm_back = jax.vjp(rms_norm, inputs, gain_in)
    normed_low = normed.astype(bfloat)
    query_lin = matmul(normed_low, full_query)
    key_lin = matmul(normed_low, full_key)
    value_lin = matmul(normed_low, full_value)
    (query_rot, key_rot), rope_back = jax.vjp(
        functools.partial(query_key, cosine, sine_part), query_lin, key_lin, gain_query, gain_key
    )
    query_low = query_rot.astype(bfloat).reshape(tok_count, KV, groups, HD)
    keys_values = jnp.stack(
        [key_rot.astype(bfloat), value_lin.astype(bfloat).reshape(tok_count, KV, HD)]
    )
    block_kv = lax.all_gather(keys_values, "fsdp", axis=1, tiled=True)
    block_len = block_kv.shape[1]
    before_kv = passed_along(block_kv, "ctx", 1)
    span_offset = block_len + lax.axis_index("fsdp") * tok_count - WINDOW
    span_kv = lax.dynamic_slice_in_dim(
        jnp.concatenate([before_kv, block_kv], axis=1), span_offset, span_len, 1
    )
    attended, log_total = attend_forward(query_low, span_kv, visible)
    attended_low = attended.astype(bfloat)
    projected = matmul(attended_low, full_out)
    narrow_low = matmul(normed_low, full_left).astype(bfloat)
    widened = matmul(narrow_low, full_right)
    mixed, mix_back = jax.vjp(mix_piece, inputs, normed, projected, widened, gain_post, gain_laurel)
    full_gate, full_up, full_down, full_pgate, full_pproj = (
        lax.all_gather(w_gate.astype(bfloat), "fsdp", axis=0, tiled=True),
        lax.all_gather(w_up.astype(bfloat), "fsdp", axis=0, tiled=True),
        lax.all_gather(w_down.astype(bfloat), "fsdp", axis=0, tiled=True),
        lax.all_gather(ple_gate.astype(bfloat), "fsdp", axis=0, tiled=True),
        lax.all_gather(ple_proj.astype(bfloat), "fsdp", axis=0, tiled=True),
    )
    ffn_normed, ffn_norm_back = jax.vjp(rms_norm, mixed, gain_ffin)
    ffn_low = ffn_normed.astype(bfloat)
    gate_lin = matmul(ffn_low, full_gate)
    up_lin = matmul(ffn_low, full_up)
    hidden, geglu_back = jax.vjp(geglu, gate_lin, up_lin)
    hidden_low = hidden.astype(bfloat)
    down_lin = matmul(hidden_low, full_down)
    layer_mid, ffn_out_back = jax.vjp(ffn_out_piece, mixed, down_lin, gain_ffout)
    layer_low = layer_mid.astype(bfloat)
    ple_lin = matmul(layer_low, full_pgate)
    ple_mid, ple_back = jax.vjp(ple_act, ple_lin, ple_input)
    ple_low = ple_mid.astype(bfloat)
    ple_wide = matmul(ple_low, full_pproj)
    out_full, final_back = jax.vjp(final_piece, layer_mid, ple_wide, gain_ple)
    full_gate, full_up, full_down, full_pgate, full_pproj = (
        lax.all_gather(w_gate.astype(bfloat), "fsdp", axis=0, tiled=True),
        lax.all_gather(w_up.astype(bfloat), "fsdp", axis=0, tiled=True),
        lax.all_gather(w_down.astype(bfloat), "fsdp", axis=0, tiled=True),
        lax.all_gather(ple_gate.astype(bfloat), "fsdp", axis=0, tiled=True),
        lax.all_gather(ple_proj.astype(bfloat), "fsdp", axis=0, tiled=True),
    )
    grad_layer, grad_pwide, grad_gple = final_back(cotangent.astype(jnp.float32))
    grad_pwide_low = grad_pwide.astype(bfloat)
    grad_pproj = settle(ple_low, grad_pwide_low)
    grad_plemid = matmul_nt(grad_pwide_low, full_pproj)
    grad_plelin, grad_pleinput = ple_back(grad_plemid)
    grad_plelin_low = grad_plelin.astype(bfloat)
    grad_pgate = settle(layer_low, grad_plelin_low)
    grad_layer = grad_layer + matmul_nt(grad_plelin_low, full_pgate)
    grad_mixed, grad_down, grad_gffout = ffn_out_back(grad_layer)
    grad_down_low = grad_down.astype(bfloat)
    grad_wdown = settle(hidden_low, grad_down_low)
    grad_hidden = matmul_nt(grad_down_low, full_down)
    grad_gate, grad_up = geglu_back(grad_hidden)
    grad_gate_low = grad_gate.astype(bfloat)
    grad_up_low = grad_up.astype(bfloat)
    grad_wgate = settle(ffn_low, grad_gate_low)
    grad_wup = settle(ffn_low, grad_up_low)
    grad_ffn = matmul_nt(grad_gate_low, full_gate) + matmul_nt(grad_up_low, full_up)
    grad_mixed_more, grad_gffin = ffn_norm_back(grad_ffn)
    grad_mixed = grad_mixed + grad_mixed_more
    full_query, full_key, full_value, full_out, full_left, full_right = (
        lax.all_gather(w_query.astype(bfloat), "fsdp", axis=0, tiled=True),
        lax.all_gather(w_key.astype(bfloat), "fsdp", axis=0, tiled=True),
        lax.all_gather(w_value.astype(bfloat), "fsdp", axis=0, tiled=True),
        lax.all_gather(w_out.astype(bfloat), "fsdp", axis=0, tiled=True),
        lax.all_gather(laurel_left.astype(bfloat), "fsdp", axis=0, tiled=True),
        lax.all_gather(laurel_right.astype(bfloat), "fsdp", axis=0, tiled=True),
    )
    grad_in_first, grad_normed, grad_proj, grad_lwide, grad_gpost, grad_glaurel = mix_back(
        grad_mixed
    )
    grad_proj_low = grad_proj.astype(bfloat)
    grad_wout = settle(attended_low, grad_proj_low)
    grad_att_low = matmul_nt(grad_proj_low, full_out).astype(bfloat)
    grad_lwide_low = grad_lwide.astype(bfloat)
    grad_wright = settle(narrow_low, grad_lwide_low)
    grad_narrow_low = matmul_nt(grad_lwide_low, full_right).astype(bfloat)
    grad_wleft = settle(normed_low, grad_narrow_low)
    grad_normed = grad_normed + matmul_nt(grad_narrow_low, full_left)
    grad_query_att, grad_span = attend_backward(
        query_low, span_kv, visible, log_total, grad_att_low.reshape(tok_count, KV, groups, HD)
    )
    whole_grad = jnp.zeros((2, 2 * block_len, KV, HD), jnp.float32)
    whole_grad = lax.dynamic_update_slice_in_dim(whole_grad, grad_span, span_offset, 1)
    returned = passed_along(whole_grad[:, :block_len].astype(jnp.bfloat16), "ctx", -1).astype(
        jnp.float32
    )
    own_grad = lax.psum_scatter(
        (whole_grad[:, block_len:] + returned).astype(jnp.bfloat16),
        "fsdp",
        scatter_dimension=1,
        tiled=True,
    ).astype(jnp.float32)
    grad_qlin, grad_klin, grad_gquery, grad_gkey = rope_back(
        (grad_query_att.reshape(tok_count, HQ, HD), own_grad[0])
    )
    grad_qlin_low = grad_qlin.astype(bfloat)
    grad_klin_low = grad_klin.astype(bfloat)
    grad_vlin_low = own_grad[1].reshape(tok_count, KV * HD).astype(bfloat)
    grad_wquery = settle(normed_low, grad_qlin_low)
    grad_wkey = settle(normed_low, grad_klin_low)
    grad_wvalue = settle(normed_low, grad_vlin_low)
    grad_normed = (
        grad_normed
        + matmul_nt(grad_qlin_low, full_query)
        + matmul_nt(grad_klin_low, full_key)
        + matmul_nt(grad_vlin_low, full_value)
    )
    grad_in_second, grad_gin = norm_back(grad_normed)
    grad_tokens = grad_in_first + grad_in_second
    sum_gin, sum_gquery, sum_gkey, sum_gpost, sum_glaurel, sum_gffin, sum_gffout, sum_gple = (
        lax.psum(
            (
                grad_gin,
                grad_gquery,
                grad_gkey,
                grad_gpost,
                grad_glaurel,
                grad_gffin,
                grad_gffout,
                grad_gple,
            ),
            ("ctx", "fsdp"),
        )
    )
    wide_rows = attn_in_gain.shape[0]
    head_rows = query_gain.shape[0]
    wide_start = lax.axis_index("fsdp") * wide_rows
    head_start = lax.axis_index("fsdp") * head_rows

    def wide_part(full_vec):
        return lax.dynamic_slice_in_dim(full_vec, wide_start, wide_rows, 0)

    def head_part(full_vec):
        return lax.dynamic_slice_in_dim(full_vec, head_start, head_rows, 0)

    return (
        out_full.astype(bfloat),
        grad_tokens,
        grad_pleinput,
        grad_wquery,
        grad_wkey,
        grad_wvalue,
        grad_wout,
        grad_wleft,
        grad_wright,
        grad_wgate,
        grad_wup,
        grad_wdown,
        grad_pgate,
        grad_pproj,
        wide_part(sum_gin),
        head_part(sum_gquery),
        head_part(sum_gkey),
        wide_part(sum_gpost),
        wide_part(sum_glaurel),
        wide_part(sum_gffin),
        wide_part(sum_gffout),
        wide_part(sum_gple),
    )

def remote(src, dst, send_sem, recv_sem, place):
    return pltpu.make_async_remote_copy(
        src_ref=src,
        dst_ref=dst,
        send_sem=send_sem,
        recv_sem=recv_sem,
        device_id={"fsdp": place},
        device_id_type=pl.DeviceIdType.MESH,
    )


def dot_nn(left_mat, right_mat):
    return jnp.dot(left_mat, right_mat, preferred_element_type=jnp.float32)


def dot_nt(left_mat, right_mat):
    return lax.dot_general(
        left_mat, right_mat, (((1,), (1,)), ((), ())), preferred_element_type=jnp.float32
    )


PIECES = 4


def line_scratch(chips, tok_count, width):
    dma = pltpu.SemaphoreType.DMA
    shard = (tok_count, width)
    return [
        pltpu.VMEM((chips, 2) + shard, jnp.bfloat16),
        dma((chips, 2)),
        dma((chips, 3)),
        dma,
        pltpu.VMEM((chips, 2) + shard, jnp.bfloat16),
        pltpu.VMEM((chips,) + shard, jnp.bfloat16),
        pltpu.VMEM((chips,) + shard, jnp.bfloat16),
        pltpu.VMEM((chips,) + shard, jnp.bfloat16),
        dma((chips,)),
        dma((chips,)),
        dma((chips, PIECES)),
        dma((chips, PIECES)),
        dma((chips, PIECES)),
    ]


LINE_REFS = 13


class Line:
    def __init__(self, chips, refs):
        (
            self.slots,
            self.slot_recv,
            self.slot_send,
            self.own_sem,
            self.parts,
            self.from_core,
            self.from_left,
            self.from_right,
            self.core_send,
            self.core_recv,
            self.flow_send,
            self.left_recv,
            self.right_recv,
        ) = refs
        self.chips = chips
        me = lax.axis_index("fsdp")
        self.chip = me // 2
        self.core = me % 2
        self.tok = self.slots.shape[2]
        self.piece = self.tok // PIECES

    def place(self, chip, core):
        return chip * 2 + core

    def order(self, step):
        picked = 0
        for chip in range(self.chips):
            near = sorted(range(self.chips), key=lambda other: (abs(other - chip), other))
            picked = picked + jnp.where(self.chip == chip, near[step], 0)
        return picked

    def barrier(self):
        sem = pltpu.get_barrier_semaphore()

        def greet(place):
            pl.semaphore_signal(
                sem, inc=1, device_id={"fsdp": place}, device_id_type=pl.DeviceIdType.MESH
            )

        greet(self.place(self.chip, 1 - self.core))

        @pl.when(self.chip > 0)
        def _():
            greet(self.place(self.chip - 1, self.core))

        @pl.when(self.chip < self.chips - 1)
        def _():
            greet(self.place(self.chip + 1, self.core))

        ends = jnp.where(self.chip == 0, 1, 0) + jnp.where(self.chip == self.chips - 1, 1, 0)
        pl.semaphore_wait(sem, 3 - ends)

    def slot_copy(self, src, chip, way):
        place = (
            self.place(self.chip + 1, self.core),
            self.place(self.chip - 1, self.core),
            self.place(self.chip, 1 - self.core),
        )[way]
        return remote(
            src,
            self.slots.at[chip, self.core],
            self.slot_send.at[chip, way],
            self.slot_recv.at[chip, self.core],
            place,
        )

    def own_copy(self, own_ref):
        return pltpu.make_async_copy(own_ref, self.slots.at[self.chip, self.core], self.own_sem)

    def gather_begin(self, own_ref):
        @pl.when(self.chip < self.chips - 1)
        def _():
            self.slot_copy(own_ref, self.chip, 0).start()

        @pl.when(self.chip > 0)
        def _():
            self.slot_copy(own_ref, self.chip, 1).start()

        self.slot_copy(own_ref, self.chip, 2).start()
        self.own_copy(own_ref).start()

    def gather_step(self, distance):
        for chip, there, way, onward in (
            (self.chip - distance, self.chip >= distance, 0, self.chip < self.chips - 1),
            (self.chip + distance, self.chip + distance < self.chips, 1, self.chip > 0),
        ):

            @pl.when(there)
            def _(chip=chip, way=way, onward=onward):
                src = self.slots.at[chip, self.core]
                self.slot_copy(src, chip, way).wait_recv()

                @pl.when(onward)
                def _():
                    self.slot_copy(src, chip, way).start()

                self.slot_copy(src, chip, 2).start()

    def gather_other(self, chip):
        dst = self.slots.at[chip, 1 - self.core]
        remote(
            dst,
            dst,
            self.slot_send.at[chip, 2],
            self.slot_recv.at[chip, 1 - self.core],
            self.place(self.chip, 1 - self.core),
        ).wait_recv()

    def gather_end(self):
        for chip in range(self.chips):
            src = self.slots.at[chip, self.core]

            @pl.when((self.chip >= chip) & (self.chip < self.chips - 1))
            def _(src=src, chip=chip):
                self.slot_copy(src, chip, 0).wait_send()

            @pl.when((self.chip <= chip) & (self.chip > 0))
            def _(src=src, chip=chip):
                self.slot_copy(src, chip, 1).wait_send()

            self.slot_copy(src, chip, 2).wait_send()

    def core_copy(self, chip):
        return remote(
            self.parts.at[chip, 1 - self.core],
            self.from_core.at[chip],
            self.core_send.at[chip],
            self.core_recv.at[chip],
            self.place(self.chip, 1 - self.core),
        )

    def flow_copy(self, chip, piece, right):
        rows = pl.ds(piece * self.piece, self.piece)
        return remote(
            self.parts.at[chip, self.core, rows],
            (self.from_left if right else self.from_right).at[chip, rows],
            self.flow_send.at[chip, piece],
            (self.left_recv if right else self.right_recv).at[chip, piece],
            self.place(self.chip + (1 if right else -1), self.core),
        )

    def flow(self, chip, right, incoming):
        self.core_copy(chip).wait_recv()

        @pl.loop(0, PIECES)
        def _(piece):
            rows = pl.ds(pl.multiple_of(piece * self.piece, self.piece), self.piece)
            total = self.parts[chip, self.core, rows].astype(jnp.float32)
            total = total + self.from_core[chip, rows].astype(jnp.float32)
            if incoming:
                self.flow_copy(chip, piece, right).wait_recv()
                source = self.from_left if right else self.from_right
                total = total + source[chip, rows].astype(jnp.float32)
            self.parts[chip, self.core, rows] = total.astype(jnp.bfloat16)
            self.flow_copy(chip, piece, right).start()

    def scatter_first(self, chip):
        @pl.when((self.chip == 0) & (chip > 0))
        def _():
            self.flow(chip, True, False)

        @pl.when((self.chip == self.chips - 1) & (chip < self.chips - 1))
        def _():
            self.flow(chip, False, False)

    def scatter_rest(self, result_ref):
        for rank in range(3, 2 * self.chips - 2):
            right = rank - self.chip

            @pl.when((self.chip > 0) & (right > self.chip) & (right < self.chips))
            def _(right=right):
                self.flow(right, True, True)

            left = 2 * (self.chips - 1) - self.chip - rank

            @pl.when((self.chip < self.chips - 1) & (left < self.chip) & (left >= 0))
            def _(left=left):
                self.flow(left, False, True)

        own = self.chip
        self.core_copy(own).wait_recv()

        @pl.loop(0, PIECES)
        def _(piece):
            rows = pl.ds(pl.multiple_of(piece * self.piece, self.piece), self.piece)
            total = self.parts[own, self.core, rows].astype(jnp.float32)
            total = total + self.from_core[own, rows].astype(jnp.float32)
            result_ref[rows] = total

        @pl.when(own > 0)
        def _():
            @pl.loop(0, PIECES)
            def _(piece):
                rows = pl.ds(pl.multiple_of(piece * self.piece, self.piece), self.piece)
                self.flow_copy(own, piece, True).wait_recv()
                result_ref[rows] += self.from_left[own, rows].astype(jnp.float32)

        @pl.when(own < self.chips - 1)
        def _():
            @pl.loop(0, PIECES)
            def _(piece):
                rows = pl.ds(pl.multiple_of(piece * self.piece, self.piece), self.piece)
                self.flow_copy(own, piece, False).wait_recv()
                result_ref[rows] += self.from_right[own, rows].astype(jnp.float32)

        for chip in range(self.chips):
            self.core_copy(chip).wait_send()

            @pl.when(self.chip != chip)
            def _(chip=chip):
                for piece in range(PIECES):
                    self.flow_copy(chip, piece, True).wait_send()


def ffn_forward_kernel(
    chips,
    own_ref,
    gateup_hbm,
    down_hbm,
    result_ref,
    all_hbm,
    hidden_hbm,
    act_hbm,
    slope_hbm,
    *scratch,
):
    line = Line(chips, scratch[:LINE_REFS])
    gateup, down, hidden, act, slope, load_sems, store_sems = scratch[LINE_REFS:]
    ff_part = down.shape[0]
    width = down.shape[1]
    pair = 2 * line.tok
    load_gateup = pltpu.make_async_copy(gateup_hbm, gateup, load_sems.at[0])
    load_down = pltpu.make_async_copy(down_hbm, down, load_sems.at[1])
    load_gateup.start()
    load_down.start()
    line.barrier()
    line.gather_begin(own_ref)
    line.own_copy(own_ref).wait()

    def stores(chip):
        rows = pl.ds(pl.multiple_of(chip * pair, pair), pair)
        return [
            pltpu.make_async_copy(line.slots.at[chip], all_hbm.at[chip], store_sems.at[chip, 0]),
            pltpu.make_async_copy(hidden.at[rows], hidden_hbm.at[rows], store_sems.at[chip, 1]),
            pltpu.make_async_copy(act.at[rows], act_hbm.at[rows], store_sems.at[chip, 2]),
            pltpu.make_async_copy(slope.at[rows], slope_hbm.at[rows], store_sems.at[chip, 3]),
        ]

    tile = 256
    for step in range(chips):
        if step > 0:
            line.gather_step(step)
        chip = line.order(step)
        line.gather_other(chip)
        if step == 0:
            load_gateup.wait()
            load_down.wait()
        rows = pl.ds(pl.multiple_of(chip * pair, pair), pair)

        @pl.loop(0, ff_part // tile)
        def _(at, chip=chip, rows=rows):
            inputs = line.slots[chip].reshape(pair, width)
            gate_cols = pl.ds(pl.multiple_of(at * tile, tile), tile)
            up_cols = pl.ds(pl.multiple_of(ff_part + at * tile, tile), tile)
            gate = dot_nn(inputs, gateup[:, gate_cols])
            up = dot_nn(inputs, gateup[:, up_cols])
            square = gate * gate
            bent = jnp.tanh(GELU_ROOT * gate * (1.0 + GELU_CUBE * square))
            half = 0.5 + 0.5 * bent
            activated = gate * half
            rise = half + 0.5 * gate * (1.0 - bent * bent) * (
                GELU_ROOT * (1.0 + 3.0 * GELU_CUBE * square)
            )
            hidden[rows, gate_cols] = (activated * up).astype(jnp.bfloat16)
            act[rows, gate_cols] = activated.astype(jnp.bfloat16)
            slope[rows, gate_cols] = (rise * up).astype(jnp.bfloat16)

        for copy in stores(chip):
            copy.start()

        wide = 512

        @pl.loop(0, width // wide)
        def _(at, chip=chip, rows=rows):
            cols = pl.ds(pl.multiple_of(at * wide, wide), wide)
            sums = dot_nn(hidden[rows, :], down[:, cols]).astype(jnp.bfloat16)
            line.parts[chip, :, :, cols] = sums.reshape(2, line.tok, wide)

        line.core_copy(chip).start()
        if step > 0:
            line.scatter_first(line.order(step - 1))
    line.scatter_first(line.order(chips - 1))
    line.scatter_rest(result_ref)
    line.gather_end()
    for chip in range(chips):
        for copy in stores(chip):
            copy.wait()


def ffn_forward(own, gateup, down, chips):
    tok_count, width = own.shape
    ff_part = down.shape[0]
    block = 2 * chips * tok_count
    bfloat = jnp.bfloat16
    anywhere = pl.BlockSpec(memory_space=pl.ANY)
    vmem = pl.BlockSpec(memory_space=pltpu.VMEM)
    part = jax.ShapeDtypeStruct((block, ff_part), bfloat)
    result, gathered, hidden, act, slope = pl.pallas_call(
        functools.partial(ffn_forward_kernel, chips),
        out_shape=[
            jax.ShapeDtypeStruct((tok_count, width), jnp.float32),
            jax.ShapeDtypeStruct((chips, 2, tok_count, width), bfloat),
            part,
            part,
            part,
        ],
        in_specs=[vmem, anywhere, anywhere],
        out_specs=[vmem, anywhere, anywhere, anywhere, anywhere],
        scratch_shapes=line_scratch(chips, tok_count, width)
        + [
            pltpu.VMEM(gateup.shape, bfloat),
            pltpu.VMEM(down.shape, bfloat),
            pltpu.VMEM((block, ff_part), bfloat),
            pltpu.VMEM((block, ff_part), bfloat),
            pltpu.VMEM((block, ff_part), bfloat),
            pltpu.SemaphoreType.DMA((2,)),
            pltpu.SemaphoreType.DMA((chips, 4)),
        ],
        compiler_params=pltpu.CompilerParams(
            collective_id=1, has_side_effects=True, vmem_limit_bytes=KERNEL_VMEM
        ),
        cost_estimate=pl.CostEstimate(
            flops=6 * block * width * ff_part,
            bytes_accessed=40 << 20,
            transcendentals=block * ff_part,
        ),
        name="ffn_forward",
    )(own, gateup, down)
    return result, gathered.reshape(block, width), hidden, act, slope


def ffn_backward_kernel(
    chips,
    own_ref,
    gateup_hbm,
    down_hbm,
    act_hbm,
    slope_hbm,
    result_ref,
    all_hbm,
    grad_hbm,
    *scratch,
):
    line = Line(chips, scratch[:LINE_REFS])
    gateup, down, act, slope, grad, load_sems, store_sems = scratch[LINE_REFS:]
    ff_part = down.shape[0]
    width = down.shape[1]
    pair = 2 * line.tok
    loads = [
        pltpu.make_async_copy(down_hbm, down, load_sems.at[0]),
        pltpu.make_async_copy(act_hbm, act, load_sems.at[1]),
        pltpu.make_async_copy(slope_hbm, slope, load_sems.at[2]),
        pltpu.make_async_copy(gateup_hbm, gateup, load_sems.at[3]),
    ]
    for load in loads:
        load.start()
    line.barrier()
    line.gather_begin(own_ref)
    line.own_copy(own_ref).wait()

    def stores(chip):
        rows = pl.ds(pl.multiple_of(chip * pair, pair), pair)
        return [
            pltpu.make_async_copy(line.slots.at[chip], all_hbm.at[chip], store_sems.at[chip, 0]),
            pltpu.make_async_copy(grad.at[rows], grad_hbm.at[rows], store_sems.at[chip, 1]),
        ]

    tile = 256
    for step in range(chips):
        if step > 0:
            line.gather_step(step)
        chip = line.order(step)
        line.gather_other(chip)
        if step == 0:
            for load in loads:
                load.wait()
        rows = pl.ds(pl.multiple_of(chip * pair, pair), pair)

        @pl.loop(0, ff_part // tile)
        def _(at, chip=chip, rows=rows):
            grads = line.slots[chip].reshape(pair, width)
            gate_cols = pl.ds(pl.multiple_of(at * tile, tile), tile)
            up_cols = pl.ds(pl.multiple_of(ff_part + at * tile, tile), tile)
            grad_hidden = dot_nt(grads, down[gate_cols, :])
            grad[rows, gate_cols] = (
                grad_hidden * slope[rows, gate_cols].astype(jnp.float32)
            ).astype(jnp.bfloat16)
            grad[rows, up_cols] = (grad_hidden * act[rows, gate_cols].astype(jnp.float32)).astype(
                jnp.bfloat16
            )

        for copy in stores(chip):
            copy.start()

        wide = 512

        @pl.loop(0, width // wide)
        def _(at, chip=chip, rows=rows):
            cols = pl.ds(pl.multiple_of(at * wide, wide), wide)
            sums = dot_nt(grad[rows, :], gateup[cols, :]).astype(jnp.bfloat16)
            line.parts[chip, :, :, cols] = sums.reshape(2, line.tok, wide)

        line.core_copy(chip).start()
        if step > 0:
            line.scatter_first(line.order(step - 1))
    line.scatter_first(line.order(chips - 1))
    line.scatter_rest(result_ref)
    line.gather_end()
    for chip in range(chips):
        for copy in stores(chip):
            copy.wait()


def ffn_backward(own, gateup, down, act, slope, chips):
    tok_count, width = own.shape
    ff_part = down.shape[0]
    block = 2 * chips * tok_count
    bfloat = jnp.bfloat16
    anywhere = pl.BlockSpec(memory_space=pl.ANY)
    vmem = pl.BlockSpec(memory_space=pltpu.VMEM)
    result, gathered, grad = pl.pallas_call(
        functools.partial(ffn_backward_kernel, chips),
        out_shape=[
            jax.ShapeDtypeStruct((tok_count, width), jnp.float32),
            jax.ShapeDtypeStruct((chips, 2, tok_count, width), bfloat),
            jax.ShapeDtypeStruct((block, 2 * ff_part), bfloat),
        ],
        in_specs=[vmem] + [anywhere] * 4,
        out_specs=[vmem, anywhere, anywhere],
        scratch_shapes=line_scratch(chips, tok_count, width)
        + [
            pltpu.VMEM(gateup.shape, bfloat),
            pltpu.VMEM(down.shape, bfloat),
            pltpu.VMEM((block, ff_part), bfloat),
            pltpu.VMEM((block, ff_part), bfloat),
            pltpu.VMEM((block, 2 * ff_part), bfloat),
            pltpu.SemaphoreType.DMA((4,)),
            pltpu.SemaphoreType.DMA((chips, 2)),
        ],
        compiler_params=pltpu.CompilerParams(
            collective_id=2, has_side_effects=True, vmem_limit_bytes=KERNEL_VMEM
        ),
        cost_estimate=pl.CostEstimate(
            flops=6 * block * width * ff_part, bytes_accessed=40 << 20, transcendentals=0
        ),
        name="ffn_backward",
    )(own, gateup, down, act, slope)
    return result, gathered.reshape(block, width), grad

def to_columns(pieces, ctx_count):
    packed = jnp.concatenate(pieces, axis=2)
    quarter = packed.shape[0] // ctx_count
    start = lax.axis_index("ctx") * quarter
    mine = lax.dynamic_slice_in_dim(packed, start, quarter, 0).astype(jnp.bfloat16)
    spread = lax.all_to_all(mine, "fsdp", split_axis=1, concat_axis=0, tiled=False)
    whole = lax.all_gather(spread, "ctx", axis=1, tiled=True)
    return whole.reshape(-1, whole.shape[-1])


def to_rows(partial, fsdp_count):
    parts = partial.astype(jnp.bfloat16).reshape(fsdp_count, -1, partial.shape[-1])
    summed = lax.psum_scatter(parts, "ctx", scatter_dimension=1, tiled=True)
    swapped = lax.all_to_all(summed, "fsdp", split_axis=0, concat_axis=1, tiled=False)
    return swapped


def gather_rows(part):
    return lax.all_gather(part, "ctx", axis=0, tiled=True).astype(jnp.float32)


def scatter_tokens(partial):
    return lax.psum_scatter(
        partial.astype(jnp.bfloat16), "fsdp", scatter_dimension=0, tiled=True
    ).astype(jnp.float32)


def gather_tokens(part):
    return lax.all_gather(part, "fsdp", axis=0, tiled=True)


def small_sum(partial):
    rows = lax.psum_scatter(partial.astype(jnp.bfloat16), "fsdp", scatter_dimension=0, tiled=True)
    return lax.psum(rows, "ctx").astype(jnp.float32)


def row_sum(partial):
    return lax.psum(partial.astype(jnp.bfloat16), "ctx").astype(jnp.float32)


def head_rope(cosine, sine_part, lin, gain_vec):
    return rotate(rms_norm(lin, gain_vec), cosine, sine_part)


def by_heads(
    tokens,
    per_layer,
    cotangent,
    doc_lengths,
    positions,
    w_query,
    w_key,
    w_value,
    w_out,
    laurel_left,
    laurel_right,
    w_gate,
    w_up,
    w_down,
    ple_gate,
    ple_proj,
    attn_in_gain,
    query_gain,
    key_gain,
    attn_out_gain,
    laurel_gain,
    ffn_in_gain,
    ffn_out_gain,
    ple_gain,
):
    bfloat = jnp.bfloat16
    ctx_count = lax.axis_size("ctx")
    fsdp_count = lax.axis_size("fsdp")
    tok_count = tokens.shape[0]
    block_len = tok_count * fsdp_count
    chips = fsdp_count // 2
    rows = w_query.shape[0]
    ff_part = w_gate.shape[1] // fsdp_count
    scale_factor = 1.0 / math.sqrt(HD)
    ctx_at = lax.axis_index("ctx")
    fsdp_at = lax.axis_index("fsdp")

    gain_list = [
        attn_in_gain,
        query_gain,
        key_gain,
        attn_out_gain,
        laurel_gain,
        ffn_in_gain,
        ffn_out_gain,
        ple_gain,
    ]
    gain_sizes = [g.shape[0] for g in gain_list]
    gain_offsets = [sum(gain_sizes[:n]) for n in range(len(gain_sizes) + 1)]
    all_gains = lax.all_gather(jnp.concatenate(gain_list), "fsdp", axis=0, tiled=False)
    gain_in, gain_query, gain_key, gain_post, gain_laurel, gain_ffin, gain_ffout, gain_ple = (
        all_gains[:, gain_offsets[n] : gain_offsets[n + 1]].reshape(-1) for n in range(8)
    )
    block_positions = lax.all_gather(positions, "fsdp", axis=0, tiled=True)
    cosine, sine_part = rope_tables(block_positions, HD)
    cosine, sine_part = cosine[:, 0], sine_part[:, 0]

    query_parts = w_query.reshape(rows, fsdp_count, HD)
    group_size = HQ // KV
    key_parts = jnp.repeat(w_key.reshape(rows, KV, HD), group_size, axis=1)
    value_parts = jnp.repeat(w_value.reshape(rows, KV, HD), group_size, axis=1)
    col_qkv = to_columns([query_parts, key_parts, value_parts], ctx_count)
    col_gateup = to_columns(
        [w_gate.reshape(rows, fsdp_count, ff_part), w_up.reshape(rows, fsdp_count, ff_part)],
        ctx_count,
    )
    out_low = w_out.astype(bfloat)
    down_low = w_down.astype(bfloat)
    full_left, full_right, full_pgate, full_pproj = (
        lax.all_gather(w.astype(bfloat), "fsdp", axis=0, tiled=True)
        for w in (laurel_left, laurel_right, ple_gate, ple_proj)
    )

    inputs = tokens.astype(jnp.float32)
    ple_input = per_layer.astype(jnp.float32)
    normed, norm_back = jax.vjp(rms_norm, inputs, gain_in)
    normed_low = normed.astype(bfloat)
    normed_all = gather_tokens(normed_low)
    qkv_lin = matmul(normed_all, col_qkv)
    query_lin, key_lin, value_lin = qkv_lin[:, :HD], qkv_lin[:, HD : 2 * HD], qkv_lin[:, 2 * HD :]
    rope_here = functools.partial(head_rope, cosine, sine_part)
    query_rot, query_back = jax.vjp(rope_here, query_lin, gain_query)
    key_rot, key_back = jax.vjp(rope_here, key_lin, gain_key)
    query_low = query_rot.astype(bfloat)
    own_kv = jnp.stack([key_rot.astype(bfloat), value_lin.astype(bfloat)])
    before_kv = passed_along(own_kv[:, block_len - WINDOW :], "ctx", 1)
    span_kv = jnp.concatenate([before_kv, own_kv], axis=1)

    chunk = 256
    span_len = WINDOW + chunk
    block_start = ctx_at * block_len
    prob_list, attended_list = [], []
    for begin in range(0, block_len, chunk):
        visible = visibility(
            doc_lengths, block_start + begin, block_start + begin - WINDOW, chunk, span_len
        )
        keys = span_kv[0, begin : begin + span_len]
        values = span_kv[1, begin : begin + span_len]
        scores = matmul_nt(query_low[begin : begin + chunk], keys) * scale_factor
        scores = jnp.where(visible, scores, NEGATIVE)
        shifted = jnp.exp(scores - jnp.max(scores, axis=-1, keepdims=True))
        probs = shifted / jnp.sum(shifted, axis=-1, keepdims=True)
        prob_list.append(probs)
        attended_list.append(matmul(probs.astype(bfloat), values))
    attended_low = jnp.concatenate(attended_list, axis=0).astype(bfloat)
    projected = scatter_tokens(matmul(attended_low, out_low))
    narrow_low = matmul(normed_low, full_left).astype(bfloat)
    widened = matmul(narrow_low, full_right)
    mixed, mix_back = jax.vjp(mix_piece, inputs, normed, projected, widened, gain_post, gain_laurel)
    ffn_normed, ffn_norm_back = jax.vjp(rms_norm, mixed, gain_ffin)
    down_lin, ffn_all, hidden_low, act_low, slope_low = ffn_forward(
        ffn_normed.astype(bfloat), col_gateup, down_low, chips
    )
    layer_mid, ffn_out_back = jax.vjp(ffn_out_piece, mixed, down_lin, gain_ffout)
    layer_low = layer_mid.astype(bfloat)
    ple_lin = matmul(layer_low, full_pgate)
    ple_mid, ple_back = jax.vjp(ple_act, ple_lin, ple_input)
    ple_low = ple_mid.astype(bfloat)
    ple_wide = matmul(ple_low, full_pproj)
    out_full, final_back = jax.vjp(final_piece, layer_mid, ple_wide, gain_ple)

    grad_layer, grad_pwide, grad_gple = final_back(cotangent.astype(jnp.float32))
    grad_pwide_low = grad_pwide.astype(bfloat)
    grad_pproj = small_sum(matmul_tn(ple_low, grad_pwide_low))
    grad_plemid = matmul_nt(grad_pwide_low, full_pproj)
    grad_plelin, grad_pleinput = ple_back(grad_plemid)
    grad_plelin_low = grad_plelin.astype(bfloat)
    grad_pgate = small_sum(matmul_tn(layer_low, grad_plelin_low))
    grad_layer = grad_layer + matmul_nt(grad_plelin_low, full_pgate)
    grad_mixed, grad_down, grad_gffout = ffn_out_back(grad_layer)
    grad_ffn, grad_down_all, grad_gateup_low = ffn_backward(
        grad_down.astype(bfloat), col_gateup, down_low, act_low, slope_low, chips
    )
    grad_wdown = row_sum(matmul_tn(hidden_low, grad_down_all))
    gateup_rows = to_rows(matmul_tn(ffn_all, grad_gateup_low), fsdp_count)
    gateup_rows = gather_rows(gateup_rows)
    grad_wgate = gateup_rows[:, :, :ff_part].reshape(rows, -1)
    grad_wup = gateup_rows[:, :, ff_part:].reshape(rows, -1)
    grad_mixed_more, grad_gffin = ffn_norm_back(grad_ffn)
    grad_mixed = grad_mixed + grad_mixed_more
    grad_in_first, grad_normed, grad_proj, grad_lwide, grad_gpost, grad_glaurel = mix_back(
        grad_mixed
    )
    grad_proj_all = gather_tokens(grad_proj.astype(bfloat))
    grad_wout = row_sum(matmul_tn(attended_low, grad_proj_all))
    grad_att_low = matmul_nt(grad_proj_all, out_low).astype(bfloat)
    grad_lwide_low = grad_lwide.astype(bfloat)
    grad_wright = small_sum(matmul_tn(narrow_low, grad_lwide_low))
    grad_narrow_low = matmul_nt(grad_lwide_low, full_right).astype(bfloat)
    grad_wleft = small_sum(matmul_tn(normed_low, grad_narrow_low))
    grad_normed = grad_normed + matmul_nt(grad_narrow_low, full_left)

    grad_query_list = []
    grad_keys = jnp.zeros((WINDOW + block_len, HD), jnp.float32)
    grad_values = jnp.zeros((WINDOW + block_len, HD), jnp.float32)
    for at, begin in enumerate(range(0, block_len, chunk)):
        keys = span_kv[0, begin : begin + span_len]
        values = span_kv[1, begin : begin + span_len]
        probs = prob_list[at]
        grad_rows = grad_att_low[begin : begin + chunk]
        grad_probs = matmul_nt(grad_rows, values)
        inner_sum = jnp.sum(probs * grad_probs, axis=-1, keepdims=True)
        grad_scores = (probs * (grad_probs - inner_sum)).astype(bfloat)
        grad_query_list.append(matmul(grad_scores, keys) * scale_factor)
        grad_keys = grad_keys.at[begin : begin + span_len].add(
            matmul_tn(grad_scores, query_low[begin : begin + chunk]) * scale_factor
        )
        grad_values = grad_values.at[begin : begin + span_len].add(
            matmul_tn(probs.astype(bfloat), grad_rows)
        )
    returned = passed_along(
        jnp.stack([grad_keys[:WINDOW], grad_values[:WINDOW]]).astype(bfloat), "ctx", -1
    ).astype(jnp.float32)
    returned = jnp.pad(returned, ((0, 0), (block_len - WINDOW, 0), (0, 0)))
    grad_qlin, grad_gquery = query_back(jnp.concatenate(grad_query_list, axis=0))
    grad_klin, grad_gkey = key_back(grad_keys[WINDOW:] + returned[0])
    grad_vlin = grad_values[WINDOW:] + returned[1]
    grad_qkv_low = jnp.concatenate([grad_qlin, grad_klin, grad_vlin], axis=1).astype(bfloat)
    qkv_rows = to_rows(matmul_tn(normed_all, grad_qkv_low), fsdp_count)
    kv_rows = qkv_rows[:, :, HD:].astype(jnp.float32)
    kv_rows = jnp.sum(kv_rows.reshape(kv_rows.shape[0], KV, group_size, 2 * HD), axis=2)
    quarter = rows // ctx_count
    qkv_rows = gather_rows(
        jnp.concatenate(
            [
                qkv_rows[:, :, :HD].reshape(quarter, HQ * HD),
                kv_rows[:, :, :HD].reshape(quarter, KV * HD).astype(bfloat),
                kv_rows[:, :, HD:].reshape(quarter, KV * HD).astype(bfloat),
            ],
            axis=1,
        )
    )
    grad_wquery = qkv_rows[:, : HQ * HD]
    grad_wkey = qkv_rows[:, HQ * HD : (HQ + KV) * HD]
    grad_wvalue = qkv_rows[:, (HQ + KV) * HD :]
    grad_normed = grad_normed + scatter_tokens(matmul_nt(grad_qkv_low, col_qkv))
    grad_in_second, grad_gin = norm_back(grad_normed)
    grad_tokens = grad_in_first + grad_in_second

    grad_gains = [
        grad_gin,
        grad_gquery,
        grad_gkey,
        grad_gpost,
        grad_glaurel,
        grad_gffin,
        grad_gffout,
        grad_gple,
    ]
    gain_rows = jnp.concatenate([g.reshape(fsdp_count, -1) for g in grad_gains], axis=1)
    gain_sums = lax.psum(gain_rows, ("ctx", "fsdp"))
    gain_sums = lax.dynamic_index_in_dim(gain_sums, fsdp_at, 0, keepdims=False)
    return (
        out_full.astype(bfloat),
        grad_tokens,
        grad_pleinput,
        grad_wquery,
        grad_wkey,
        grad_wvalue,
        grad_wout,
        grad_wleft,
        grad_wright,
        grad_wgate,
        grad_wup,
        grad_wdown,
        grad_pgate,
        grad_pproj,
        *(gain_sums[gain_offsets[n] : gain_offsets[n + 1]] for n in range(8)),
    )


def solution(mesh):
    in_specs = (
        P(("ctx", "fsdp"), None),
        P(("ctx", "fsdp"), None),
        P(("ctx", "fsdp"), None),
        P(),
        P(("ctx", "fsdp")),
        P("fsdp", None),
        P("fsdp", None),
        P("fsdp", None),
        P("fsdp", None),
        P("fsdp", None),
        P("fsdp", None),
        P("fsdp", None),
        P("fsdp", None),
        P("fsdp", None),
        P("fsdp", None),
        P("fsdp", None),
        P("fsdp"),
        P("fsdp"),
        P("fsdp"),
        P("fsdp"),
        P("fsdp"),
        P("fsdp"),
        P("fsdp"),
        P("fsdp"),
    )
    out_specs = (
        P(("ctx", "fsdp"), None),
        P(("ctx", "fsdp"), None),
        P(("ctx", "fsdp"), None),
        P("fsdp", None),
        P("fsdp", None),
        P("fsdp", None),
        P("fsdp", None),
        P("fsdp", None),
        P("fsdp", None),
        P("fsdp", None),
        P("fsdp", None),
        P("fsdp", None),
        P("fsdp", None),
        P("fsdp", None),
        P("fsdp"),
        P("fsdp"),
        P("fsdp"),
        P("fsdp"),
        P("fsdp"),
        P("fsdp"),
        P("fsdp"),
        P("fsdp"),
    )
    run = by_heads if mesh.shape["fsdp"] == HQ else local
    return jax.shard_map(run, mesh=mesh, in_specs=in_specs, out_specs=out_specs, check_vma=False)
```

```python
import functools
import math

import jax
import jax.numpy as jnp
from jax import lax
from jax.experimental import pallas as pl
from jax.experimental.pallas import tpu as pltpu
from jax.sharding import PartitionSpec as P

HQ = 8
KV = 2
HD = 256
WINDOW = 1024


EPSILON = 1e-06
NEGATIVE = -1e30
ROPE_BASE = 10000.0
HALF_ROOT = 1.0 / math.sqrt(2.0)
GELU_ROOT = math.sqrt(2.0 / math.pi)
GELU_CUBE = 0.044715
KERNEL_VMEM = 56 << 20


def passed_along(block, axis, distance):
    devices = range(lax.axis_size(axis))
    route = [(i - distance, i) for i in devices if i - distance in devices]
    return lax.ppermute(block, axis, route)


def matmul(left_mat, right_mat):
    return jnp.dot(left_mat, right_mat, preferred_element_type=jnp.float32)


def matmul_tn(left_mat, right_mat):
    return lax.dot_general(
        left_mat, right_mat, (((0,), (0,)), ((), ())), preferred_element_type=jnp.float32
    )


def matmul_nt(left_mat, right_mat):
    return lax.dot_general(
        left_mat, right_mat, (((1,), (1,)), ((), ())), preferred_element_type=jnp.float32
    )


def rms_norm(values, gain_vec):
    return (
        values * lax.rsqrt(jnp.mean(values * values, axis=-1, keepdims=True) + EPSILON) * gain_vec
    )


def rope_tables(positions, width):
    half_width = width // 2
    frequency = jnp.exp(
        jnp.arange(half_width, dtype=jnp.float32) * (-2.0 * math.log(ROPE_BASE) / width)
    )
    angles = positions.astype(jnp.float32)[:, None] * frequency[None, :]
    return (jnp.cos(angles)[:, None, :], jnp.sin(angles)[:, None, :])


def rotate(values, cosine, sine_part):
    half_width = values.shape[-1] // 2
    first_half = values[..., :half_width]
    second_half = values[..., half_width:]
    return jnp.concatenate(
        [
            first_half * cosine - second_half * sine_part,
            second_half * cosine + first_half * sine_part,
        ],
        axis=-1,
    )


def document_ids(doc_lengths, places):
    doc_ends = jnp.cumsum(doc_lengths)
    return jnp.sum((places[:, None] >= doc_ends[None, :-1]).astype(jnp.int32), axis=1)


def query_key(cosine, sine_part, query_lin, key_lin, gain_query, gain_key):
    tok_count = query_lin.shape[0]
    query_rot = rotate(
        rms_norm(query_lin.reshape(tok_count, HQ, HD), gain_query), cosine, sine_part
    )
    key_rot = rotate(rms_norm(key_lin.reshape(tok_count, KV, HD), gain_key), cosine, sine_part)
    return (query_rot, key_rot)


def mix_piece(inputs, normed, projected, widened, gain_post, gain_laurel):
    return (
        inputs + rms_norm(projected, gain_post) + normed + rms_norm(widened, gain_laurel)
    ) * HALF_ROOT


def geglu(gate_lin, up_lin):
    return jax.nn.gelu(gate_lin, approximate=True) * up_lin


def ffn_out_piece(mixed, down_lin, gain_ffout):
    return mixed + rms_norm(down_lin, gain_ffout)


def ple_act(ple_lin, ple_input):
    return jax.nn.gelu(ple_lin, approximate=True) * ple_input


def final_piece(layer_mid, ple_wide, gain_ple):
    return layer_mid + rms_norm(ple_wide, gain_ple)


def visibility(doc_lengths, query_start, key_start, tok_count, span_len):
    query_places = query_start + jnp.arange(tok_count, dtype=jnp.int32)
    key_places = key_start + jnp.arange(span_len, dtype=jnp.int32)
    distance = query_places[:, None] - key_places[None, :]
    query_docs = document_ids(doc_lengths, query_places)
    key_docs = document_ids(doc_lengths, key_places)
    return (
        (distance >= 0)
        & (distance < WINDOW)
        & (key_places[None, :] >= 0)
        & (query_docs[:, None] == key_docs[None, :])
    )


def attend_forward(query_low, span_kv, visible):
    tok_count = query_low.shape[0]
    scale_factor = 1.0 / math.sqrt(HD)
    scores = (
        jnp.einsum("tkgh,skh->kgts", query_low, span_kv[0], preferred_element_type=jnp.float32)
        * scale_factor
    )
    scores = jnp.where(visible, scores, NEGATIVE)
    row_top = jnp.max(scores, axis=-1, keepdims=True)
    shifted = jnp.exp(scores - row_top)
    row_total = jnp.sum(shifted, axis=-1, keepdims=True)
    attn_probs = shifted / row_total
    attended = jnp.einsum(
        "kgts,skh->tkgh",
        attn_probs.astype(jnp.bfloat16),
        span_kv[1],
        preferred_element_type=jnp.float32,
    )
    return (attended.reshape(tok_count, -1), row_top + jnp.log(row_total))


def attend_backward(query_low, span_kv, visible, log_total, grad_out_low):
    scale_factor = 1.0 / math.sqrt(HD)
    scores = (
        jnp.einsum("tkgh,skh->kgts", query_low, span_kv[0], preferred_element_type=jnp.float32)
        * scale_factor
    )
    attn_probs = jnp.where(visible, jnp.exp(jnp.where(visible, scores, NEGATIVE) - log_total), 0.0)
    grad_probs = jnp.einsum(
        "tkgh,skh->kgts", grad_out_low, span_kv[1], preferred_element_type=jnp.float32
    )
    inner_sum = jnp.sum(attn_probs * grad_probs, axis=-1, keepdims=True)
    grad_scores = (attn_probs * (grad_probs - inner_sum)).astype(jnp.bfloat16)
    grad_query = (
        jnp.einsum("kgts,skh->tkgh", grad_scores, span_kv[0], preferred_element_type=jnp.float32)
        * scale_factor
    )
    grad_keys = (
        jnp.einsum("kgts,tkgh->skh", grad_scores, query_low, preferred_element_type=jnp.float32)
        * scale_factor
    )
    grad_values = jnp.einsum(
        "kgts,tkgh->skh",
        attn_probs.astype(jnp.bfloat16),
        grad_out_low,
        preferred_element_type=jnp.float32,
    )
    return (grad_query, jnp.stack([grad_keys, grad_values]))


def settle(act_low, grad_low):
    act_cols = lax.all_to_all(act_low, "fsdp", split_axis=1, concat_axis=0, tiled=True)
    shard_rows = matmul_tn(act_cols, lax.all_gather(grad_low, "fsdp", axis=0, tiled=True))
    return lax.psum(shard_rows.astype(jnp.bfloat16), "ctx").astype(jnp.float32)


def local(
    tokens,
    per_layer,
    cotangent,
    doc_lengths,
    positions,
    w_query,
    w_key,
    w_value,
    w_out,
    laurel_left,
    laurel_right,
    w_gate,
    w_up,
    w_down,
    ple_gate,
    ple_proj,
    attn_in_gain,
    query_gain,
    key_gain,
    attn_out_gain,
    laurel_gain,
    ffn_in_gain,
    ffn_out_gain,
    ple_gain,
):
    bfloat = jnp.bfloat16
    tok_count = tokens.shape[0]
    span_len = WINDOW + tok_count
    groups = HQ // KV
    dev_index = lax.axis_index("ctx") * lax.axis_size("fsdp") + lax.axis_index("fsdp")
    query_start = dev_index * tok_count
    key_start = query_start - WINDOW
    visible = visibility(doc_lengths, query_start, key_start, tok_count, span_len)
    cosine, sine_part = rope_tables(positions, HD)
    gain_in, gain_query, gain_key, gain_post, gain_laurel, gain_ffin, gain_ffout, gain_ple = (
        lax.all_gather(attn_in_gain, "fsdp", axis=0, tiled=True),
        lax.all_gather(query_gain, "fsdp", axis=0, tiled=True),
        lax.all_gather(key_gain, "fsdp", axis=0, tiled=True),
        lax.all_gather(attn_out_gain, "fsdp", axis=0, tiled=True),
        lax.all_gather(laurel_gain, "fsdp", axis=0, tiled=True),
        lax.all_gather(ffn_in_gain, "fsdp", axis=0, tiled=True),
        lax.all_gather(ffn_out_gain, "fsdp", axis=0, tiled=True),
        lax.all_gather(ple_gain, "fsdp", axis=0, tiled=True),
    )
    full_query, full_key, full_value, full_out, full_left, full_right = (
        lax.all_gather(w_query.astype(bfloat), "fsdp", axis=0, tiled=True),
        lax.all_gather(w_key.astype(bfloat), "fsdp", axis=0, tiled=True),
        lax.all_gather(w_value.astype(bfloat), "fsdp", axis=0, tiled=True),
        lax.all_gather(w_out.astype(bfloat), "fsdp", axis=0, tiled=True),
        lax.all_gather(laurel_left.astype(bfloat), "fsdp", axis=0, tiled=True),
        lax.all_gather(laurel_right.astype(bfloat), "fsdp", axis=0, tiled=True),
    )
    inputs = tokens.astype(jnp.float32)
    ple_input = per_layer.astype(jnp.float32)
    normed, norm_back = jax.vjp(rms_norm, inputs, gain_in)
    normed_low = normed.astype(bfloat)
    query_lin = matmul(normed_low, full_query)
    key_lin = matmul(normed_low, full_key)
    value_lin = matmul(normed_low, full_value)
    (query_rot, key_rot), rope_back = jax.vjp(
        functools.partial(query_key, cosine, sine_part), query_lin, key_lin, gain_query, gain_key
    )
    query_low = query_rot.astype(bfloat).reshape(tok_count, KV, groups, HD)
    keys_values = jnp.stack(
        [key_rot.astype(bfloat), value_lin.astype(bfloat).reshape(tok_count, KV, HD)]
    )
    block_kv = lax.all_gather(keys_values, "fsdp", axis=1, tiled=True)
    block_len = block_kv.shape[1]
    before_kv = passed_along(block_kv, "ctx", 1)
    span_offset = block_len + lax.axis_index("fsdp") * tok_count - WINDOW
    span_kv = lax.dynamic_slice_in_dim(
        jnp.concatenate([before_kv, block_kv], axis=1), span_offset, span_len, 1
    )
    attended, log_total = attend_forward(query_low, span_kv, visible)
    attended_low = attended.astype(bfloat)
    projected = matmul(attended_low, full_out)
    narrow_low = matmul(normed_low, full_left).astype(bfloat)
    widened = matmul(narrow_low, full_right)
    mixed, mix_back = jax.vjp(mix_piece, inputs, normed, projected, widened, gain_post, gain_laurel)
    full_gate, full_up, full_down, full_pgate, full_pproj = (
        lax.all_gather(w_gate.astype(bfloat), "fsdp", axis=0, tiled=True),
        lax.all_gather(w_up.astype(bfloat), "fsdp", axis=0, tiled=True),
        lax.all_gather(w_down.astype(bfloat), "fsdp", axis=0, tiled=True),
        lax.all_gather(ple_gate.astype(bfloat), "fsdp", axis=0, tiled=True),
        lax.all_gather(ple_proj.astype(bfloat), "fsdp", axis=0, tiled=True),
    )
    ffn_normed, ffn_norm_back = jax.vjp(rms_norm, mixed, gain_ffin)
    ffn_low = ffn_normed.astype(bfloat)
    gate_lin = matmul(ffn_low, full_gate)
    up_lin = matmul(ffn_low, full_up)
    hidden, geglu_back = jax.vjp(geglu, gate_lin, up_lin)
    hidden_low = hidden.astype(bfloat)
    down_lin = matmul(hidden_low, full_down)
    layer_mid, ffn_out_back = jax.vjp(ffn_out_piece, mixed, down_lin, gain_ffout)
    layer_low = layer_mid.astype(bfloat)
    ple_lin = matmul(layer_low, full_pgate)
    ple_mid, ple_back = jax.vjp(ple_act, ple_lin, ple_input)
    ple_low = ple_mid.astype(bfloat)
    ple_wide = matmul(ple_low, full_pproj)
    out_full, final_back = jax.vjp(final_piece, layer_mid, ple_wide, gain_ple)
    full_gate, full_up, full_down, full_pgate, full_pproj = (
        lax.all_gather(w_gate.astype(bfloat), "fsdp", axis=0, tiled=True),
        lax.all_gather(w_up.astype(bfloat), "fsdp", axis=0, tiled=True),
        lax.all_gather(w_down.astype(bfloat), "fsdp", axis=0, tiled=True),
        lax.all_gather(ple_gate.astype(bfloat), "fsdp", axis=0, tiled=True),
        lax.all_gather(ple_proj.astype(bfloat), "fsdp", axis=0, tiled=True),
    )
    grad_layer, grad_pwide, grad_gple = final_back(cotangent.astype(jnp.float32))
    grad_pwide_low = grad_pwide.astype(bfloat)
    grad_pproj = settle(ple_low, grad_pwide_low)
    grad_plemid = matmul_nt(grad_pwide_low, full_pproj)
    grad_plelin, grad_pleinput = ple_back(grad_plemid)
    grad_plelin_low = grad_plelin.astype(bfloat)
    grad_pgate = settle(layer_low, grad_plelin_low)
    grad_layer = grad_layer + matmul_nt(grad_plelin_low, full_pgate)
    grad_mixed, grad_down, grad_gffout = ffn_out_back(grad_layer)
    grad_down_low = grad_down.astype(bfloat)
    grad_wdown = settle(hidden_low, grad_down_low)
    grad_hidden = matmul_nt(grad_down_low, full_down)
    grad_gate, grad_up = geglu_back(grad_hidden)
    grad_gate_low = grad_gate.astype(bfloat)
    grad_up_low = grad_up.astype(bfloat)
    grad_wgate = settle(ffn_low, grad_gate_low)
    grad_wup = settle(ffn_low, grad_up_low)
    grad_ffn = matmul_nt(grad_gate_low, full_gate) + matmul_nt(grad_up_low, full_up)
    grad_mixed_more, grad_gffin = ffn_norm_back(grad_ffn)
    grad_mixed = grad_mixed + grad_mixed_more
    full_query, full_key, full_value, full_out, full_left, full_right = (
        lax.all_gather(w_query.astype(bfloat), "fsdp", axis=0, tiled=True),
        lax.all_gather(w_key.astype(bfloat), "fsdp", axis=0, tiled=True),
        lax.all_gather(w_value.astype(bfloat), "fsdp", axis=0, tiled=True),
        lax.all_gather(w_out.astype(bfloat), "fsdp", axis=0, tiled=True),
        lax.all_gather(laurel_left.astype(bfloat), "fsdp", axis=0, tiled=True),
        lax.all_gather(laurel_right.astype(bfloat), "fsdp", axis=0, tiled=True),
    )
    grad_in_first, grad_normed, grad_proj, grad_lwide, grad_gpost, grad_glaurel = mix_back(
        grad_mixed
    )
    grad_proj_low = grad_proj.astype(bfloat)
    grad_wout = settle(attended_low, grad_proj_low)
    grad_att_low = matmul_nt(grad_proj_low, full_out).astype(bfloat)
    grad_lwide_low = grad_lwide.astype(bfloat)
    grad_wright = settle(narrow_low, grad_lwide_low)
    grad_narrow_low = matmul_nt(grad_lwide_low, full_right).astype(bfloat)
    grad_wleft = settle(normed_low, grad_narrow_low)
    grad_normed = grad_normed + matmul_nt(grad_narrow_low, full_left)
    grad_query_att, grad_span = attend_backward(
        query_low, span_kv, visible, log_total, grad_att_low.reshape(tok_count, KV, groups, HD)
    )
    whole_grad = jnp.zeros((2, 2 * block_len, KV, HD), jnp.float32)
    whole_grad = lax.dynamic_update_slice_in_dim(whole_grad, grad_span, span_offset, 1)
    returned = passed_along(whole_grad[:, :block_len].astype(jnp.bfloat16), "ctx", -1).astype(
        jnp.float32
    )
    own_grad = lax.psum_scatter(
        (whole_grad[:, block_len:] + returned).astype(jnp.bfloat16),
        "fsdp",
        scatter_dimension=1,
        tiled=True,
    ).astype(jnp.float32)
    grad_qlin, grad_klin, grad_gquery, grad_gkey = rope_back(
        (grad_query_att.reshape(tok_count, HQ, HD), own_grad[0])
    )
    grad_qlin_low = grad_qlin.astype(bfloat)
    grad_klin_low = grad_klin.astype(bfloat)
    grad_vlin_low = own_grad[1].reshape(tok_count, KV * HD).astype(bfloat)
    grad_wquery = settle(normed_low, grad_qlin_low)
    grad_wkey = settle(normed_low, grad_klin_low)
    grad_wvalue = settle(normed_low, grad_vlin_low)
    grad_normed = (
        grad_normed
        + matmul_nt(grad_qlin_low, full_query)
        + matmul_nt(grad_klin_low, full_key)
        + matmul_nt(grad_vlin_low, full_value)
    )
    grad_in_second, grad_gin = norm_back(grad_normed)
    grad_tokens = grad_in_first + grad_in_second
    sum_gin, sum_gquery, sum_gkey, sum_gpost, sum_glaurel, sum_gffin, sum_gffout, sum_gple = (
        lax.psum(
            (
                grad_gin,
                grad_gquery,
                grad_gkey,
                grad_gpost,
                grad_glaurel,
                grad_gffin,
                grad_gffout,
                grad_gple,
            ),
            ("ctx", "fsdp"),
        )
    )
    wide_rows = attn_in_gain.shape[0]
    head_rows = query_gain.shape[0]
    wide_start = lax.axis_index("fsdp") * wide_rows
    head_start = lax.axis_index("fsdp") * head_rows

    def wide_part(full_vec):
        return lax.dynamic_slice_in_dim(full_vec, wide_start, wide_rows, 0)

    def head_part(full_vec):
        return lax.dynamic_slice_in_dim(full_vec, head_start, head_rows, 0)

    return (
        out_full.astype(bfloat),
        grad_tokens,
        grad_pleinput,
        grad_wquery,
        grad_wkey,
        grad_wvalue,
        grad_wout,
        grad_wleft,
        grad_wright,
        grad_wgate,
        grad_wup,
        grad_wdown,
        grad_pgate,
        grad_pproj,
        wide_part(sum_gin),
        head_part(sum_gquery),
        head_part(sum_gkey),
        wide_part(sum_gpost),
        wide_part(sum_glaurel),
        wide_part(sum_gffin),
        wide_part(sum_gffout),
        wide_part(sum_gple),
    )

def remote(src, dst, send_sem, recv_sem, place):
    return pltpu.make_async_remote_copy(
        src_ref=src,
        dst_ref=dst,
        send_sem=send_sem,
        recv_sem=recv_sem,
        device_id={"fsdp": place},
        device_id_type=pl.DeviceIdType.MESH,
    )


def dot_nn(left_mat, right_mat):
    return jnp.dot(left_mat, right_mat, preferred_element_type=jnp.float32)


def dot_nt(left_mat, right_mat):
    return lax.dot_general(
        left_mat, right_mat, (((1,), (1,)), ((), ())), preferred_element_type=jnp.float32
    )


PIECES = 4


def line_scratch(chips, tok_count, width):
    dma = pltpu.SemaphoreType.DMA
    shard = (tok_count, width)
    return [
        pltpu.VMEM((chips, 2) + shard, jnp.bfloat16),
        dma((chips, 2)),
        dma((chips, 3)),
        dma,
        pltpu.VMEM((chips, 2) + shard, jnp.bfloat16),
        pltpu.VMEM((chips,) + shard, jnp.bfloat16),
        pltpu.VMEM((chips,) + shard, jnp.bfloat16),
        pltpu.VMEM((chips,) + shard, jnp.bfloat16),
        dma((chips,)),
        dma((chips,)),
        dma((chips, PIECES)),
        dma((chips, PIECES)),
        dma((chips, PIECES)),
    ]


LINE_REFS = 13


class Line:
    def __init__(self, chips, refs):
        (
            self.slots,
            self.slot_recv,
            self.slot_send,
            self.own_sem,
            self.parts,
            self.from_core,
            self.from_left,
            self.from_right,
            self.core_send,
            self.core_recv,
            self.flow_send,
            self.left_recv,
            self.right_recv,
        ) = refs
        self.chips = chips
        me = lax.axis_index("fsdp")
        self.chip = me // 2
        self.core = me % 2
        self.tok = self.slots.shape[2]
        self.piece = self.tok // PIECES

    def place(self, chip, core):
        return chip * 2 + core

    def order(self, step):
        picked = 0
        for chip in range(self.chips):
            near = sorted(range(self.chips), key=lambda other: (abs(other - chip), other))
            picked = picked + jnp.where(self.chip == chip, near[step], 0)
        return picked

    def barrier(self):
        sem = pltpu.get_barrier_semaphore()

        def greet(place):
            pl.semaphore_signal(
                sem, inc=1, device_id={"fsdp": place}, device_id_type=pl.DeviceIdType.MESH
            )

        greet(self.place(self.chip, 1 - self.core))

        @pl.when(self.chip > 0)
        def _():
            greet(self.place(self.chip - 1, self.core))

        @pl.when(self.chip < self.chips - 1)
        def _():
            greet(self.place(self.chip + 1, self.core))

        ends = jnp.where(self.chip == 0, 1, 0) + jnp.where(self.chip == self.chips - 1, 1, 0)
        pl.semaphore_wait(sem, 3 - ends)

    def slot_copy(self, src, chip, way):
        place = (
            self.place(self.chip + 1, self.core),
            self.place(self.chip - 1, self.core),
            self.place(self.chip, 1 - self.core),
        )[way]
        return remote(
            src,
            self.slots.at[chip, self.core],
            self.slot_send.at[chip, way],
            self.slot_recv.at[chip, self.core],
            place,
        )

    def own_copy(self, own_ref):
        return pltpu.make_async_copy(own_ref, self.slots.at[self.chip, self.core], self.own_sem)

    def gather_begin(self, own_ref):
        @pl.when(self.chip < self.chips - 1)
        def _():
            self.slot_copy(own_ref, self.chip, 0).start()

        @pl.when(self.chip > 0)
        def _():
            self.slot_copy(own_ref, self.chip, 1).start()

        self.slot_copy(own_ref, self.chip, 2).start()
        self.own_copy(own_ref).start()

    def gather_step(self, distance):
        for chip, there, way, onward in (
            (self.chip - distance, self.chip >= distance, 0, self.chip < self.chips - 1),
            (self.chip + distance, self.chip + distance < self.chips, 1, self.chip > 0),
        ):

            @pl.when(there)
            def _(chip=chip, way=way, onward=onward):
                src = self.slots.at[chip, self.core]
                self.slot_copy(src, chip, way).wait_recv()

                @pl.when(onward)
                def _():
                    self.slot_copy(src, chip, way).start()

                self.slot_copy(src, chip, 2).start()

    def gather_other(self, chip):
        dst = self.slots.at[chip, 1 - self.core]
        remote(
            dst,
            dst,
            self.slot_send.at[chip, 2],
            self.slot_recv.at[chip, 1 - self.core],
            self.place(self.chip, 1 - self.core),
        ).wait_recv()

    def gather_end(self):
        for chip in range(self.chips):
            src = self.slots.at[chip, self.core]

            @pl.when((self.chip >= chip) & (self.chip < self.chips - 1))
            def _(src=src, chip=chip):
                self.slot_copy(src, chip, 0).wait_send()

            @pl.when((self.chip <= chip) & (self.chip > 0))
            def _(src=src, chip=chip):
                self.slot_copy(src, chip, 1).wait_send()

            self.slot_copy(src, chip, 2).wait_send()

    def core_copy(self, chip):
        return remote(
            self.parts.at[chip, 1 - self.core],
            self.from_core.at[chip],
            self.core_send.at[chip],
            self.core_recv.at[chip],
            self.place(self.chip, 1 - self.core),
        )

    def flow_copy(self, chip, piece, right):
        rows = pl.ds(piece * self.piece, self.piece)
        return remote(
            self.parts.at[chip, self.core, rows],
            (self.from_left if right else self.from_right).at[chip, rows],
            self.flow_send.at[chip, piece],
            (self.left_recv if right else self.right_recv).at[chip, piece],
            self.place(self.chip + (1 if right else -1), self.core),
        )

    def flow(self, chip, right, incoming):
        self.core_copy(chip).wait_recv()

        @pl.loop(0, PIECES)
        def _(piece):
            rows = pl.ds(pl.multiple_of(piece * self.piece, self.piece), self.piece)
            total = self.parts[chip, self.core, rows].astype(jnp.float32)
            total = total + self.from_core[chip, rows].astype(jnp.float32)
            if incoming:
                self.flow_copy(chip, piece, right).wait_recv()
                source = self.from_left if right else self.from_right
                total = total + source[chip, rows].astype(jnp.float32)
            self.parts[chip, self.core, rows] = total.astype(jnp.bfloat16)
            self.flow_copy(chip, piece, right).start()

    def scatter_first(self, chip):
        @pl.when((self.chip == 0) & (chip > 0))
        def _():
            self.flow(chip, True, False)

        @pl.when((self.chip == self.chips - 1) & (chip < self.chips - 1))
        def _():
            self.flow(chip, False, False)

    def scatter_rest(self, result_ref):
        for rank in range(3, 2 * self.chips - 2):
            right = rank - self.chip

            @pl.when((self.chip > 0) & (right > self.chip) & (right < self.chips))
            def _(right=right):
                self.flow(right, True, True)

            left = 2 * (self.chips - 1) - self.chip - rank

            @pl.when((self.chip < self.chips - 1) & (left < self.chip) & (left >= 0))
            def _(left=left):
                self.flow(left, False, True)

        own = self.chip
        self.core_copy(own).wait_recv()

        @pl.loop(0, PIECES)
        def _(piece):
            rows = pl.ds(pl.multiple_of(piece * self.piece, self.piece), self.piece)
            total = self.parts[own, self.core, rows].astype(jnp.float32)
            total = total + self.from_core[own, rows].astype(jnp.float32)
            result_ref[rows] = total

        @pl.when(own > 0)
        def _():
            @pl.loop(0, PIECES)
            def _(piece):
                rows = pl.ds(pl.multiple_of(piece * self.piece, self.piece), self.piece)
                self.flow_copy(own, piece, True).wait_recv()
                result_ref[rows] += self.from_left[own, rows].astype(jnp.float32)

        @pl.when(own < self.chips - 1)
        def _():
            @pl.loop(0, PIECES)
            def _(piece):
                rows = pl.ds(pl.multiple_of(piece * self.piece, self.piece), self.piece)
                self.flow_copy(own, piece, False).wait_recv()
                result_ref[rows] += self.from_right[own, rows].astype(jnp.float32)

        for chip in range(self.chips):
            self.core_copy(chip).wait_send()

            @pl.when(self.chip != chip)
            def _(chip=chip):
                for piece in range(PIECES):
                    self.flow_copy(chip, piece, True).wait_send()


def ffn_forward_kernel(
    chips,
    own_ref,
    gateup_hbm,
    down_hbm,
    result_ref,
    all_hbm,
    hidden_hbm,
    act_hbm,
    slope_hbm,
    *scratch,
):
    line = Line(chips, scratch[:LINE_REFS])
    gateup, down, hidden, act, slope, load_sems, store_sems = scratch[LINE_REFS:]
    ff_part = down.shape[0]
    width = down.shape[1]
    pair = 2 * line.tok
    load_gateup = pltpu.make_async_copy(gateup_hbm, gateup, load_sems.at[0])
    load_down = pltpu.make_async_copy(down_hbm, down, load_sems.at[1])
    load_gateup.start()
    load_down.start()
    line.barrier()
    line.gather_begin(own_ref)
    line.own_copy(own_ref).wait()

    def stores(chip):
        rows = pl.ds(pl.multiple_of(chip * pair, pair), pair)
        return [
            pltpu.make_async_copy(line.slots.at[chip], all_hbm.at[chip], store_sems.at[chip, 0]),
            pltpu.make_async_copy(hidden.at[rows], hidden_hbm.at[rows], store_sems.at[chip, 1]),
            pltpu.make_async_copy(act.at[rows], act_hbm.at[rows], store_sems.at[chip, 2]),
            pltpu.make_async_copy(slope.at[rows], slope_hbm.at[rows], store_sems.at[chip, 3]),
        ]

    tile = 256
    for step in range(chips):
        if step > 0:
            line.gather_step(step)
        chip = line.order(step)
        line.gather_other(chip)
        if step == 0:
            load_gateup.wait()
            load_down.wait()
        rows = pl.ds(pl.multiple_of(chip * pair, pair), pair)

        @pl.loop(0, ff_part // tile)
        def _(at, chip=chip, rows=rows):
            inputs = line.slots[chip].reshape(pair, width)
            gate_cols = pl.ds(pl.multiple_of(at * tile, tile), tile)
            up_cols = pl.ds(pl.multiple_of(ff_part + at * tile, tile), tile)
            gate = dot_nn(inputs, gateup[:, gate_cols])
            up = dot_nn(inputs, gateup[:, up_cols])
            square = gate * gate
            bent = jnp.tanh(GELU_ROOT * gate * (1.0 + GELU_CUBE * square))
            half = 0.5 + 0.5 * bent
            activated = gate * half
            rise = half + 0.5 * gate * (1.0 - bent * bent) * (
                GELU_ROOT * (1.0 + 3.0 * GELU_CUBE * square)
            )
            hidden[rows, gate_cols] = (activated * up).astype(jnp.bfloat16)
            act[rows, gate_cols] = activated.astype(jnp.bfloat16)
            slope[rows, gate_cols] = (rise * up).astype(jnp.bfloat16)

        for copy in stores(chip):
            copy.start()

        wide = 512

        @pl.loop(0, width // wide)
        def _(at, chip=chip, rows=rows):
            cols = pl.ds(pl.multiple_of(at * wide, wide), wide)
            sums = dot_nn(hidden[rows, :], down[:, cols]).astype(jnp.bfloat16)
            line.parts[chip, :, :, cols] = sums.reshape(2, line.tok, wide)

        line.core_copy(chip).start()
        if step > 0:
            line.scatter_first(line.order(step - 1))
    line.scatter_first(line.order(chips - 1))
    line.scatter_rest(result_ref)
    line.gather_end()
    for chip in range(chips):
        for copy in stores(chip):
            copy.wait()


def ffn_forward(own, gateup, down, chips):
    tok_count, width = own.shape
    ff_part = down.shape[0]
    block = 2 * chips * tok_count
    bfloat = jnp.bfloat16
    anywhere = pl.BlockSpec(memory_space=pl.ANY)
    vmem = pl.BlockSpec(memory_space=pltpu.VMEM)
    part = jax.ShapeDtypeStruct((block, ff_part), bfloat)
    result, gathered, hidden, act, slope = pl.pallas_call(
        functools.partial(ffn_forward_kernel, chips),
        out_shape=[
            jax.ShapeDtypeStruct((tok_count, width), jnp.float32),
            jax.ShapeDtypeStruct((chips, 2, tok_count, width), bfloat),
            part,
            part,
            part,
        ],
        in_specs=[vmem, anywhere, anywhere],
        out_specs=[vmem, anywhere, anywhere, anywhere, anywhere],
        scratch_shapes=line_scratch(chips, tok_count, width)
        + [
            pltpu.VMEM(gateup.shape, bfloat),
            pltpu.VMEM(down.shape, bfloat),
            pltpu.VMEM((block, ff_part), bfloat),
            pltpu.VMEM((block, ff_part), bfloat),
            pltpu.VMEM((block, ff_part), bfloat),
            pltpu.SemaphoreType.DMA((2,)),
            pltpu.SemaphoreType.DMA((chips, 4)),
        ],
        compiler_params=pltpu.CompilerParams(
            collective_id=1, has_side_effects=True, vmem_limit_bytes=KERNEL_VMEM
        ),
        cost_estimate=pl.CostEstimate(
            flops=6 * block * width * ff_part,
            bytes_accessed=40 << 20,
            transcendentals=block * ff_part,
        ),
        name="ffn_forward",
    )(own, gateup, down)
    return result, gathered.reshape(block, width), hidden, act, slope


def ffn_backward_kernel(
    chips,
    own_ref,
    gateup_hbm,
    down_hbm,
    act_hbm,
    slope_hbm,
    result_ref,
    all_hbm,
    grad_hbm,
    *scratch,
):
    line = Line(chips, scratch[:LINE_REFS])
    gateup, down, act, slope, grad, load_sems, store_sems = scratch[LINE_REFS:]
    ff_part = down.shape[0]
    width = down.shape[1]
    pair = 2 * line.tok
    loads = [
        pltpu.make_async_copy(down_hbm, down, load_sems.at[0]),
        pltpu.make_async_copy(act_hbm, act, load_sems.at[1]),
        pltpu.make_async_copy(slope_hbm, slope, load_sems.at[2]),
        pltpu.make_async_copy(gateup_hbm, gateup, load_sems.at[3]),
    ]
    for load in loads:
        load.start()
    line.barrier()
    line.gather_begin(own_ref)
    line.own_copy(own_ref).wait()

    def stores(chip):
        rows = pl.ds(pl.multiple_of(chip * pair, pair), pair)
        return [
            pltpu.make_async_copy(line.slots.at[chip], all_hbm.at[chip], store_sems.at[chip, 0]),
            pltpu.make_async_copy(grad.at[rows], grad_hbm.at[rows], store_sems.at[chip, 1]),
        ]

    tile = 256
    for step in range(chips):
        if step > 0:
            line.gather_step(step)
        chip = line.order(step)
        line.gather_other(chip)
        if step == 0:
            for load in loads:
                load.wait()
        rows = pl.ds(pl.multiple_of(chip * pair, pair), pair)

        @pl.loop(0, ff_part // tile)
        def _(at, chip=chip, rows=rows):
            grads = line.slots[chip].reshape(pair, width)
            gate_cols = pl.ds(pl.multiple_of(at * tile, tile), tile)
            up_cols = pl.ds(pl.multiple_of(ff_part + at * tile, tile), tile)
            grad_hidden = dot_nt(grads, down[gate_cols, :])
            grad[rows, gate_cols] = (
                grad_hidden * slope[rows, gate_cols].astype(jnp.float32)
            ).astype(jnp.bfloat16)
            grad[rows, up_cols] = (grad_hidden * act[rows, gate_cols].astype(jnp.float32)).astype(
                jnp.bfloat16
            )

        for copy in stores(chip):
            copy.start()

        wide = 512

        @pl.loop(0, width // wide)
        def _(at, chip=chip, rows=rows):
            cols = pl.ds(pl.multiple_of(at * wide, wide), wide)
            sums = dot_nt(grad[rows, :], gateup[cols, :]).astype(jnp.bfloat16)
            line.parts[chip, :, :, cols] = sums.reshape(2, line.tok, wide)

        line.core_copy(chip).start()
        if step > 0:
            line.scatter_first(line.order(step - 1))
    line.scatter_first(line.order(chips - 1))
    line.scatter_rest(result_ref)
    line.gather_end()
    for chip in range(chips):
        for copy in stores(chip):
            copy.wait()


def ffn_backward(own, gateup, down, act, slope, chips):
    tok_count, width = own.shape
    ff_part = down.shape[0]
    block = 2 * chips * tok_count
    bfloat = jnp.bfloat16
    anywhere = pl.BlockSpec(memory_space=pl.ANY)
    vmem = pl.BlockSpec(memory_space=pltpu.VMEM)
    result, gathered, grad = pl.pallas_call(
        functools.partial(ffn_backward_kernel, chips),
        out_shape=[
            jax.ShapeDtypeStruct((tok_count, width), jnp.float32),
            jax.ShapeDtypeStruct((chips, 2, tok_count, width), bfloat),
            jax.ShapeDtypeStruct((block, 2 * ff_part), bfloat),
        ],
        in_specs=[vmem] + [anywhere] * 4,
        out_specs=[vmem, anywhere, anywhere],
        scratch_shapes=line_scratch(chips, tok_count, width)
        + [
            pltpu.VMEM(gateup.shape, bfloat),
            pltpu.VMEM(down.shape, bfloat),
            pltpu.VMEM((block, ff_part), bfloat),
            pltpu.VMEM((block, ff_part), bfloat),
            pltpu.VMEM((block, 2 * ff_part), bfloat),
            pltpu.SemaphoreType.DMA((4,)),
            pltpu.SemaphoreType.DMA((chips, 2)),
        ],
        compiler_params=pltpu.CompilerParams(
            collective_id=2, has_side_effects=True, vmem_limit_bytes=KERNEL_VMEM
        ),
        cost_estimate=pl.CostEstimate(
            flops=6 * block * width * ff_part, bytes_accessed=40 << 20, transcendentals=0
        ),
        name="ffn_backward",
    )(own, gateup, down, act, slope)
    return result, gathered.reshape(block, width), grad

class Share:
    def __init__(self, refs, columns):
        self.columns = columns
        self.source, self.final, self.kept, self.taken, self.last = refs[:5]
        self.load_sem, self.sum_send, self.sum_recv, self.spread_send, self.spread_recv = refs[5:10]
        if columns:
            self.swap_send, self.swap_recv, self.swap_own = refs[10:13]
        at = lax.axis_index("ctx")
        self.at_x, self.at_y = at % 2, at // 2
        self.beside = (at + 1 - 2 * (at % 2), (at + 2) % 4)
        self.me = lax.axis_index("fsdp")
        self.members = lax.axis_size("fsdp")
        self.half = self.source.shape[-2] // 2
        self.quarter = self.half // 2
        self.eighth = self.half // 4

    def rows(self, ref, start, size):
        start = pl.multiple_of(start, size)
        return ref.at[:, pl.ds(start, size)] if self.columns else ref.at[pl.ds(start, size)]

    def sides(self, half):
        return (self.at_x, self.at_y) if half == 0 else (self.at_y, self.at_x)

    def kept_start(self, half):
        return half * self.half + self.sides(half)[0] * self.quarter

    def given_start(self, half):
        return half * self.half + (1 - self.sides(half)[0]) * self.quarter

    def own_start(self, half):
        return self.kept_start(half) + self.sides(half)[1] * self.eighth

    def copy(self, src, dst, send_sem, recv_sem, half, stage):
        return pltpu.make_async_remote_copy(
            src_ref=src,
            dst_ref=dst,
            send_sem=send_sem.at[half, stage],
            recv_sem=recv_sem.at[half, stage],
            device_id={"ctx": self.beside[(half + stage) % 2]},
            device_id_type=pl.DeviceIdType.MESH,
        )

    def load(self, half):
        return pltpu.make_async_copy(
            self.rows(self.source, self.kept_start(half), self.quarter),
            self.kept.at[half],
            self.load_sem.at[half],
        )

    def first(self, half):
        return self.copy(
            self.rows(self.source, self.given_start(half), self.quarter),
            self.taken.at[half],
            self.sum_send,
            self.sum_recv,
            half,
            0,
        )

    def second(self, half):
        other = (1 - self.sides(half)[1]) * self.eighth
        return self.copy(
            self.rows(self.kept.at[half], other, self.eighth),
            self.last.at[half],
            self.sum_send,
            self.sum_recv,
            half,
            1,
        )

    def begin(self):
        for half in (0, 1):
            self.first(half).start()
            self.load(half).start()

    def add(self, half, start, more, more_start):
        step = min(32, self.eighth)
        blocks = self.eighth // step
        layers = self.source.shape[0] if self.columns else 1

        @pl.loop(0, layers * blocks)
        def _(at):
            layer, block = at // blocks, at % blocks
            here = pl.ds(pl.multiple_of(start + block * step, step), step)
            there = pl.ds(pl.multiple_of(more_start + block * step, step), step)
            if self.columns:
                total = self.kept[half, layer, here].astype(jnp.float32)
                total = total + more[half, layer, there].astype(jnp.float32)
                self.kept[half, layer, here] = total.astype(jnp.bfloat16)
            else:
                total = self.kept[half, here].astype(jnp.float32)
                total = total + more[half, there].astype(jnp.float32)
                self.kept[half, here] = total.astype(jnp.bfloat16)

    def middle(self):
        for half in (0, 1):
            self.load(half).wait()
            self.first(half).wait_recv()
            side = self.sides(half)[1]
            other = (1 - side) * self.eighth
            self.add(half, other, self.taken, other)
            self.second(half).start()
            mine = side * self.eighth
            self.add(half, mine, self.taken, mine)

    def finish(self):
        for half in (0, 1):
            self.second(half).wait_recv()
            self.add(half, self.sides(half)[1] * self.eighth, self.last, 0)

    def own_rows(self, half):
        return self.rows(self.kept.at[half], self.sides(half)[1] * self.eighth, self.eighth)

    def place(self, half):
        return pltpu.make_async_copy(
            self.own_rows(half),
            self.rows(self.final, self.own_start(half), self.eighth),
            self.load_sem.at[half],
        )

    def swap_copy(self, half, hop, src_member):
        target = lax.rem(self.me + hop, self.members)
        side = self.sides(half)[1] * self.eighth
        rows = pl.ds(pl.multiple_of(side, self.eighth), self.eighth)
        final_rows = pl.ds(pl.multiple_of(self.own_start(half), self.eighth), self.eighth)
        return remote(
            self.kept.at[half, target, rows],
            self.final.at[src_member, final_rows],
            self.swap_send.at[hop, half],
            self.swap_recv.at[hop, half],
            target,
        )

    def swap_local(self, half):
        side = self.sides(half)[1] * self.eighth
        rows = pl.ds(pl.multiple_of(side, self.eighth), self.eighth)
        final_rows = pl.ds(pl.multiple_of(self.own_start(half), self.eighth), self.eighth)
        return pltpu.make_async_copy(
            self.kept.at[half, self.me, rows],
            self.final.at[self.me, final_rows],
            self.swap_own.at[half],
        )

    def swap_begin(self):
        for half in (0, 1):
            for hop in range(1, self.members):
                self.swap_copy(half, hop, self.me).start()
            self.swap_local(half).start()

    def swap_end(self):
        for half in (0, 1):
            for hop in range(1, self.members):
                source = lax.rem(self.me + self.members - hop, self.members)
                self.swap_copy(half, hop, source).wait_recv()
            self.swap_local(half).wait()

    def spread_copy(self, half, stage):
        if stage == 0:
            rows = self.rows(self.final, self.own_start(half), self.eighth)
        else:
            rows = self.rows(self.final, self.kept_start(half), self.quarter)
        return self.copy(rows, rows, self.spread_send, self.spread_recv, half, 1 - stage)

    def spread_wait(self, half, stage):
        side = self.sides(half)[1]
        if stage == 0:
            start = self.kept_start(half) + (1 - side) * self.eighth
            rows = self.rows(self.final, start, self.eighth)
        else:
            rows = self.rows(self.final, self.given_start(half), self.quarter)
        self.copy(rows, rows, self.spread_send, self.spread_recv, half, 1 - stage).wait_recv()

    def spread_begin(self):
        for half in (0, 1):
            self.spread_copy(half, 0).start()

    def spread_on(self):
        for half in (0, 1):
            self.spread_wait(half, 0)
            self.spread_copy(half, 1).start()

    def spread_end(self):
        for half in (0, 1):
            self.spread_wait(half, 1)

    def sent(self):
        for half in (0, 1):
            self.first(half).wait_send()
            self.second(half).wait_send()
            self.spread_copy(half, 0).wait_send()
            self.spread_copy(half, 1).wait_send()
            if self.columns:
                for hop in range(1, self.members):
                    self.swap_copy(half, hop, self.me).wait_send()


def share_scratch(shape, columns):
    dma = pltpu.SemaphoreType.DMA
    rows, width = shape[-2:]
    lead = shape[:-2]

    def buffer(count):
        return pltpu.VMEM((2,) + lead + (count, width), jnp.bfloat16)

    scratch = [
        pltpu.VMEM(shape, jnp.bfloat16),
        buffer(rows // 4),
        buffer(rows // 4),
        buffer(rows // 8),
        dma((2,)),
        dma((2, 2)),
        dma((2, 2)),
        dma((2, 2)),
        dma((2, 2)),
    ]
    if columns:
        scratch += [dma((shape[0], 2)), dma((shape[0], 2)), dma((2,))]
    return scratch


def gradient_sum_kernel(columns, *refs):
    count = len(columns)
    sources, results = refs[:count], refs[count : 2 * count + 1]
    scratch = list(refs[2 * count + 1 :])
    store_sem = scratch.pop()
    shares = []
    for source, by_column in zip(sources, columns):
        size = 12 if by_column else 9
        shares.append(Share([source] + scratch[:size], by_column))
        del scratch[:size]

    ctx_at = lax.axis_index("ctx")
    fsdp_at = lax.axis_index("fsdp")
    members = lax.axis_size("fsdp")
    sem = pltpu.get_barrier_semaphore()
    mesh_id = pl.DeviceIdType.MESH
    for beside in shares[0].beside:
        pl.semaphore_signal(sem, inc=1, device_id={"ctx": beside}, device_id_type=mesh_id)
    for hop in range(1, members):
        other = lax.rem(fsdp_at + hop, members)
        pl.semaphore_signal(sem, inc=1, device_id={"fsdp": other}, device_id_type=mesh_id)
    pl.semaphore_wait(sem, members + 1)

    def stores(at):
        share = shares[at]
        if at > 0:
            return [pltpu.make_async_copy(share.final, results[at + 1], store_sem.at[0, at])]
        part = share.final.shape[2] // 2
        return [
            pltpu.make_async_copy(
                share.final.at[member, :, pl.ds(side * part, part)],
                results[side].at[:, pl.ds(member * part, part)],
                store_sem.at[1 + side, member],
            )
            for member in range(share.final.shape[0])
            for side in (0, 1)
        ]

    for share in shares:
        share.begin()
    for share in shares:
        share.middle()
    for share in shares:
        share.finish()
        if share.columns:
            share.swap_begin()
        else:
            for half in (0, 1):
                share.place(half).start()
                share.place(half).wait()
            share.spread_begin()
    for share in shares:
        if share.columns:
            share.swap_end()
            share.spread_begin()
        else:
            share.spread_on()
    for share in shares:
        if share.columns:
            share.spread_on()
    for at, share in enumerate(shares):
        share.spread_end()
        for store in stores(at):
            store.start()
    for share in shares:
        share.sent()
    for at in range(count):
        for store in stores(at):
            store.wait()


def gradient_sum(grads):
    members, rows, width = grads[0].shape
    wide = jax.ShapeDtypeStruct((rows, members * width // 2), jnp.bfloat16)
    columns = [grad.ndim == 3 for grad in grads]
    anywhere = pl.BlockSpec(memory_space=pl.ANY)
    scratch = []
    for grad, by_column in zip(grads, columns):
        scratch += share_scratch(grad.shape, by_column)
    return pl.pallas_call(
        functools.partial(gradient_sum_kernel, columns),
        out_shape=[wide, wide]
        + [jax.ShapeDtypeStruct(grad.shape, jnp.bfloat16) for grad in grads[1:]],
        in_specs=[anywhere] * len(grads),
        out_specs=[anywhere] * (len(grads) + 1),
        scratch_shapes=scratch + [pltpu.SemaphoreType.DMA((3, members))],
        compiler_params=pltpu.CompilerParams(
            collective_id=3, has_side_effects=True, vmem_limit_bytes=KERNEL_VMEM
        ),
        cost_estimate=pl.CostEstimate(flops=0, bytes_accessed=300 << 20, transcendentals=0),
        name="gradient_sum",
    )(*grads)

def to_columns(pieces, ctx_count):
    packed = jnp.concatenate(pieces, axis=2)
    quarter = packed.shape[0] // ctx_count
    start = lax.axis_index("ctx") * quarter
    mine = lax.dynamic_slice_in_dim(packed, start, quarter, 0).astype(jnp.bfloat16)
    spread = lax.all_to_all(mine, "fsdp", split_axis=1, concat_axis=0, tiled=False)
    whole = lax.all_gather(spread, "ctx", axis=1, tiled=True)
    return whole.reshape(-1, whole.shape[-1])


def scatter_tokens(partial):
    return lax.psum_scatter(
        partial.astype(jnp.bfloat16), "fsdp", scatter_dimension=0, tiled=True
    ).astype(jnp.float32)


def gather_tokens(part):
    return lax.all_gather(part, "fsdp", axis=0, tiled=True)


def head_rope(cosine, sine_part, lin, gain_vec):
    return rotate(rms_norm(lin, gain_vec), cosine, sine_part)


def by_heads(
    tokens,
    per_layer,
    cotangent,
    doc_lengths,
    positions,
    w_query,
    w_key,
    w_value,
    w_out,
    laurel_left,
    laurel_right,
    w_gate,
    w_up,
    w_down,
    ple_gate,
    ple_proj,
    attn_in_gain,
    query_gain,
    key_gain,
    attn_out_gain,
    laurel_gain,
    ffn_in_gain,
    ffn_out_gain,
    ple_gain,
):
    bfloat = jnp.bfloat16
    ctx_count = lax.axis_size("ctx")
    fsdp_count = lax.axis_size("fsdp")
    tok_count = tokens.shape[0]
    block_len = tok_count * fsdp_count
    chips = fsdp_count // 2
    rows = w_query.shape[0]
    ff_part = w_gate.shape[1] // fsdp_count
    scale_factor = 1.0 / math.sqrt(HD)
    ctx_at = lax.axis_index("ctx")
    fsdp_at = lax.axis_index("fsdp")

    gain_list = [
        attn_in_gain,
        query_gain,
        key_gain,
        attn_out_gain,
        laurel_gain,
        ffn_in_gain,
        ffn_out_gain,
        ple_gain,
    ]
    gain_sizes = [g.shape[0] for g in gain_list]
    gain_offsets = [sum(gain_sizes[:n]) for n in range(len(gain_sizes) + 1)]
    all_gains = lax.all_gather(jnp.concatenate(gain_list), "fsdp", axis=0, tiled=False)
    gain_in, gain_query, gain_key, gain_post, gain_laurel, gain_ffin, gain_ffout, gain_ple = (
        all_gains[:, gain_offsets[n] : gain_offsets[n + 1]].reshape(-1) for n in range(8)
    )
    block_positions = lax.all_gather(positions, "fsdp", axis=0, tiled=True)
    cosine, sine_part = rope_tables(block_positions, HD)
    cosine, sine_part = cosine[:, 0], sine_part[:, 0]

    query_parts = w_query.reshape(rows, fsdp_count, HD)
    group_size = HQ // KV
    key_parts = jnp.repeat(w_key.reshape(rows, KV, HD), group_size, axis=1)
    value_parts = jnp.repeat(w_value.reshape(rows, KV, HD), group_size, axis=1)
    col_qkv = to_columns([query_parts, key_parts, value_parts], ctx_count)
    col_gateup = to_columns(
        [w_gate.reshape(rows, fsdp_count, ff_part), w_up.reshape(rows, fsdp_count, ff_part)],
        ctx_count,
    )
    out_low = w_out.astype(bfloat)
    down_low = w_down.astype(bfloat)
    full_left, full_right, full_pgate, full_pproj = (
        lax.all_gather(w.astype(bfloat), "fsdp", axis=0, tiled=True)
        for w in (laurel_left, laurel_right, ple_gate, ple_proj)
    )

    inputs = tokens.astype(jnp.float32)
    ple_input = per_layer.astype(jnp.float32)
    normed, norm_back = jax.vjp(rms_norm, inputs, gain_in)
    normed_low = normed.astype(bfloat)
    normed_all = gather_tokens(normed_low)
    qkv_lin = matmul(normed_all, col_qkv)
    query_lin, key_lin, value_lin = qkv_lin[:, :HD], qkv_lin[:, HD : 2 * HD], qkv_lin[:, 2 * HD :]
    rope_here = functools.partial(head_rope, cosine, sine_part)
    query_rot, query_back = jax.vjp(rope_here, query_lin, gain_query)
    key_rot, key_back = jax.vjp(rope_here, key_lin, gain_key)
    query_low = query_rot.astype(bfloat)
    own_kv = jnp.stack([key_rot.astype(bfloat), value_lin.astype(bfloat)])
    before_kv = passed_along(own_kv[:, block_len - WINDOW :], "ctx", 1)
    span_kv = jnp.concatenate([before_kv, own_kv], axis=1)

    chunk = 256
    span_len = WINDOW + chunk
    block_start = ctx_at * block_len
    prob_list, attended_list = [], []
    for begin in range(0, block_len, chunk):
        visible = visibility(
            doc_lengths, block_start + begin, block_start + begin - WINDOW, chunk, span_len
        )
        keys = span_kv[0, begin : begin + span_len]
        values = span_kv[1, begin : begin + span_len]
        scores = matmul_nt(query_low[begin : begin + chunk], keys) * scale_factor
        scores = jnp.where(visible, scores, NEGATIVE)
        shifted = jnp.exp(scores - jnp.max(scores, axis=-1, keepdims=True))
        probs = shifted / jnp.sum(shifted, axis=-1, keepdims=True)
        prob_list.append(probs)
        attended_list.append(matmul(probs.astype(bfloat), values))
    attended_low = jnp.concatenate(attended_list, axis=0).astype(bfloat)
    projected = scatter_tokens(matmul(attended_low, out_low))
    narrow_low = matmul(normed_low, full_left).astype(bfloat)
    widened = matmul(narrow_low, full_right)
    mixed, mix_back = jax.vjp(mix_piece, inputs, normed, projected, widened, gain_post, gain_laurel)
    ffn_normed, ffn_norm_back = jax.vjp(rms_norm, mixed, gain_ffin)
    down_lin, ffn_all, hidden_low, act_low, slope_low = ffn_forward(
        ffn_normed.astype(bfloat), col_gateup, down_low, chips
    )
    layer_mid, ffn_out_back = jax.vjp(ffn_out_piece, mixed, down_lin, gain_ffout)
    layer_low = layer_mid.astype(bfloat)
    ple_lin = matmul(layer_low, full_pgate)
    ple_mid, ple_back = jax.vjp(ple_act, ple_lin, ple_input)
    ple_low = ple_mid.astype(bfloat)
    ple_wide = matmul(ple_low, full_pproj)
    out_full, final_back = jax.vjp(final_piece, layer_mid, ple_wide, gain_ple)

    grad_layer, grad_pwide, grad_gple = final_back(cotangent.astype(jnp.float32))
    grad_pwide_low = grad_pwide.astype(bfloat)
    part_pproj = matmul_tn(ple_low, grad_pwide_low)
    grad_plemid = matmul_nt(grad_pwide_low, full_pproj)
    grad_plelin, grad_pleinput = ple_back(grad_plemid)
    grad_plelin_low = grad_plelin.astype(bfloat)
    part_pgate = matmul_tn(layer_low, grad_plelin_low)
    grad_layer = grad_layer + matmul_nt(grad_plelin_low, full_pgate)
    grad_mixed, grad_down, grad_gffout = ffn_out_back(grad_layer)
    grad_ffn, grad_down_all, grad_gateup_low = ffn_backward(
        grad_down.astype(bfloat), col_gateup, down_low, act_low, slope_low, chips
    )
    part_wdown = matmul_tn(hidden_low, grad_down_all).astype(bfloat)
    part_gateup = matmul_tn(ffn_all, grad_gateup_low).astype(bfloat).reshape(fsdp_count, rows, -1)
    grad_mixed_more, grad_gffin = ffn_norm_back(grad_ffn)
    grad_mixed = grad_mixed + grad_mixed_more
    grad_in_first, grad_normed, grad_proj, grad_lwide, grad_gpost, grad_glaurel = mix_back(
        grad_mixed
    )
    grad_proj_all = gather_tokens(grad_proj.astype(bfloat))
    part_wout = matmul_tn(attended_low, grad_proj_all).astype(bfloat)
    grad_att_low = matmul_nt(grad_proj_all, out_low).astype(bfloat)
    grad_lwide_low = grad_lwide.astype(bfloat)
    part_right = matmul_tn(narrow_low, grad_lwide_low)
    grad_narrow_low = matmul_nt(grad_lwide_low, full_right).astype(bfloat)
    part_left = matmul_tn(normed_low, grad_narrow_low)
    grad_normed = grad_normed + matmul_nt(grad_narrow_low, full_left)

    grad_query_list = []
    grad_keys = jnp.zeros((WINDOW + block_len, HD), jnp.float32)
    grad_values = jnp.zeros((WINDOW + block_len, HD), jnp.float32)
    for at, begin in enumerate(range(0, block_len, chunk)):
        keys = span_kv[0, begin : begin + span_len]
        values = span_kv[1, begin : begin + span_len]
        probs = prob_list[at]
        grad_rows = grad_att_low[begin : begin + chunk]
        grad_probs = matmul_nt(grad_rows, values)
        inner_sum = jnp.sum(probs * grad_probs, axis=-1, keepdims=True)
        grad_scores = (probs * (grad_probs - inner_sum)).astype(bfloat)
        grad_query_list.append(matmul(grad_scores, keys) * scale_factor)
        grad_keys = grad_keys.at[begin : begin + span_len].add(
            matmul_tn(grad_scores, query_low[begin : begin + chunk]) * scale_factor
        )
        grad_values = grad_values.at[begin : begin + span_len].add(
            matmul_tn(probs.astype(bfloat), grad_rows)
        )
    returned = passed_along(
        jnp.stack([grad_keys[:WINDOW], grad_values[:WINDOW]]).astype(bfloat), "ctx", -1
    ).astype(jnp.float32)
    returned = jnp.pad(returned, ((0, 0), (block_len - WINDOW, 0), (0, 0)))
    grad_qlin, grad_gquery = query_back(jnp.concatenate(grad_query_list, axis=0))
    grad_klin, grad_gkey = key_back(grad_keys[WINDOW:] + returned[0])
    grad_vlin = grad_values[WINDOW:] + returned[1]
    grad_qkv_low = jnp.concatenate([grad_qlin, grad_klin, grad_vlin], axis=1).astype(bfloat)
    part_qkv = matmul_tn(normed_all, grad_qkv_low).astype(bfloat).reshape(fsdp_count, rows, -1)
    small_parts = [
        part.astype(bfloat).reshape(fsdp_count, -1, inputs.shape[1])
        for part in (part_pgate, part_pproj, part_left, part_right)
    ]
    small_sizes = [part.shape[1] for part in small_parts]
    small_total = sum(small_sizes)
    small_rows = -(-small_total // 128) * 128
    small_parts.append(
        jnp.zeros((fsdp_count, small_rows - small_total, inputs.shape[1]), bfloat)
    )
    small = lax.psum_scatter(
        jnp.concatenate(small_parts, axis=1), "fsdp", scatter_dimension=0, tiled=False
    )
    grad_normed = grad_normed + scatter_tokens(matmul_nt(grad_qkv_low, col_qkv))
    grad_in_second, grad_gin = norm_back(grad_normed)
    grad_tokens = grad_in_first + grad_in_second

    grad_gains = [
        grad_gin,
        grad_gquery,
        grad_gkey,
        grad_gpost,
        grad_glaurel,
        grad_gffin,
        grad_gffout,
        grad_gple,
    ]
    gain_parts = jnp.concatenate([g.reshape(fsdp_count, -1) for g in grad_gains], axis=1)
    gain_parts = jnp.pad(gain_parts, ((0, 0), (0, 128 * 128 - gain_parts.shape[1])))
    gain_parts = gain_parts.astype(bfloat).reshape(fsdp_count, 128, 128)

    sum_wgate, sum_wup, sum_wdown, sum_wout, sum_qkv, sum_small, sum_gains = gradient_sum(
        [part_gateup, part_wdown, part_wout, part_qkv, small, gain_parts]
    )
    gain_sums = jnp.sum(sum_gains.astype(jnp.float32), axis=0).reshape(-1)
    grad_wgate = sum_wgate.astype(jnp.float32)
    grad_wup = sum_wup.astype(jnp.float32)
    grad_wdown = sum_wdown.astype(jnp.float32)
    grad_wout = sum_wout.astype(jnp.float32)
    sum_qkv = sum_qkv.astype(jnp.float32)
    grad_wquery = jnp.transpose(sum_qkv[:, :, :HD], (1, 0, 2)).reshape(rows, -1)
    sum_kv = jnp.sum(sum_qkv[:, :, HD:].reshape(KV, group_size, rows, 2 * HD), axis=1)
    sum_kv = jnp.transpose(sum_kv, (1, 0, 2))
    grad_wkey = sum_kv[:, :, :HD].reshape(rows, -1)
    grad_wvalue = sum_kv[:, :, HD:].reshape(rows, -1)
    sum_small = sum_small.astype(jnp.float32)
    small_ends = [sum(small_sizes[:n]) for n in range(5)]
    grad_pgate, grad_pproj, grad_wleft, grad_wright = (
        sum_small[small_ends[n] : small_ends[n + 1]].reshape(weight.shape)
        for n, weight in enumerate((ple_gate, ple_proj, laurel_left, laurel_right))
    )
    return (
        out_full.astype(bfloat),
        grad_tokens,
        grad_pleinput,
        grad_wquery,
        grad_wkey,
        grad_wvalue,
        grad_wout,
        grad_wleft,
        grad_wright,
        grad_wgate,
        grad_wup,
        grad_wdown,
        grad_pgate,
        grad_pproj,
        *(gain_sums[gain_offsets[n] : gain_offsets[n + 1]] for n in range(8)),
    )


def solution(mesh):
    in_specs = (
        P(("ctx", "fsdp"), None),
        P(("ctx", "fsdp"), None),
        P(("ctx", "fsdp"), None),
        P(),
        P(("ctx", "fsdp")),
        P("fsdp", None),
        P("fsdp", None),
        P("fsdp", None),
        P("fsdp", None),
        P("fsdp", None),
        P("fsdp", None),
        P("fsdp", None),
        P("fsdp", None),
        P("fsdp", None),
        P("fsdp", None),
        P("fsdp", None),
        P("fsdp"),
        P("fsdp"),
        P("fsdp"),
        P("fsdp"),
        P("fsdp"),
        P("fsdp"),
        P("fsdp"),
        P("fsdp"),
    )
    out_specs = (
        P(("ctx", "fsdp"), None),
        P(("ctx", "fsdp"), None),
        P(("ctx", "fsdp"), None),
        P("fsdp", None),
        P("fsdp", None),
        P("fsdp", None),
        P("fsdp", None),
        P("fsdp", None),
        P("fsdp", None),
        P("fsdp", None),
        P("fsdp", None),
        P("fsdp", None),
        P("fsdp", None),
        P("fsdp", None),
        P("fsdp"),
        P("fsdp"),
        P("fsdp"),
        P("fsdp"),
        P("fsdp"),
        P("fsdp"),
        P("fsdp"),
        P("fsdp"),
    )
    run = by_heads if mesh.shape["fsdp"] == HQ and mesh.shape["ctx"] == 4 else local
    return jax.shard_map(run, mesh=mesh, in_specs=in_specs, out_specs=out_specs, check_vma=False)
```

```python
import functools
import math

import jax
import jax.numpy as jnp
from jax import lax
from jax.experimental import pallas as pl
from jax.experimental.pallas import tpu as pltpu
from jax.sharding import PartitionSpec as P

HQ = 8
KV = 2
HD = 256
WINDOW = 1024


EPSILON = 1e-06
NEGATIVE = -1e30
ROPE_BASE = 10000.0
HALF_ROOT = 1.0 / math.sqrt(2.0)
GELU_ROOT = math.sqrt(2.0 / math.pi)
GELU_CUBE = 0.044715
SCORE_SCALE = 1.0 / math.sqrt(HD)
KERNEL_VMEM = 60 << 20


def passed_along(block, axis, distance):
    devices = range(lax.axis_size(axis))
    route = [(i - distance, i) for i in devices if i - distance in devices]
    return lax.ppermute(block, axis, route)


def matmul(left_mat, right_mat):
    return jnp.dot(left_mat, right_mat, preferred_element_type=jnp.float32)


def matmul_tn(left_mat, right_mat):
    return lax.dot_general(
        left_mat, right_mat, (((0,), (0,)), ((), ())), preferred_element_type=jnp.float32
    )


def matmul_nt(left_mat, right_mat):
    return lax.dot_general(
        left_mat, right_mat, (((1,), (1,)), ((), ())), preferred_element_type=jnp.float32
    )


def rms_norm(values, gain_vec):
    return (
        values * lax.rsqrt(jnp.mean(values * values, axis=-1, keepdims=True) + EPSILON) * gain_vec
    )


def rope_tables(positions, width):
    half_width = width // 2
    frequency = jnp.exp(
        jnp.arange(half_width, dtype=jnp.float32) * (-2.0 * math.log(ROPE_BASE) / width)
    )
    angles = positions.astype(jnp.float32)[:, None] * frequency[None, :]
    return (jnp.cos(angles)[:, None, :], jnp.sin(angles)[:, None, :])


def rotate(values, cosine, sine_part):
    half_width = values.shape[-1] // 2
    first_half = values[..., :half_width]
    second_half = values[..., half_width:]
    return jnp.concatenate(
        [
            first_half * cosine - second_half * sine_part,
            second_half * cosine + first_half * sine_part,
        ],
        axis=-1,
    )


def document_ids(doc_lengths, places):
    doc_ends = jnp.cumsum(doc_lengths)
    return jnp.sum((places[:, None] >= doc_ends[None, :-1]).astype(jnp.int32), axis=1)


def query_key(cosine, sine_part, query_lin, key_lin, gain_query, gain_key):
    tok_count = query_lin.shape[0]
    query_rot = rotate(
        rms_norm(query_lin.reshape(tok_count, HQ, HD), gain_query), cosine, sine_part
    )
    key_rot = rotate(rms_norm(key_lin.reshape(tok_count, KV, HD), gain_key), cosine, sine_part)
    return (query_rot, key_rot)


def mix_piece(inputs, normed, projected, widened, gain_post, gain_laurel):
    return (
        inputs + rms_norm(projected, gain_post) + normed + rms_norm(widened, gain_laurel)
    ) * HALF_ROOT


def geglu(gate_lin, up_lin):
    return jax.nn.gelu(gate_lin, approximate=True) * up_lin


def ffn_out_piece(mixed, down_lin, gain_ffout):
    return mixed + rms_norm(down_lin, gain_ffout)


def ple_act(ple_lin, ple_input):
    return jax.nn.gelu(ple_lin, approximate=True) * ple_input


def final_piece(layer_mid, ple_wide, gain_ple):
    return layer_mid + rms_norm(ple_wide, gain_ple)


def visibility(doc_lengths, query_start, key_start, tok_count, span_len):
    query_places = query_start + jnp.arange(tok_count, dtype=jnp.int32)
    key_places = key_start + jnp.arange(span_len, dtype=jnp.int32)
    distance = query_places[:, None] - key_places[None, :]
    query_docs = document_ids(doc_lengths, query_places)
    key_docs = document_ids(doc_lengths, key_places)
    return (
        (distance >= 0)
        & (distance < WINDOW)
        & (key_places[None, :] >= 0)
        & (query_docs[:, None] == key_docs[None, :])
    )


def attend_forward(query_low, span_kv, visible):
    tok_count = query_low.shape[0]
    scale_factor = 1.0 / math.sqrt(HD)
    scores = (
        jnp.einsum("tkgh,skh->kgts", query_low, span_kv[0], preferred_element_type=jnp.float32)
        * scale_factor
    )
    scores = jnp.where(visible, scores, NEGATIVE)
    row_top = jnp.max(scores, axis=-1, keepdims=True)
    shifted = jnp.exp(scores - row_top)
    row_total = jnp.sum(shifted, axis=-1, keepdims=True)
    attn_probs = shifted / row_total
    attended = jnp.einsum(
        "kgts,skh->tkgh",
        attn_probs.astype(jnp.bfloat16),
        span_kv[1],
        preferred_element_type=jnp.float32,
    )
    return (attended.reshape(tok_count, -1), row_top + jnp.log(row_total))


def attend_backward(query_low, span_kv, visible, log_total, grad_out_low):
    scale_factor = 1.0 / math.sqrt(HD)
    scores = (
        jnp.einsum("tkgh,skh->kgts", query_low, span_kv[0], preferred_element_type=jnp.float32)
        * scale_factor
    )
    attn_probs = jnp.where(visible, jnp.exp(jnp.where(visible, scores, NEGATIVE) - log_total), 0.0)
    grad_probs = jnp.einsum(
        "tkgh,skh->kgts", grad_out_low, span_kv[1], preferred_element_type=jnp.float32
    )
    inner_sum = jnp.sum(attn_probs * grad_probs, axis=-1, keepdims=True)
    grad_scores = (attn_probs * (grad_probs - inner_sum)).astype(jnp.bfloat16)
    grad_query = (
        jnp.einsum("kgts,skh->tkgh", grad_scores, span_kv[0], preferred_element_type=jnp.float32)
        * scale_factor
    )
    grad_keys = (
        jnp.einsum("kgts,tkgh->skh", grad_scores, query_low, preferred_element_type=jnp.float32)
        * scale_factor
    )
    grad_values = jnp.einsum(
        "kgts,tkgh->skh",
        attn_probs.astype(jnp.bfloat16),
        grad_out_low,
        preferred_element_type=jnp.float32,
    )
    return (grad_query, jnp.stack([grad_keys, grad_values]))


def settle(act_low, grad_low):
    act_cols = lax.all_to_all(act_low, "fsdp", split_axis=1, concat_axis=0, tiled=True)
    shard_rows = matmul_tn(act_cols, lax.all_gather(grad_low, "fsdp", axis=0, tiled=True))
    return lax.psum(shard_rows.astype(jnp.bfloat16), "ctx").astype(jnp.float32)


def local(
    tokens,
    per_layer,
    cotangent,
    doc_lengths,
    positions,
    w_query,
    w_key,
    w_value,
    w_out,
    laurel_left,
    laurel_right,
    w_gate,
    w_up,
    w_down,
    ple_gate,
    ple_proj,
    attn_in_gain,
    query_gain,
    key_gain,
    attn_out_gain,
    laurel_gain,
    ffn_in_gain,
    ffn_out_gain,
    ple_gain,
):
    bfloat = jnp.bfloat16
    tok_count = tokens.shape[0]
    span_len = WINDOW + tok_count
    groups = HQ // KV
    dev_index = lax.axis_index("ctx") * lax.axis_size("fsdp") + lax.axis_index("fsdp")
    query_start = dev_index * tok_count
    key_start = query_start - WINDOW
    visible = visibility(doc_lengths, query_start, key_start, tok_count, span_len)
    cosine, sine_part = rope_tables(positions, HD)
    gain_in, gain_query, gain_key, gain_post, gain_laurel, gain_ffin, gain_ffout, gain_ple = (
        lax.all_gather(attn_in_gain, "fsdp", axis=0, tiled=True),
        lax.all_gather(query_gain, "fsdp", axis=0, tiled=True),
        lax.all_gather(key_gain, "fsdp", axis=0, tiled=True),
        lax.all_gather(attn_out_gain, "fsdp", axis=0, tiled=True),
        lax.all_gather(laurel_gain, "fsdp", axis=0, tiled=True),
        lax.all_gather(ffn_in_gain, "fsdp", axis=0, tiled=True),
        lax.all_gather(ffn_out_gain, "fsdp", axis=0, tiled=True),
        lax.all_gather(ple_gain, "fsdp", axis=0, tiled=True),
    )
    full_query, full_key, full_value, full_out, full_left, full_right = (
        lax.all_gather(w_query.astype(bfloat), "fsdp", axis=0, tiled=True),
        lax.all_gather(w_key.astype(bfloat), "fsdp", axis=0, tiled=True),
        lax.all_gather(w_value.astype(bfloat), "fsdp", axis=0, tiled=True),
        lax.all_gather(w_out.astype(bfloat), "fsdp", axis=0, tiled=True),
        lax.all_gather(laurel_left.astype(bfloat), "fsdp", axis=0, tiled=True),
        lax.all_gather(laurel_right.astype(bfloat), "fsdp", axis=0, tiled=True),
    )
    inputs = tokens.astype(jnp.float32)
    ple_input = per_layer.astype(jnp.float32)
    normed, norm_back = jax.vjp(rms_norm, inputs, gain_in)
    normed_low = normed.astype(bfloat)
    query_lin = matmul(normed_low, full_query)
    key_lin = matmul(normed_low, full_key)
    value_lin = matmul(normed_low, full_value)
    (query_rot, key_rot), rope_back = jax.vjp(
        functools.partial(query_key, cosine, sine_part), query_lin, key_lin, gain_query, gain_key
    )
    query_low = query_rot.astype(bfloat).reshape(tok_count, KV, groups, HD)
    keys_values = jnp.stack(
        [key_rot.astype(bfloat), value_lin.astype(bfloat).reshape(tok_count, KV, HD)]
    )
    block_kv = lax.all_gather(keys_values, "fsdp", axis=1, tiled=True)
    block_len = block_kv.shape[1]
    before_kv = passed_along(block_kv, "ctx", 1)
    span_offset = block_len + lax.axis_index("fsdp") * tok_count - WINDOW
    span_kv = lax.dynamic_slice_in_dim(
        jnp.concatenate([before_kv, block_kv], axis=1), span_offset, span_len, 1
    )
    attended, log_total = attend_forward(query_low, span_kv, visible)
    attended_low = attended.astype(bfloat)
    projected = matmul(attended_low, full_out)
    narrow_low = matmul(normed_low, full_left).astype(bfloat)
    widened = matmul(narrow_low, full_right)
    mixed, mix_back = jax.vjp(mix_piece, inputs, normed, projected, widened, gain_post, gain_laurel)
    full_gate, full_up, full_down, full_pgate, full_pproj = (
        lax.all_gather(w_gate.astype(bfloat), "fsdp", axis=0, tiled=True),
        lax.all_gather(w_up.astype(bfloat), "fsdp", axis=0, tiled=True),
        lax.all_gather(w_down.astype(bfloat), "fsdp", axis=0, tiled=True),
        lax.all_gather(ple_gate.astype(bfloat), "fsdp", axis=0, tiled=True),
        lax.all_gather(ple_proj.astype(bfloat), "fsdp", axis=0, tiled=True),
    )
    ffn_normed, ffn_norm_back = jax.vjp(rms_norm, mixed, gain_ffin)
    ffn_low = ffn_normed.astype(bfloat)
    gate_lin = matmul(ffn_low, full_gate)
    up_lin = matmul(ffn_low, full_up)
    hidden, geglu_back = jax.vjp(geglu, gate_lin, up_lin)
    hidden_low = hidden.astype(bfloat)
    down_lin = matmul(hidden_low, full_down)
    layer_mid, ffn_out_back = jax.vjp(ffn_out_piece, mixed, down_lin, gain_ffout)
    layer_low = layer_mid.astype(bfloat)
    ple_lin = matmul(layer_low, full_pgate)
    ple_mid, ple_back = jax.vjp(ple_act, ple_lin, ple_input)
    ple_low = ple_mid.astype(bfloat)
    ple_wide = matmul(ple_low, full_pproj)
    out_full, final_back = jax.vjp(final_piece, layer_mid, ple_wide, gain_ple)
    full_gate, full_up, full_down, full_pgate, full_pproj = (
        lax.all_gather(w_gate.astype(bfloat), "fsdp", axis=0, tiled=True),
        lax.all_gather(w_up.astype(bfloat), "fsdp", axis=0, tiled=True),
        lax.all_gather(w_down.astype(bfloat), "fsdp", axis=0, tiled=True),
        lax.all_gather(ple_gate.astype(bfloat), "fsdp", axis=0, tiled=True),
        lax.all_gather(ple_proj.astype(bfloat), "fsdp", axis=0, tiled=True),
    )
    grad_layer, grad_pwide, grad_gple = final_back(cotangent.astype(jnp.float32))
    grad_pwide_low = grad_pwide.astype(bfloat)
    grad_pproj = settle(ple_low, grad_pwide_low)
    grad_plemid = matmul_nt(grad_pwide_low, full_pproj)
    grad_plelin, grad_pleinput = ple_back(grad_plemid)
    grad_plelin_low = grad_plelin.astype(bfloat)
    grad_pgate = settle(layer_low, grad_plelin_low)
    grad_layer = grad_layer + matmul_nt(grad_plelin_low, full_pgate)
    grad_mixed, grad_down, grad_gffout = ffn_out_back(grad_layer)
    grad_down_low = grad_down.astype(bfloat)
    grad_wdown = settle(hidden_low, grad_down_low)
    grad_hidden = matmul_nt(grad_down_low, full_down)
    grad_gate, grad_up = geglu_back(grad_hidden)
    grad_gate_low = grad_gate.astype(bfloat)
    grad_up_low = grad_up.astype(bfloat)
    grad_wgate = settle(ffn_low, grad_gate_low)
    grad_wup = settle(ffn_low, grad_up_low)
    grad_ffn = matmul_nt(grad_gate_low, full_gate) + matmul_nt(grad_up_low, full_up)
    grad_mixed_more, grad_gffin = ffn_norm_back(grad_ffn)
    grad_mixed = grad_mixed + grad_mixed_more
    full_query, full_key, full_value, full_out, full_left, full_right = (
        lax.all_gather(w_query.astype(bfloat), "fsdp", axis=0, tiled=True),
        lax.all_gather(w_key.astype(bfloat), "fsdp", axis=0, tiled=True),
        lax.all_gather(w_value.astype(bfloat), "fsdp", axis=0, tiled=True),
        lax.all_gather(w_out.astype(bfloat), "fsdp", axis=0, tiled=True),
        lax.all_gather(laurel_left.astype(bfloat), "fsdp", axis=0, tiled=True),
        lax.all_gather(laurel_right.astype(bfloat), "fsdp", axis=0, tiled=True),
    )
    grad_in_first, grad_normed, grad_proj, grad_lwide, grad_gpost, grad_glaurel = mix_back(
        grad_mixed
    )
    grad_proj_low = grad_proj.astype(bfloat)
    grad_wout = settle(attended_low, grad_proj_low)
    grad_att_low = matmul_nt(grad_proj_low, full_out).astype(bfloat)
    grad_lwide_low = grad_lwide.astype(bfloat)
    grad_wright = settle(narrow_low, grad_lwide_low)
    grad_narrow_low = matmul_nt(grad_lwide_low, full_right).astype(bfloat)
    grad_wleft = settle(normed_low, grad_narrow_low)
    grad_normed = grad_normed + matmul_nt(grad_narrow_low, full_left)
    grad_query_att, grad_span = attend_backward(
        query_low, span_kv, visible, log_total, grad_att_low.reshape(tok_count, KV, groups, HD)
    )
    whole_grad = jnp.zeros((2, 2 * block_len, KV, HD), jnp.float32)
    whole_grad = lax.dynamic_update_slice_in_dim(whole_grad, grad_span, span_offset, 1)
    returned = passed_along(whole_grad[:, :block_len].astype(jnp.bfloat16), "ctx", -1).astype(
        jnp.float32
    )
    own_grad = lax.psum_scatter(
        (whole_grad[:, block_len:] + returned).astype(jnp.bfloat16),
        "fsdp",
        scatter_dimension=1,
        tiled=True,
    ).astype(jnp.float32)
    grad_qlin, grad_klin, grad_gquery, grad_gkey = rope_back(
        (grad_query_att.reshape(tok_count, HQ, HD), own_grad[0])
    )
    grad_qlin_low = grad_qlin.astype(bfloat)
    grad_klin_low = grad_klin.astype(bfloat)
    grad_vlin_low = own_grad[1].reshape(tok_count, KV * HD).astype(bfloat)
    grad_wquery = settle(normed_low, grad_qlin_low)
    grad_wkey = settle(normed_low, grad_klin_low)
    grad_wvalue = settle(normed_low, grad_vlin_low)
    grad_normed = (
        grad_normed
        + matmul_nt(grad_qlin_low, full_query)
        + matmul_nt(grad_klin_low, full_key)
        + matmul_nt(grad_vlin_low, full_value)
    )
    grad_in_second, grad_gin = norm_back(grad_normed)
    grad_tokens = grad_in_first + grad_in_second
    sum_gin, sum_gquery, sum_gkey, sum_gpost, sum_glaurel, sum_gffin, sum_gffout, sum_gple = (
        lax.psum(
            (
                grad_gin,
                grad_gquery,
                grad_gkey,
                grad_gpost,
                grad_glaurel,
                grad_gffin,
                grad_gffout,
                grad_gple,
            ),
            ("ctx", "fsdp"),
        )
    )
    wide_rows = attn_in_gain.shape[0]
    head_rows = query_gain.shape[0]
    wide_start = lax.axis_index("fsdp") * wide_rows
    head_start = lax.axis_index("fsdp") * head_rows

    def wide_part(full_vec):
        return lax.dynamic_slice_in_dim(full_vec, wide_start, wide_rows, 0)

    def head_part(full_vec):
        return lax.dynamic_slice_in_dim(full_vec, head_start, head_rows, 0)

    return (
        out_full.astype(bfloat),
        grad_tokens,
        grad_pleinput,
        grad_wquery,
        grad_wkey,
        grad_wvalue,
        grad_wout,
        grad_wleft,
        grad_wright,
        grad_wgate,
        grad_wup,
        grad_wdown,
        grad_pgate,
        grad_pproj,
        wide_part(sum_gin),
        head_part(sum_gquery),
        head_part(sum_gkey),
        wide_part(sum_gpost),
        wide_part(sum_glaurel),
        wide_part(sum_gffin),
        wide_part(sum_gffout),
        wide_part(sum_gple),
    )

def remote(src, dst, send_sem, recv_sem, place):
    return pltpu.make_async_remote_copy(
        src_ref=src,
        dst_ref=dst,
        send_sem=send_sem,
        recv_sem=recv_sem,
        device_id={"fsdp": place},
        device_id_type=pl.DeviceIdType.MESH,
    )


def dot_nn(left_mat, right_mat):
    return jnp.dot(left_mat, right_mat, preferred_element_type=jnp.float32)


def dot_nt(left_mat, right_mat):
    return lax.dot_general(
        left_mat, right_mat, (((1,), (1,)), ((), ())), preferred_element_type=jnp.float32
    )


def dot_tn(left_mat, right_mat):
    return lax.dot_general(
        left_mat, right_mat, (((0,), (0,)), ((), ())), preferred_element_type=jnp.float32
    )


def greet_all():
    sem = pltpu.get_barrier_semaphore()
    members, planes = lax.axis_size("fsdp"), lax.axis_size("ctx")
    mesh_id = pl.DeviceIdType.MESH
    for hop in range(1, planes):
        other = lax.rem(lax.axis_index("ctx") + hop, planes)
        pl.semaphore_signal(sem, inc=1, device_id={"ctx": other}, device_id_type=mesh_id)
    for hop in range(1, members):
        other = lax.rem(lax.axis_index("fsdp") + hop, members)
        pl.semaphore_signal(sem, inc=1, device_id={"fsdp": other}, device_id_type=mesh_id)
    pl.semaphore_wait(sem, members + planes - 2)


PIECES = 4


def line_scratch(chips, tok_count, width):
    dma = pltpu.SemaphoreType.DMA
    shard = (tok_count, width)
    return [
        pltpu.VMEM((chips, 2) + shard, jnp.bfloat16),
        dma((chips, 2)),
        dma((chips, 3)),
        dma,
        pltpu.VMEM((chips, 2) + shard, jnp.bfloat16),
        pltpu.VMEM((chips,) + shard, jnp.bfloat16),
        pltpu.VMEM((chips,) + shard, jnp.bfloat16),
        pltpu.VMEM((chips,) + shard, jnp.bfloat16),
        dma((chips,)),
        dma((chips,)),
        dma((chips, PIECES)),
        dma((chips, PIECES)),
        dma((chips, PIECES)),
    ]


LINE_REFS = 13


class Line:
    def __init__(self, chips, refs):
        (
            self.slots,
            self.slot_recv,
            self.slot_send,
            self.own_sem,
            self.parts,
            self.from_core,
            self.from_left,
            self.from_right,
            self.core_send,
            self.core_recv,
            self.flow_send,
            self.left_recv,
            self.right_recv,
        ) = refs
        self.chips = chips
        me = lax.axis_index("fsdp")
        self.chip = me // 2
        self.core = me % 2
        self.tok = self.slots.shape[2]
        self.piece = self.tok // PIECES

    def place(self, chip, core):
        return chip * 2 + core

    def order(self, step):
        picked = 0
        for chip in range(self.chips):
            near = sorted(range(self.chips), key=lambda other: (abs(other - chip), other))
            picked = picked + jnp.where(self.chip == chip, near[step], 0)
        return picked

    def barrier(self):
        sem = pltpu.get_barrier_semaphore()

        def greet(place):
            pl.semaphore_signal(
                sem, inc=1, device_id={"fsdp": place}, device_id_type=pl.DeviceIdType.MESH
            )

        greet(self.place(self.chip, 1 - self.core))

        @pl.when(self.chip > 0)
        def _():
            greet(self.place(self.chip - 1, self.core))

        @pl.when(self.chip < self.chips - 1)
        def _():
            greet(self.place(self.chip + 1, self.core))

        ends = jnp.where(self.chip == 0, 1, 0) + jnp.where(self.chip == self.chips - 1, 1, 0)
        pl.semaphore_wait(sem, 3 - ends)

    def slot_copy(self, src, chip, way):
        place = (
            self.place(self.chip + 1, self.core),
            self.place(self.chip - 1, self.core),
            self.place(self.chip, 1 - self.core),
        )[way]
        return remote(
            src,
            self.slots.at[chip, self.core],
            self.slot_send.at[chip, way],
            self.slot_recv.at[chip, self.core],
            place,
        )

    def own_copy(self, own_ref):
        return pltpu.make_async_copy(own_ref, self.slots.at[self.chip, self.core], self.own_sem)

    def gather_begin(self, own_ref):
        @pl.when(self.chip < self.chips - 1)
        def _():
            self.slot_copy(own_ref, self.chip, 0).start()

        @pl.when(self.chip > 0)
        def _():
            self.slot_copy(own_ref, self.chip, 1).start()

        self.slot_copy(own_ref, self.chip, 2).start()
        self.own_copy(own_ref).start()

    def gather_step(self, distance):
        for chip, there, way, onward in (
            (self.chip - distance, self.chip >= distance, 0, self.chip < self.chips - 1),
            (self.chip + distance, self.chip + distance < self.chips, 1, self.chip > 0),
        ):

            @pl.when(there)
            def _(chip=chip, way=way, onward=onward):
                src = self.slots.at[chip, self.core]
                self.slot_copy(src, chip, way).wait_recv()

                @pl.when(onward)
                def _():
                    self.slot_copy(src, chip, way).start()

                self.slot_copy(src, chip, 2).start()

    def gather_other(self, chip):
        dst = self.slots.at[chip, 1 - self.core]
        remote(
            dst,
            dst,
            self.slot_send.at[chip, 2],
            self.slot_recv.at[chip, 1 - self.core],
            self.place(self.chip, 1 - self.core),
        ).wait_recv()

    def gather_end(self):
        for chip in range(self.chips):
            src = self.slots.at[chip, self.core]

            @pl.when((self.chip >= chip) & (self.chip < self.chips - 1))
            def _(src=src, chip=chip):
                self.slot_copy(src, chip, 0).wait_send()

            @pl.when((self.chip <= chip) & (self.chip > 0))
            def _(src=src, chip=chip):
                self.slot_copy(src, chip, 1).wait_send()

            self.slot_copy(src, chip, 2).wait_send()

    def core_copy(self, chip):
        return remote(
            self.parts.at[chip, 1 - self.core],
            self.from_core.at[chip],
            self.core_send.at[chip],
            self.core_recv.at[chip],
            self.place(self.chip, 1 - self.core),
        )

    def flow_copy(self, chip, piece, right):
        rows = pl.ds(piece * self.piece, self.piece)
        return remote(
            self.parts.at[chip, self.core, rows],
            (self.from_left if right else self.from_right).at[chip, rows],
            self.flow_send.at[chip, piece],
            (self.left_recv if right else self.right_recv).at[chip, piece],
            self.place(self.chip + (1 if right else -1), self.core),
        )

    def flow(self, chip, right, incoming):
        self.core_copy(chip).wait_recv()

        @pl.loop(0, PIECES)
        def _(piece):
            rows = pl.ds(pl.multiple_of(piece * self.piece, self.piece), self.piece)
            total = self.parts[chip, self.core, rows].astype(jnp.float32)
            total = total + self.from_core[chip, rows].astype(jnp.float32)
            if incoming:
                self.flow_copy(chip, piece, right).wait_recv()
                source = self.from_left if right else self.from_right
                total = total + source[chip, rows].astype(jnp.float32)
            self.parts[chip, self.core, rows] = total.astype(jnp.bfloat16)
            self.flow_copy(chip, piece, right).start()

    def scatter_first(self, chip):
        @pl.when((self.chip == 0) & (chip > 0))
        def _():
            self.flow(chip, True, False)

        @pl.when((self.chip == self.chips - 1) & (chip < self.chips - 1))
        def _():
            self.flow(chip, False, False)

    def scatter_rest(self, result_ref):
        for rank in range(3, 2 * self.chips - 2):
            right = rank - self.chip

            @pl.when((self.chip > 0) & (right > self.chip) & (right < self.chips))
            def _(right=right):
                self.flow(right, True, True)

            left = 2 * (self.chips - 1) - self.chip - rank

            @pl.when((self.chip < self.chips - 1) & (left < self.chip) & (left >= 0))
            def _(left=left):
                self.flow(left, False, True)

        own = self.chip
        self.core_copy(own).wait_recv()

        @pl.loop(0, PIECES)
        def _(piece):
            rows = pl.ds(pl.multiple_of(piece * self.piece, self.piece), self.piece)
            total = self.parts[own, self.core, rows].astype(jnp.float32)
            total = total + self.from_core[own, rows].astype(jnp.float32)
            result_ref[rows] = total

        @pl.when(own > 0)
        def _():
            @pl.loop(0, PIECES)
            def _(piece):
                rows = pl.ds(pl.multiple_of(piece * self.piece, self.piece), self.piece)
                self.flow_copy(own, piece, True).wait_recv()
                result_ref[rows] += self.from_left[own, rows].astype(jnp.float32)

        @pl.when(own < self.chips - 1)
        def _():
            @pl.loop(0, PIECES)
            def _(piece):
                rows = pl.ds(pl.multiple_of(piece * self.piece, self.piece), self.piece)
                self.flow_copy(own, piece, False).wait_recv()
                result_ref[rows] += self.from_right[own, rows].astype(jnp.float32)

        for chip in range(self.chips):
            self.core_copy(chip).wait_send()

            @pl.when(self.chip != chip)
            def _(chip=chip):
                for piece in range(PIECES):
                    self.flow_copy(chip, piece, True).wait_send()


def ffn_forward_kernel(
    chips,
    own_ref,
    gateup_hbm,
    down_hbm,
    result_ref,
    all_hbm,
    hidden_hbm,
    act_hbm,
    slope_hbm,
    *scratch,
):
    line = Line(chips, scratch[:LINE_REFS])
    gateup, down, hidden, act, slope, load_sems, store_sems = scratch[LINE_REFS:]
    ff_part = down.shape[0]
    width = down.shape[1]
    pair = 2 * line.tok
    load_gateup = pltpu.make_async_copy(gateup_hbm, gateup, load_sems.at[0])
    load_down = pltpu.make_async_copy(down_hbm, down, load_sems.at[1])
    load_gateup.start()
    load_down.start()
    line.barrier()
    line.gather_begin(own_ref)
    line.own_copy(own_ref).wait()

    def stores(chip):
        rows = pl.ds(pl.multiple_of(chip * pair, pair), pair)
        return [
            pltpu.make_async_copy(line.slots.at[chip], all_hbm.at[chip], store_sems.at[chip, 0]),
            pltpu.make_async_copy(hidden.at[rows], hidden_hbm.at[rows], store_sems.at[chip, 1]),
            pltpu.make_async_copy(act.at[rows], act_hbm.at[rows], store_sems.at[chip, 2]),
            pltpu.make_async_copy(slope.at[rows], slope_hbm.at[rows], store_sems.at[chip, 3]),
        ]

    tile = 256
    for step in range(chips):
        if step > 0:
            line.gather_step(step)
        chip = line.order(step)
        line.gather_other(chip)
        if step == 0:
            load_gateup.wait()
            load_down.wait()
        rows = pl.ds(pl.multiple_of(chip * pair, pair), pair)

        @pl.loop(0, ff_part // tile)
        def _(at, chip=chip, rows=rows):
            inputs = line.slots[chip].reshape(pair, width)
            gate_cols = pl.ds(pl.multiple_of(at * tile, tile), tile)
            up_cols = pl.ds(pl.multiple_of(ff_part + at * tile, tile), tile)
            gate = dot_nn(inputs, gateup[:, gate_cols])
            up = dot_nn(inputs, gateup[:, up_cols])
            square = gate * gate
            bent = jnp.tanh(GELU_ROOT * gate * (1.0 + GELU_CUBE * square))
            half = 0.5 + 0.5 * bent
            activated = gate * half
            rise = half + 0.5 * gate * (1.0 - bent * bent) * (
                GELU_ROOT * (1.0 + 3.0 * GELU_CUBE * square)
            )
            hidden[rows, gate_cols] = (activated * up).astype(jnp.bfloat16)
            act[rows, gate_cols] = activated.astype(jnp.bfloat16)
            slope[rows, gate_cols] = (rise * up).astype(jnp.bfloat16)

        for copy in stores(chip):
            copy.start()

        wide = 512

        @pl.loop(0, width // wide)
        def _(at, chip=chip, rows=rows):
            cols = pl.ds(pl.multiple_of(at * wide, wide), wide)
            sums = dot_nn(hidden[rows, :], down[:, cols]).astype(jnp.bfloat16)
            line.parts[chip, :, :, cols] = sums.reshape(2, line.tok, wide)

        line.core_copy(chip).start()
        if step > 0:
            line.scatter_first(line.order(step - 1))
    line.scatter_first(line.order(chips - 1))
    line.scatter_rest(result_ref)
    line.gather_end()
    for chip in range(chips):
        for copy in stores(chip):
            copy.wait()


def ffn_forward(own, gateup, down, chips):
    tok_count, width = own.shape
    ff_part = down.shape[0]
    block = 2 * chips * tok_count
    bfloat = jnp.bfloat16
    anywhere = pl.BlockSpec(memory_space=pl.ANY)
    vmem = pl.BlockSpec(memory_space=pltpu.VMEM)
    part = jax.ShapeDtypeStruct((block, ff_part), bfloat)
    result, gathered, hidden, act, slope = pl.pallas_call(
        functools.partial(ffn_forward_kernel, chips),
        out_shape=[
            jax.ShapeDtypeStruct((tok_count, width), jnp.float32),
            jax.ShapeDtypeStruct((chips, 2, tok_count, width), bfloat),
            part,
            part,
            part,
        ],
        in_specs=[vmem, anywhere, anywhere],
        out_specs=[vmem, anywhere, anywhere, anywhere, anywhere],
        scratch_shapes=line_scratch(chips, tok_count, width)
        + [
            pltpu.VMEM(gateup.shape, bfloat),
            pltpu.VMEM(down.shape, bfloat),
            pltpu.VMEM((block, ff_part), bfloat),
            pltpu.VMEM((block, ff_part), bfloat),
            pltpu.VMEM((block, ff_part), bfloat),
            pltpu.SemaphoreType.DMA((2,)),
            pltpu.SemaphoreType.DMA((chips, 4)),
        ],
        compiler_params=pltpu.CompilerParams(
            collective_id=1, has_side_effects=True, vmem_limit_bytes=KERNEL_VMEM
        ),
        cost_estimate=pl.CostEstimate(
            flops=6 * block * width * ff_part,
            bytes_accessed=40 << 20,
            transcendentals=block * ff_part,
        ),
        name="ffn_forward",
    )(own, gateup, down)
    return result, gathered.reshape(block, width), hidden, act, slope


def ffn_backward_kernel(
    chips,
    own_ref,
    gateup_hbm,
    down_hbm,
    act_hbm,
    slope_hbm,
    result_ref,
    all_hbm,
    grad_hbm,
    *scratch,
):
    line = Line(chips, scratch[:LINE_REFS])
    gateup, down, act, slope, grad, load_sems, store_sems = scratch[LINE_REFS:]
    ff_part = down.shape[0]
    width = down.shape[1]
    pair = 2 * line.tok
    loads = [
        pltpu.make_async_copy(down_hbm, down, load_sems.at[0]),
        pltpu.make_async_copy(act_hbm, act, load_sems.at[1]),
        pltpu.make_async_copy(slope_hbm, slope, load_sems.at[2]),
        pltpu.make_async_copy(gateup_hbm, gateup, load_sems.at[3]),
    ]
    for load in loads:
        load.start()
    line.barrier()
    line.gather_begin(own_ref)
    line.own_copy(own_ref).wait()

    def stores(chip):
        rows = pl.ds(pl.multiple_of(chip * pair, pair), pair)
        return [
            pltpu.make_async_copy(line.slots.at[chip], all_hbm.at[chip], store_sems.at[chip, 0]),
            pltpu.make_async_copy(grad.at[rows], grad_hbm.at[rows], store_sems.at[chip, 1]),
        ]

    tile = 256
    for step in range(chips):
        if step > 0:
            line.gather_step(step)
        chip = line.order(step)
        line.gather_other(chip)
        if step == 0:
            for load in loads:
                load.wait()
        rows = pl.ds(pl.multiple_of(chip * pair, pair), pair)

        @pl.loop(0, ff_part // tile)
        def _(at, chip=chip, rows=rows):
            grads = line.slots[chip].reshape(pair, width)
            gate_cols = pl.ds(pl.multiple_of(at * tile, tile), tile)
            up_cols = pl.ds(pl.multiple_of(ff_part + at * tile, tile), tile)
            grad_hidden = dot_nt(grads, down[gate_cols, :])
            grad[rows, gate_cols] = (
                grad_hidden * slope[rows, gate_cols].astype(jnp.float32)
            ).astype(jnp.bfloat16)
            grad[rows, up_cols] = (grad_hidden * act[rows, gate_cols].astype(jnp.float32)).astype(
                jnp.bfloat16
            )

        for copy in stores(chip):
            copy.start()

        wide = 512

        @pl.loop(0, width // wide)
        def _(at, chip=chip, rows=rows):
            cols = pl.ds(pl.multiple_of(at * wide, wide), wide)
            sums = dot_nt(grad[rows, :], gateup[cols, :]).astype(jnp.bfloat16)
            line.parts[chip, :, :, cols] = sums.reshape(2, line.tok, wide)

        line.core_copy(chip).start()
        if step > 0:
            line.scatter_first(line.order(step - 1))
    line.scatter_first(line.order(chips - 1))
    line.scatter_rest(result_ref)
    line.gather_end()
    for chip in range(chips):
        for copy in stores(chip):
            copy.wait()


def ffn_backward(own, gateup, down, act, slope, chips):
    tok_count, width = own.shape
    ff_part = down.shape[0]
    block = 2 * chips * tok_count
    bfloat = jnp.bfloat16
    anywhere = pl.BlockSpec(memory_space=pl.ANY)
    vmem = pl.BlockSpec(memory_space=pltpu.VMEM)
    result, gathered, grad = pl.pallas_call(
        functools.partial(ffn_backward_kernel, chips),
        out_shape=[
            jax.ShapeDtypeStruct((tok_count, width), jnp.float32),
            jax.ShapeDtypeStruct((chips, 2, tok_count, width), bfloat),
            jax.ShapeDtypeStruct((block, 2 * ff_part), bfloat),
        ],
        in_specs=[vmem] + [anywhere] * 4,
        out_specs=[vmem, anywhere, anywhere],
        scratch_shapes=line_scratch(chips, tok_count, width)
        + [
            pltpu.VMEM(gateup.shape, bfloat),
            pltpu.VMEM(down.shape, bfloat),
            pltpu.VMEM((block, ff_part), bfloat),
            pltpu.VMEM((block, ff_part), bfloat),
            pltpu.VMEM((block, 2 * ff_part), bfloat),
            pltpu.SemaphoreType.DMA((4,)),
            pltpu.SemaphoreType.DMA((chips, 2)),
        ],
        compiler_params=pltpu.CompilerParams(
            collective_id=2, has_side_effects=True, vmem_limit_bytes=KERNEL_VMEM
        ),
        cost_estimate=pl.CostEstimate(
            flops=6 * block * width * ff_part, bytes_accessed=40 << 20, transcendentals=0
        ),
        name="ffn_backward",
    )(own, gateup, down, act, slope)
    return result, gathered.reshape(block, width), grad

class Plane:
    def locate(self, columns, rows):
        self.columns = columns
        at = lax.axis_index("ctx")
        self.at_x, self.at_y = at % 2, at // 2
        self.beside = (at + 1 - 2 * (at % 2), (at + 2) % 4)
        self.me = lax.axis_index("fsdp")
        self.members = lax.axis_size("fsdp")
        self.half = rows // 2
        self.quarter = rows // 4
        self.eighth = rows // 8

    def rows(self, ref, start, size):
        start = pl.multiple_of(start, size)
        return ref.at[:, pl.ds(start, size)] if self.columns else ref.at[pl.ds(start, size)]

    def sides(self, half):
        return (self.at_x, self.at_y) if half == 0 else (self.at_y, self.at_x)

    def kept_start(self, half):
        return half * self.half + self.sides(half)[0] * self.quarter

    def given_start(self, half):
        return half * self.half + (1 - self.sides(half)[0]) * self.quarter

    def own_start(self, half):
        return self.kept_start(half) + self.sides(half)[1] * self.eighth

    def copy(self, src, dst, send_sem, recv_sem, half, stage):
        return pltpu.make_async_remote_copy(
            src_ref=src,
            dst_ref=dst,
            send_sem=send_sem.at[half, stage],
            recv_sem=recv_sem.at[half, stage],
            device_id={"ctx": self.beside[(half + stage) % 2]},
            device_id_type=pl.DeviceIdType.MESH,
        )


class Summed(Plane):
    def __init__(self, source, refs, columns):
        self.source = source
        self.kept, self.taken, self.last, self.load_sem, self.sum_send, self.sum_recv = refs
        self.locate(columns, source.shape[-2])

    def load(self, half):
        return pltpu.make_async_copy(
            self.rows(self.source, self.kept_start(half), self.quarter),
            self.kept.at[half],
            self.load_sem.at[half],
        )

    def first(self, half):
        return self.copy(
            self.rows(self.source, self.given_start(half), self.quarter),
            self.taken.at[half],
            self.sum_send,
            self.sum_recv,
            half,
            0,
        )

    def second(self, half):
        other = (1 - self.sides(half)[1]) * self.eighth
        return self.copy(
            self.rows(self.kept.at[half], other, self.eighth),
            self.last.at[half],
            self.sum_send,
            self.sum_recv,
            half,
            1,
        )

    def begin(self):
        for half in (0, 1):
            self.first(half).start()
            self.load(half).start()

    def add(self, half, start, more, more_start):
        step = min(32, self.eighth)
        blocks = self.eighth // step
        layers = self.source.shape[0] if self.columns else 1

        @pl.loop(0, layers * blocks)
        def _(at):
            layer, block = at // blocks, at % blocks
            here = pl.ds(pl.multiple_of(start + block * step, step), step)
            there = pl.ds(pl.multiple_of(more_start + block * step, step), step)
            if self.columns:
                total = self.kept[half, layer, here].astype(jnp.float32)
                total = total + more[half, layer, there].astype(jnp.float32)
                self.kept[half, layer, here] = total.astype(jnp.bfloat16)
            else:
                total = self.kept[half, here].astype(jnp.float32)
                total = total + more[half, there].astype(jnp.float32)
                self.kept[half, here] = total.astype(jnp.bfloat16)

    def middle(self):
        for half in (0, 1):
            self.load(half).wait()
            self.first(half).wait_recv()
            side = self.sides(half)[1]
            other = (1 - side) * self.eighth
            self.add(half, other, self.taken, other)
            self.second(half).start()
            mine = side * self.eighth
            self.add(half, mine, self.taken, mine)

    def finish(self):
        for half in (0, 1):
            self.second(half).wait_recv()
            self.add(half, self.sides(half)[1] * self.eighth, self.last, 0)

    def own_rows(self, half):
        return self.rows(self.kept.at[half], self.sides(half)[1] * self.eighth, self.eighth)

    def held(self, half, member):
        side = self.sides(half)[1] * self.eighth
        return self.kept.at[half, member, pl.ds(pl.multiple_of(side, self.eighth), self.eighth)]

    def sum_sent(self):
        for half in (0, 1):
            self.first(half).wait_send()
            self.second(half).wait_send()


class Held:
    def __init__(self, kept):
        self.kept = kept

    def own_rows(self, half):
        return self.kept.at[half]

    def held(self, half, member):
        return self.kept.at[half, member]


class Spread(Plane):
    def __init__(self, source, refs, columns):
        self.own_rows, self.held = source.own_rows, source.held
        self.final, self.spread_send, self.spread_recv, self.place_sem = refs[:4]
        if columns:
            self.swap_send, self.swap_recv = refs[4:]
        self.locate(columns, self.final.shape[-2])

    def place(self, half):
        return pltpu.make_async_copy(
            self.own_rows(half),
            self.rows(self.final, self.own_start(half), self.eighth),
            self.place_sem.at[half],
        )

    def place_all(self):
        for half in (0, 1):
            self.place(half).start()
        for half in (0, 1):
            self.place(half).wait()

    def swap_copy(self, half, hop, src_member):
        target = lax.rem(self.me + hop, self.members)
        final_rows = pl.ds(pl.multiple_of(self.own_start(half), self.eighth), self.eighth)
        return remote(
            self.held(half, target),
            self.final.at[src_member, final_rows],
            self.swap_send.at[hop, half],
            self.swap_recv.at[hop, half],
            target,
        )

    def swap_local(self, half):
        final_rows = pl.ds(pl.multiple_of(self.own_start(half), self.eighth), self.eighth)
        return pltpu.make_async_copy(
            self.held(half, self.me),
            self.final.at[self.me, final_rows],
            self.place_sem.at[half],
        )

    def swap_begin(self):
        for half in (0, 1):
            for hop in range(1, self.members):
                self.swap_copy(half, hop, self.me).start()
            self.swap_local(half).start()

    def swap_end(self):
        for half in (0, 1):
            for hop in range(1, self.members):
                source = lax.rem(self.me + self.members - hop, self.members)
                self.swap_copy(half, hop, source).wait_recv()
            self.swap_local(half).wait()

    def spread_copy(self, half, stage):
        if stage == 0:
            rows = self.rows(self.final, self.own_start(half), self.eighth)
        else:
            rows = self.rows(self.final, self.kept_start(half), self.quarter)
        return self.copy(rows, rows, self.spread_send, self.spread_recv, half, 1 - stage)

    def spread_wait(self, half, stage):
        side = self.sides(half)[1]
        if stage == 0:
            start = self.kept_start(half) + (1 - side) * self.eighth
            rows = self.rows(self.final, start, self.eighth)
        else:
            rows = self.rows(self.final, self.given_start(half), self.quarter)
        self.copy(rows, rows, self.spread_send, self.spread_recv, half, 1 - stage).wait_recv()

    def spread_begin(self):
        for half in (0, 1):
            self.spread_copy(half, 0).start()

    def spread_on(self):
        for half in (0, 1):
            self.spread_wait(half, 0)
            self.spread_copy(half, 1).start()

    def spread_end(self):
        for half in (0, 1):
            self.spread_wait(half, 1)

    def spread_sent(self):
        for half in (0, 1):
            self.spread_copy(half, 0).wait_send()
            self.spread_copy(half, 1).wait_send()
            if self.columns:
                for hop in range(1, self.members):
                    self.swap_copy(half, hop, self.me).wait_send()


def sum_scratch(shape):
    dma = pltpu.SemaphoreType.DMA
    rows, width = shape[-2:]

    def buffer(count):
        return pltpu.VMEM((2,) + shape[:-2] + (count, width), jnp.bfloat16)

    buffers = [buffer(rows // 4), buffer(rows // 4), buffer(rows // 8)]
    return buffers + [dma((2,)), dma((2, 2)), dma((2, 2))]


SUM_REFS = 6


def spread_scratch(shape):
    dma = pltpu.SemaphoreType.DMA
    scratch = [pltpu.VMEM(shape, jnp.bfloat16), dma((2, 2)), dma((2, 2)), dma((2,))]
    if len(shape) == 3:
        scratch += [dma((shape[0], 2)), dma((shape[0], 2))]
    return scratch


def spread_refs(columns):
    return 6 if columns else 4


def gradient_sum_kernel(held_columns, columns, *refs):
    refs = list(refs)
    helds, sources = refs[: len(held_columns)], refs[len(held_columns) :][: len(columns)]
    count = len(helds) + len(sources)
    results = refs[count : 2 * count + 1]
    scratch = refs[2 * count + 1 :]
    store_sem = scratch.pop()
    sums, spreads = [], []
    for kept, by_column in zip(helds, held_columns):
        size = spread_refs(by_column)
        spreads.append(Spread(Held(kept), scratch[:size], by_column))
        del scratch[:size]
    for source, by_column in zip(sources, columns):
        sums.append(Summed(source, scratch[:SUM_REFS], by_column))
        del scratch[:SUM_REFS]
        size = spread_refs(by_column)
        spreads.append(Spread(sums[-1], scratch[:size], by_column))
        del scratch[:size]
    early, late = spreads[: len(helds)], spreads[len(helds) :]
    greet_all()

    def stores(at):
        final = spreads[at].final
        if at > 0:
            return [pltpu.make_async_copy(final, results[at + 1], store_sem.at[0, at])]
        part = final.shape[2] // 2
        return [
            pltpu.make_async_copy(
                final.at[member, :, pl.ds(side * part, part)],
                results[side].at[:, pl.ds(member * part, part)],
                store_sem.at[1 + side, member],
            )
            for member in range(final.shape[0])
            for side in (0, 1)
        ]

    def launch(spread):
        if spread.columns:
            spread.swap_begin()
        else:
            spread.place_all()
            spread.spread_begin()

    for share in sums:
        share.begin()
    for spread in early:
        launch(spread)
    for share in sums:
        share.middle()
    for spread in early:
        if spread.columns:
            spread.swap_end()
            spread.spread_begin()
        else:
            spread.spread_on()
    for share, spread in zip(sums, late):
        share.finish()
        launch(spread)
    for spread in early:
        if spread.columns:
            spread.spread_on()
    for spread in late:
        if spread.columns:
            spread.swap_end()
            spread.spread_begin()
        else:
            spread.spread_on()
    for spread in late:
        if spread.columns:
            spread.spread_on()
    for at, spread in enumerate(spreads):
        spread.spread_end()
        for store in stores(at):
            store.start()
    for share in sums:
        share.sum_sent()
    for spread in spreads:
        spread.spread_sent()
    for at in range(count):
        for store in stores(at):
            store.wait()


def gradient_sum(helds, grads):
    held_shapes = [held.shape[1:-2] + (8 * held.shape[-2], held.shape[-1]) for held in helds]
    members, rows, width = held_shapes[0]
    wide = (rows, members * width // 2)
    shapes = held_shapes + [grad.shape for grad in grads]
    held_columns = [len(shape) == 3 for shape in held_shapes]
    columns = [grad.ndim == 3 for grad in grads]
    anywhere = pl.BlockSpec(memory_space=pl.ANY)
    scratch = []
    for shape in held_shapes:
        scratch += spread_scratch(shape)
    for grad in grads:
        scratch += sum_scratch(grad.shape) + spread_scratch(grad.shape)
    return pl.pallas_call(
        functools.partial(gradient_sum_kernel, held_columns, columns),
        out_shape=[
            jax.ShapeDtypeStruct(shape, jnp.bfloat16) for shape in [wide, wide] + shapes[1:]
        ],
        in_specs=[anywhere] * len(shapes),
        out_specs=[anywhere] * (len(shapes) + 1),
        scratch_shapes=scratch + [pltpu.SemaphoreType.DMA((3, members))],
        compiler_params=pltpu.CompilerParams(
            collective_id=3, has_side_effects=True, vmem_limit_bytes=KERNEL_VMEM
        ),
        cost_estimate=pl.CostEstimate(flops=0, bytes_accessed=300 << 20, transcendentals=0),
        name="gradient_sum",
    )(*helds, *grads)

def rope_norm(lin, gain, cosine, sine_part):
    scale = lax.rsqrt(jnp.mean(lin * lin, axis=-1, keepdims=True) + EPSILON)
    scaled = lin * scale * gain
    first, second = scaled[:, : HD // 2], scaled[:, HD // 2 :]
    return jnp.concatenate(
        [first * cosine - second * sine_part, second * cosine + first * sine_part], axis=-1
    )


def attention_forward_kernel(
    chips,
    own_ref,
    qkv_own,
    gate_own,
    up_own,
    out_hbm,
    cos_ref,
    sin_ref,
    gain_query_ref,
    gain_key_ref,
    query_docs_ref,
    key_docs_ref,
    result_ref,
    all_hbm,
    qkv_hbm,
    gateup_hbm,
    lin_hbm,
    query_hbm,
    span_hbm,
    probs_hbm,
    attended_hbm,
    *scratch,
):
    scratch = list(scratch)
    line = Line(chips, scratch[:LINE_REFS])
    del scratch[:LINE_REFS]
    spreads = []
    for kept in (qkv_own, gate_own, up_own):
        spreads.append(Spread(Held(kept), scratch[: spread_refs(True)], True))
        del scratch[: spread_refs(True)]
    qkv, gate, up = spreads
    out, lin, query, span, probs, attended = scratch[:6]
    load_sem, store_sem, span_send, span_recv = scratch[6:]
    width = line.slots.shape[3]
    pair = 2 * line.tok
    block = chips * pair
    ctx_at = lax.axis_index("ctx")
    planes = lax.axis_size("ctx")
    ff_part = gate.final.shape[2]
    bfloat = jnp.bfloat16

    load_out = pltpu.make_async_copy(out_hbm, out, load_sem)
    load_out.start()
    greet_all()
    qkv.swap_begin()
    line.gather_begin(own_ref)
    line.gather_step(1)
    qkv.swap_end()
    qkv.spread_begin()
    line.gather_step(2)
    qkv.spread_on()
    for distance in range(3, chips):
        line.gather_step(distance)
    gate.swap_begin()
    up.swap_begin()
    line.own_copy(own_ref).wait()
    for chip in range(chips):
        line.gather_other(chip)
    qkv.spread_end()
    stores = [
        pltpu.make_async_copy(line.slots, all_hbm, store_sem.at[0]),
        pltpu.make_async_copy(qkv.final, qkv_hbm, store_sem.at[1]),
        pltpu.make_async_copy(lin, lin_hbm, store_sem.at[2]),
        pltpu.make_async_copy(query, query_hbm, store_sem.at[3]),
        pltpu.make_async_copy(span, span_hbm, store_sem.at[4]),
        pltpu.make_async_copy(probs, probs_hbm, store_sem.at[5]),
        pltpu.make_async_copy(attended, attended_hbm, store_sem.at[6]),
        pltpu.make_async_copy(
            gate.final, gateup_hbm.at[:, :, pl.ds(0, ff_part)], store_sem.at[7]
        ),
        pltpu.make_async_copy(
            up.final, gateup_hbm.at[:, :, pl.ds(ff_part, ff_part)], store_sem.at[8]
        ),
    ]
    stores[0].start()
    stores[1].start()

    @pl.loop(0, chips)
    def _(chip):
        rows = pl.ds(pl.multiple_of(chip * pair, pair), pair)
        span_rows = pl.ds(pl.multiple_of(WINDOW + chip * pair, pair), pair)
        inputs = line.slots[chip].reshape(pair, width)
        weights = qkv.final[...].reshape(width, 3 * HD)
        key_lin = dot_nn(inputs, weights[:, HD : 2 * HD])
        lin[rows, HD : 2 * HD] = key_lin
        span[0, span_rows] = rope_norm(
            key_lin, gain_key_ref[...], cos_ref[rows], sin_ref[rows]
        ).astype(bfloat)
        span[1, span_rows] = dot_nn(inputs, weights[:, 2 * HD :]).astype(bfloat)

    part = WINDOW // 2

    def span_copy(start, to_start, way, device):
        return pltpu.make_async_remote_copy(
            src_ref=span.at[:, pl.ds(pl.multiple_of(start, part), part)],
            dst_ref=span.at[:, pl.ds(pl.multiple_of(to_start, part), part)],
            send_sem=span_send.at[way],
            recv_sem=span_recv.at[way],
            device_id=device,
            device_id_type=pl.DeviceIdType.MESH,
        )

    mine = line.core * part
    others = (1 - line.core) * part
    onward = span_copy(block + mine, mine, 0, {"ctx": lax.rem(ctx_at + 1, planes)})
    across = span_copy(mine, mine, 1, {"fsdp": line.place(line.chip, 1 - line.core)})
    arrived = span_copy(others, others, 1, {"fsdp": line.place(line.chip, 1 - line.core)})

    @pl.when(ctx_at < planes - 1)
    def _():
        onward.start()

    @pl.when(ctx_at == 0)
    def _():
        span[:, pl.ds(0, WINDOW)] = jnp.zeros((2, WINDOW, HD), bfloat)

    @pl.loop(0, chips)
    def _(chip):
        rows = pl.ds(pl.multiple_of(chip * pair, pair), pair)
        inputs = line.slots[chip].reshape(pair, width)
        weights = qkv.final[...].reshape(width, 3 * HD)
        query_lin = dot_nn(inputs, weights[:, :HD])
        lin[rows, :HD] = query_lin
        rotated = rope_norm(query_lin, gain_query_ref[...], cos_ref[rows], sin_ref[rows])
        query[rows] = (rotated.astype(bfloat).astype(jnp.float32) * SCORE_SCALE).astype(bfloat)

    @pl.when(ctx_at > 0)
    def _():
        onward.wait_recv()
        across.start()
        arrived.wait_recv()

    for store in stores[2:5]:
        store.start()
    load_out.wait()

    span_len = WINDOW + pair
    for step in range(chips):
        chip = line.order(chips - 1 - step)
        rows = pl.ds(pl.multiple_of(chip * pair, pair), pair)
        span_rows = pl.ds(pl.multiple_of(chip * pair, pair), span_len)
        scores = dot_nt(query[rows], span[0, span_rows])
        distance = (
            WINDOW
            + lax.broadcasted_iota(jnp.int32, (pair, span_len), 0)
            - lax.broadcasted_iota(jnp.int32, (pair, span_len), 1)
        )
        visible = (
            (distance >= 0)
            & (distance < WINDOW)
            & (query_docs_ref[rows] == key_docs_ref[:, span_rows])
        )
        scores = jnp.where(visible, scores, NEGATIVE)
        shifted = jnp.exp(scores - jnp.max(scores, axis=-1, keepdims=True))
        prob = (shifted / jnp.sum(shifted, axis=-1, keepdims=True)).astype(bfloat)
        probs[rows] = prob
        attended[rows] = dot_nn(prob, span[1, span_rows]).astype(bfloat)

        wide = 512

        @pl.loop(0, width // wide)
        def _(at, chip=chip, rows=rows):
            cols = pl.ds(pl.multiple_of(at * wide, wide), wide)
            sums = dot_nn(attended[rows], out[:, cols]).astype(bfloat)
            line.parts[chip, :, :, cols] = sums.reshape(2, line.tok, wide)

        line.core_copy(chip).start()
        if step > 0:
            line.scatter_first(line.order(chips - step))
        if step == 1:
            gate.swap_end()
            gate.spread_begin()
    line.scatter_first(line.order(0))
    for store in stores[5:7]:
        store.start()
    gate.spread_on()
    up.swap_end()
    up.spread_begin()
    line.scatter_rest(result_ref)
    up.spread_on()
    gate.spread_end()
    stores[7].start()
    up.spread_end()
    stores[8].start()
    line.gather_end()
    for spread in spreads:
        spread.spread_sent()

    @pl.when(ctx_at < planes - 1)
    def _():
        onward.wait_send()

    @pl.when(ctx_at > 0)
    def _():
        across.wait_send()

    for store in stores:
        store.wait()


def attention_forward(
    own, qkv_own, gate_own, up_own, out, cosine, sine_part, gain_query, gain_key, query_docs, key_docs
):
    tok_count, width = own.shape
    members = qkv_own.shape[1]
    chips = members // 2
    block = members * tok_count
    span_len = WINDOW + block
    rows = 8 * qkv_own.shape[2]
    ff_part = gate_own.shape[3]
    bfloat = jnp.bfloat16
    anywhere = pl.BlockSpec(memory_space=pl.ANY)
    vmem = pl.BlockSpec(memory_space=pltpu.VMEM)
    dma = pltpu.SemaphoreType.DMA
    kept = [
        ((block, 2 * HD), jnp.float32),
        ((block, HD), bfloat),
        ((2, span_len, HD), bfloat),
        ((block, WINDOW + 2 * tok_count), bfloat),
        ((block, HD), bfloat),
    ]
    outputs = [
        ((tok_count, width), jnp.float32),
        ((chips, 2, tok_count, width), bfloat),
        ((members, rows, 3 * HD), bfloat),
        ((members, rows, 2 * ff_part), bfloat),
    ] + kept
    return pl.pallas_call(
        functools.partial(attention_forward_kernel, chips),
        out_shape=[jax.ShapeDtypeStruct(*output) for output in outputs],
        in_specs=[vmem] + [anywhere] * 4 + [vmem] * 6,
        out_specs=[vmem] + [anywhere] * 8,
        scratch_shapes=line_scratch(chips, tok_count, width)
        + spread_scratch((members, rows, 3 * HD))
        + spread_scratch((members, rows, ff_part))
        + spread_scratch((members, rows, ff_part))
        + [pltpu.VMEM(out.shape, bfloat)]
        + [pltpu.VMEM(*one) for one in kept]
        + [dma, dma((9,)), dma((2,)), dma((2,))],
        compiler_params=pltpu.CompilerParams(
            collective_id=4, has_side_effects=True, vmem_limit_bytes=KERNEL_VMEM
        ),
        cost_estimate=pl.CostEstimate(
            flops=8 << 30, bytes_accessed=300 << 20, transcendentals=block * 1280
        ),
        name="attention_forward",
    )(
        own,
        qkv_own,
        gate_own,
        up_own,
        out,
        cosine,
        sine_part,
        gain_query,
        gain_key,
        query_docs,
        key_docs,
    )

def rope_norm_back(grad, lin, gain, cosine, sine_part):
    first, second = grad[:, : HD // 2], grad[:, HD // 2 :]
    turned = jnp.concatenate(
        [first * cosine + second * sine_part, second * cosine - first * sine_part], axis=-1
    )
    scale = lax.rsqrt(jnp.mean(lin * lin, axis=-1, keepdims=True) + EPSILON)
    scaled = turned * gain
    along = jnp.mean(lin * scaled, axis=-1, keepdims=True)
    grad_lin = scale * scaled - lin * (scale * scale * scale * along)
    return grad_lin, jnp.sum(lin * scale * turned, axis=0, keepdims=True)


def attention_backward_kernel(
    chips,
    own_ref,
    out_hbm,
    qkv_hbm,
    lin_hbm,
    query_hbm,
    span_hbm,
    probs_hbm,
    cos_ref,
    sin_ref,
    gain_query_ref,
    gain_key_ref,
    gateup_hbm,
    down_hbm,
    result_ref,
    all_hbm,
    grad_hbm,
    gains_ref,
    gateup_kept,
    down_kept,
    *scratch,
):
    scratch = list(scratch)
    line = Line(chips, scratch[:LINE_REFS])
    del scratch[:LINE_REFS]
    shares = []
    for source, columns in ((gateup_hbm, True), (down_hbm, False)):
        shares.append(Summed(source, scratch[:SUM_REFS], columns))
        del scratch[:SUM_REFS]
    gateup, down = shares
    out, qkv, lin, query, span, probs, grad, grad_span, back, across, returned = scratch[:11]
    load_sem, store_sem, back_send, back_recv, grad_out = scratch[11:]
    width = line.slots.shape[3]
    pair = 2 * line.tok
    block = chips * pair
    ctx_at = lax.axis_index("ctx")
    planes = lax.axis_size("ctx")
    bfloat = jnp.bfloat16
    loads = [
        pltpu.make_async_copy(src, dst, load_sem.at[at])
        for at, (src, dst) in enumerate(
            (
                (out_hbm, out),
                (span_hbm, span),
                (probs_hbm, probs),
                (lin_hbm, lin),
                (query_hbm, query),
                (qkv_hbm, qkv),
            )
        )
    ]
    for load in loads:
        load.start()
    greet_all()
    line.gather_begin(own_ref)
    gateup.begin()
    grad_span[...] = jnp.zeros_like(grad_span)
    gains_ref[...] = jnp.zeros_like(gains_ref)
    line.own_copy(own_ref).wait()
    for load in loads:
        load.wait()

    span_len = WINDOW + pair
    for step in range(chips):
        if step > 0:
            line.gather_step(step)
        chip = line.order(step)
        line.gather_other(chip)
        rows = pl.ds(pl.multiple_of(chip * pair, pair), pair)
        span_rows = pl.ds(pl.multiple_of(chip * pair, pair), span_len)
        grad_out[rows] = dot_nt(line.slots[chip].reshape(pair, width), out[...]).astype(bfloat)
        grad_prob = dot_nt(grad_out[rows], span[1, span_rows])
        prob = probs[rows].astype(jnp.float32)
        inner = jnp.sum(prob * grad_prob, axis=-1, keepdims=True)
        grad_score = (prob * (grad_prob - inner)).astype(bfloat)
        grad_query = dot_nn(grad_score, span[0, span_rows]) * SCORE_SCALE
        grad_lin, grad_gain = rope_norm_back(
            grad_query, lin[rows, :HD], gain_query_ref[...], cos_ref[rows], sin_ref[rows]
        )
        grad[rows, :HD] = grad_lin.astype(bfloat)
        gains_ref[0:1] += grad_gain
        grad_span[0, span_rows] += dot_tn(grad_score, query[rows])
        grad_span[1, span_rows] += dot_tn(probs[rows], grad_out[rows])

    store_all = pltpu.make_async_copy(line.slots, all_hbm, store_sem.at[0])
    store_all.start()

    part = WINDOW // 2
    mine, others = line.core * part, (1 - line.core) * part
    back[...] = grad_span[:, pl.ds(pl.multiple_of(others, part), part)].astype(bfloat)
    to_core = remote(
        back, across, back_send.at[0], back_recv.at[0], line.place(line.chip, 1 - line.core)
    )
    to_core.start()
    to_core.wait()
    total = grad_span[:, pl.ds(pl.multiple_of(mine, part), part)]
    back[...] = (total + across[...].astype(jnp.float32)).astype(bfloat)
    to_before = pltpu.make_async_remote_copy(
        src_ref=back,
        dst_ref=returned,
        send_sem=back_send.at[1],
        recv_sem=back_recv.at[1],
        device_id={"ctx": lax.rem(ctx_at + planes - 1, planes)},
        device_id_type=pl.DeviceIdType.MESH,
    )

    @pl.when(ctx_at > 0)
    def _():
        to_before.start()

    down.begin()

    @pl.when(ctx_at < planes - 1)
    def _():
        to_before.wait_recv()
        here = pl.ds(pl.multiple_of(block + mine, part), part)
        grad_span[:, here] += returned[...].astype(jnp.float32)

    for step in range(chips):
        chip = line.order(chips - 1 - step)
        rows = pl.ds(pl.multiple_of(chip * pair, pair), pair)
        span_rows = pl.ds(pl.multiple_of(WINDOW + chip * pair, pair), pair)
        grad_lin, grad_gain = rope_norm_back(
            grad_span[0, span_rows], lin[rows, HD:], gain_key_ref[...], cos_ref[rows], sin_ref[rows]
        )
        grad[rows, HD : 2 * HD] = grad_lin.astype(bfloat)
        gains_ref[1:2] += grad_gain
        grad[rows, 2 * HD :] = grad_span[1, span_rows].astype(bfloat)
        wide = 512

        @pl.loop(0, width // wide)
        def _(at, chip=chip, rows=rows):
            cols = pl.ds(pl.multiple_of(at * wide, wide), wide)
            sums = dot_nt(grad[rows], qkv[cols]).astype(bfloat)
            line.parts[chip, :, :, cols] = sums.reshape(2, line.tok, wide)

        line.core_copy(chip).start()
        if step > 0:
            line.scatter_first(line.order(chips - step))
    line.scatter_first(line.order(0))
    store_grad = pltpu.make_async_copy(grad, grad_hbm, store_sem.at[1])
    store_grad.start()
    gateup.middle()
    line.scatter_rest(result_ref)
    down.middle()
    gateup.finish()
    down.finish()
    stores = []
    for at, (share, kept) in enumerate(((gateup, gateup_kept), (down, down_kept))):
        for half in (0, 1):
            stores.append(
                pltpu.make_async_copy(
                    share.own_rows(half), kept.at[half], store_sem.at[2 + 2 * at + half]
                )
            )
    for store in stores:
        store.start()
    line.gather_end()
    for share in shares:
        share.sum_sent()

    @pl.when(ctx_at > 0)
    def _():
        to_before.wait_send()

    store_all.wait()
    store_grad.wait()
    for store in stores:
        store.wait()


def attention_backward(
    own,
    out,
    qkv,
    lin,
    query,
    span,
    probs,
    cosine,
    sine_part,
    gain_query,
    gain_key,
    part_gateup,
    part_down,
):
    tok_count, width = own.shape
    members = part_gateup.shape[0]
    chips = members // 2
    block = members * tok_count
    bfloat = jnp.bfloat16
    anywhere = pl.BlockSpec(memory_space=pl.ANY)
    vmem = pl.BlockSpec(memory_space=pltpu.VMEM)
    dma = pltpu.SemaphoreType.DMA
    eighth = part_gateup.shape[1] // 8
    outputs = [
        ((tok_count, width), jnp.float32),
        ((chips, 2, tok_count, width), bfloat),
        ((block, 3 * HD), bfloat),
        ((2, HD), jnp.float32),
        ((2, members, eighth, part_gateup.shape[2]), bfloat),
        ((2, part_down.shape[0] // 8, part_down.shape[1]), bfloat),
    ]
    half_span = (2, WINDOW // 2, HD)
    return pl.pallas_call(
        functools.partial(attention_backward_kernel, chips),
        out_shape=[jax.ShapeDtypeStruct(*output) for output in outputs],
        in_specs=[vmem] + [anywhere] * 6 + [vmem] * 4 + [anywhere] * 2,
        out_specs=[vmem, anywhere, anywhere, vmem, anywhere, anywhere],
        scratch_shapes=line_scratch(chips, tok_count, width)
        + sum_scratch(part_gateup.shape)
        + sum_scratch(part_down.shape)
        + [pltpu.VMEM(one.shape, one.dtype) for one in (out, qkv, lin, query, span, probs)]
        + [
            pltpu.VMEM((block, 3 * HD), bfloat),
            pltpu.VMEM(span.shape, jnp.float32),
            pltpu.VMEM(half_span, bfloat),
            pltpu.VMEM(half_span, bfloat),
            pltpu.VMEM(half_span, bfloat),
            dma((6,)),
            dma((6,)),
            dma((2,)),
            dma((2,)),
            pltpu.VMEM((block, HD), bfloat),
        ],
        compiler_params=pltpu.CompilerParams(
            collective_id=5, has_side_effects=True, vmem_limit_bytes=KERNEL_VMEM
        ),
        cost_estimate=pl.CostEstimate(
            flops=8 << 30, bytes_accessed=300 << 20, transcendentals=0
        ),
        name="attention_backward",
    )(
        own,
        out,
        qkv,
        lin,
        query,
        span,
        probs,
        cosine,
        sine_part,
        gain_query,
        gain_key,
        part_gateup,
        part_down,
    )

def by_heads(
    tokens,
    per_layer,
    cotangent,
    doc_lengths,
    positions,
    w_query,
    w_key,
    w_value,
    w_out,
    laurel_left,
    laurel_right,
    w_gate,
    w_up,
    w_down,
    ple_gate,
    ple_proj,
    attn_in_gain,
    query_gain,
    key_gain,
    attn_out_gain,
    laurel_gain,
    ffn_in_gain,
    ffn_out_gain,
    ple_gain,
):
    bfloat = jnp.bfloat16
    ctx_count = lax.axis_size("ctx")
    fsdp_count = lax.axis_size("fsdp")
    tok_count = tokens.shape[0]
    block_len = tok_count * fsdp_count
    chips = fsdp_count // 2
    rows = w_query.shape[0]
    ff_part = w_gate.shape[1] // fsdp_count
    ctx_at = lax.axis_index("ctx")
    fsdp_at = lax.axis_index("fsdp")

    gain_list = [
        attn_in_gain,
        query_gain,
        key_gain,
        attn_out_gain,
        laurel_gain,
        ffn_in_gain,
        ffn_out_gain,
        ple_gain,
    ]
    gain_sizes = [g.shape[0] for g in gain_list]
    gain_offsets = [sum(gain_sizes[:n]) for n in range(len(gain_sizes) + 1)]
    packed = jnp.concatenate(gain_list + [positions.astype(jnp.float32)])
    packed = jnp.pad(packed, (0, -packed.shape[0] % 1024)).reshape(1, -1, 128)
    packed = lax.all_gather(packed, "fsdp", axis=0, tiled=True).reshape(fsdp_count, -1)
    gain_in, gain_query, gain_key, gain_post, gain_laurel, gain_ffin, gain_ffout, gain_ple = (
        packed[:, gain_offsets[n] : gain_offsets[n + 1]].reshape(-1) for n in range(8)
    )
    block_positions = packed[:, gain_offsets[8] : gain_offsets[8] + tok_count].reshape(-1)
    cosine, sine_part = rope_tables(block_positions, HD)
    cosine, sine_part = cosine[:, 0], sine_part[:, 0]

    group_size = HQ // KV
    eighth = rows // 8
    at_x, at_y = ctx_at % 2, ctx_at // 2

    def own_rows(weight, width):
        starts = (at_x * 2 + at_y, 4 + at_y * 2 + at_x)
        halves = [lax.dynamic_slice_in_dim(weight, n * eighth, eighth, 0) for n in starts]
        held = jnp.stack(halves).astype(bfloat)
        return jnp.transpose(held.reshape(2, eighth, -1, width), (0, 2, 1, 3))

    qkv_own = jnp.concatenate(
        [
            own_rows(w_query, HD),
            jnp.repeat(own_rows(w_key, HD), group_size, axis=1),
            jnp.repeat(own_rows(w_value, HD), group_size, axis=1),
        ],
        axis=3,
    )
    gate_own, up_own = own_rows(w_gate, ff_part), own_rows(w_up, ff_part)
    out_low = w_out.astype(bfloat)
    down_low = w_down.astype(bfloat)
    full_left, full_right, full_pgate, full_pproj = (
        lax.all_gather(w.astype(bfloat), "fsdp", axis=0, tiled=True)
        for w in (laurel_left, laurel_right, ple_gate, ple_proj)
    )

    inputs = tokens.astype(jnp.float32)
    ple_input = per_layer.astype(jnp.float32)
    normed, norm_back = jax.vjp(rms_norm, inputs, gain_in)
    normed_low = normed.astype(bfloat)
    block_start = ctx_at * block_len
    places = block_start - WINDOW + jnp.arange(WINDOW + block_len, dtype=jnp.int32)
    key_docs = jnp.where(places >= 0, document_ids(doc_lengths, places), -1)
    projected, normed_all, qkv_full, gateup_full, qk_lin, query_low, span_kv, probs, attended_low = (
        attention_forward(
            normed_low,
            qkv_own,
            gate_own,
            up_own,
            out_low,
            cosine,
            sine_part,
            gain_query[None, :],
            gain_key[None, :],
            key_docs[WINDOW:, None],
            key_docs[None, :],
        )
    )
    normed_all = normed_all.reshape(block_len, -1)
    col_qkv = qkv_full.reshape(normed_all.shape[1], -1)
    col_gateup = gateup_full.reshape(normed_all.shape[1], -1)
    narrow_low = matmul(normed_low, full_left).astype(bfloat)
    widened = matmul(narrow_low, full_right)
    mixed, mix_back = jax.vjp(mix_piece, inputs, normed, projected, widened, gain_post, gain_laurel)
    ffn_normed, ffn_norm_back = jax.vjp(rms_norm, mixed, gain_ffin)
    down_lin, ffn_all, hidden_low, act_low, slope_low = ffn_forward(
        ffn_normed.astype(bfloat), col_gateup, down_low, chips
    )
    layer_mid, ffn_out_back = jax.vjp(ffn_out_piece, mixed, down_lin, gain_ffout)
    layer_low = layer_mid.astype(bfloat)
    ple_lin = matmul(layer_low, full_pgate)
    ple_mid, ple_back = jax.vjp(ple_act, ple_lin, ple_input)
    ple_low = ple_mid.astype(bfloat)
    ple_wide = matmul(ple_low, full_pproj)
    out_full, final_back = jax.vjp(final_piece, layer_mid, ple_wide, gain_ple)

    grad_layer, grad_pwide, grad_gple = final_back(cotangent.astype(jnp.float32))
    grad_pwide_low = grad_pwide.astype(bfloat)
    part_pproj = matmul_tn(ple_low, grad_pwide_low)
    grad_plemid = matmul_nt(grad_pwide_low, full_pproj)
    grad_plelin, grad_pleinput = ple_back(grad_plemid)
    grad_plelin_low = grad_plelin.astype(bfloat)
    part_pgate = matmul_tn(layer_low, grad_plelin_low)
    grad_layer = grad_layer + matmul_nt(grad_plelin_low, full_pgate)
    grad_mixed, grad_down, grad_gffout = ffn_out_back(grad_layer)
    grad_ffn, grad_down_all, grad_gateup_low = ffn_backward(
        grad_down.astype(bfloat), col_gateup, down_low, act_low, slope_low, chips
    )
    part_wdown = matmul_tn(hidden_low, grad_down_all).astype(bfloat)
    part_gateup = matmul_tn(ffn_all, grad_gateup_low).astype(bfloat).reshape(fsdp_count, rows, -1)
    grad_mixed_more, grad_gffin = ffn_norm_back(grad_ffn)
    grad_mixed = grad_mixed + grad_mixed_more
    grad_in_first, grad_normed, grad_proj, grad_lwide, grad_gpost, grad_glaurel = mix_back(
        grad_mixed
    )
    grad_lwide_low = grad_lwide.astype(bfloat)
    part_right = matmul_tn(narrow_low, grad_lwide_low)
    grad_narrow_low = matmul_nt(grad_lwide_low, full_right).astype(bfloat)
    part_left = matmul_tn(normed_low, grad_narrow_low)
    grad_normed = grad_normed + matmul_nt(grad_narrow_low, full_left)

    grad_normed_more, grad_proj_all, grad_qkv_low, grad_head_gains, held_gateup, held_wdown = (
        attention_backward(
            grad_proj.astype(bfloat),
            out_low,
            col_qkv,
            qk_lin,
            query_low,
            span_kv,
            probs,
            cosine,
            sine_part,
            gain_query[None, :],
            gain_key[None, :],
            part_gateup,
            part_wdown,
        )
    )
    grad_gquery, grad_gkey = grad_head_gains[0], grad_head_gains[1]
    part_wout = matmul_tn(attended_low, grad_proj_all.reshape(block_len, -1)).astype(bfloat)
    part_qkv = matmul_tn(normed_all, grad_qkv_low).astype(bfloat).reshape(fsdp_count, rows, -1)
    small_parts = [
        part.astype(bfloat).reshape(fsdp_count, -1, inputs.shape[1])
        for part in (part_pgate, part_pproj, part_left, part_right)
    ]
    small_sizes = [part.shape[1] for part in small_parts]
    small_total = sum(small_sizes)
    small_rows = -(-small_total // 128) * 128
    small_parts.append(
        jnp.zeros((fsdp_count, small_rows - small_total, inputs.shape[1]), bfloat)
    )
    small = lax.psum_scatter(
        jnp.concatenate(small_parts, axis=1), "fsdp", scatter_dimension=0, tiled=False
    )
    grad_normed = grad_normed + grad_normed_more
    grad_in_second, grad_gin = norm_back(grad_normed)
    grad_tokens = grad_in_first + grad_in_second

    grad_gains = [
        grad_gin,
        grad_gquery,
        grad_gkey,
        grad_gpost,
        grad_glaurel,
        grad_gffin,
        grad_gffout,
        grad_gple,
    ]
    gain_parts = jnp.concatenate([g.reshape(fsdp_count, -1) for g in grad_gains], axis=1)
    gain_parts = jnp.pad(gain_parts, ((0, 0), (0, 128 * 128 - gain_parts.shape[1])))
    gain_parts = gain_parts.astype(bfloat).reshape(fsdp_count, 128, 128)

    sum_wgate, sum_wup, sum_wdown, sum_wout, sum_qkv, sum_small, sum_gains = gradient_sum(
        [held_gateup, held_wdown], [part_wout, part_qkv, small, gain_parts]
    )
    gain_sums = jnp.sum(sum_gains.astype(jnp.float32), axis=0).reshape(-1)
    grad_wgate = sum_wgate.astype(jnp.float32)
    grad_wup = sum_wup.astype(jnp.float32)
    grad_wdown = sum_wdown.astype(jnp.float32)
    grad_wout = sum_wout.astype(jnp.float32)
    sum_qkv = sum_qkv.astype(jnp.float32)
    grad_wquery = jnp.transpose(sum_qkv[:, :, :HD], (1, 0, 2)).reshape(rows, -1)
    sum_kv = jnp.sum(sum_qkv[:, :, HD:].reshape(KV, group_size, rows, 2 * HD), axis=1)
    sum_kv = jnp.transpose(sum_kv, (1, 0, 2))
    grad_wkey = sum_kv[:, :, :HD].reshape(rows, -1)
    grad_wvalue = sum_kv[:, :, HD:].reshape(rows, -1)
    sum_small = sum_small.astype(jnp.float32)
    small_ends = [sum(small_sizes[:n]) for n in range(5)]
    grad_pgate, grad_pproj, grad_wleft, grad_wright = (
        sum_small[small_ends[n] : small_ends[n + 1]].reshape(weight.shape)
        for n, weight in enumerate((ple_gate, ple_proj, laurel_left, laurel_right))
    )
    return (
        out_full.astype(bfloat),
        grad_tokens,
        grad_pleinput,
        grad_wquery,
        grad_wkey,
        grad_wvalue,
        grad_wout,
        grad_wleft,
        grad_wright,
        grad_wgate,
        grad_wup,
        grad_wdown,
        grad_pgate,
        grad_pproj,
        *(gain_sums[gain_offsets[n] : gain_offsets[n + 1]] for n in range(8)),
    )


def solution(mesh):
    in_specs = (
        P(("ctx", "fsdp"), None),
        P(("ctx", "fsdp"), None),
        P(("ctx", "fsdp"), None),
        P(),
        P(("ctx", "fsdp")),
        P("fsdp", None),
        P("fsdp", None),
        P("fsdp", None),
        P("fsdp", None),
        P("fsdp", None),
        P("fsdp", None),
        P("fsdp", None),
        P("fsdp", None),
        P("fsdp", None),
        P("fsdp", None),
        P("fsdp", None),
        P("fsdp"),
        P("fsdp"),
        P("fsdp"),
        P("fsdp"),
        P("fsdp"),
        P("fsdp"),
        P("fsdp"),
        P("fsdp"),
    )
    out_specs = (
        P(("ctx", "fsdp"), None),
        P(("ctx", "fsdp"), None),
        P(("ctx", "fsdp"), None),
        P("fsdp", None),
        P("fsdp", None),
        P("fsdp", None),
        P("fsdp", None),
        P("fsdp", None),
        P("fsdp", None),
        P("fsdp", None),
        P("fsdp", None),
        P("fsdp", None),
        P("fsdp", None),
        P("fsdp", None),
        P("fsdp"),
        P("fsdp"),
        P("fsdp"),
        P("fsdp"),
        P("fsdp"),
        P("fsdp"),
        P("fsdp"),
        P("fsdp"),
    )
    run = by_heads if mesh.shape["fsdp"] == HQ and mesh.shape["ctx"] == 4 else local
    return jax.shard_map(run, mesh=mesh, in_specs=in_specs, out_specs=out_specs, check_vma=False)
```

```python
import dataclasses
import functools
import math

import jax
import jax.numpy as jnp
from jax import lax
from jax.experimental import pallas as pl
from jax.experimental.pallas import tpu as pltpu
from jax.sharding import PartitionSpec as P

HQ = 8
KV = 2
HD = 256
WINDOW = 1024


EPSILON = 1e-06
NEGATIVE = -1e30
ROPE_BASE = 10000.0
HALF_ROOT = 1.0 / math.sqrt(2.0)
GELU_ROOT = math.sqrt(2.0 / math.pi)
GELU_CUBE = 0.044715
SCORE_SCALE = 1.0 / math.sqrt(HD)
KERNEL_VMEM = 62 << 20


def passed_along(block, axis, distance):
    devices = range(lax.axis_size(axis))
    route = [(i - distance, i) for i in devices if i - distance in devices]
    return lax.ppermute(block, axis, route)


def matmul(left_mat, right_mat):
    return jnp.dot(left_mat, right_mat, preferred_element_type=jnp.float32)


def matmul_tn(left_mat, right_mat):
    return lax.dot_general(
        left_mat, right_mat, (((0,), (0,)), ((), ())), preferred_element_type=jnp.float32
    )


def matmul_nt(left_mat, right_mat):
    return lax.dot_general(
        left_mat, right_mat, (((1,), (1,)), ((), ())), preferred_element_type=jnp.float32
    )


def rms_norm(values, gain_vec):
    return (
        values * lax.rsqrt(jnp.mean(values * values, axis=-1, keepdims=True) + EPSILON) * gain_vec
    )


def rope_tables(positions, width):
    half_width = width // 2
    frequency = jnp.exp(
        jnp.arange(half_width, dtype=jnp.float32) * (-2.0 * math.log(ROPE_BASE) / width)
    )
    angles = positions.astype(jnp.float32)[:, None] * frequency[None, :]
    return (jnp.cos(angles)[:, None, :], jnp.sin(angles)[:, None, :])


def rotate(values, cosine, sine_part):
    half_width = values.shape[-1] // 2
    first_half = values[..., :half_width]
    second_half = values[..., half_width:]
    return jnp.concatenate(
        [
            first_half * cosine - second_half * sine_part,
            second_half * cosine + first_half * sine_part,
        ],
        axis=-1,
    )


def document_ids(doc_lengths, places):
    doc_ends = jnp.cumsum(doc_lengths)
    return jnp.sum((places[:, None] >= doc_ends[None, :-1]).astype(jnp.int32), axis=1)


def query_key(cosine, sine_part, query_lin, key_lin, gain_query, gain_key):
    tok_count = query_lin.shape[0]
    query_rot = rotate(
        rms_norm(query_lin.reshape(tok_count, HQ, HD), gain_query), cosine, sine_part
    )
    key_rot = rotate(rms_norm(key_lin.reshape(tok_count, KV, HD), gain_key), cosine, sine_part)
    return (query_rot, key_rot)


def mix_piece(inputs, normed, projected, widened, gain_post, gain_laurel):
    return (
        inputs + rms_norm(projected, gain_post) + normed + rms_norm(widened, gain_laurel)
    ) * HALF_ROOT


def geglu(gate_lin, up_lin):
    return jax.nn.gelu(gate_lin, approximate=True) * up_lin


def ffn_out_piece(mixed, down_lin, gain_ffout):
    return mixed + rms_norm(down_lin, gain_ffout)


def ple_act(ple_lin, ple_input):
    return jax.nn.gelu(ple_lin, approximate=True) * ple_input


def final_piece(layer_mid, ple_wide, gain_ple):
    return layer_mid + rms_norm(ple_wide, gain_ple)


def visibility(doc_lengths, query_start, key_start, tok_count, span_len):
    query_places = query_start + jnp.arange(tok_count, dtype=jnp.int32)
    key_places = key_start + jnp.arange(span_len, dtype=jnp.int32)
    distance = query_places[:, None] - key_places[None, :]
    query_docs = document_ids(doc_lengths, query_places)
    key_docs = document_ids(doc_lengths, key_places)
    return (
        (distance >= 0)
        & (distance < WINDOW)
        & (key_places[None, :] >= 0)
        & (query_docs[:, None] == key_docs[None, :])
    )


def attend_forward(query_low, span_kv, visible):
    tok_count = query_low.shape[0]
    scale_factor = 1.0 / math.sqrt(HD)
    scores = (
        jnp.einsum("tkgh,skh->kgts", query_low, span_kv[0], preferred_element_type=jnp.float32)
        * scale_factor
    )
    scores = jnp.where(visible, scores, NEGATIVE)
    row_top = jnp.max(scores, axis=-1, keepdims=True)
    shifted = jnp.exp(scores - row_top)
    row_total = jnp.sum(shifted, axis=-1, keepdims=True)
    attn_probs = shifted / row_total
    attended = jnp.einsum(
        "kgts,skh->tkgh",
        attn_probs.astype(jnp.bfloat16),
        span_kv[1],
        preferred_element_type=jnp.float32,
    )
    return (attended.reshape(tok_count, -1), row_top + jnp.log(row_total))


def attend_backward(query_low, span_kv, visible, log_total, grad_out_low):
    scale_factor = 1.0 / math.sqrt(HD)
    scores = (
        jnp.einsum("tkgh,skh->kgts", query_low, span_kv[0], preferred_element_type=jnp.float32)
        * scale_factor
    )
    attn_probs = jnp.where(visible, jnp.exp(jnp.where(visible, scores, NEGATIVE) - log_total), 0.0)
    grad_probs = jnp.einsum(
        "tkgh,skh->kgts", grad_out_low, span_kv[1], preferred_element_type=jnp.float32
    )
    inner_sum = jnp.sum(attn_probs * grad_probs, axis=-1, keepdims=True)
    grad_scores = (attn_probs * (grad_probs - inner_sum)).astype(jnp.bfloat16)
    grad_query = (
        jnp.einsum("kgts,skh->tkgh", grad_scores, span_kv[0], preferred_element_type=jnp.float32)
        * scale_factor
    )
    grad_keys = (
        jnp.einsum("kgts,tkgh->skh", grad_scores, query_low, preferred_element_type=jnp.float32)
        * scale_factor
    )
    grad_values = jnp.einsum(
        "kgts,tkgh->skh",
        attn_probs.astype(jnp.bfloat16),
        grad_out_low,
        preferred_element_type=jnp.float32,
    )
    return (grad_query, jnp.stack([grad_keys, grad_values]))


def settle(act_low, grad_low):
    act_cols = lax.all_to_all(act_low, "fsdp", split_axis=1, concat_axis=0, tiled=True)
    shard_rows = matmul_tn(act_cols, lax.all_gather(grad_low, "fsdp", axis=0, tiled=True))
    return lax.psum(shard_rows.astype(jnp.bfloat16), "ctx").astype(jnp.float32)


def local(
    tokens,
    per_layer,
    cotangent,
    doc_lengths,
    positions,
    w_query,
    w_key,
    w_value,
    w_out,
    laurel_left,
    laurel_right,
    w_gate,
    w_up,
    w_down,
    ple_gate,
    ple_proj,
    attn_in_gain,
    query_gain,
    key_gain,
    attn_out_gain,
    laurel_gain,
    ffn_in_gain,
    ffn_out_gain,
    ple_gain,
):
    bfloat = jnp.bfloat16
    tok_count = tokens.shape[0]
    span_len = WINDOW + tok_count
    groups = HQ // KV
    dev_index = lax.axis_index("ctx") * lax.axis_size("fsdp") + lax.axis_index("fsdp")
    query_start = dev_index * tok_count
    key_start = query_start - WINDOW
    visible = visibility(doc_lengths, query_start, key_start, tok_count, span_len)
    cosine, sine_part = rope_tables(positions, HD)
    gain_in, gain_query, gain_key, gain_post, gain_laurel, gain_ffin, gain_ffout, gain_ple = (
        lax.all_gather(attn_in_gain, "fsdp", axis=0, tiled=True),
        lax.all_gather(query_gain, "fsdp", axis=0, tiled=True),
        lax.all_gather(key_gain, "fsdp", axis=0, tiled=True),
        lax.all_gather(attn_out_gain, "fsdp", axis=0, tiled=True),
        lax.all_gather(laurel_gain, "fsdp", axis=0, tiled=True),
        lax.all_gather(ffn_in_gain, "fsdp", axis=0, tiled=True),
        lax.all_gather(ffn_out_gain, "fsdp", axis=0, tiled=True),
        lax.all_gather(ple_gain, "fsdp", axis=0, tiled=True),
    )
    full_query, full_key, full_value, full_out, full_left, full_right = (
        lax.all_gather(w_query.astype(bfloat), "fsdp", axis=0, tiled=True),
        lax.all_gather(w_key.astype(bfloat), "fsdp", axis=0, tiled=True),
        lax.all_gather(w_value.astype(bfloat), "fsdp", axis=0, tiled=True),
        lax.all_gather(w_out.astype(bfloat), "fsdp", axis=0, tiled=True),
        lax.all_gather(laurel_left.astype(bfloat), "fsdp", axis=0, tiled=True),
        lax.all_gather(laurel_right.astype(bfloat), "fsdp", axis=0, tiled=True),
    )
    inputs = tokens.astype(jnp.float32)
    ple_input = per_layer.astype(jnp.float32)
    normed, norm_back = jax.vjp(rms_norm, inputs, gain_in)
    normed_low = normed.astype(bfloat)
    query_lin = matmul(normed_low, full_query)
    key_lin = matmul(normed_low, full_key)
    value_lin = matmul(normed_low, full_value)
    (query_rot, key_rot), rope_back = jax.vjp(
        functools.partial(query_key, cosine, sine_part), query_lin, key_lin, gain_query, gain_key
    )
    query_low = query_rot.astype(bfloat).reshape(tok_count, KV, groups, HD)
    keys_values = jnp.stack(
        [key_rot.astype(bfloat), value_lin.astype(bfloat).reshape(tok_count, KV, HD)]
    )
    block_kv = lax.all_gather(keys_values, "fsdp", axis=1, tiled=True)
    block_len = block_kv.shape[1]
    before_kv = passed_along(block_kv, "ctx", 1)
    span_offset = block_len + lax.axis_index("fsdp") * tok_count - WINDOW
    span_kv = lax.dynamic_slice_in_dim(
        jnp.concatenate([before_kv, block_kv], axis=1), span_offset, span_len, 1
    )
    attended, log_total = attend_forward(query_low, span_kv, visible)
    attended_low = attended.astype(bfloat)
    projected = matmul(attended_low, full_out)
    narrow_low = matmul(normed_low, full_left).astype(bfloat)
    widened = matmul(narrow_low, full_right)
    mixed, mix_back = jax.vjp(mix_piece, inputs, normed, projected, widened, gain_post, gain_laurel)
    full_gate, full_up, full_down, full_pgate, full_pproj = (
        lax.all_gather(w_gate.astype(bfloat), "fsdp", axis=0, tiled=True),
        lax.all_gather(w_up.astype(bfloat), "fsdp", axis=0, tiled=True),
        lax.all_gather(w_down.astype(bfloat), "fsdp", axis=0, tiled=True),
        lax.all_gather(ple_gate.astype(bfloat), "fsdp", axis=0, tiled=True),
        lax.all_gather(ple_proj.astype(bfloat), "fsdp", axis=0, tiled=True),
    )
    ffn_normed, ffn_norm_back = jax.vjp(rms_norm, mixed, gain_ffin)
    ffn_low = ffn_normed.astype(bfloat)
    gate_lin = matmul(ffn_low, full_gate)
    up_lin = matmul(ffn_low, full_up)
    hidden, geglu_back = jax.vjp(geglu, gate_lin, up_lin)
    hidden_low = hidden.astype(bfloat)
    down_lin = matmul(hidden_low, full_down)
    layer_mid, ffn_out_back = jax.vjp(ffn_out_piece, mixed, down_lin, gain_ffout)
    layer_low = layer_mid.astype(bfloat)
    ple_lin = matmul(layer_low, full_pgate)
    ple_mid, ple_back = jax.vjp(ple_act, ple_lin, ple_input)
    ple_low = ple_mid.astype(bfloat)
    ple_wide = matmul(ple_low, full_pproj)
    out_full, final_back = jax.vjp(final_piece, layer_mid, ple_wide, gain_ple)
    full_gate, full_up, full_down, full_pgate, full_pproj = (
        lax.all_gather(w_gate.astype(bfloat), "fsdp", axis=0, tiled=True),
        lax.all_gather(w_up.astype(bfloat), "fsdp", axis=0, tiled=True),
        lax.all_gather(w_down.astype(bfloat), "fsdp", axis=0, tiled=True),
        lax.all_gather(ple_gate.astype(bfloat), "fsdp", axis=0, tiled=True),
        lax.all_gather(ple_proj.astype(bfloat), "fsdp", axis=0, tiled=True),
    )
    grad_layer, grad_pwide, grad_gple = final_back(cotangent.astype(jnp.float32))
    grad_pwide_low = grad_pwide.astype(bfloat)
    grad_pproj = settle(ple_low, grad_pwide_low)
    grad_plemid = matmul_nt(grad_pwide_low, full_pproj)
    grad_plelin, grad_pleinput = ple_back(grad_plemid)
    grad_plelin_low = grad_plelin.astype(bfloat)
    grad_pgate = settle(layer_low, grad_plelin_low)
    grad_layer = grad_layer + matmul_nt(grad_plelin_low, full_pgate)
    grad_mixed, grad_down, grad_gffout = ffn_out_back(grad_layer)
    grad_down_low = grad_down.astype(bfloat)
    grad_wdown = settle(hidden_low, grad_down_low)
    grad_hidden = matmul_nt(grad_down_low, full_down)
    grad_gate, grad_up = geglu_back(grad_hidden)
    grad_gate_low = grad_gate.astype(bfloat)
    grad_up_low = grad_up.astype(bfloat)
    grad_wgate = settle(ffn_low, grad_gate_low)
    grad_wup = settle(ffn_low, grad_up_low)
    grad_ffn = matmul_nt(grad_gate_low, full_gate) + matmul_nt(grad_up_low, full_up)
    grad_mixed_more, grad_gffin = ffn_norm_back(grad_ffn)
    grad_mixed = grad_mixed + grad_mixed_more
    full_query, full_key, full_value, full_out, full_left, full_right = (
        lax.all_gather(w_query.astype(bfloat), "fsdp", axis=0, tiled=True),
        lax.all_gather(w_key.astype(bfloat), "fsdp", axis=0, tiled=True),
        lax.all_gather(w_value.astype(bfloat), "fsdp", axis=0, tiled=True),
        lax.all_gather(w_out.astype(bfloat), "fsdp", axis=0, tiled=True),
        lax.all_gather(laurel_left.astype(bfloat), "fsdp", axis=0, tiled=True),
        lax.all_gather(laurel_right.astype(bfloat), "fsdp", axis=0, tiled=True),
    )
    grad_in_first, grad_normed, grad_proj, grad_lwide, grad_gpost, grad_glaurel = mix_back(
        grad_mixed
    )
    grad_proj_low = grad_proj.astype(bfloat)
    grad_wout = settle(attended_low, grad_proj_low)
    grad_att_low = matmul_nt(grad_proj_low, full_out).astype(bfloat)
    grad_lwide_low = grad_lwide.astype(bfloat)
    grad_wright = settle(narrow_low, grad_lwide_low)
    grad_narrow_low = matmul_nt(grad_lwide_low, full_right).astype(bfloat)
    grad_wleft = settle(normed_low, grad_narrow_low)
    grad_normed = grad_normed + matmul_nt(grad_narrow_low, full_left)
    grad_query_att, grad_span = attend_backward(
        query_low, span_kv, visible, log_total, grad_att_low.reshape(tok_count, KV, groups, HD)
    )
    whole_grad = jnp.zeros((2, 2 * block_len, KV, HD), jnp.float32)
    whole_grad = lax.dynamic_update_slice_in_dim(whole_grad, grad_span, span_offset, 1)
    returned = passed_along(whole_grad[:, :block_len].astype(jnp.bfloat16), "ctx", -1).astype(
        jnp.float32
    )
    own_grad = lax.psum_scatter(
        (whole_grad[:, block_len:] + returned).astype(jnp.bfloat16),
        "fsdp",
        scatter_dimension=1,
        tiled=True,
    ).astype(jnp.float32)
    grad_qlin, grad_klin, grad_gquery, grad_gkey = rope_back(
        (grad_query_att.reshape(tok_count, HQ, HD), own_grad[0])
    )
    grad_qlin_low = grad_qlin.astype(bfloat)
    grad_klin_low = grad_klin.astype(bfloat)
    grad_vlin_low = own_grad[1].reshape(tok_count, KV * HD).astype(bfloat)
    grad_wquery = settle(normed_low, grad_qlin_low)
    grad_wkey = settle(normed_low, grad_klin_low)
    grad_wvalue = settle(normed_low, grad_vlin_low)
    grad_normed = (
        grad_normed
        + matmul_nt(grad_qlin_low, full_query)
        + matmul_nt(grad_klin_low, full_key)
        + matmul_nt(grad_vlin_low, full_value)
    )
    grad_in_second, grad_gin = norm_back(grad_normed)
    grad_tokens = grad_in_first + grad_in_second
    sum_gin, sum_gquery, sum_gkey, sum_gpost, sum_glaurel, sum_gffin, sum_gffout, sum_gple = (
        lax.psum(
            (
                grad_gin,
                grad_gquery,
                grad_gkey,
                grad_gpost,
                grad_glaurel,
                grad_gffin,
                grad_gffout,
                grad_gple,
            ),
            ("ctx", "fsdp"),
        )
    )
    wide_rows = attn_in_gain.shape[0]
    head_rows = query_gain.shape[0]
    wide_start = lax.axis_index("fsdp") * wide_rows
    head_start = lax.axis_index("fsdp") * head_rows

    def wide_part(full_vec):
        return lax.dynamic_slice_in_dim(full_vec, wide_start, wide_rows, 0)

    def head_part(full_vec):
        return lax.dynamic_slice_in_dim(full_vec, head_start, head_rows, 0)

    return (
        out_full.astype(bfloat),
        grad_tokens,
        grad_pleinput,
        grad_wquery,
        grad_wkey,
        grad_wvalue,
        grad_wout,
        grad_wleft,
        grad_wright,
        grad_wgate,
        grad_wup,
        grad_wdown,
        grad_pgate,
        grad_pproj,
        wide_part(sum_gin),
        head_part(sum_gquery),
        head_part(sum_gkey),
        wide_part(sum_gpost),
        wide_part(sum_glaurel),
        wide_part(sum_gffin),
        wide_part(sum_gffout),
        wide_part(sum_gple),
    )

class Plane:
    def locate(self, columns, rows):
        self.columns = columns
        at = lax.axis_index("ctx")
        self.at_x, self.at_y = at % 2, at // 2
        self.beside = (at + 1 - 2 * (at % 2), (at + 2) % 4)
        self.me = lax.axis_index("fsdp")
        self.members = lax.axis_size("fsdp")
        self.half = rows // 2
        self.quarter = rows // 4
        self.eighth = rows // 8

    def rows(self, ref, start, size):
        start = pl.multiple_of(start, size)
        return ref.at[:, pl.ds(start, size)] if self.columns else ref.at[pl.ds(start, size)]

    def sides(self, half):
        return (self.at_x, self.at_y) if half == 0 else (self.at_y, self.at_x)

    def kept_start(self, half):
        return half * self.half + self.sides(half)[0] * self.quarter

    def given_start(self, half):
        return half * self.half + (1 - self.sides(half)[0]) * self.quarter

    def own_start(self, half):
        return self.kept_start(half) + self.sides(half)[1] * self.eighth

    def copy(self, src, dst, send_sem, recv_sem, half, stage):
        return pltpu.make_async_remote_copy(
            src_ref=src,
            dst_ref=dst,
            send_sem=send_sem.at[half, stage],
            recv_sem=recv_sem.at[half, stage],
            device_id={"ctx": self.beside[(half + stage) % 2]},
            device_id_type=pl.DeviceIdType.MESH,
        )


class Summed(Plane):
    def __init__(self, source, refs, columns):
        self.source = source
        self.kept, self.taken, self.last, self.load_sem, self.sum_send, self.sum_recv = refs
        self.locate(columns, source.shape[-2])

    def load(self, half):
        return pltpu.make_async_copy(
            self.rows(self.source, self.kept_start(half), self.quarter),
            self.kept.at[half],
            self.load_sem.at[half],
        )

    def first(self, half):
        return self.copy(
            self.rows(self.source, self.given_start(half), self.quarter),
            self.taken.at[half],
            self.sum_send,
            self.sum_recv,
            half,
            0,
        )

    def second(self, half):
        other = (1 - self.sides(half)[1]) * self.eighth
        return self.copy(
            self.rows(self.kept.at[half], other, self.eighth),
            self.last.at[half],
            self.sum_send,
            self.sum_recv,
            half,
            1,
        )

    def begin(self):
        for half in (0, 1):
            self.first(half).start()
            self.load(half).start()

    def add(self, half, start, more, more_start):
        step = min(32, self.eighth)
        blocks = self.eighth // step
        layers = self.source.shape[0] if self.columns else 1

        @pl.loop(0, layers * blocks)
        def _(at):
            layer, block = at // blocks, at % blocks
            here = pl.ds(pl.multiple_of(start + block * step, step), step)
            there = pl.ds(pl.multiple_of(more_start + block * step, step), step)
            if self.columns:
                self.kept[half, layer, here] += more[half, layer, there]
            else:
                self.kept[half, here] += more[half, there]

    def middle(self):
        for half in (0, 1):
            self.load(half).wait()
            self.first(half).wait_recv()
            side = self.sides(half)[1]
            other = (1 - side) * self.eighth
            self.add(half, other, self.taken, other)
            self.second(half).start()
            mine = side * self.eighth
            self.add(half, mine, self.taken, mine)

    def finish(self):
        for half in (0, 1):
            self.second(half).wait_recv()
            self.add(half, self.sides(half)[1] * self.eighth, self.last, 0)

    def own_rows(self, half):
        return self.rows(self.kept.at[half], self.sides(half)[1] * self.eighth, self.eighth)

    def held(self, half, member):
        side = self.sides(half)[1] * self.eighth
        return self.kept.at[half, member, pl.ds(pl.multiple_of(side, self.eighth), self.eighth)]

    def sum_sent(self):
        for half in (0, 1):
            self.first(half).wait_send()
            self.second(half).wait_send()


class Held:
    def __init__(self, kept, side=0, sides=1):
        self.kept = kept
        width = kept.shape[-1] // sides
        self.cols = pl.ds(side * width, width)

    def own_rows(self, half):
        return self.kept.at[half]

    def held(self, half, member):
        return self.kept.at[half, member, :, self.cols]


class Spread(Plane):
    def __init__(self, source, refs, columns):
        self.own_rows, self.held = source.own_rows, source.held
        self.final, self.spread_send, self.spread_recv, self.place_sem = refs[:4]
        if columns:
            self.swap_send, self.swap_recv = refs[4:]
        self.locate(columns, self.final.shape[-2])

    def place(self, half):
        return pltpu.make_async_copy(
            self.own_rows(half),
            self.rows(self.final, self.own_start(half), self.eighth),
            self.place_sem.at[half],
        )

    def place_all(self):
        for half in (0, 1):
            self.place(half).start()
        for half in (0, 1):
            self.place(half).wait()

    def swap_place(self, half, member):
        start = pl.multiple_of(self.own_start(half), self.eighth)
        return self.final.at[member, pl.ds(start, self.eighth)]

    def swap_copy(self, half, hop, src_member):
        target = lax.rem(self.me + hop, self.members)
        return remote(
            self.held(half, target),
            self.swap_place(half, src_member),
            self.swap_send.at[hop, half],
            self.swap_recv.at[hop, half],
            target,
        )

    def swap_local(self, half):
        return pltpu.make_async_copy(
            self.held(half, self.me),
            self.swap_place(half, self.me),
            self.place_sem.at[half],
        )

    def swap_begin(self):
        for half in (0, 1):
            for hop in range(1, self.members):
                self.swap_copy(half, hop, self.me).start()
            self.swap_local(half).start()

    def swap_end(self):
        for half in (0, 1):
            for hop in range(1, self.members):
                source = lax.rem(self.me + self.members - hop, self.members)
                self.swap_copy(half, hop, source).wait_recv()
            self.swap_local(half).wait()

    def spread_copy(self, half, stage):
        if stage == 0:
            rows = self.rows(self.final, self.own_start(half), self.eighth)
        else:
            rows = self.rows(self.final, self.kept_start(half), self.quarter)
        return self.copy(rows, rows, self.spread_send, self.spread_recv, half, 1 - stage)

    def spread_wait(self, half, stage):
        side = self.sides(half)[1]
        if stage == 0:
            start = self.kept_start(half) + (1 - side) * self.eighth
            rows = self.rows(self.final, start, self.eighth)
        else:
            rows = self.rows(self.final, self.given_start(half), self.quarter)
        self.copy(rows, rows, self.spread_send, self.spread_recv, half, 1 - stage).wait_recv()

    def spread_begin(self):
        for half in (0, 1):
            self.spread_copy(half, 0).start()

    def spread_on(self):
        for half in (0, 1):
            self.spread_wait(half, 0)
            self.spread_copy(half, 1).start()

    def spread_end(self):
        for half in (0, 1):
            self.spread_wait(half, 1)

    def spread_sent(self):
        for half in (0, 1):
            self.spread_copy(half, 0).wait_send()
            self.spread_copy(half, 1).wait_send()
            if self.columns:
                for hop in range(1, self.members):
                    self.swap_copy(half, hop, self.me).wait_send()


class GroupSpread(Spread):
    def __init__(self, source, refs):
        self.landing = refs[0]
        super().__init__(source, refs[1:], True)

    def swap_place(self, half, member):
        return self.landing.at[half, member]

    def swap_end(self):
        super().swap_end()
        groups = self.final.shape[0]
        size = self.landing.shape[1] // groups
        for half in (0, 1):
            rows = pl.ds(pl.multiple_of(self.own_start(half), self.eighth), self.eighth)
            for group in range(groups):
                total = self.landing[half, group * size].astype(jnp.float32)
                for member in range(group * size + 1, (group + 1) * size):
                    total = total + self.landing[half, member].astype(jnp.float32)
                self.final[group, rows] = total.astype(jnp.bfloat16)


def sum_scratch(shape):
    dma = pltpu.SemaphoreType.DMA
    rows, width = shape[-2:]

    def buffer(count):
        return pltpu.VMEM((2,) + shape[:-2] + (count, width), jnp.bfloat16)

    buffers = [buffer(rows // 4), buffer(rows // 4), buffer(rows // 8)]
    return buffers + [dma((2,)), dma((2, 2)), dma((2, 2))]


SUM_REFS = 6


def spread_scratch(shape, members=None):
    dma = pltpu.SemaphoreType.DMA
    scratch = [pltpu.VMEM(shape, jnp.bfloat16), dma((2, 2)), dma((2, 2)), dma((2,))]
    if len(shape) == 3:
        count = members or shape[0]
        scratch += [dma((count, 2)), dma((count, 2))]
    return scratch


def spread_refs(columns):
    return 6 if columns else 4


def gradient_sum_kernel(plan, *refs):
    refs = list(refs)
    count = len(plan)
    sources = refs[:count]
    results_count = sum(max(1, one.sides) for one in plan)
    results = refs[count : count + results_count]
    scratch = refs[count + results_count :]
    store_sem = scratch.pop()

    def take(size):
        taken = scratch[:size]
        del scratch[:size]
        return taken

    sums, spreads, late = [], [], []
    for source, one in zip(sources, plan):
        if one.summed:
            held = Held(source, *one.part)
        else:
            held = Summed(source, take(SUM_REFS), one.columns)
            sums.append(held)
        size = spread_refs(one.columns)
        if one.groups:
            spreads.append(GroupSpread(held, take(size + 1)))
        else:
            spreads.append(Spread(held, take(size), one.columns))
        if not one.summed:
            late.append(spreads[-1])
    early = [spread for spread in spreads if spread not in late]
    greet_all()

    def stores(at):
        final, sides = spreads[at].final, plan[at].sides
        first = sum(max(1, one.sides) for one in plan[:at])
        if sides == 0:
            return [pltpu.make_async_copy(final, results[first], store_sem.at[at, 0, 0])]
        part = final.shape[2] // sides
        return [
            pltpu.make_async_copy(
                final.at[member, :, pl.ds(side * part, part)],
                results[first + side].at[:, pl.ds(member * part, part)],
                store_sem.at[at, side, member],
            )
            for member in range(final.shape[0])
            for side in range(sides)
        ]

    def launch(spread):
        if spread.columns:
            spread.swap_begin()
        else:
            spread.place_all()
            spread.spread_begin()

    for share in sums:
        share.begin()
    for spread in early:
        launch(spread)
    for share in sums:
        share.middle()
    for spread in early[:1]:
        spread.swap_end()
        spread.spread_begin()
    for share, spread in zip(sums, late):
        share.finish()
        launch(spread)
    for spread in early[:1]:
        spread.spread_on()
    for spread in early[1:]:
        spread.swap_end()
        spread.spread_begin()
    for spread in late:
        if spread.columns:
            spread.swap_end()
            spread.spread_begin()
        else:
            spread.spread_on()
    for spread in early[1:]:
        spread.spread_on()
    for spread in late:
        if spread.columns:
            spread.spread_on()
    for at in sorted(range(count), key=lambda one: spreads[one] in early):
        spreads[at].spread_end()
        for store in stores(at):
            store.start()
    for share in sums:
        share.sum_sent()
    for spread in spreads:
        spread.spread_sent()
    for at in range(count):
        for store in stores(at):
            store.wait()


@dataclasses.dataclass
class Source:
    array: jax.Array
    summed: bool = False
    part: tuple = (0, 1)
    groups: int = 0
    sides: int = 0

    @property
    def columns(self):
        return self.array.ndim - self.summed == 3

    @property
    def shape(self):
        shape = self.array.shape
        if self.summed:
            shape = shape[1:-2] + (8 * shape[-2], shape[-1] // self.part[1])
        return shape


def gradient_sum(sources):
    members = lax.axis_size("fsdp")
    anywhere = pl.BlockSpec(memory_space=pl.ANY)
    scratch, results = [], []
    for one in sources:
        shape = one.shape
        if not one.summed:
            scratch += sum_scratch(shape)
        if one.groups:
            landing = (2, members, shape[1] // 8, shape[2])
            scratch.append(pltpu.VMEM(landing, jnp.bfloat16))
            shape = (one.groups,) + shape[1:]
        scratch += spread_scratch(shape, members)
        if one.sides == 0:
            results.append(shape)
        else:
            results += [(shape[1], shape[0] * shape[2] // one.sides)] * one.sides
    return pl.pallas_call(
        functools.partial(gradient_sum_kernel, sources),
        out_shape=[jax.ShapeDtypeStruct(shape, jnp.bfloat16) for shape in results],
        in_specs=[anywhere] * len(sources),
        out_specs=[anywhere] * len(results),
        scratch_shapes=scratch + [pltpu.SemaphoreType.DMA((len(sources), 2, members))],
        compiler_params=pltpu.CompilerParams(
            collective_id=3, has_side_effects=True, vmem_limit_bytes=KERNEL_VMEM
        ),
        cost_estimate=pl.CostEstimate(flops=0, bytes_accessed=300 << 20, transcendentals=0),
        name="gradient_sum",
    )(*(one.array for one in sources))

def remote(src, dst, send_sem, recv_sem, place):
    return pltpu.make_async_remote_copy(
        src_ref=src,
        dst_ref=dst,
        send_sem=send_sem,
        recv_sem=recv_sem,
        device_id={"fsdp": place},
        device_id_type=pl.DeviceIdType.MESH,
    )


def dot_nn(left_mat, right_mat):
    return jnp.dot(left_mat, right_mat, preferred_element_type=jnp.float32)


def dot_nt(left_mat, right_mat):
    return lax.dot_general(
        left_mat, right_mat, (((1,), (1,)), ((), ())), preferred_element_type=jnp.float32
    )


def dot_tn(left_mat, right_mat):
    return lax.dot_general(
        left_mat, right_mat, (((0,), (0,)), ((), ())), preferred_element_type=jnp.float32
    )


def greet_all():
    sem = pltpu.get_barrier_semaphore()
    members, planes = lax.axis_size("fsdp"), lax.axis_size("ctx")
    mesh_id = pl.DeviceIdType.MESH
    for hop in range(1, planes):
        other = lax.rem(lax.axis_index("ctx") + hop, planes)
        pl.semaphore_signal(sem, inc=1, device_id={"ctx": other}, device_id_type=mesh_id)
    for hop in range(1, members):
        other = lax.rem(lax.axis_index("fsdp") + hop, members)
        pl.semaphore_signal(sem, inc=1, device_id={"fsdp": other}, device_id_type=mesh_id)
    pl.semaphore_wait(sem, members + planes - 2)


PIECES = 4


def line_scratch(chips, tok_count, width):
    dma = pltpu.SemaphoreType.DMA
    shard = (tok_count, width)
    return [
        pltpu.VMEM((chips, 2) + shard, jnp.bfloat16),
        dma((chips, 2)),
        dma((chips, 3)),
        dma,
        pltpu.VMEM((chips, 2) + shard, jnp.bfloat16),
        pltpu.VMEM((chips,) + shard, jnp.bfloat16),
        pltpu.VMEM((chips,) + shard, jnp.bfloat16),
        pltpu.VMEM((chips,) + shard, jnp.bfloat16),
        dma((chips,)),
        dma((chips,)),
        dma((chips, PIECES)),
        dma((chips, PIECES)),
        dma((chips, PIECES)),
    ]


LINE_REFS = 13


class Line:
    def __init__(self, chips, refs):
        (
            self.slots,
            self.slot_recv,
            self.slot_send,
            self.own_sem,
            self.parts,
            self.from_core,
            self.from_left,
            self.from_right,
            self.core_send,
            self.core_recv,
            self.flow_send,
            self.left_recv,
            self.right_recv,
        ) = refs
        self.chips = chips
        me = lax.axis_index("fsdp")
        self.chip = me // 2
        self.core = me % 2
        self.tok = self.slots.shape[2]
        self.piece = self.tok // PIECES

    def place(self, chip, core):
        return chip * 2 + core

    def order(self, step):
        picked = 0
        for chip in range(self.chips):
            near = sorted(range(self.chips), key=lambda other: (abs(other - chip), other))
            picked = picked + jnp.where(self.chip == chip, near[step], 0)
        return picked

    def barrier(self):
        sem = pltpu.get_barrier_semaphore()

        def greet(place):
            pl.semaphore_signal(
                sem, inc=1, device_id={"fsdp": place}, device_id_type=pl.DeviceIdType.MESH
            )

        greet(self.place(self.chip, 1 - self.core))

        @pl.when(self.chip > 0)
        def _():
            greet(self.place(self.chip - 1, self.core))

        @pl.when(self.chip < self.chips - 1)
        def _():
            greet(self.place(self.chip + 1, self.core))

        ends = jnp.where(self.chip == 0, 1, 0) + jnp.where(self.chip == self.chips - 1, 1, 0)
        pl.semaphore_wait(sem, 3 - ends)

    def slot_copy(self, src, chip, way):
        place = (
            self.place(self.chip + 1, self.core),
            self.place(self.chip - 1, self.core),
            self.place(self.chip, 1 - self.core),
        )[way]
        return remote(
            src,
            self.slots.at[chip, self.core],
            self.slot_send.at[chip, way],
            self.slot_recv.at[chip, self.core],
            place,
        )

    def own_copy(self, own_ref):
        return pltpu.make_async_copy(own_ref, self.slots.at[self.chip, self.core], self.own_sem)

    def gather_begin(self, own_ref):
        @pl.when(self.chip < self.chips - 1)
        def _():
            self.slot_copy(own_ref, self.chip, 0).start()

        @pl.when(self.chip > 0)
        def _():
            self.slot_copy(own_ref, self.chip, 1).start()

        self.slot_copy(own_ref, self.chip, 2).start()
        self.own_copy(own_ref).start()

    def gather_step(self, distance):
        for chip, there, way, onward in (
            (self.chip - distance, self.chip >= distance, 0, self.chip < self.chips - 1),
            (self.chip + distance, self.chip + distance < self.chips, 1, self.chip > 0),
        ):

            @pl.when(there)
            def _(chip=chip, way=way, onward=onward):
                src = self.slots.at[chip, self.core]
                self.slot_copy(src, chip, way).wait_recv()

                @pl.when(onward)
                def _():
                    self.slot_copy(src, chip, way).start()

                self.slot_copy(src, chip, 2).start()

    def gather_other(self, chip):
        dst = self.slots.at[chip, 1 - self.core]
        remote(
            dst,
            dst,
            self.slot_send.at[chip, 2],
            self.slot_recv.at[chip, 1 - self.core],
            self.place(self.chip, 1 - self.core),
        ).wait_recv()

    def gather_end(self):
        for chip in range(self.chips):
            src = self.slots.at[chip, self.core]

            @pl.when((self.chip >= chip) & (self.chip < self.chips - 1))
            def _(src=src, chip=chip):
                self.slot_copy(src, chip, 0).wait_send()

            @pl.when((self.chip <= chip) & (self.chip > 0))
            def _(src=src, chip=chip):
                self.slot_copy(src, chip, 1).wait_send()

            self.slot_copy(src, chip, 2).wait_send()

    def core_copy(self, chip):
        return remote(
            self.parts.at[chip, 1 - self.core],
            self.from_core.at[chip],
            self.core_send.at[chip],
            self.core_recv.at[chip],
            self.place(self.chip, 1 - self.core),
        )

    def flow_copy(self, chip, piece, right):
        rows = pl.ds(piece * self.piece, self.piece)
        return remote(
            self.parts.at[chip, self.core, rows],
            (self.from_left if right else self.from_right).at[chip, rows],
            self.flow_send.at[chip, piece],
            (self.left_recv if right else self.right_recv).at[chip, piece],
            self.place(self.chip + (1 if right else -1), self.core),
        )

    def flow(self, chip, right, incoming):
        self.core_copy(chip).wait_recv()

        @pl.loop(0, PIECES)
        def _(piece):
            rows = pl.ds(pl.multiple_of(piece * self.piece, self.piece), self.piece)
            total = self.parts[chip, self.core, rows].astype(jnp.float32)
            total = total + self.from_core[chip, rows].astype(jnp.float32)
            if incoming:
                self.flow_copy(chip, piece, right).wait_recv()
                source = self.from_left if right else self.from_right
                total = total + source[chip, rows].astype(jnp.float32)
            self.parts[chip, self.core, rows] = total.astype(jnp.bfloat16)
            self.flow_copy(chip, piece, right).start()

    def scatter_first(self, chip):
        @pl.when((self.chip == 0) & (chip > 0))
        def _():
            self.flow(chip, True, False)

        @pl.when((self.chip == self.chips - 1) & (chip < self.chips - 1))
        def _():
            self.flow(chip, False, False)

    def scatter_rest(self, result_ref, between=None):
        for rank in range(3, 2 * self.chips - 2):
            right = rank - self.chip

            @pl.when((self.chip > 0) & (right > self.chip) & (right < self.chips))
            def _(right=right):
                self.flow(right, True, True)

            left = 2 * (self.chips - 1) - self.chip - rank

            @pl.when((self.chip < self.chips - 1) & (left < self.chip) & (left >= 0))
            def _(left=left):
                self.flow(left, False, True)

            if between is not None:
                between(rank)

        own = self.chip
        self.core_copy(own).wait_recv()

        @pl.loop(0, PIECES)
        def _(piece):
            rows = pl.ds(pl.multiple_of(piece * self.piece, self.piece), self.piece)
            total = self.parts[own, self.core, rows].astype(jnp.float32)
            total = total + self.from_core[own, rows].astype(jnp.float32)
            result_ref[rows] = total

        @pl.when(own > 0)
        def _():
            @pl.loop(0, PIECES)
            def _(piece):
                rows = pl.ds(pl.multiple_of(piece * self.piece, self.piece), self.piece)
                self.flow_copy(own, piece, True).wait_recv()
                result_ref[rows] += self.from_left[own, rows].astype(jnp.float32)

        @pl.when(own < self.chips - 1)
        def _():
            @pl.loop(0, PIECES)
            def _(piece):
                rows = pl.ds(pl.multiple_of(piece * self.piece, self.piece), self.piece)
                self.flow_copy(own, piece, False).wait_recv()
                result_ref[rows] += self.from_right[own, rows].astype(jnp.float32)

        for chip in range(self.chips):
            self.core_copy(chip).wait_send()

            @pl.when(self.chip != chip)
            def _(chip=chip):
                for piece in range(PIECES):
                    self.flow_copy(chip, piece, True).wait_send()


def ffn_forward_kernel(
    chips,
    own_ref,
    gateup_hbm,
    down_hbm,
    result_ref,
    all_hbm,
    hidden_hbm,
    act_hbm,
    slope_hbm,
    *scratch,
):
    line = Line(chips, scratch[:LINE_REFS])
    gateup, down, hidden, act, slope, load_sems, store_sems = scratch[LINE_REFS:]
    ff_part = down.shape[0]
    width = down.shape[1]
    pair = 2 * line.tok
    load_gateup = pltpu.make_async_copy(gateup_hbm, gateup, load_sems.at[0])
    load_down = pltpu.make_async_copy(down_hbm, down, load_sems.at[1])
    load_gateup.start()
    load_down.start()
    line.barrier()
    line.gather_begin(own_ref)
    line.own_copy(own_ref).wait()

    def stores(chip):
        rows = pl.ds(pl.multiple_of(chip * pair, pair), pair)
        return [
            pltpu.make_async_copy(line.slots.at[chip], all_hbm.at[chip], store_sems.at[chip, 0]),
            pltpu.make_async_copy(hidden.at[rows], hidden_hbm.at[rows], store_sems.at[chip, 1]),
            pltpu.make_async_copy(act.at[rows], act_hbm.at[rows], store_sems.at[chip, 2]),
            pltpu.make_async_copy(slope.at[rows], slope_hbm.at[rows], store_sems.at[chip, 3]),
        ]

    tile = 256
    for step in range(chips):
        if step > 0:
            line.gather_step(step)
        chip = line.order(step)
        line.gather_other(chip)
        if step == 0:
            load_gateup.wait()
            load_down.wait()
        rows = pl.ds(pl.multiple_of(chip * pair, pair), pair)

        @pl.loop(0, ff_part // tile)
        def _(at, chip=chip, rows=rows):
            inputs = line.slots[chip].reshape(pair, width)
            gate_cols = pl.ds(pl.multiple_of(at * tile, tile), tile)
            up_cols = pl.ds(pl.multiple_of(ff_part + at * tile, tile), tile)
            gate = dot_nn(inputs, gateup[:, gate_cols])
            up = dot_nn(inputs, gateup[:, up_cols])
            square = gate * gate
            bent = jnp.tanh(GELU_ROOT * gate * (1.0 + GELU_CUBE * square))
            half = 0.5 + 0.5 * bent
            activated = gate * half
            rise = half + 0.5 * gate * (1.0 - bent * bent) * (
                GELU_ROOT * (1.0 + 3.0 * GELU_CUBE * square)
            )
            hidden[rows, gate_cols] = (activated * up).astype(jnp.bfloat16)
            act[rows, gate_cols] = activated.astype(jnp.bfloat16)
            slope[rows, gate_cols] = (rise * up).astype(jnp.bfloat16)

        for copy in stores(chip):
            copy.start()

        wide = 512

        @pl.loop(0, width // wide)
        def _(at, chip=chip, rows=rows):
            cols = pl.ds(pl.multiple_of(at * wide, wide), wide)
            sums = dot_nn(hidden[rows, :], down[:, cols]).astype(jnp.bfloat16)
            line.parts[chip, :, :, cols] = sums.reshape(2, line.tok, wide)

        line.core_copy(chip).start()
        if step > 0:
            line.scatter_first(line.order(step - 1))
    line.scatter_first(line.order(chips - 1))
    line.scatter_rest(result_ref)
    line.gather_end()
    for chip in range(chips):
        for copy in stores(chip):
            copy.wait()


def ffn_forward(own, gateup, down, chips):
    tok_count, width = own.shape
    ff_part = down.shape[0]
    block = 2 * chips * tok_count
    bfloat = jnp.bfloat16
    anywhere = pl.BlockSpec(memory_space=pl.ANY)
    vmem = pl.BlockSpec(memory_space=pltpu.VMEM)
    part = jax.ShapeDtypeStruct((block, ff_part), bfloat)
    result, gathered, hidden, act, slope = pl.pallas_call(
        functools.partial(ffn_forward_kernel, chips),
        out_shape=[
            jax.ShapeDtypeStruct((tok_count, width), jnp.float32),
            jax.ShapeDtypeStruct((chips, 2, tok_count, width), bfloat),
            part,
            part,
            part,
        ],
        in_specs=[vmem, anywhere, anywhere],
        out_specs=[vmem, anywhere, anywhere, anywhere, anywhere],
        scratch_shapes=line_scratch(chips, tok_count, width)
        + [
            pltpu.VMEM(gateup.shape, bfloat),
            pltpu.VMEM(down.shape, bfloat),
            pltpu.VMEM((block, ff_part), bfloat),
            pltpu.VMEM((block, ff_part), bfloat),
            pltpu.VMEM((block, ff_part), bfloat),
            pltpu.SemaphoreType.DMA((2,)),
            pltpu.SemaphoreType.DMA((chips, 4)),
        ],
        compiler_params=pltpu.CompilerParams(
            collective_id=1, has_side_effects=True, vmem_limit_bytes=KERNEL_VMEM
        ),
        cost_estimate=pl.CostEstimate(
            flops=6 * block * width * ff_part,
            bytes_accessed=40 << 20,
            transcendentals=block * ff_part,
        ),
        name="ffn_forward",
    )(own, gateup, down)
    return result, gathered.reshape(block, width), hidden, act, slope


def ffn_backward_kernel(
    chips,
    own_ref,
    gateup_hbm,
    down_hbm,
    hidden_hbm,
    act_hbm,
    slope_hbm,
    inputs_hbm,
    pgate_hbm,
    pproj_hbm,
    result_ref,
    part_hbm,
    down_kept,
    pgate_kept,
    pproj_kept,
    *scratch,
):
    line = Line(chips, scratch[:LINE_REFS])
    scratch = scratch[LINE_REFS:]
    gateup, down, hidden, act, slope, inputs, grad, part_down, staged = scratch[:9]
    load_sems, store_sems, kept_sems = scratch[9:12]
    share = Summed(part_down, scratch[12 : 12 + SUM_REFS], False)
    small = [
        Summed(pgate_hbm, scratch[12 + SUM_REFS : 12 + 2 * SUM_REFS], True),
        Summed(pproj_hbm, scratch[12 + 2 * SUM_REFS :], True),
    ]
    ff_part = down.shape[0]
    width = down.shape[1]
    pair = 2 * line.tok
    loads = [
        pltpu.make_async_copy(src, dst, load_sems.at[at])
        for at, (src, dst) in enumerate(
            (
                (down_hbm, down),
                (act_hbm, act),
                (slope_hbm, slope),
                (gateup_hbm, gateup),
                (hidden_hbm, hidden),
                (inputs_hbm, inputs),
            )
        )
    ]
    for load in loads:
        load.start()
    greet_all()
    line.gather_begin(own_ref)
    for one in small:
        one.begin()
    line.own_copy(own_ref).wait()

    tile = 256
    wide = 512
    for step in range(chips):
        if step > 0:
            line.gather_step(step)
        chip = line.order(step)
        line.gather_other(chip)
        if step == 0:
            for load in loads[:4]:
                load.wait()
        rows = pl.ds(pl.multiple_of(chip * pair, pair), pair)

        @pl.loop(0, ff_part // tile)
        def _(at, chip=chip, rows=rows):
            grads = line.slots[chip].reshape(pair, width)
            gate_cols = pl.ds(pl.multiple_of(at * tile, tile), tile)
            up_cols = pl.ds(pl.multiple_of(ff_part + at * tile, tile), tile)
            grad_hidden = dot_nt(grads, down[gate_cols, :])
            grad[rows, gate_cols] = (
                grad_hidden * slope[rows, gate_cols].astype(jnp.float32)
            ).astype(jnp.bfloat16)
            grad[rows, up_cols] = (grad_hidden * act[rows, gate_cols].astype(jnp.float32)).astype(
                jnp.bfloat16
            )

        @pl.loop(0, width // wide)
        def _(at, chip=chip, rows=rows):
            cols = pl.ds(pl.multiple_of(at * wide, wide), wide)
            sums = dot_nt(grad[rows, :], gateup[cols, :]).astype(jnp.bfloat16)
            line.parts[chip, :, :, cols] = sums.reshape(2, line.tok, wide)

        line.core_copy(chip).start()
        if step > 0:
            line.scatter_first(line.order(step - 1))
    line.scatter_first(line.order(chips - 1))
    for one in small:
        one.middle()
    for load in loads[4:]:
        load.wait()

    block = chips * pair

    def down_grads():
        @pl.loop(0, ff_part // tile)
        def _(at):
            rows = pl.ds(pl.multiple_of(at * tile, tile), tile)
            left = hidden[:, rows]
            for start in range(0, width, wide):
                right = line.slots[:, :, :, start : start + wide].reshape(block, wide)
                part_down[rows, start : start + wide] = dot_tn(left, right).astype(jnp.bfloat16)

    def part_store(at):
        slot = at % 2
        return pltpu.make_async_copy(
            staged.at[slot], part_hbm.at[at], store_sems.at[slot]
        )

    def gateup_grads(first, last):
        @pl.loop(first, last)
        def _(at):
            cols = pl.ds(pl.multiple_of(at * tile, tile), tile)

            @pl.when(at >= 2)
            def _():
                part_store(at - 2).wait()

            left = inputs[:, cols]
            for start in range(0, 2 * ff_part, wide):
                staged[at % 2, :, start : start + wide] = dot_tn(
                    left, grad[:, start : start + wide]
                ).astype(jnp.bfloat16)
            part_store(at).start()

    tiles = width // tile
    done = [0]

    def between(rank):
        if rank == 3:
            down_grads()
            share.begin()
            for one in small:
                one.finish()
        else:
            upto = min(tiles, done[0] + 2)
            gateup_grads(done[0], upto)
            done[0] = upto

    line.scatter_rest(result_ref, between)
    share.middle()
    gateup_grads(done[0], tiles)
    share.finish()
    stores = [
        pltpu.make_async_copy(one.own_rows(half), kept.at[half], kept_sems.at[at, half])
        for at, (one, kept) in enumerate(
            ((share, down_kept), (small[0], pgate_kept), (small[1], pproj_kept))
        )
        for half in (0, 1)
    ]
    for store in stores:
        store.start()
    line.gather_end()
    for one in [share] + small:
        one.sum_sent()
    for at in (tiles - 2, tiles - 1):
        part_store(at).wait()
    for store in stores:
        store.wait()


def ffn_backward(own, gateup, down, hidden, act, slope, inputs, pgate, pproj, chips):
    tok_count, width = own.shape
    ff_part = down.shape[0]
    block = 2 * chips * tok_count
    bfloat = jnp.bfloat16
    anywhere = pl.BlockSpec(memory_space=pl.ANY)
    vmem = pl.BlockSpec(memory_space=pltpu.VMEM)
    dma = pltpu.SemaphoreType.DMA
    tile = 256
    held = (gateup, down, hidden, act, slope, inputs)
    return pl.pallas_call(
        functools.partial(ffn_backward_kernel, chips),
        out_shape=[
            jax.ShapeDtypeStruct((tok_count, width), jnp.float32),
            jax.ShapeDtypeStruct((width // tile, tile, 2 * ff_part), bfloat),
            jax.ShapeDtypeStruct((2, ff_part // 8, width), bfloat),
        ]
        + [
            jax.ShapeDtypeStruct((2, one.shape[0], one.shape[1] // 8, one.shape[2]), bfloat)
            for one in (pgate, pproj)
        ],
        in_specs=[vmem] + [anywhere] * 8,
        out_specs=[vmem] + [anywhere] * 4,
        scratch_shapes=line_scratch(chips, tok_count, width)
        + [pltpu.VMEM(one.shape, bfloat) for one in held]
        + [
            pltpu.VMEM((block, 2 * ff_part), bfloat),
            pltpu.VMEM(down.shape, bfloat),
            pltpu.VMEM((2, tile, 2 * ff_part), bfloat),
            dma((6,)),
            dma((2,)),
            dma((3, 2)),
        ]
        + sum_scratch(down.shape)
        + sum_scratch(pgate.shape)
        + sum_scratch(pproj.shape),
        compiler_params=pltpu.CompilerParams(
            collective_id=2, has_side_effects=True, vmem_limit_bytes=KERNEL_VMEM
        ),
        cost_estimate=pl.CostEstimate(
            flops=12 * block * width * ff_part, bytes_accessed=40 << 20, transcendentals=0
        ),
        name="ffn_backward",
    )(own, *held, pgate, pproj)

def rope_norm(lin, gain, cosine, sine_part):
    scale = lax.rsqrt(jnp.mean(lin * lin, axis=-1, keepdims=True) + EPSILON)
    scaled = lin * scale * gain
    first, second = scaled[:, : HD // 2], scaled[:, HD // 2 :]
    return jnp.concatenate(
        [first * cosine - second * sine_part, second * cosine + first * sine_part], axis=-1
    )


def attention_forward_kernel(
    chips,
    own_ref,
    qkv_own,
    gate_own,
    up_own,
    out_hbm,
    cos_ref,
    sin_ref,
    gain_query_ref,
    gain_key_ref,
    query_docs_ref,
    key_docs_ref,
    result_ref,
    all_hbm,
    qkv_hbm,
    gateup_hbm,
    lin_hbm,
    query_hbm,
    span_hbm,
    probs_hbm,
    attended_hbm,
    *scratch,
):
    scratch = list(scratch)
    line = Line(chips, scratch[:LINE_REFS])
    del scratch[:LINE_REFS]
    spreads = []
    for kept in (qkv_own, gate_own, up_own):
        spreads.append(Spread(Held(kept), scratch[: spread_refs(True)], True))
        del scratch[: spread_refs(True)]
    qkv, gate, up = spreads
    out, lin, query, span, probs, attended = scratch[:6]
    load_sem, store_sem, span_send, span_recv = scratch[6:]
    width = line.slots.shape[3]
    pair = 2 * line.tok
    block = chips * pair
    ctx_at = lax.axis_index("ctx")
    planes = lax.axis_size("ctx")
    ff_part = gate.final.shape[2]
    bfloat = jnp.bfloat16

    load_out = pltpu.make_async_copy(out_hbm, out, load_sem)
    load_out.start()
    greet_all()
    qkv.swap_begin()
    line.gather_begin(own_ref)
    line.gather_step(1)
    qkv.swap_end()
    qkv.spread_begin()
    line.gather_step(2)
    qkv.spread_on()
    for distance in range(3, chips):
        line.gather_step(distance)
    gate.swap_begin()
    up.swap_begin()
    line.own_copy(own_ref).wait()
    for chip in range(chips):
        line.gather_other(chip)
    qkv.spread_end()
    stores = [
        pltpu.make_async_copy(line.slots, all_hbm, store_sem.at[0]),
        pltpu.make_async_copy(qkv.final, qkv_hbm, store_sem.at[1]),
        pltpu.make_async_copy(lin, lin_hbm, store_sem.at[2]),
        pltpu.make_async_copy(query, query_hbm, store_sem.at[3]),
        pltpu.make_async_copy(span, span_hbm, store_sem.at[4]),
        pltpu.make_async_copy(probs, probs_hbm, store_sem.at[5]),
        pltpu.make_async_copy(attended, attended_hbm, store_sem.at[6]),
        pltpu.make_async_copy(
            gate.final, gateup_hbm.at[:, :, pl.ds(0, ff_part)], store_sem.at[7]
        ),
        pltpu.make_async_copy(
            up.final, gateup_hbm.at[:, :, pl.ds(ff_part, ff_part)], store_sem.at[8]
        ),
    ]
    stores[0].start()
    stores[1].start()

    @pl.loop(0, chips)
    def _(chip):
        rows = pl.ds(pl.multiple_of(chip * pair, pair), pair)
        span_rows = pl.ds(pl.multiple_of(WINDOW + chip * pair, pair), pair)
        inputs = line.slots[chip].reshape(pair, width)
        weights = qkv.final[...].reshape(width, 3 * HD)
        key_lin = dot_nn(inputs, weights[:, HD : 2 * HD])
        lin[rows, HD : 2 * HD] = key_lin
        span[0, span_rows] = rope_norm(
            key_lin, gain_key_ref[...], cos_ref[rows], sin_ref[rows]
        ).astype(bfloat)
        span[1, span_rows] = dot_nn(inputs, weights[:, 2 * HD :]).astype(bfloat)

    part = WINDOW // 2

    def span_copy(start, to_start, way, device):
        return pltpu.make_async_remote_copy(
            src_ref=span.at[:, pl.ds(pl.multiple_of(start, part), part)],
            dst_ref=span.at[:, pl.ds(pl.multiple_of(to_start, part), part)],
            send_sem=span_send.at[way],
            recv_sem=span_recv.at[way],
            device_id=device,
            device_id_type=pl.DeviceIdType.MESH,
        )

    mine = line.core * part
    others = (1 - line.core) * part
    onward = span_copy(block + mine, mine, 0, {"ctx": lax.rem(ctx_at + 1, planes)})
    across = span_copy(mine, mine, 1, {"fsdp": line.place(line.chip, 1 - line.core)})
    arrived = span_copy(others, others, 1, {"fsdp": line.place(line.chip, 1 - line.core)})

    @pl.when(ctx_at < planes - 1)
    def _():
        onward.start()

    @pl.when(ctx_at == 0)
    def _():
        span[:, pl.ds(0, WINDOW)] = jnp.zeros((2, WINDOW, HD), bfloat)

    @pl.loop(0, chips)
    def _(chip):
        rows = pl.ds(pl.multiple_of(chip * pair, pair), pair)
        inputs = line.slots[chip].reshape(pair, width)
        weights = qkv.final[...].reshape(width, 3 * HD)
        query_lin = dot_nn(inputs, weights[:, :HD])
        lin[rows, :HD] = query_lin
        rotated = rope_norm(query_lin, gain_query_ref[...], cos_ref[rows], sin_ref[rows])
        query[rows] = (rotated.astype(bfloat).astype(jnp.float32) * SCORE_SCALE).astype(bfloat)

    @pl.when(ctx_at > 0)
    def _():
        onward.wait_recv()
        across.start()
        arrived.wait_recv()

    for store in stores[2:5]:
        store.start()
    load_out.wait()

    span_len = WINDOW + pair
    for step in range(chips):
        chip = line.order(chips - 1 - step)
        rows = pl.ds(pl.multiple_of(chip * pair, pair), pair)
        span_rows = pl.ds(pl.multiple_of(chip * pair, pair), span_len)
        scores = dot_nt(query[rows], span[0, span_rows])
        distance = (
            WINDOW
            + lax.broadcasted_iota(jnp.int32, (pair, span_len), 0)
            - lax.broadcasted_iota(jnp.int32, (pair, span_len), 1)
        )
        visible = (
            (distance >= 0)
            & (distance < WINDOW)
            & (query_docs_ref[rows] == key_docs_ref[:, span_rows])
        )
        scores = jnp.where(visible, scores, NEGATIVE)
        shifted = jnp.exp(scores - jnp.max(scores, axis=-1, keepdims=True))
        prob = (shifted / jnp.sum(shifted, axis=-1, keepdims=True)).astype(bfloat)
        probs[rows] = prob
        attended[rows] = dot_nn(prob, span[1, span_rows]).astype(bfloat)

        wide = 512

        @pl.loop(0, width // wide)
        def _(at, chip=chip, rows=rows):
            cols = pl.ds(pl.multiple_of(at * wide, wide), wide)
            sums = dot_nn(attended[rows], out[:, cols]).astype(bfloat)
            line.parts[chip, :, :, cols] = sums.reshape(2, line.tok, wide)

        line.core_copy(chip).start()
        if step > 0:
            line.scatter_first(line.order(chips - step))
        if step == 1:
            gate.swap_end()
            gate.spread_begin()
    line.scatter_first(line.order(0))
    for store in stores[5:7]:
        store.start()
    gate.spread_on()
    up.swap_end()
    up.spread_begin()
    line.scatter_rest(result_ref)
    up.spread_on()
    gate.spread_end()
    stores[7].start()
    up.spread_end()
    stores[8].start()
    line.gather_end()
    for spread in spreads:
        spread.spread_sent()

    @pl.when(ctx_at < planes - 1)
    def _():
        onward.wait_send()

    @pl.when(ctx_at > 0)
    def _():
        across.wait_send()

    for store in stores:
        store.wait()


def attention_forward(
    own, qkv_own, gate_own, up_own, out, cosine, sine_part, gain_query, gain_key, query_docs, key_docs
):
    tok_count, width = own.shape
    members = qkv_own.shape[1]
    chips = members // 2
    block = members * tok_count
    span_len = WINDOW + block
    rows = 8 * qkv_own.shape[2]
    ff_part = gate_own.shape[3]
    bfloat = jnp.bfloat16
    anywhere = pl.BlockSpec(memory_space=pl.ANY)
    vmem = pl.BlockSpec(memory_space=pltpu.VMEM)
    dma = pltpu.SemaphoreType.DMA
    kept = [
        ((block, 2 * HD), jnp.float32),
        ((block, HD), bfloat),
        ((2, span_len, HD), bfloat),
        ((block, WINDOW + 2 * tok_count), bfloat),
        ((block, HD), bfloat),
    ]
    outputs = [
        ((tok_count, width), jnp.float32),
        ((chips, 2, tok_count, width), bfloat),
        ((members, rows, 3 * HD), bfloat),
        ((members, rows, 2 * ff_part), bfloat),
    ] + kept
    return pl.pallas_call(
        functools.partial(attention_forward_kernel, chips),
        out_shape=[jax.ShapeDtypeStruct(*output) for output in outputs],
        in_specs=[vmem] + [anywhere] * 4 + [vmem] * 6,
        out_specs=[vmem] + [anywhere] * 8,
        scratch_shapes=line_scratch(chips, tok_count, width)
        + spread_scratch((members, rows, 3 * HD))
        + spread_scratch((members, rows, ff_part))
        + spread_scratch((members, rows, ff_part))
        + [pltpu.VMEM(out.shape, bfloat)]
        + [pltpu.VMEM(*one) for one in kept]
        + [dma, dma((9,)), dma((2,)), dma((2,))],
        compiler_params=pltpu.CompilerParams(
            collective_id=4, has_side_effects=True, vmem_limit_bytes=KERNEL_VMEM
        ),
        cost_estimate=pl.CostEstimate(
            flops=8 << 30, bytes_accessed=300 << 20, transcendentals=block * 1280
        ),
        name="attention_forward",
    )(
        own,
        qkv_own,
        gate_own,
        up_own,
        out,
        cosine,
        sine_part,
        gain_query,
        gain_key,
        query_docs,
        key_docs,
    )

def rope_norm_back(grad, lin, gain, cosine, sine_part):
    first, second = grad[:, : HD // 2], grad[:, HD // 2 :]
    turned = jnp.concatenate(
        [first * cosine + second * sine_part, second * cosine - first * sine_part], axis=-1
    )
    scale = lax.rsqrt(jnp.mean(lin * lin, axis=-1, keepdims=True) + EPSILON)
    scaled = turned * gain
    along = jnp.mean(lin * scaled, axis=-1, keepdims=True)
    grad_lin = scale * scaled - lin * (scale * scale * scale * along)
    return grad_lin, jnp.sum(lin * scale * turned, axis=0, keepdims=True)


def attention_backward_kernel(
    chips,
    own_ref,
    out_hbm,
    qkv_hbm,
    lin_hbm,
    query_hbm,
    span_hbm,
    probs_hbm,
    cos_ref,
    sin_ref,
    gain_query_ref,
    gain_key_ref,
    gateup_hbm,
    down_kept,
    inputs_hbm,
    attended_hbm,
    result_ref,
    query_part_hbm,
    kv_part_hbm,
    out_part_hbm,
    gains_ref,
    gateup_kept,
    down_sum,
    *scratch,
):
    scratch = list(scratch)
    line = Line(chips, scratch[:LINE_REFS])
    del scratch[:LINE_REFS]
    gateup = Summed(gateup_hbm, scratch[:SUM_REFS], True)
    del scratch[:SUM_REFS]
    down = Spread(Held(down_kept), scratch[: spread_refs(False)], False)
    del scratch[: spread_refs(False)]
    out, qkv, lin, query, span, probs, grad, grad_span, back, across, returned = scratch[:11]
    load_sem, store_sem, back_send, back_recv, grad_out = scratch[11:16]
    inputs, attended, query_part, kv_part, out_part = scratch[16:]
    width = line.slots.shape[3]
    pair = 2 * line.tok
    block = chips * pair
    ctx_at = lax.axis_index("ctx")
    planes = lax.axis_size("ctx")
    bfloat = jnp.bfloat16
    loads = [
        pltpu.make_async_copy(src, dst, load_sem.at[at])
        for at, (src, dst) in enumerate(
            (
                (out_hbm, out),
                (span_hbm, span),
                (probs_hbm, probs),
                (lin_hbm, lin),
                (query_hbm, query),
                (qkv_hbm, qkv),
                (inputs_hbm, inputs),
                (attended_hbm, attended),
            )
        )
    ]
    for load in loads:
        load.start()
    greet_all()
    line.gather_begin(own_ref)
    gateup.begin()
    grad_span[...] = jnp.zeros_like(grad_span)
    gains_ref[...] = jnp.zeros_like(gains_ref)
    line.own_copy(own_ref).wait()
    for load in loads[:6]:
        load.wait()

    span_len = WINDOW + pair
    for step in range(chips):
        if step > 0:
            line.gather_step(step)
        chip = line.order(step)
        line.gather_other(chip)
        rows = pl.ds(pl.multiple_of(chip * pair, pair), pair)
        span_rows = pl.ds(pl.multiple_of(chip * pair, pair), span_len)
        grad_out[rows] = dot_nt(line.slots[chip].reshape(pair, width), out[...]).astype(bfloat)
        grad_prob = dot_nt(grad_out[rows], span[1, span_rows])
        prob = probs[rows].astype(jnp.float32)
        inner = jnp.sum(prob * grad_prob, axis=-1, keepdims=True)
        grad_score = (prob * (grad_prob - inner)).astype(bfloat)
        grad_query = dot_nn(grad_score, span[0, span_rows]) * SCORE_SCALE
        grad_lin, grad_gain = rope_norm_back(
            grad_query, lin[rows, :HD], gain_query_ref[...], cos_ref[rows], sin_ref[rows]
        )
        grad[rows, :HD] = grad_lin.astype(bfloat)
        gains_ref[0:1] += grad_gain
        grad_span[0, span_rows] += dot_tn(grad_score, query[rows])
        grad_span[1, span_rows] += dot_tn(probs[rows], grad_out[rows])

    part = WINDOW // 2
    mine, others = line.core * part, (1 - line.core) * part
    back[...] = grad_span[:, pl.ds(pl.multiple_of(others, part), part)].astype(bfloat)
    to_core = remote(
        back, across, back_send.at[0], back_recv.at[0], line.place(line.chip, 1 - line.core)
    )
    to_core.start()
    to_core.wait()
    total = grad_span[:, pl.ds(pl.multiple_of(mine, part), part)]
    back[...] = (total + across[...].astype(jnp.float32)).astype(bfloat)
    to_before = pltpu.make_async_remote_copy(
        src_ref=back,
        dst_ref=returned,
        send_sem=back_send.at[1],
        recv_sem=back_recv.at[1],
        device_id={"ctx": lax.rem(ctx_at + planes - 1, planes)},
        device_id_type=pl.DeviceIdType.MESH,
    )

    @pl.when(ctx_at > 0)
    def _():
        to_before.start()

    down.place_all()
    down.spread_begin()

    @pl.when(ctx_at < planes - 1)
    def _():
        to_before.wait_recv()
        here = pl.ds(pl.multiple_of(block + mine, part), part)
        grad_span[:, here] += returned[...].astype(jnp.float32)

    for step in range(chips):
        chip = line.order(chips - 1 - step)
        rows = pl.ds(pl.multiple_of(chip * pair, pair), pair)
        span_rows = pl.ds(pl.multiple_of(WINDOW + chip * pair, pair), pair)
        grad_lin, grad_gain = rope_norm_back(
            grad_span[0, span_rows], lin[rows, HD:], gain_key_ref[...], cos_ref[rows], sin_ref[rows]
        )
        grad[rows, HD : 2 * HD] = grad_lin.astype(bfloat)
        gains_ref[1:2] += grad_gain
        grad[rows, 2 * HD :] = grad_span[1, span_rows].astype(bfloat)

    wide = 512

    @pl.loop(0, width // wide)
    def _(at):
        cols = pl.ds(pl.multiple_of(at * wide, wide), wide)
        sums = dot_nt(grad[...], qkv[cols]).astype(bfloat)
        line.parts[:, :, :, cols] = sums.reshape(chips, 2, line.tok, wide)

    for step in range(chips):
        line.core_copy(line.order(chips - 1 - step)).start()
    for step in range(chips - 1):
        line.scatter_first(line.order(chips - 1 - step))
    for load in loads[6:]:
        load.wait()
    part_stores = [
        pltpu.make_async_copy(out_part, out_part_hbm, store_sem.at[0]),
        pltpu.make_async_copy(query_part, query_part_hbm, store_sem.at[1]),
        pltpu.make_async_copy(kv_part, kv_part_hbm, store_sem.at[5]),
    ]

    def between(rank):
        if rank == 3:
            for start in range(0, width, wide):
                right = line.slots[:, :, :, start : start + wide].reshape(block, wide)
                out_part[:, start : start + wide] = dot_tn(attended[...], right).astype(bfloat)
            part_stores[0].start()
        if rank == 4:

            @pl.loop(0, width // HD)
            def _(at):
                left = inputs[:, pl.ds(pl.multiple_of(at * HD, HD), HD)]
                query_part[at] = dot_tn(left, grad[:, :HD]).astype(bfloat)
                kv_part[at] = dot_tn(left, grad[:, HD:]).astype(bfloat)

            part_stores[1].start()
            part_stores[2].start()

    gateup.middle()
    down.spread_on()
    line.scatter_rest(result_ref, between)
    gateup.finish()
    stores = [
        pltpu.make_async_copy(gateup.own_rows(half), gateup_kept.at[half], store_sem.at[2 + half])
        for half in (0, 1)
    ]
    down.spread_end()
    stores.append(pltpu.make_async_copy(down.final, down_sum, store_sem.at[4]))
    for store in stores:
        store.start()
    line.gather_end()
    gateup.sum_sent()
    down.spread_sent()

    @pl.when(ctx_at > 0)
    def _():
        to_before.wait_send()

    for store in stores + part_stores:
        store.wait()


def attention_backward(
    own,
    out,
    qkv,
    lin,
    query,
    span,
    probs,
    cosine,
    sine_part,
    gain_query,
    gain_key,
    part_gateup,
    held_down,
    inputs,
    attended,
):
    tok_count, width = own.shape
    members = part_gateup.shape[0]
    chips = members // 2
    block = members * tok_count
    bfloat = jnp.bfloat16
    anywhere = pl.BlockSpec(memory_space=pl.ANY)
    vmem = pl.BlockSpec(memory_space=pltpu.VMEM)
    dma = pltpu.SemaphoreType.DMA
    eighth = part_gateup.shape[1] // 8
    down_shape = (8 * held_down.shape[1], held_down.shape[2])
    outputs = [
        ((tok_count, width), jnp.float32),
        ((members, HD, HD), bfloat),
        ((members, HD, 2 * HD), bfloat),
        ((HD, width), bfloat),
        ((2, HD), jnp.float32),
        ((2, members, eighth, part_gateup.shape[2]), bfloat),
        (down_shape, bfloat),
    ]
    half_span = (2, WINDOW // 2, HD)
    return pl.pallas_call(
        functools.partial(attention_backward_kernel, chips),
        out_shape=[jax.ShapeDtypeStruct(*output) for output in outputs],
        in_specs=[vmem] + [anywhere] * 6 + [vmem] * 4 + [anywhere] * 4,
        out_specs=[vmem, anywhere, anywhere, anywhere, vmem, anywhere, anywhere],
        scratch_shapes=line_scratch(chips, tok_count, width)
        + sum_scratch(part_gateup.shape)
        + spread_scratch(down_shape)
        + [pltpu.VMEM(one.shape, one.dtype) for one in (out, qkv, lin, query, span, probs)]
        + [
            pltpu.VMEM((block, 3 * HD), bfloat),
            pltpu.VMEM(span.shape, jnp.float32),
            pltpu.VMEM(half_span, bfloat),
            pltpu.VMEM(half_span, bfloat),
            pltpu.VMEM(half_span, bfloat),
            dma((8,)),
            dma((6,)),
            dma((2,)),
            dma((2,)),
            pltpu.VMEM((block, HD), bfloat),
            pltpu.VMEM((block, width), bfloat),
            pltpu.VMEM((block, HD), bfloat),
            pltpu.VMEM((members, HD, HD), bfloat),
            pltpu.VMEM((members, HD, 2 * HD), bfloat),
            pltpu.VMEM((HD, width), bfloat),
        ],
        compiler_params=pltpu.CompilerParams(
            collective_id=5, has_side_effects=True, vmem_limit_bytes=KERNEL_VMEM
        ),
        cost_estimate=pl.CostEstimate(
            flops=8 << 30, bytes_accessed=300 << 20, transcendentals=0
        ),
        name="attention_backward",
    )(
        own,
        out,
        qkv,
        lin,
        query,
        span,
        probs,
        cosine,
        sine_part,
        gain_query,
        gain_key,
        part_gateup,
        held_down,
        inputs,
        attended,
    )

def by_heads(
    tokens,
    per_layer,
    cotangent,
    doc_lengths,
    positions,
    w_query,
    w_key,
    w_value,
    w_out,
    laurel_left,
    laurel_right,
    w_gate,
    w_up,
    w_down,
    ple_gate,
    ple_proj,
    attn_in_gain,
    query_gain,
    key_gain,
    attn_out_gain,
    laurel_gain,
    ffn_in_gain,
    ffn_out_gain,
    ple_gain,
):
    bfloat = jnp.bfloat16
    ctx_count = lax.axis_size("ctx")
    fsdp_count = lax.axis_size("fsdp")
    tok_count = tokens.shape[0]
    block_len = tok_count * fsdp_count
    chips = fsdp_count // 2
    rows = w_query.shape[0]
    ff_part = w_gate.shape[1] // fsdp_count
    ctx_at = lax.axis_index("ctx")
    fsdp_at = lax.axis_index("fsdp")

    gain_list = [
        attn_in_gain,
        query_gain,
        key_gain,
        attn_out_gain,
        laurel_gain,
        ffn_in_gain,
        ffn_out_gain,
        ple_gain,
    ]
    gain_sizes = [g.shape[0] for g in gain_list]
    gain_offsets = [sum(gain_sizes[:n]) for n in range(len(gain_sizes) + 1)]
    packed = jnp.concatenate(gain_list + [positions.astype(jnp.float32)])
    packed = jnp.pad(packed, (0, -packed.shape[0] % 1024)).reshape(1, -1, 128)
    packed = lax.all_gather(packed, "fsdp", axis=0, tiled=True).reshape(fsdp_count, -1)
    gain_in, gain_query, gain_key, gain_post, gain_laurel, gain_ffin, gain_ffout, gain_ple = (
        packed[:, gain_offsets[n] : gain_offsets[n + 1]].reshape(-1) for n in range(8)
    )
    block_positions = packed[:, gain_offsets[8] : gain_offsets[8] + tok_count].reshape(-1)
    cosine, sine_part = rope_tables(block_positions, HD)
    cosine, sine_part = cosine[:, 0], sine_part[:, 0]

    group_size = HQ // KV
    eighth = rows // 8
    at_x, at_y = ctx_at % 2, ctx_at // 2

    def own_rows(weight, width):
        starts = (at_x * 2 + at_y, 4 + at_y * 2 + at_x)
        halves = [lax.dynamic_slice_in_dim(weight, n * eighth, eighth, 0) for n in starts]
        held = jnp.stack(halves).astype(bfloat)
        return jnp.transpose(held.reshape(2, eighth, -1, width), (0, 2, 1, 3))

    qkv_own = jnp.concatenate(
        [
            own_rows(w_query, HD),
            jnp.repeat(own_rows(w_key, HD), group_size, axis=1),
            jnp.repeat(own_rows(w_value, HD), group_size, axis=1),
        ],
        axis=3,
    )
    gate_own, up_own = own_rows(w_gate, ff_part), own_rows(w_up, ff_part)
    out_low = w_out.astype(bfloat)
    down_low = w_down.astype(bfloat)
    width = tokens.shape[1]
    small_weights = (ple_gate, ple_proj, laurel_left, laurel_right)
    small_sizes = [weight.size // width for weight in small_weights]
    small_total = sum(small_sizes)
    share_rows = -(-small_total // (8 * ctx_count)) * 8
    small_packed = jnp.concatenate(
        [weight.astype(bfloat).reshape(-1, width) for weight in small_weights]
        + [jnp.zeros((share_rows * ctx_count - small_total, width), bfloat)]
    )
    small_share = lax.dynamic_slice_in_dim(small_packed, ctx_at * share_rows, share_rows, 0)
    small_full = lax.all_gather(small_share, ("ctx", "fsdp"), axis=0, tiled=False)
    small_full = small_full.reshape(ctx_count, fsdp_count, share_rows, width)
    small_full = jnp.transpose(small_full, (1, 0, 2, 3)).reshape(fsdp_count, -1, width)
    small_ends = [sum(small_sizes[:n]) for n in range(5)]
    full_pgate, full_pproj, full_left, full_right = (
        small_full[:, small_ends[n] : small_ends[n + 1]].reshape(-1, weight.shape[1])
        for n, weight in enumerate(small_weights)
    )

    inputs = tokens.astype(jnp.float32)
    ple_input = per_layer.astype(jnp.float32)
    normed, norm_back = jax.vjp(rms_norm, inputs, gain_in)
    normed_low = normed.astype(bfloat)
    block_start = ctx_at * block_len
    places = block_start - WINDOW + jnp.arange(WINDOW + block_len, dtype=jnp.int32)
    key_docs = jnp.where(places >= 0, document_ids(doc_lengths, places), -1)
    projected, normed_all, qkv_full, gateup_full, qk_lin, query_low, span_kv, probs, attended_low = (
        attention_forward(
            normed_low,
            qkv_own,
            gate_own,
            up_own,
            out_low,
            cosine,
            sine_part,
            gain_query[None, :],
            gain_key[None, :],
            key_docs[WINDOW:, None],
            key_docs[None, :],
        )
    )
    normed_all = normed_all.reshape(block_len, -1)
    col_qkv = qkv_full.reshape(normed_all.shape[1], -1)
    col_gateup = gateup_full.reshape(normed_all.shape[1], -1)
    narrow_low = matmul(normed_low, full_left).astype(bfloat)
    widened = matmul(narrow_low, full_right)
    mixed, mix_back = jax.vjp(mix_piece, inputs, normed, projected, widened, gain_post, gain_laurel)
    ffn_normed, ffn_norm_back = jax.vjp(rms_norm, mixed, gain_ffin)
    down_lin, ffn_all, hidden_low, act_low, slope_low = ffn_forward(
        ffn_normed.astype(bfloat), col_gateup, down_low, chips
    )
    layer_mid, ffn_out_back = jax.vjp(ffn_out_piece, mixed, down_lin, gain_ffout)
    layer_low = layer_mid.astype(bfloat)
    ple_lin = matmul(layer_low, full_pgate)
    ple_mid, ple_back = jax.vjp(ple_act, ple_lin, ple_input)
    ple_low = ple_mid.astype(bfloat)
    ple_wide = matmul(ple_low, full_pproj)
    out_full, final_back = jax.vjp(final_piece, layer_mid, ple_wide, gain_ple)

    grad_layer, grad_pwide, grad_gple = final_back(cotangent.astype(jnp.float32))
    grad_pwide_low = grad_pwide.astype(bfloat)
    part_pproj = matmul_tn(ple_low, grad_pwide_low)
    grad_plemid = matmul_nt(grad_pwide_low, full_pproj)
    grad_plelin, grad_pleinput = ple_back(grad_plemid)
    grad_plelin_low = grad_plelin.astype(bfloat)
    part_pgate = matmul_tn(layer_low, grad_plelin_low)
    grad_layer = grad_layer + matmul_nt(grad_plelin_low, full_pgate)
    grad_mixed, grad_down, grad_gffout = ffn_out_back(grad_layer)
    grad_ffn, part_gateup, held_wdown, held_pgate, held_pproj = ffn_backward(
        grad_down.astype(bfloat),
        col_gateup,
        down_low,
        hidden_low,
        act_low,
        slope_low,
        ffn_all,
        part_pgate.astype(bfloat).reshape(fsdp_count, rows, -1),
        part_pproj.astype(bfloat).reshape(fsdp_count, 128, -1),
        chips,
    )
    part_gateup = part_gateup.reshape(fsdp_count, rows, -1)
    grad_mixed_more, grad_gffin = ffn_norm_back(grad_ffn)
    grad_mixed = grad_mixed + grad_mixed_more
    grad_in_first, grad_normed, grad_proj, grad_lwide, grad_gpost, grad_glaurel = mix_back(
        grad_mixed
    )
    grad_lwide_low = grad_lwide.astype(bfloat)
    part_right = matmul_tn(narrow_low, grad_lwide_low)
    grad_narrow_low = matmul_nt(grad_lwide_low, full_right).astype(bfloat)
    part_left = matmul_tn(normed_low, grad_narrow_low)
    grad_normed = grad_normed + matmul_nt(grad_narrow_low, full_left)

    (
        grad_normed_more,
        part_query,
        part_kv,
        part_wout,
        grad_head_gains,
        held_gateup,
        sum_wdown,
    ) = (
        attention_backward(
            grad_proj.astype(bfloat),
            out_low,
            col_qkv,
            qk_lin,
            query_low,
            span_kv,
            probs,
            cosine,
            sine_part,
            gain_query[None, :],
            gain_key[None, :],
            part_gateup,
            held_wdown,
            normed_all,
            attended_low,
        )
    )
    grad_gquery, grad_gkey = grad_head_gains[0], grad_head_gains[1]
    part_laurel = jnp.concatenate(
        [part.astype(bfloat).reshape(fsdp_count, 128, -1) for part in (part_left, part_right)],
        axis=2,
    )
    grad_normed = grad_normed + grad_normed_more
    grad_in_second, grad_gin = norm_back(grad_normed)
    grad_tokens = grad_in_first + grad_in_second

    grad_gains = [
        grad_gin,
        grad_gquery,
        grad_gkey,
        grad_gpost,
        grad_glaurel,
        grad_gffin,
        grad_gffout,
        grad_gple,
    ]
    gain_parts = jnp.concatenate([g.reshape(fsdp_count, -1) for g in grad_gains], axis=1)
    gain_parts = jnp.pad(gain_parts, ((0, 0), (0, 128 * 128 - gain_parts.shape[1])))
    gain_parts = gain_parts.astype(bfloat).reshape(fsdp_count, 128, 128)

    (
        sum_wgate,
        sum_wup,
        sum_wquery,
        sum_wkey,
        sum_wvalue,
        sum_wout,
        sum_pgate,
        sum_pproj,
        sum_laurel,
        sum_gains,
    ) = gradient_sum(
        [
            Source(held_gateup, summed=True, part=(0, 2), sides=1),
            Source(held_gateup, summed=True, part=(1, 2), sides=1),
            Source(part_query, sides=1),
            Source(part_kv, groups=KV, sides=2),
            Source(part_wout),
            Source(held_pgate, summed=True, groups=1, sides=1),
            Source(held_pproj, summed=True, groups=1, sides=1),
            Source(part_laurel, groups=1, sides=1),
            Source(gain_parts),
        ]
    )
    gain_sums = jnp.sum(sum_gains.astype(jnp.float32), axis=0).reshape(-1)
    grad_wgate = sum_wgate.astype(jnp.float32)
    grad_wup = sum_wup.astype(jnp.float32)
    grad_wdown = sum_wdown.astype(jnp.float32)
    grad_wout = sum_wout.astype(jnp.float32)
    grad_wquery = sum_wquery.astype(jnp.float32)
    grad_wkey = sum_wkey.astype(jnp.float32)
    grad_wvalue = sum_wvalue.astype(jnp.float32)
    grad_pgate = sum_pgate.astype(jnp.float32)
    grad_pproj = sum_pproj.astype(jnp.float32).reshape(ple_proj.shape)
    left_part = sum_laurel.shape[1] // 2
    grad_wleft = sum_laurel[:, :left_part].astype(jnp.float32).reshape(laurel_left.shape)
    grad_wright = sum_laurel[:, left_part:].astype(jnp.float32).reshape(laurel_right.shape)
    return (
        out_full.astype(bfloat),
        grad_tokens,
        grad_pleinput,
        grad_wquery,
        grad_wkey,
        grad_wvalue,
        grad_wout,
        grad_wleft,
        grad_wright,
        grad_wgate,
        grad_wup,
        grad_wdown,
        grad_pgate,
        grad_pproj,
        *(gain_sums[gain_offsets[n] : gain_offsets[n + 1]] for n in range(8)),
    )


def solution(mesh):
    in_specs = (
        P(("ctx", "fsdp"), None),
        P(("ctx", "fsdp"), None),
        P(("ctx", "fsdp"), None),
        P(),
        P(("ctx", "fsdp")),
        P("fsdp", None),
        P("fsdp", None),
        P("fsdp", None),
        P("fsdp", None),
        P("fsdp", None),
        P("fsdp", None),
        P("fsdp", None),
        P("fsdp", None),
        P("fsdp", None),
        P("fsdp", None),
        P("fsdp", None),
        P("fsdp"),
        P("fsdp"),
        P("fsdp"),
        P("fsdp"),
        P("fsdp"),
        P("fsdp"),
        P("fsdp"),
        P("fsdp"),
    )
    out_specs = (
        P(("ctx", "fsdp"), None),
        P(("ctx", "fsdp"), None),
        P(("ctx", "fsdp"), None),
        P("fsdp", None),
        P("fsdp", None),
        P("fsdp", None),
        P("fsdp", None),
        P("fsdp", None),
        P("fsdp", None),
        P("fsdp", None),
        P("fsdp", None),
        P("fsdp", None),
        P("fsdp", None),
        P("fsdp", None),
        P("fsdp"),
        P("fsdp"),
        P("fsdp"),
        P("fsdp"),
        P("fsdp"),
        P("fsdp"),
        P("fsdp"),
        P("fsdp"),
    )
    run = by_heads if mesh.shape["fsdp"] == HQ and mesh.shape["ctx"] == 4 else local
    return jax.shard_map(run, mesh=mesh, in_specs=in_specs, out_specs=out_specs, check_vma=False)
```

```python
import dataclasses
import functools
import math

import jax
import jax.numpy as jnp
from jax import lax
from jax.experimental import pallas as pl
from jax.experimental.pallas import tpu as pltpu
from jax.sharding import PartitionSpec as P

HQ = 8
KV = 2
HD = 256
WINDOW = 1024


EPSILON = 1e-06
NEGATIVE = -1e30
ROPE_BASE = 10000.0
HALF_ROOT = 1.0 / math.sqrt(2.0)
GELU_ROOT = math.sqrt(2.0 / math.pi)
GELU_CUBE = 0.044715
SCORE_SCALE = 1.0 / math.sqrt(HD)
KERNEL_VMEM = 62 << 20


def passed_along(block, axis, distance):
    devices = range(lax.axis_size(axis))
    route = [(i - distance, i) for i in devices if i - distance in devices]
    return lax.ppermute(block, axis, route)


def matmul(left_mat, right_mat):
    return jnp.dot(left_mat, right_mat, preferred_element_type=jnp.float32)


def matmul_tn(left_mat, right_mat):
    return lax.dot_general(
        left_mat, right_mat, (((0,), (0,)), ((), ())), preferred_element_type=jnp.float32
    )


def matmul_nt(left_mat, right_mat):
    return lax.dot_general(
        left_mat, right_mat, (((1,), (1,)), ((), ())), preferred_element_type=jnp.float32
    )


def rms_norm(values, gain_vec):
    return (
        values * lax.rsqrt(jnp.mean(values * values, axis=-1, keepdims=True) + EPSILON) * gain_vec
    )


def rope_tables(positions, width):
    half_width = width // 2
    frequency = jnp.exp(
        jnp.arange(half_width, dtype=jnp.float32) * (-2.0 * math.log(ROPE_BASE) / width)
    )
    angles = positions.astype(jnp.float32)[:, None] * frequency[None, :]
    return (jnp.cos(angles)[:, None, :], jnp.sin(angles)[:, None, :])


def rotate(values, cosine, sine_part):
    half_width = values.shape[-1] // 2
    first_half = values[..., :half_width]
    second_half = values[..., half_width:]
    return jnp.concatenate(
        [
            first_half * cosine - second_half * sine_part,
            second_half * cosine + first_half * sine_part,
        ],
        axis=-1,
    )


def document_ids(doc_lengths, places):
    doc_ends = jnp.cumsum(doc_lengths)
    return jnp.sum((places[:, None] >= doc_ends[None, :-1]).astype(jnp.int32), axis=1)


def query_key(cosine, sine_part, query_lin, key_lin, gain_query, gain_key):
    tok_count = query_lin.shape[0]
    query_rot = rotate(
        rms_norm(query_lin.reshape(tok_count, HQ, HD), gain_query), cosine, sine_part
    )
    key_rot = rotate(rms_norm(key_lin.reshape(tok_count, KV, HD), gain_key), cosine, sine_part)
    return (query_rot, key_rot)


def mix_piece(inputs, normed, projected, widened, gain_post, gain_laurel):
    return (
        inputs + rms_norm(projected, gain_post) + normed + rms_norm(widened, gain_laurel)
    ) * HALF_ROOT


def geglu(gate_lin, up_lin):
    return jax.nn.gelu(gate_lin, approximate=True) * up_lin


def ffn_out_piece(mixed, down_lin, gain_ffout):
    return mixed + rms_norm(down_lin, gain_ffout)


def ple_act(ple_lin, ple_input):
    return jax.nn.gelu(ple_lin, approximate=True) * ple_input


def final_piece(layer_mid, ple_wide, gain_ple):
    return layer_mid + rms_norm(ple_wide, gain_ple)


def visibility(doc_lengths, query_start, key_start, tok_count, span_len):
    query_places = query_start + jnp.arange(tok_count, dtype=jnp.int32)
    key_places = key_start + jnp.arange(span_len, dtype=jnp.int32)
    distance = query_places[:, None] - key_places[None, :]
    query_docs = document_ids(doc_lengths, query_places)
    key_docs = document_ids(doc_lengths, key_places)
    return (
        (distance >= 0)
        & (distance < WINDOW)
        & (key_places[None, :] >= 0)
        & (query_docs[:, None] == key_docs[None, :])
    )


def attend_forward(query_low, span_kv, visible):
    tok_count = query_low.shape[0]
    scale_factor = 1.0 / math.sqrt(HD)
    scores = (
        jnp.einsum("tkgh,skh->kgts", query_low, span_kv[0], preferred_element_type=jnp.float32)
        * scale_factor
    )
    scores = jnp.where(visible, scores, NEGATIVE)
    row_top = jnp.max(scores, axis=-1, keepdims=True)
    shifted = jnp.exp(scores - row_top)
    row_total = jnp.sum(shifted, axis=-1, keepdims=True)
    attn_probs = shifted / row_total
    attended = jnp.einsum(
        "kgts,skh->tkgh",
        attn_probs.astype(jnp.bfloat16),
        span_kv[1],
        preferred_element_type=jnp.float32,
    )
    return (attended.reshape(tok_count, -1), row_top + jnp.log(row_total))


def attend_backward(query_low, span_kv, visible, log_total, grad_out_low):
    scale_factor = 1.0 / math.sqrt(HD)
    scores = (
        jnp.einsum("tkgh,skh->kgts", query_low, span_kv[0], preferred_element_type=jnp.float32)
        * scale_factor
    )
    attn_probs = jnp.where(visible, jnp.exp(jnp.where(visible, scores, NEGATIVE) - log_total), 0.0)
    grad_probs = jnp.einsum(
        "tkgh,skh->kgts", grad_out_low, span_kv[1], preferred_element_type=jnp.float32
    )
    inner_sum = jnp.sum(attn_probs * grad_probs, axis=-1, keepdims=True)
    grad_scores = (attn_probs * (grad_probs - inner_sum)).astype(jnp.bfloat16)
    grad_query = (
        jnp.einsum("kgts,skh->tkgh", grad_scores, span_kv[0], preferred_element_type=jnp.float32)
        * scale_factor
    )
    grad_keys = (
        jnp.einsum("kgts,tkgh->skh", grad_scores, query_low, preferred_element_type=jnp.float32)
        * scale_factor
    )
    grad_values = jnp.einsum(
        "kgts,tkgh->skh",
        attn_probs.astype(jnp.bfloat16),
        grad_out_low,
        preferred_element_type=jnp.float32,
    )
    return (grad_query, jnp.stack([grad_keys, grad_values]))


def settle(act_low, grad_low):
    act_cols = lax.all_to_all(act_low, "fsdp", split_axis=1, concat_axis=0, tiled=True)
    shard_rows = matmul_tn(act_cols, lax.all_gather(grad_low, "fsdp", axis=0, tiled=True))
    return lax.psum(shard_rows.astype(jnp.bfloat16), "ctx").astype(jnp.float32)


def local(
    tokens,
    per_layer,
    cotangent,
    doc_lengths,
    positions,
    w_query,
    w_key,
    w_value,
    w_out,
    laurel_left,
    laurel_right,
    w_gate,
    w_up,
    w_down,
    ple_gate,
    ple_proj,
    attn_in_gain,
    query_gain,
    key_gain,
    attn_out_gain,
    laurel_gain,
    ffn_in_gain,
    ffn_out_gain,
    ple_gain,
):
    bfloat = jnp.bfloat16
    tok_count = tokens.shape[0]
    span_len = WINDOW + tok_count
    groups = HQ // KV
    dev_index = lax.axis_index("ctx") * lax.axis_size("fsdp") + lax.axis_index("fsdp")
    query_start = dev_index * tok_count
    key_start = query_start - WINDOW
    visible = visibility(doc_lengths, query_start, key_start, tok_count, span_len)
    cosine, sine_part = rope_tables(positions, HD)
    gain_in, gain_query, gain_key, gain_post, gain_laurel, gain_ffin, gain_ffout, gain_ple = (
        lax.all_gather(attn_in_gain, "fsdp", axis=0, tiled=True),
        lax.all_gather(query_gain, "fsdp", axis=0, tiled=True),
        lax.all_gather(key_gain, "fsdp", axis=0, tiled=True),
        lax.all_gather(attn_out_gain, "fsdp", axis=0, tiled=True),
        lax.all_gather(laurel_gain, "fsdp", axis=0, tiled=True),
        lax.all_gather(ffn_in_gain, "fsdp", axis=0, tiled=True),
        lax.all_gather(ffn_out_gain, "fsdp", axis=0, tiled=True),
        lax.all_gather(ple_gain, "fsdp", axis=0, tiled=True),
    )
    full_query, full_key, full_value, full_out, full_left, full_right = (
        lax.all_gather(w_query.astype(bfloat), "fsdp", axis=0, tiled=True),
        lax.all_gather(w_key.astype(bfloat), "fsdp", axis=0, tiled=True),
        lax.all_gather(w_value.astype(bfloat), "fsdp", axis=0, tiled=True),
        lax.all_gather(w_out.astype(bfloat), "fsdp", axis=0, tiled=True),
        lax.all_gather(laurel_left.astype(bfloat), "fsdp", axis=0, tiled=True),
        lax.all_gather(laurel_right.astype(bfloat), "fsdp", axis=0, tiled=True),
    )
    inputs = tokens.astype(jnp.float32)
    ple_input = per_layer.astype(jnp.float32)
    normed, norm_back = jax.vjp(rms_norm, inputs, gain_in)
    normed_low = normed.astype(bfloat)
    query_lin = matmul(normed_low, full_query)
    key_lin = matmul(normed_low, full_key)
    value_lin = matmul(normed_low, full_value)
    (query_rot, key_rot), rope_back = jax.vjp(
        functools.partial(query_key, cosine, sine_part), query_lin, key_lin, gain_query, gain_key
    )
    query_low = query_rot.astype(bfloat).reshape(tok_count, KV, groups, HD)
    keys_values = jnp.stack(
        [key_rot.astype(bfloat), value_lin.astype(bfloat).reshape(tok_count, KV, HD)]
    )
    block_kv = lax.all_gather(keys_values, "fsdp", axis=1, tiled=True)
    block_len = block_kv.shape[1]
    before_kv = passed_along(block_kv, "ctx", 1)
    span_offset = block_len + lax.axis_index("fsdp") * tok_count - WINDOW
    span_kv = lax.dynamic_slice_in_dim(
        jnp.concatenate([before_kv, block_kv], axis=1), span_offset, span_len, 1
    )
    attended, log_total = attend_forward(query_low, span_kv, visible)
    attended_low = attended.astype(bfloat)
    projected = matmul(attended_low, full_out)
    narrow_low = matmul(normed_low, full_left).astype(bfloat)
    widened = matmul(narrow_low, full_right)
    mixed, mix_back = jax.vjp(mix_piece, inputs, normed, projected, widened, gain_post, gain_laurel)
    full_gate, full_up, full_down, full_pgate, full_pproj = (
        lax.all_gather(w_gate.astype(bfloat), "fsdp", axis=0, tiled=True),
        lax.all_gather(w_up.astype(bfloat), "fsdp", axis=0, tiled=True),
        lax.all_gather(w_down.astype(bfloat), "fsdp", axis=0, tiled=True),
        lax.all_gather(ple_gate.astype(bfloat), "fsdp", axis=0, tiled=True),
        lax.all_gather(ple_proj.astype(bfloat), "fsdp", axis=0, tiled=True),
    )
    ffn_normed, ffn_norm_back = jax.vjp(rms_norm, mixed, gain_ffin)
    ffn_low = ffn_normed.astype(bfloat)
    gate_lin = matmul(ffn_low, full_gate)
    up_lin = matmul(ffn_low, full_up)
    hidden, geglu_back = jax.vjp(geglu, gate_lin, up_lin)
    hidden_low = hidden.astype(bfloat)
    down_lin = matmul(hidden_low, full_down)
    layer_mid, ffn_out_back = jax.vjp(ffn_out_piece, mixed, down_lin, gain_ffout)
    layer_low = layer_mid.astype(bfloat)
    ple_lin = matmul(layer_low, full_pgate)
    ple_mid, ple_back = jax.vjp(ple_act, ple_lin, ple_input)
    ple_low = ple_mid.astype(bfloat)
    ple_wide = matmul(ple_low, full_pproj)
    out_full, final_back = jax.vjp(final_piece, layer_mid, ple_wide, gain_ple)
    full_gate, full_up, full_down, full_pgate, full_pproj = (
        lax.all_gather(w_gate.astype(bfloat), "fsdp", axis=0, tiled=True),
        lax.all_gather(w_up.astype(bfloat), "fsdp", axis=0, tiled=True),
        lax.all_gather(w_down.astype(bfloat), "fsdp", axis=0, tiled=True),
        lax.all_gather(ple_gate.astype(bfloat), "fsdp", axis=0, tiled=True),
        lax.all_gather(ple_proj.astype(bfloat), "fsdp", axis=0, tiled=True),
    )
    grad_layer, grad_pwide, grad_gple = final_back(cotangent.astype(jnp.float32))
    grad_pwide_low = grad_pwide.astype(bfloat)
    grad_pproj = settle(ple_low, grad_pwide_low)
    grad_plemid = matmul_nt(grad_pwide_low, full_pproj)
    grad_plelin, grad_pleinput = ple_back(grad_plemid)
    grad_plelin_low = grad_plelin.astype(bfloat)
    grad_pgate = settle(layer_low, grad_plelin_low)
    grad_layer = grad_layer + matmul_nt(grad_plelin_low, full_pgate)
    grad_mixed, grad_down, grad_gffout = ffn_out_back(grad_layer)
    grad_down_low = grad_down.astype(bfloat)
    grad_wdown = settle(hidden_low, grad_down_low)
    grad_hidden = matmul_nt(grad_down_low, full_down)
    grad_gate, grad_up = geglu_back(grad_hidden)
    grad_gate_low = grad_gate.astype(bfloat)
    grad_up_low = grad_up.astype(bfloat)
    grad_wgate = settle(ffn_low, grad_gate_low)
    grad_wup = settle(ffn_low, grad_up_low)
    grad_ffn = matmul_nt(grad_gate_low, full_gate) + matmul_nt(grad_up_low, full_up)
    grad_mixed_more, grad_gffin = ffn_norm_back(grad_ffn)
    grad_mixed = grad_mixed + grad_mixed_more
    full_query, full_key, full_value, full_out, full_left, full_right = (
        lax.all_gather(w_query.astype(bfloat), "fsdp", axis=0, tiled=True),
        lax.all_gather(w_key.astype(bfloat), "fsdp", axis=0, tiled=True),
        lax.all_gather(w_value.astype(bfloat), "fsdp", axis=0, tiled=True),
        lax.all_gather(w_out.astype(bfloat), "fsdp", axis=0, tiled=True),
        lax.all_gather(laurel_left.astype(bfloat), "fsdp", axis=0, tiled=True),
        lax.all_gather(laurel_right.astype(bfloat), "fsdp", axis=0, tiled=True),
    )
    grad_in_first, grad_normed, grad_proj, grad_lwide, grad_gpost, grad_glaurel = mix_back(
        grad_mixed
    )
    grad_proj_low = grad_proj.astype(bfloat)
    grad_wout = settle(attended_low, grad_proj_low)
    grad_att_low = matmul_nt(grad_proj_low, full_out).astype(bfloat)
    grad_lwide_low = grad_lwide.astype(bfloat)
    grad_wright = settle(narrow_low, grad_lwide_low)
    grad_narrow_low = matmul_nt(grad_lwide_low, full_right).astype(bfloat)
    grad_wleft = settle(normed_low, grad_narrow_low)
    grad_normed = grad_normed + matmul_nt(grad_narrow_low, full_left)
    grad_query_att, grad_span = attend_backward(
        query_low, span_kv, visible, log_total, grad_att_low.reshape(tok_count, KV, groups, HD)
    )
    whole_grad = jnp.zeros((2, 2 * block_len, KV, HD), jnp.float32)
    whole_grad = lax.dynamic_update_slice_in_dim(whole_grad, grad_span, span_offset, 1)
    returned = passed_along(whole_grad[:, :block_len].astype(jnp.bfloat16), "ctx", -1).astype(
        jnp.float32
    )
    own_grad = lax.psum_scatter(
        (whole_grad[:, block_len:] + returned).astype(jnp.bfloat16),
        "fsdp",
        scatter_dimension=1,
        tiled=True,
    ).astype(jnp.float32)
    grad_qlin, grad_klin, grad_gquery, grad_gkey = rope_back(
        (grad_query_att.reshape(tok_count, HQ, HD), own_grad[0])
    )
    grad_qlin_low = grad_qlin.astype(bfloat)
    grad_klin_low = grad_klin.astype(bfloat)
    grad_vlin_low = own_grad[1].reshape(tok_count, KV * HD).astype(bfloat)
    grad_wquery = settle(normed_low, grad_qlin_low)
    grad_wkey = settle(normed_low, grad_klin_low)
    grad_wvalue = settle(normed_low, grad_vlin_low)
    grad_normed = (
        grad_normed
        + matmul_nt(grad_qlin_low, full_query)
        + matmul_nt(grad_klin_low, full_key)
        + matmul_nt(grad_vlin_low, full_value)
    )
    grad_in_second, grad_gin = norm_back(grad_normed)
    grad_tokens = grad_in_first + grad_in_second
    sum_gin, sum_gquery, sum_gkey, sum_gpost, sum_glaurel, sum_gffin, sum_gffout, sum_gple = (
        lax.psum(
            (
                grad_gin,
                grad_gquery,
                grad_gkey,
                grad_gpost,
                grad_glaurel,
                grad_gffin,
                grad_gffout,
                grad_gple,
            ),
            ("ctx", "fsdp"),
        )
    )
    wide_rows = attn_in_gain.shape[0]
    head_rows = query_gain.shape[0]
    wide_start = lax.axis_index("fsdp") * wide_rows
    head_start = lax.axis_index("fsdp") * head_rows

    def wide_part(full_vec):
        return lax.dynamic_slice_in_dim(full_vec, wide_start, wide_rows, 0)

    def head_part(full_vec):
        return lax.dynamic_slice_in_dim(full_vec, head_start, head_rows, 0)

    return (
        out_full.astype(bfloat),
        grad_tokens,
        grad_pleinput,
        grad_wquery,
        grad_wkey,
        grad_wvalue,
        grad_wout,
        grad_wleft,
        grad_wright,
        grad_wgate,
        grad_wup,
        grad_wdown,
        grad_pgate,
        grad_pproj,
        wide_part(sum_gin),
        head_part(sum_gquery),
        head_part(sum_gkey),
        wide_part(sum_gpost),
        wide_part(sum_glaurel),
        wide_part(sum_gffin),
        wide_part(sum_gffout),
        wide_part(sum_gple),
    )

class Plane:
    def locate(self, columns, rows):
        self.columns = columns
        at = lax.axis_index("ctx")
        self.at_x, self.at_y = at % 2, at // 2
        self.beside = (at + 1 - 2 * (at % 2), (at + 2) % 4)
        self.me = lax.axis_index("fsdp")
        self.members = lax.axis_size("fsdp")
        self.half = rows // 2
        self.quarter = rows // 4
        self.eighth = rows // 8

    def rows(self, ref, start, size):
        start = pl.multiple_of(start, size)
        return ref.at[:, pl.ds(start, size)] if self.columns else ref.at[pl.ds(start, size)]

    def sides(self, half):
        return (self.at_x, self.at_y) if half == 0 else (self.at_y, self.at_x)

    def kept_start(self, half):
        return half * self.half + self.sides(half)[0] * self.quarter

    def given_start(self, half):
        return half * self.half + (1 - self.sides(half)[0]) * self.quarter

    def own_start(self, half):
        return self.kept_start(half) + self.sides(half)[1] * self.eighth

    def copy(self, src, dst, send_sem, recv_sem, half, stage):
        return pltpu.make_async_remote_copy(
            src_ref=src,
            dst_ref=dst,
            send_sem=send_sem.at[half, stage],
            recv_sem=recv_sem.at[half, stage],
            device_id={"ctx": self.beside[(half + stage) % 2]},
            device_id_type=pl.DeviceIdType.MESH,
        )


class Summed(Plane):
    def __init__(self, source, refs, columns):
        self.source = source
        self.kept, self.taken, self.last, self.load_sem, self.sum_send, self.sum_recv = refs
        self.locate(columns, source.shape[-2])

    def load(self, half):
        return pltpu.make_async_copy(
            self.rows(self.source, self.kept_start(half), self.quarter),
            self.kept.at[half],
            self.load_sem.at[half],
        )

    def first(self, half):
        return self.copy(
            self.rows(self.source, self.given_start(half), self.quarter),
            self.taken.at[half],
            self.sum_send,
            self.sum_recv,
            half,
            0,
        )

    def second(self, half):
        other = (1 - self.sides(half)[1]) * self.eighth
        return self.copy(
            self.rows(self.kept.at[half], other, self.eighth),
            self.last.at[half],
            self.sum_send,
            self.sum_recv,
            half,
            1,
        )

    def begin(self):
        for half in (0, 1):
            self.first(half).start()
            self.load(half).start()

    def add(self, half, start, more, more_start):
        step = min(32, self.eighth)
        blocks = self.eighth // step
        layers = self.source.shape[0] if self.columns else 1

        @pl.loop(0, layers * blocks)
        def _(at):
            layer, block = at // blocks, at % blocks
            here = pl.ds(pl.multiple_of(start + block * step, step), step)
            there = pl.ds(pl.multiple_of(more_start + block * step, step), step)
            if self.columns:
                self.kept[half, layer, here] += more[half, layer, there]
            else:
                self.kept[half, here] += more[half, there]

    def middle(self):
        for half in (0, 1):
            self.load(half).wait()
            self.first(half).wait_recv()
            side = self.sides(half)[1]
            other = (1 - side) * self.eighth
            self.add(half, other, self.taken, other)
            self.second(half).start()
            mine = side * self.eighth
            self.add(half, mine, self.taken, mine)

    def finish(self):
        for half in (0, 1):
            self.second(half).wait_recv()
            self.add(half, self.sides(half)[1] * self.eighth, self.last, 0)

    def own_rows(self, half):
        return self.rows(self.kept.at[half], self.sides(half)[1] * self.eighth, self.eighth)

    def held(self, half, member):
        side = self.sides(half)[1] * self.eighth
        return self.kept.at[half, member, pl.ds(pl.multiple_of(side, self.eighth), self.eighth)]

    def sum_sent(self):
        for half in (0, 1):
            self.first(half).wait_send()
            self.second(half).wait_send()


class Held:
    def __init__(self, kept, side=0, sides=1):
        self.kept = kept
        width = kept.shape[-1] // sides
        self.cols = pl.ds(side * width, width)

    def own_rows(self, half):
        return self.kept.at[half]

    def held(self, half, member):
        return self.kept.at[half, member, :, self.cols]


class Spread(Plane):
    def __init__(self, source, refs, columns):
        self.own_rows, self.held = source.own_rows, source.held
        self.final, self.spread_send, self.spread_recv, self.place_sem = refs[:4]
        if columns:
            self.swap_send, self.swap_recv = refs[4:]
        self.locate(columns, self.final.shape[-2])

    def place(self, half):
        return pltpu.make_async_copy(
            self.own_rows(half),
            self.rows(self.final, self.own_start(half), self.eighth),
            self.place_sem.at[half],
        )

    def place_all(self):
        for half in (0, 1):
            self.place(half).start()
        for half in (0, 1):
            self.place(half).wait()

    def swap_place(self, half, member):
        start = pl.multiple_of(self.own_start(half), self.eighth)
        return self.final.at[member, pl.ds(start, self.eighth)]

    def swap_copy(self, half, hop, src_member):
        target = lax.rem(self.me + hop, self.members)
        return remote(
            self.held(half, target),
            self.swap_place(half, src_member),
            self.swap_send.at[hop, half],
            self.swap_recv.at[hop, half],
            target,
        )

    def swap_local(self, half):
        return pltpu.make_async_copy(
            self.held(half, self.me),
            self.swap_place(half, self.me),
            self.place_sem.at[half],
        )

    def swap_begin(self):
        for half in (0, 1):
            for hop in range(1, self.members):
                self.swap_copy(half, hop, self.me).start()
            self.swap_local(half).start()

    def swap_end(self):
        for half in (0, 1):
            for hop in range(1, self.members):
                source = lax.rem(self.me + self.members - hop, self.members)
                self.swap_copy(half, hop, source).wait_recv()
            self.swap_local(half).wait()

    def spread_copy(self, half, stage):
        if stage == 0:
            rows = self.rows(self.final, self.own_start(half), self.eighth)
        else:
            rows = self.rows(self.final, self.kept_start(half), self.quarter)
        return self.copy(rows, rows, self.spread_send, self.spread_recv, half, 1 - stage)

    def spread_wait(self, half, stage):
        side = self.sides(half)[1]
        if stage == 0:
            start = self.kept_start(half) + (1 - side) * self.eighth
            rows = self.rows(self.final, start, self.eighth)
        else:
            rows = self.rows(self.final, self.given_start(half), self.quarter)
        self.copy(rows, rows, self.spread_send, self.spread_recv, half, 1 - stage).wait_recv()

    def spread_begin(self):
        for half in (0, 1):
            self.spread_copy(half, 0).start()

    def spread_on(self):
        for half in (0, 1):
            self.spread_wait(half, 0)
            self.spread_copy(half, 1).start()

    def spread_end(self):
        for half in (0, 1):
            self.spread_wait(half, 1)

    def spread_sent(self):
        for half in (0, 1):
            self.spread_copy(half, 0).wait_send()
            self.spread_copy(half, 1).wait_send()
            if self.columns:
                for hop in range(1, self.members):
                    self.swap_copy(half, hop, self.me).wait_send()


class GroupSpread(Spread):
    def __init__(self, source, refs):
        self.landing = refs[0]
        super().__init__(source, refs[1:], True)

    def swap_place(self, half, member):
        return self.landing.at[half, member]

    def swap_end(self):
        super().swap_end()
        groups = self.final.shape[0]
        size = self.landing.shape[1] // groups
        for half in (0, 1):
            rows = pl.ds(pl.multiple_of(self.own_start(half), self.eighth), self.eighth)
            for group in range(groups):
                total = self.landing[half, group * size].astype(jnp.float32)
                for member in range(group * size + 1, (group + 1) * size):
                    total = total + self.landing[half, member].astype(jnp.float32)
                self.final[group, rows] = total.astype(jnp.bfloat16)


class Everywhere(Spread):
    def swap_begin(self):
        chips = self.members // 2
        for half in (0, 1):
            own = self.own_rows(half)
            for hop in range(1, chips):
                self.hand_to(half, hop, own, lax.rem(self.me + 2 * hop, self.members)).start()
            self.pass_on(half, self.me // 2, own).start()
            self.swap_local(half).start()

    def hand_to(self, half, hop, own, place):
        return remote(
            own,
            self.swap_place(half, self.me),
            self.swap_send.at[0, hop, half],
            self.swap_recv.at[0, hop, half],
            place,
        )

    def pass_on(self, half, chip, source):
        core = self.me % 2
        return remote(
            source,
            self.swap_place(half, 2 * chip + core),
            self.swap_send.at[1, chip, half],
            self.swap_recv.at[1, chip, half],
            self.me + 1 - 2 * core,
        )

    def swap_on(self):
        chips = self.members // 2
        for hop in range(1, chips):
            sender = lax.rem(self.me + self.members - 2 * hop, self.members)
            for half in (0, 1):
                place = self.swap_place(half, sender)
                remote(
                    place,
                    place,
                    self.swap_send.at[0, hop, half],
                    self.swap_recv.at[0, hop, half],
                    sender,
                ).wait_recv()
                self.pass_on(half, sender // 2, place).start()

    def swap_end(self):
        core = self.me % 2
        for chip in range(self.members // 2):
            for half in (0, 1):
                place = self.swap_place(half, 2 * chip + 1 - core)
                remote(
                    place,
                    place,
                    self.swap_send.at[1, chip, half],
                    self.swap_recv.at[1, chip, half],
                    self.me + 1 - 2 * core,
                ).wait_recv()
        for half in (0, 1):
            self.swap_local(half).wait()

    def spread_sent(self):
        chips = self.members // 2
        for half in (0, 1):
            self.spread_copy(half, 0).wait_send()
            self.spread_copy(half, 1).wait_send()
            own = self.own_rows(half)
            for hop in range(1, chips):
                self.hand_to(half, hop, own, lax.rem(self.me + 2 * hop, self.members)).wait_send()
            for chip in range(chips):
                self.pass_on(half, chip, own).wait_send()


def sum_scratch(shape):
    dma = pltpu.SemaphoreType.DMA
    rows, width = shape[-2:]

    def buffer(count):
        return pltpu.VMEM((2,) + shape[:-2] + (count, width), jnp.bfloat16)

    buffers = [buffer(rows // 4), buffer(rows // 4), buffer(rows // 8)]
    return buffers + [dma((2,)), dma((2, 2)), dma((2, 2))]


SUM_REFS = 6


def spread_scratch(shape, members=None):
    dma = pltpu.SemaphoreType.DMA
    scratch = [pltpu.VMEM(shape, jnp.bfloat16), dma((2, 2)), dma((2, 2)), dma((2,))]
    if len(shape) == 3:
        count = members or shape[0]
        scratch += [dma((count, 2)), dma((count, 2))]
    return scratch


def everywhere_scratch(shape):
    dma = pltpu.SemaphoreType.DMA
    chips = shape[0] // 2
    scratch = [pltpu.VMEM(shape, jnp.bfloat16), dma((2, 2)), dma((2, 2)), dma((2,))]
    return scratch + [dma((2, chips, 2)), dma((2, chips, 2))]


def spread_refs(columns):
    return 6 if columns else 4


def gradient_sum_kernel(plan, *refs):
    refs = list(refs)
    count = len(plan)
    sources = refs[:count]
    results_count = sum(max(1, one.sides) for one in plan)
    results = refs[count : count + results_count]
    scratch = refs[count + results_count :]
    store_sem = scratch.pop()

    def take(size):
        taken = scratch[:size]
        del scratch[:size]
        return taken

    sums, spreads, late = [], [], []
    for source, one in zip(sources, plan):
        if one.summed:
            held = Held(source, *one.part)
        else:
            held = Summed(source, take(SUM_REFS), one.columns)
            sums.append(held)
        size = spread_refs(one.columns)
        if one.groups:
            spreads.append(GroupSpread(held, take(size + 1)))
        else:
            spreads.append(Spread(held, take(size), one.columns))
        if not one.summed:
            late.append(spreads[-1])
    early = [spread for spread in spreads if spread not in late]
    greet_all()

    def stores(at):
        final, sides = spreads[at].final, plan[at].sides
        first = sum(max(1, one.sides) for one in plan[:at])
        if sides == 0:
            return [pltpu.make_async_copy(final, results[first], store_sem.at[at, 0, 0])]
        part = final.shape[2] // sides
        return [
            pltpu.make_async_copy(
                final.at[member, :, pl.ds(side * part, part)],
                results[first + side].at[:, pl.ds(member * part, part)],
                store_sem.at[at, side, member],
            )
            for member in range(final.shape[0])
            for side in range(sides)
        ]

    def launch(spread):
        if spread.columns:
            spread.swap_begin()
        else:
            spread.place_all()
            spread.spread_begin()

    for share in sums:
        share.begin()
    for spread in early:
        launch(spread)
    for share in sums:
        share.middle()
    for spread in early[:1]:
        spread.swap_end()
        spread.spread_begin()
    for share, spread in zip(sums, late):
        share.finish()
        launch(spread)
    for spread in early[:1]:
        spread.spread_on()
    for spread in early[1:]:
        spread.swap_end()
        spread.spread_begin()
    for spread in late:
        if spread.columns:
            spread.swap_end()
            spread.spread_begin()
        else:
            spread.spread_on()
    for spread in early[1:]:
        spread.spread_on()
    for spread in late:
        if spread.columns:
            spread.spread_on()
    for at in sorted(range(count), key=lambda one: spreads[one] in early):
        spreads[at].spread_end()
        for store in stores(at):
            store.start()
    for share in sums:
        share.sum_sent()
    for spread in spreads:
        spread.spread_sent()
    for at in range(count):
        for store in stores(at):
            store.wait()


@dataclasses.dataclass
class Source:
    array: jax.Array
    summed: bool = False
    part: tuple = (0, 1)
    groups: int = 0
    sides: int = 0

    @property
    def columns(self):
        return self.array.ndim - self.summed == 3

    @property
    def shape(self):
        shape = self.array.shape
        if self.summed:
            shape = shape[1:-2] + (8 * shape[-2], shape[-1] // self.part[1])
        return shape


def gradient_sum(sources):
    members = lax.axis_size("fsdp")
    anywhere = pl.BlockSpec(memory_space=pl.ANY)
    scratch, results = [], []
    for one in sources:
        shape = one.shape
        if not one.summed:
            scratch += sum_scratch(shape)
        if one.groups:
            landing = (2, members, shape[1] // 8, shape[2])
            scratch.append(pltpu.VMEM(landing, jnp.bfloat16))
            shape = (one.groups,) + shape[1:]
        scratch += spread_scratch(shape, members)
        if one.sides == 0:
            results.append(shape)
        else:
            results += [(shape[1], shape[0] * shape[2] // one.sides)] * one.sides
    return pl.pallas_call(
        functools.partial(gradient_sum_kernel, sources),
        out_shape=[jax.ShapeDtypeStruct(shape, jnp.bfloat16) for shape in results],
        in_specs=[anywhere] * len(sources),
        out_specs=[anywhere] * len(results),
        scratch_shapes=scratch + [pltpu.SemaphoreType.DMA((len(sources), 2, members))],
        compiler_params=pltpu.CompilerParams(
            collective_id=3, has_side_effects=True, vmem_limit_bytes=KERNEL_VMEM
        ),
        cost_estimate=pl.CostEstimate(flops=0, bytes_accessed=300 << 20, transcendentals=0),
        name="gradient_sum",
    )(*(one.array for one in sources))

def remote(src, dst, send_sem, recv_sem, place):
    return pltpu.make_async_remote_copy(
        src_ref=src,
        dst_ref=dst,
        send_sem=send_sem,
        recv_sem=recv_sem,
        device_id={"fsdp": place},
        device_id_type=pl.DeviceIdType.MESH,
    )


def dot_nn(left_mat, right_mat):
    return jnp.dot(left_mat, right_mat, preferred_element_type=jnp.float32)


def dot_nt(left_mat, right_mat):
    return lax.dot_general(
        left_mat, right_mat, (((1,), (1,)), ((), ())), preferred_element_type=jnp.float32
    )


def dot_tn(left_mat, right_mat):
    return lax.dot_general(
        left_mat, right_mat, (((0,), (0,)), ((), ())), preferred_element_type=jnp.float32
    )


def greet_all():
    sem = pltpu.get_barrier_semaphore()
    members, planes = lax.axis_size("fsdp"), lax.axis_size("ctx")
    mesh_id = pl.DeviceIdType.MESH
    for hop in range(1, planes):
        other = lax.rem(lax.axis_index("ctx") + hop, planes)
        pl.semaphore_signal(sem, inc=1, device_id={"ctx": other}, device_id_type=mesh_id)
    for hop in range(1, members):
        other = lax.rem(lax.axis_index("fsdp") + hop, members)
        pl.semaphore_signal(sem, inc=1, device_id={"fsdp": other}, device_id_type=mesh_id)
    pl.semaphore_wait(sem, members + planes - 2)


PIECES = 4


def line_scratch(chips, tok_count, width):
    dma = pltpu.SemaphoreType.DMA
    shard = (tok_count, width)
    return [
        pltpu.VMEM((chips, 2) + shard, jnp.bfloat16),
        dma((chips, 2)),
        dma((chips, 3)),
        dma,
        pltpu.VMEM((chips, 2) + shard, jnp.bfloat16),
        pltpu.VMEM((chips,) + shard, jnp.bfloat16),
        pltpu.VMEM((chips,) + shard, jnp.bfloat16),
        pltpu.VMEM((chips,) + shard, jnp.bfloat16),
        dma((chips,)),
        dma((chips,)),
        dma((chips, PIECES)),
        dma((chips, PIECES)),
        dma((chips, PIECES)),
    ]


LINE_REFS = 13


class Line:
    def __init__(self, chips, refs):
        (
            self.slots,
            self.slot_recv,
            self.slot_send,
            self.own_sem,
            self.parts,
            self.from_core,
            self.from_left,
            self.from_right,
            self.core_send,
            self.core_recv,
            self.flow_send,
            self.left_recv,
            self.right_recv,
        ) = refs
        self.chips = chips
        me = lax.axis_index("fsdp")
        self.chip = me // 2
        self.core = me % 2
        self.tok = self.slots.shape[2]
        self.piece = self.tok // PIECES

    def place(self, chip, core):
        return chip * 2 + core

    def order(self, step):
        picked = 0
        for chip in range(self.chips):
            near = sorted(range(self.chips), key=lambda other: (abs(other - chip), other))
            picked = picked + jnp.where(self.chip == chip, near[step], 0)
        return picked

    def barrier(self):
        sem = pltpu.get_barrier_semaphore()

        def greet(place):
            pl.semaphore_signal(
                sem, inc=1, device_id={"fsdp": place}, device_id_type=pl.DeviceIdType.MESH
            )

        greet(self.place(self.chip, 1 - self.core))

        @pl.when(self.chip > 0)
        def _():
            greet(self.place(self.chip - 1, self.core))

        @pl.when(self.chip < self.chips - 1)
        def _():
            greet(self.place(self.chip + 1, self.core))

        ends = jnp.where(self.chip == 0, 1, 0) + jnp.where(self.chip == self.chips - 1, 1, 0)
        pl.semaphore_wait(sem, 3 - ends)

    def slot_copy(self, src, chip, way):
        place = (
            self.place(self.chip + 1, self.core),
            self.place(self.chip - 1, self.core),
            self.place(self.chip, 1 - self.core),
        )[way]
        return remote(
            src,
            self.slots.at[chip, self.core],
            self.slot_send.at[chip, way],
            self.slot_recv.at[chip, self.core],
            place,
        )

    def own_copy(self, own_ref):
        return pltpu.make_async_copy(own_ref, self.slots.at[self.chip, self.core], self.own_sem)

    def gather_begin(self, own_ref):
        @pl.when(self.chip < self.chips - 1)
        def _():
            self.slot_copy(own_ref, self.chip, 0).start()

        @pl.when(self.chip > 0)
        def _():
            self.slot_copy(own_ref, self.chip, 1).start()

        self.slot_copy(own_ref, self.chip, 2).start()
        self.own_copy(own_ref).start()

    def gather_step(self, distance):
        for chip, there, way, onward in (
            (self.chip - distance, self.chip >= distance, 0, self.chip < self.chips - 1),
            (self.chip + distance, self.chip + distance < self.chips, 1, self.chip > 0),
        ):

            @pl.when(there)
            def _(chip=chip, way=way, onward=onward):
                src = self.slots.at[chip, self.core]
                self.slot_copy(src, chip, way).wait_recv()

                @pl.when(onward)
                def _():
                    self.slot_copy(src, chip, way).start()

                self.slot_copy(src, chip, 2).start()

    def gather_other(self, chip):
        dst = self.slots.at[chip, 1 - self.core]
        remote(
            dst,
            dst,
            self.slot_send.at[chip, 2],
            self.slot_recv.at[chip, 1 - self.core],
            self.place(self.chip, 1 - self.core),
        ).wait_recv()

    def gather_end(self):
        for chip in range(self.chips):
            src = self.slots.at[chip, self.core]

            @pl.when((self.chip >= chip) & (self.chip < self.chips - 1))
            def _(src=src, chip=chip):
                self.slot_copy(src, chip, 0).wait_send()

            @pl.when((self.chip <= chip) & (self.chip > 0))
            def _(src=src, chip=chip):
                self.slot_copy(src, chip, 1).wait_send()

            self.slot_copy(src, chip, 2).wait_send()

    def core_copy(self, chip):
        return remote(
            self.parts.at[chip, 1 - self.core],
            self.from_core.at[chip],
            self.core_send.at[chip],
            self.core_recv.at[chip],
            self.place(self.chip, 1 - self.core),
        )

    def flow_copy(self, chip, piece, right):
        rows = pl.ds(piece * self.piece, self.piece)
        return remote(
            self.parts.at[chip, self.core, rows],
            (self.from_left if right else self.from_right).at[chip, rows],
            self.flow_send.at[chip, piece],
            (self.left_recv if right else self.right_recv).at[chip, piece],
            self.place(self.chip + (1 if right else -1), self.core),
        )

    def flow(self, chip, right, incoming):
        self.core_copy(chip).wait_recv()

        @pl.loop(0, PIECES)
        def _(piece):
            rows = pl.ds(pl.multiple_of(piece * self.piece, self.piece), self.piece)
            total = self.parts[chip, self.core, rows].astype(jnp.float32)
            total = total + self.from_core[chip, rows].astype(jnp.float32)
            if incoming:
                self.flow_copy(chip, piece, right).wait_recv()
                source = self.from_left if right else self.from_right
                total = total + source[chip, rows].astype(jnp.float32)
            self.parts[chip, self.core, rows] = total.astype(jnp.bfloat16)
            self.flow_copy(chip, piece, right).start()

    def scatter_first(self, chip):
        @pl.when((self.chip == 0) & (chip > 0))
        def _():
            self.flow(chip, True, False)

        @pl.when((self.chip == self.chips - 1) & (chip < self.chips - 1))
        def _():
            self.flow(chip, False, False)

    def scatter_rest(self, result_ref, between=None):
        for rank in range(3, 2 * self.chips - 2):
            right = rank - self.chip

            @pl.when((self.chip > 0) & (right > self.chip) & (right < self.chips))
            def _(right=right):
                self.flow(right, True, True)

            left = 2 * (self.chips - 1) - self.chip - rank

            @pl.when((self.chip < self.chips - 1) & (left < self.chip) & (left >= 0))
            def _(left=left):
                self.flow(left, False, True)

            if between is not None:
                between(rank)

        own = self.chip
        self.core_copy(own).wait_recv()

        @pl.loop(0, PIECES)
        def _(piece):
            rows = pl.ds(pl.multiple_of(piece * self.piece, self.piece), self.piece)
            total = self.parts[own, self.core, rows].astype(jnp.float32)
            total = total + self.from_core[own, rows].astype(jnp.float32)
            result_ref[rows] = total

        @pl.when(own > 0)
        def _():
            @pl.loop(0, PIECES)
            def _(piece):
                rows = pl.ds(pl.multiple_of(piece * self.piece, self.piece), self.piece)
                self.flow_copy(own, piece, True).wait_recv()
                result_ref[rows] += self.from_left[own, rows].astype(jnp.float32)

        @pl.when(own < self.chips - 1)
        def _():
            @pl.loop(0, PIECES)
            def _(piece):
                rows = pl.ds(pl.multiple_of(piece * self.piece, self.piece), self.piece)
                self.flow_copy(own, piece, False).wait_recv()
                result_ref[rows] += self.from_right[own, rows].astype(jnp.float32)

        for chip in range(self.chips):
            self.core_copy(chip).wait_send()

            @pl.when(self.chip != chip)
            def _(chip=chip):
                for piece in range(PIECES):
                    self.flow_copy(chip, piece, True).wait_send()


def ffn_forward_kernel(
    chips,
    own_ref,
    gateup_hbm,
    down_hbm,
    result_ref,
    all_hbm,
    hidden_hbm,
    act_hbm,
    slope_hbm,
    *scratch,
):
    line = Line(chips, scratch[:LINE_REFS])
    gateup, down, hidden, act, slope, load_sems, store_sems = scratch[LINE_REFS:]
    ff_part = down.shape[0]
    width = down.shape[1]
    pair = 2 * line.tok
    load_gateup = pltpu.make_async_copy(gateup_hbm, gateup, load_sems.at[0])
    load_down = pltpu.make_async_copy(down_hbm, down, load_sems.at[1])
    load_gateup.start()
    load_down.start()
    line.barrier()
    line.gather_begin(own_ref)
    line.own_copy(own_ref).wait()

    def stores(chip):
        rows = pl.ds(pl.multiple_of(chip * pair, pair), pair)
        return [
            pltpu.make_async_copy(line.slots.at[chip], all_hbm.at[chip], store_sems.at[chip, 0]),
            pltpu.make_async_copy(hidden.at[rows], hidden_hbm.at[rows], store_sems.at[chip, 1]),
            pltpu.make_async_copy(act.at[rows], act_hbm.at[rows], store_sems.at[chip, 2]),
            pltpu.make_async_copy(slope.at[rows], slope_hbm.at[rows], store_sems.at[chip, 3]),
        ]

    tile = 256
    for step in range(chips):
        if step > 0:
            line.gather_step(step)
        chip = line.order(step)
        line.gather_other(chip)
        if step == 0:
            load_gateup.wait()
            load_down.wait()
        rows = pl.ds(pl.multiple_of(chip * pair, pair), pair)

        @pl.loop(0, ff_part // tile)
        def _(at, chip=chip, rows=rows):
            inputs = line.slots[chip].reshape(pair, width)
            gate_cols = pl.ds(pl.multiple_of(at * tile, tile), tile)
            up_cols = pl.ds(pl.multiple_of(ff_part + at * tile, tile), tile)
            gate = dot_nn(inputs, gateup[:, gate_cols])
            up = dot_nn(inputs, gateup[:, up_cols])
            square = gate * gate
            bent = jnp.tanh(GELU_ROOT * gate * (1.0 + GELU_CUBE * square))
            half = 0.5 + 0.5 * bent
            activated = gate * half
            rise = half + 0.5 * gate * (1.0 - bent * bent) * (
                GELU_ROOT * (1.0 + 3.0 * GELU_CUBE * square)
            )
            hidden[rows, gate_cols] = (activated * up).astype(jnp.bfloat16)
            act[rows, gate_cols] = activated.astype(jnp.bfloat16)
            slope[rows, gate_cols] = (rise * up).astype(jnp.bfloat16)

        for copy in stores(chip):
            copy.start()

        wide = 512

        @pl.loop(0, width // wide)
        def _(at, chip=chip, rows=rows):
            cols = pl.ds(pl.multiple_of(at * wide, wide), wide)
            sums = dot_nn(hidden[rows, :], down[:, cols]).astype(jnp.bfloat16)
            line.parts[chip, :, :, cols] = sums.reshape(2, line.tok, wide)

        line.core_copy(chip).start()
        line.scatter_first(chip)
    line.scatter_rest(result_ref)
    line.gather_end()
    for chip in range(chips):
        for copy in stores(chip):
            copy.wait()


def ffn_forward(own, gateup, down, chips):
    tok_count, width = own.shape
    ff_part = down.shape[0]
    block = 2 * chips * tok_count
    bfloat = jnp.bfloat16
    anywhere = pl.BlockSpec(memory_space=pl.ANY)
    vmem = pl.BlockSpec(memory_space=pltpu.VMEM)
    part = jax.ShapeDtypeStruct((block, ff_part), bfloat)
    result, gathered, hidden, act, slope = pl.pallas_call(
        functools.partial(ffn_forward_kernel, chips),
        out_shape=[
            jax.ShapeDtypeStruct((tok_count, width), jnp.float32),
            jax.ShapeDtypeStruct((chips, 2, tok_count, width), bfloat),
            part,
            part,
            part,
        ],
        in_specs=[vmem, anywhere, anywhere],
        out_specs=[vmem, anywhere, anywhere, anywhere, anywhere],
        scratch_shapes=line_scratch(chips, tok_count, width)
        + [
            pltpu.VMEM(gateup.shape, bfloat),
            pltpu.VMEM(down.shape, bfloat),
            pltpu.VMEM((block, ff_part), bfloat),
            pltpu.VMEM((block, ff_part), bfloat),
            pltpu.VMEM((block, ff_part), bfloat),
            pltpu.SemaphoreType.DMA((2,)),
            pltpu.SemaphoreType.DMA((chips, 4)),
        ],
        compiler_params=pltpu.CompilerParams(
            collective_id=1, has_side_effects=True, vmem_limit_bytes=KERNEL_VMEM
        ),
        cost_estimate=pl.CostEstimate(
            flops=6 * block * width * ff_part,
            bytes_accessed=40 << 20,
            transcendentals=block * ff_part,
        ),
        name="ffn_forward",
    )(own, gateup, down)
    return result, gathered.reshape(block, width), hidden, act, slope


def ffn_backward_kernel(
    chips,
    own_ref,
    gateup_hbm,
    down_hbm,
    hidden_hbm,
    act_hbm,
    slope_hbm,
    inputs_hbm,
    pgate_hbm,
    pproj_hbm,
    result_ref,
    part_hbm,
    down_kept,
    pgate_kept,
    pproj_kept,
    *scratch,
):
    line = Line(chips, scratch[:LINE_REFS])
    scratch = scratch[LINE_REFS:]
    gateup, down, hidden, act, slope, inputs, grad, part_down, staged = scratch[:9]
    load_sems, store_sems, kept_sems = scratch[9:12]
    share = Summed(part_down, scratch[12 : 12 + SUM_REFS], False)
    small = [
        Summed(pgate_hbm, scratch[12 + SUM_REFS : 12 + 2 * SUM_REFS], True),
        Summed(pproj_hbm, scratch[12 + 2 * SUM_REFS :], True),
    ]
    ff_part = down.shape[0]
    width = down.shape[1]
    pair = 2 * line.tok
    loads = [
        pltpu.make_async_copy(src, dst, load_sems.at[at])
        for at, (src, dst) in enumerate(
            (
                (down_hbm, down),
                (act_hbm, act),
                (slope_hbm, slope),
                (gateup_hbm, gateup),
                (hidden_hbm, hidden),
                (inputs_hbm, inputs),
            )
        )
    ]
    for load in loads:
        load.start()
    greet_all()
    line.gather_begin(own_ref)
    for one in small:
        one.begin()
    line.own_copy(own_ref).wait()

    tile = 256
    wide = 512
    for step in range(chips):
        if step > 0:
            line.gather_step(step)
        chip = line.order(step)
        line.gather_other(chip)
        if step == 0:
            for load in loads[:4]:
                load.wait()
        rows = pl.ds(pl.multiple_of(chip * pair, pair), pair)

        @pl.loop(0, ff_part // tile)
        def _(at, chip=chip, rows=rows):
            grads = line.slots[chip].reshape(pair, width)
            gate_cols = pl.ds(pl.multiple_of(at * tile, tile), tile)
            up_cols = pl.ds(pl.multiple_of(ff_part + at * tile, tile), tile)
            grad_hidden = dot_nt(grads, down[gate_cols, :])
            grad[rows, gate_cols] = (
                grad_hidden * slope[rows, gate_cols].astype(jnp.float32)
            ).astype(jnp.bfloat16)
            grad[rows, up_cols] = (grad_hidden * act[rows, gate_cols].astype(jnp.float32)).astype(
                jnp.bfloat16
            )

        @pl.loop(0, width // wide)
        def _(at, chip=chip, rows=rows):
            cols = pl.ds(pl.multiple_of(at * wide, wide), wide)
            sums = dot_nt(grad[rows, :], gateup[cols, :]).astype(jnp.bfloat16)
            line.parts[chip, :, :, cols] = sums.reshape(2, line.tok, wide)

        line.core_copy(chip).start()
        line.scatter_first(chip)
    for one in small:
        one.middle()
    for load in loads[4:]:
        load.wait()

    block = chips * pair

    def down_grads():
        @pl.loop(0, ff_part // tile)
        def _(at):
            rows = pl.ds(pl.multiple_of(at * tile, tile), tile)
            left = hidden[:, rows]
            for start in range(0, width, wide):
                right = line.slots[:, :, :, start : start + wide].reshape(block, wide)
                part_down[rows, start : start + wide] = dot_tn(left, right).astype(jnp.bfloat16)

    def part_store(at):
        slot = at % 2
        return pltpu.make_async_copy(
            staged.at[slot], part_hbm.at[at], store_sems.at[slot]
        )

    def gateup_grads(first, last):
        @pl.loop(first, last)
        def _(at):
            cols = pl.ds(pl.multiple_of(at * tile, tile), tile)

            @pl.when(at >= 2)
            def _():
                part_store(at - 2).wait()

            left = inputs[:, cols]
            for start in range(0, 2 * ff_part, wide):
                staged[at % 2, :, start : start + wide] = dot_tn(
                    left, grad[:, start : start + wide]
                ).astype(jnp.bfloat16)
            part_store(at).start()

    tiles = width // tile
    done = [0]

    def between(rank):
        upto = min(tiles, done[0] + 2)
        gateup_grads(done[0], upto)
        done[0] = upto

    down_grads()
    share.begin()
    for one in small:
        one.finish()
    line.scatter_rest(result_ref, between)
    share.middle()
    gateup_grads(done[0], tiles)
    share.finish()
    stores = [
        pltpu.make_async_copy(one.own_rows(half), kept.at[half], kept_sems.at[at, half])
        for at, (one, kept) in enumerate(
            ((share, down_kept), (small[0], pgate_kept), (small[1], pproj_kept))
        )
        for half in (0, 1)
    ]
    for store in stores:
        store.start()
    line.gather_end()
    for one in [share] + small:
        one.sum_sent()
    for at in (tiles - 2, tiles - 1):
        part_store(at).wait()
    for store in stores:
        store.wait()


def ffn_backward(own, gateup, down, hidden, act, slope, inputs, pgate, pproj, chips):
    tok_count, width = own.shape
    ff_part = down.shape[0]
    block = 2 * chips * tok_count
    bfloat = jnp.bfloat16
    anywhere = pl.BlockSpec(memory_space=pl.ANY)
    vmem = pl.BlockSpec(memory_space=pltpu.VMEM)
    dma = pltpu.SemaphoreType.DMA
    tile = 256
    held = (gateup, down, hidden, act, slope, inputs)
    return pl.pallas_call(
        functools.partial(ffn_backward_kernel, chips),
        out_shape=[
            jax.ShapeDtypeStruct((tok_count, width), jnp.float32),
            jax.ShapeDtypeStruct((width // tile, tile, 2 * ff_part), bfloat),
            jax.ShapeDtypeStruct((2, ff_part // 8, width), bfloat),
        ]
        + [
            jax.ShapeDtypeStruct((2, one.shape[0], one.shape[1] // 8, one.shape[2]), bfloat)
            for one in (pgate, pproj)
        ],
        in_specs=[vmem] + [anywhere] * 8,
        out_specs=[vmem] + [anywhere] * 4,
        scratch_shapes=line_scratch(chips, tok_count, width)
        + [pltpu.VMEM(one.shape, bfloat) for one in held]
        + [
            pltpu.VMEM((block, 2 * ff_part), bfloat),
            pltpu.VMEM(down.shape, bfloat),
            pltpu.VMEM((2, tile, 2 * ff_part), bfloat),
            dma((6,)),
            dma((2,)),
            dma((3, 2)),
        ]
        + sum_scratch(down.shape)
        + sum_scratch(pgate.shape)
        + sum_scratch(pproj.shape),
        compiler_params=pltpu.CompilerParams(
            collective_id=2, has_side_effects=True, vmem_limit_bytes=KERNEL_VMEM
        ),
        cost_estimate=pl.CostEstimate(
            flops=12 * block * width * ff_part, bytes_accessed=40 << 20, transcendentals=0
        ),
        name="ffn_backward",
    )(own, *held, pgate, pproj)

def rope_norm(lin, gain, cosine, sine_part):
    scale = lax.rsqrt(jnp.mean(lin * lin, axis=-1, keepdims=True) + EPSILON)
    scaled = lin * scale * gain
    first, second = scaled[:, : HD // 2], scaled[:, HD // 2 :]
    return jnp.concatenate(
        [first * cosine - second * sine_part, second * cosine + first * sine_part], axis=-1
    )


class RowHeld:
    def __init__(self, kept, part):
        self.kept, self.part = kept, part

    def own_rows(self, half):
        return self.kept.at[half]

    def held(self, half, member):
        cols = pl.ds(pl.multiple_of(member * self.part, self.part), self.part)
        return self.kept.at[half, :, cols]


class SameHeld:
    def __init__(self, shard, spread_rows):
        self.shard, self.spread_rows = shard, spread_rows

    def own_rows(self, half):
        start, size = self.spread_rows(half)
        return self.shard.at[pl.ds(pl.multiple_of(start, size), size)]

    def held(self, half, member):
        return self.own_rows(half)


GAIN_ROWS = 24
POSITION_ROW = 12
QUERY_ROW = 13
KEY_ROW = 15


def attention_forward_kernel(
    chips,
    tokens_ref,
    packed_ref,
    frequency_ref,
    lengths_ref,
    query_weight,
    key_weight,
    value_weight,
    gate_weight,
    up_weight,
    out_hbm,
    small_hbm,
    result_ref,
    packed_all,
    cos_ref,
    sin_ref,
    head_gains_ref,
    all_hbm,
    qkv_hbm,
    gateup_hbm,
    lin_hbm,
    query_hbm,
    span_hbm,
    probs_hbm,
    attended_hbm,
    small_all,
    *scratch,
):
    scratch = list(scratch)
    line = Line(chips, scratch[:LINE_REFS])
    del scratch[:LINE_REFS]
    qkv_kept, gate_kept, up_kept = scratch[:3]
    wide_rows, narrow_rows, row_sem = scratch[3:6]
    own_ref, gains_send, gains_recv, query_docs, key_docs = scratch[6:11]
    del scratch[:11]
    ff_part = gate_kept.shape[2] // (2 * chips)
    spreads = []
    for held in (Held(qkv_kept), RowHeld(gate_kept, ff_part), RowHeld(up_kept, ff_part)):
        spreads.append(Spread(held, scratch[: spread_refs(True)], True))
        del scratch[: spread_refs(True)]
    qkv, gate, up = spreads
    small_held = SameHeld(small_hbm, lambda half: (small.own_start(half), small.eighth))
    small = Everywhere(small_held, scratch[: spread_refs(True)], True)
    del scratch[: spread_refs(True)]
    out, lin, query, span, probs, attended = scratch[:6]
    load_sem, store_sem, span_send, span_recv = scratch[6:]
    width = line.slots.shape[3]
    pair = 2 * line.tok
    block = chips * pair
    members = 2 * chips
    ctx_at = lax.axis_index("ctx")
    planes = lax.axis_size("ctx")
    me = lax.axis_index("fsdp")
    bfloat = jnp.bfloat16

    def row_load(weight, buffer, at):
        return [
            pltpu.make_async_copy(
                weight.at[pl.ds(pl.multiple_of(qkv.own_start(half), qkv.eighth), qkv.eighth)],
                buffer.at[half],
                row_sem.at[at, half],
            )
            for half in (0, 1)
        ]

    query_rows = row_load(query_weight, wide_rows.at[0, :, :, pl.ds(0, HQ * HD)], 0)
    key_rows = row_load(key_weight, narrow_rows.at[0], 1)
    value_rows = row_load(value_weight, narrow_rows.at[1], 2)
    gate_rows = row_load(gate_weight, wide_rows.at[1], 3)
    up_rows = row_load(up_weight, wide_rows.at[0], 4)
    for load in query_rows + key_rows + value_rows + gate_rows:
        load.start()
    load_out = pltpu.make_async_copy(out_hbm, out, load_sem)
    load_out.start()
    greet_all()

    def gains_copy(hop, source):
        return remote(
            packed_ref,
            packed_all.at[source],
            gains_send.at[hop],
            gains_recv.at[hop],
            lax.rem(me + hop, members),
        )

    for hop in range(1, members):
        gains_copy(hop, me).start()
    packed_all[me] = packed_ref[...]

    for load in query_rows + key_rows + value_rows:
        load.wait()
    for half in (0, 1):
        for member in range(members):
            head = member * KV // members
            qkv_kept[half, member, :, :HD] = wide_rows[
                0, half, :, member * HD : (member + 1) * HD
            ].astype(bfloat)
            for side in (0, 1):
                qkv_kept[half, member, :, (1 + side) * HD : (2 + side) * HD] = narrow_rows[
                    side, half, :, head * HD : (head + 1) * HD
                ].astype(bfloat)
    qkv.swap_begin()
    for load in up_rows:
        load.start()
    for hop in range(1, members):
        gains_copy(hop, lax.rem(me + members - hop, members)).wait_recv()

    inputs = tokens_ref[...].astype(jnp.float32)
    scale = lax.rsqrt(jnp.mean(inputs * inputs, axis=-1, keepdims=True) + EPSILON)
    gain = jnp.concatenate(
        [packed_all[member, row : row + 1] for member in range(members) for row in (0, 1)], axis=1
    )
    own_ref[...] = (inputs * scale * gain).astype(bfloat)
    line.gather_begin(own_ref)

    for load in gate_rows + up_rows:
        load.wait()
    gate_kept[...] = wide_rows[1].astype(bfloat)
    up_kept[...] = wide_rows[0].astype(bfloat)
    for at, row in ((0, QUERY_ROW), (1, KEY_ROW)):
        total = packed_all[0, row : row + 2]
        for member in range(1, members):
            total = total + packed_all[member, row : row + 2]
        head_gains_ref[at : at + 1] = jnp.concatenate([total[0:1], total[1:2]], axis=1)
    gain_query, gain_key = head_gains_ref[0:1], head_gains_ref[1:2]

    line.gather_step(1)
    qkv.swap_end()
    qkv.spread_begin()

    places = ctx_at * block + lax.broadcasted_iota(jnp.int32, (block, 1), 0)
    spots = ctx_at * block - WINDOW + lax.broadcasted_iota(jnp.int32, (1, WINDOW + block), 1)
    doc_end = 0
    query_doc = jnp.zeros(places.shape, jnp.int32)
    key_doc = jnp.where(spots >= 0, 0, -1)
    for doc in range(lengths_ref.shape[0] - 1):
        doc_end = doc_end + lengths_ref[doc]
        query_doc = query_doc + jnp.where(places >= doc_end, 1, 0)
        key_doc = key_doc + jnp.where(spots >= doc_end, 1, 0)
    query_docs[...] = query_doc
    key_docs[...] = key_doc
    positions = jnp.concatenate(
        [packed_all[member, POSITION_ROW : POSITION_ROW + 1] for member in range(members)], axis=0
    )
    columns = jnp.transpose(positions)
    for member in range(members):
        angle = columns[:, member : member + 1] * frequency_ref[...]
        token_rows = pl.ds(member * line.tok, line.tok)
        cos_ref[token_rows] = jnp.cos(angle)
        sin_ref[token_rows] = jnp.sin(angle)

    line.gather_step(2)
    small.swap_begin()
    gate.swap_begin()
    qkv.spread_on()
    for distance in range(3, chips):
        line.gather_step(distance)
    up.swap_begin()
    line.own_copy(own_ref).wait()
    for chip in range(chips):
        line.gather_other(chip)
    qkv.spread_end()
    stores = [
        pltpu.make_async_copy(line.slots, all_hbm, store_sem.at[0]),
        pltpu.make_async_copy(qkv.final, qkv_hbm, store_sem.at[1]),
        pltpu.make_async_copy(lin, lin_hbm, store_sem.at[2]),
        pltpu.make_async_copy(query, query_hbm, store_sem.at[3]),
        pltpu.make_async_copy(span, span_hbm, store_sem.at[4]),
        pltpu.make_async_copy(probs, probs_hbm, store_sem.at[5]),
        pltpu.make_async_copy(attended, attended_hbm, store_sem.at[6]),
        pltpu.make_async_copy(
            gate.final, gateup_hbm.at[:, :, pl.ds(0, ff_part)], store_sem.at[7]
        ),
        pltpu.make_async_copy(
            up.final, gateup_hbm.at[:, :, pl.ds(ff_part, ff_part)], store_sem.at[8]
        ),
        pltpu.make_async_copy(small.final, small_all, store_sem.at[9]),
    ]
    stores[0].start()
    stores[1].start()

    @pl.loop(0, chips)
    def _(chip):
        rows = pl.ds(pl.multiple_of(chip * pair, pair), pair)
        span_rows = pl.ds(pl.multiple_of(WINDOW + chip * pair, pair), pair)
        inputs = line.slots[chip].reshape(pair, width)
        weights = qkv.final[...].reshape(width, 3 * HD)
        key_lin = dot_nn(inputs, weights[:, HD : 2 * HD])
        lin[rows, HD : 2 * HD] = key_lin
        span[0, span_rows] = rope_norm(
            key_lin, gain_key, cos_ref[rows], sin_ref[rows]
        ).astype(bfloat)
        span[1, span_rows] = dot_nn(inputs, weights[:, 2 * HD :]).astype(bfloat)

    part = WINDOW // 2

    def span_copy(start, to_start, way, device):
        return pltpu.make_async_remote_copy(
            src_ref=span.at[:, pl.ds(pl.multiple_of(start, part), part)],
            dst_ref=span.at[:, pl.ds(pl.multiple_of(to_start, part), part)],
            send_sem=span_send.at[way],
            recv_sem=span_recv.at[way],
            device_id=device,
            device_id_type=pl.DeviceIdType.MESH,
        )

    mine = line.core * part
    others = (1 - line.core) * part
    onward = span_copy(block + mine, mine, 0, {"ctx": lax.rem(ctx_at + 1, planes)})
    across = span_copy(mine, mine, 1, {"fsdp": line.place(line.chip, 1 - line.core)})
    arrived = span_copy(others, others, 1, {"fsdp": line.place(line.chip, 1 - line.core)})

    @pl.when(ctx_at < planes - 1)
    def _():
        onward.start()

    @pl.when(ctx_at == 0)
    def _():
        span[:, pl.ds(0, WINDOW)] = jnp.zeros((2, WINDOW, HD), bfloat)

    @pl.loop(0, chips)
    def _(chip):
        rows = pl.ds(pl.multiple_of(chip * pair, pair), pair)
        inputs = line.slots[chip].reshape(pair, width)
        weights = qkv.final[...].reshape(width, 3 * HD)
        query_lin = dot_nn(inputs, weights[:, :HD])
        lin[rows, :HD] = query_lin
        rotated = rope_norm(query_lin, gain_query, cos_ref[rows], sin_ref[rows])
        query[rows] = (rotated.astype(bfloat).astype(jnp.float32) * SCORE_SCALE).astype(bfloat)

    @pl.when(ctx_at > 0)
    def _():
        onward.wait_recv()
        across.start()
        arrived.wait_recv()

    for store in stores[2:5]:
        store.start()
    load_out.wait()
    small.swap_on()

    span_len = WINDOW + pair
    for step in range(chips):
        chip = line.order(chips - 1 - step)
        rows = pl.ds(pl.multiple_of(chip * pair, pair), pair)
        span_rows = pl.ds(pl.multiple_of(chip * pair, pair), span_len)
        scores = dot_nt(query[rows], span[0, span_rows])
        distance = (
            WINDOW
            + lax.broadcasted_iota(jnp.int32, (pair, span_len), 0)
            - lax.broadcasted_iota(jnp.int32, (pair, span_len), 1)
        )
        visible = (
            (distance >= 0)
            & (distance < WINDOW)
            & (query_docs[rows] == key_docs[:, span_rows])
        )
        scores = jnp.where(visible, scores, NEGATIVE)
        shifted = jnp.exp(scores - jnp.max(scores, axis=-1, keepdims=True))
        prob = (shifted / jnp.sum(shifted, axis=-1, keepdims=True)).astype(bfloat)
        probs[rows] = prob
        attended[rows] = dot_nn(prob, span[1, span_rows]).astype(bfloat)

        wide = 512

        @pl.loop(0, width // wide)
        def _(at, chip=chip, rows=rows):
            cols = pl.ds(pl.multiple_of(at * wide, wide), wide)
            sums = dot_nn(attended[rows], out[:, cols]).astype(bfloat)
            line.parts[chip, :, :, cols] = sums.reshape(2, line.tok, wide)

        line.core_copy(chip).start()
        line.scatter_first(chip)
        if step == 0:
            gate.swap_end()
            gate.spread_begin()
            small.swap_end()
            small.spread_begin()
    for store in stores[5:7]:
        store.start()
    gate.spread_on()

    def between(rank):
        if rank == 3:
            up.swap_end()
            up.spread_begin()
            small.spread_on()
        if rank == 2 * chips - 3:
            up.spread_on()

    line.scatter_rest(result_ref, between)
    gate.spread_end()
    stores[7].start()
    up.spread_end()
    stores[8].start()
    small.spread_end()
    stores[9].start()
    line.gather_end()
    for hop in range(1, members):
        gains_copy(hop, me).wait_send()
    for spread in spreads + [small]:
        spread.spread_sent()

    @pl.when(ctx_at < planes - 1)
    def _():
        onward.wait_send()

    @pl.when(ctx_at > 0)
    def _():
        across.wait_send()

    for store in stores:
        store.wait()


def attention_forward(
    tokens, packed, frequency, lengths, query_weight, key_weight, value_weight, gate, up, out, small
):
    tok_count, width = tokens.shape
    rows = query_weight.shape[0]
    members = width // rows
    chips = members // 2
    block = members * tok_count
    span_len = WINDOW + block
    ff_part = gate.shape[1] // members
    bfloat = jnp.bfloat16
    anywhere = pl.BlockSpec(memory_space=pl.ANY)
    vmem = pl.BlockSpec(memory_space=pltpu.VMEM)
    dma = pltpu.SemaphoreType.DMA
    kept = [
        ((block, 2 * HD), jnp.float32),
        ((block, HD), bfloat),
        ((2, span_len, HD), bfloat),
        ((block, WINDOW + 2 * tok_count), bfloat),
        ((block, HD), bfloat),
    ]
    outputs = [
        ((tok_count, width), jnp.float32),
        ((members,) + packed.shape, jnp.float32),
        ((block, HD // 2), jnp.float32),
        ((block, HD // 2), jnp.float32),
        ((2, HD), jnp.float32),
        ((chips, 2, tok_count, width), bfloat),
        ((members, rows, 3 * HD), bfloat),
        ((members, rows, 2 * ff_part), bfloat),
    ] + kept + [((members,) + small.shape, bfloat)]
    return pl.pallas_call(
        functools.partial(attention_forward_kernel, chips),
        out_shape=[jax.ShapeDtypeStruct(*output) for output in outputs],
        in_specs=[vmem] * 3 + [pl.BlockSpec(memory_space=pltpu.SMEM)] + [anywhere] * 7,
        out_specs=[vmem] * 5 + [anywhere] * 9,
        scratch_shapes=line_scratch(chips, tok_count, width)
        + [
            pltpu.VMEM((2, members, rows // 8, 3 * HD), bfloat),
            pltpu.VMEM((2, rows // 8, gate.shape[1]), bfloat),
            pltpu.VMEM((2, rows // 8, gate.shape[1]), bfloat),
            pltpu.VMEM((2, 2, rows // 8, gate.shape[1]), jnp.float32),
            pltpu.VMEM((2, 2, rows // 8, KV * HD), jnp.float32),
            dma((5, 2)),
            pltpu.VMEM((tok_count, width), bfloat),
            dma((members,)),
            dma((members,)),
            pltpu.VMEM((block, 1), jnp.int32),
            pltpu.VMEM((1, span_len), jnp.int32),
        ]
        + spread_scratch((members, rows, 3 * HD))
        + spread_scratch((members, rows, ff_part))
        + spread_scratch((members, rows, ff_part))
        + everywhere_scratch((members,) + small.shape)
        + [pltpu.VMEM(out.shape, bfloat)]
        + [pltpu.VMEM(*one) for one in kept]
        + [dma, dma((10,)), dma((2,)), dma((2,))],
        compiler_params=pltpu.CompilerParams(
            collective_id=4, has_side_effects=True, vmem_limit_bytes=KERNEL_VMEM
        ),
        cost_estimate=pl.CostEstimate(
            flops=8 << 30, bytes_accessed=300 << 20, transcendentals=block * 1280
        ),
        name="attention_forward",
    )(
        tokens,
        packed,
        frequency,
        lengths,
        query_weight,
        key_weight,
        value_weight,
        gate,
        up,
        out,
        small,
    )

def rope_norm_back(grad, lin, gain, cosine, sine_part):
    first, second = grad[:, : HD // 2], grad[:, HD // 2 :]
    turned = jnp.concatenate(
        [first * cosine + second * sine_part, second * cosine - first * sine_part], axis=-1
    )
    scale = lax.rsqrt(jnp.mean(lin * lin, axis=-1, keepdims=True) + EPSILON)
    scaled = turned * gain
    along = jnp.mean(lin * scaled, axis=-1, keepdims=True)
    grad_lin = scale * scaled - lin * (scale * scale * scale * along)
    return grad_lin, jnp.sum(lin * scale * turned, axis=0, keepdims=True)


def attention_backward_kernel(
    chips,
    own_ref,
    out_hbm,
    qkv_hbm,
    lin_hbm,
    query_hbm,
    span_hbm,
    probs_hbm,
    cos_ref,
    sin_ref,
    gain_query_ref,
    gain_key_ref,
    gateup_hbm,
    down_kept,
    inputs_hbm,
    attended_hbm,
    result_ref,
    query_part_hbm,
    kv_part_hbm,
    out_part_hbm,
    gains_ref,
    gateup_kept,
    down_sum,
    *scratch,
):
    scratch = list(scratch)
    line = Line(chips, scratch[:LINE_REFS])
    del scratch[:LINE_REFS]
    gateup = Summed(gateup_hbm, scratch[:SUM_REFS], True)
    del scratch[:SUM_REFS]
    down = Spread(Held(down_kept), scratch[: spread_refs(False)], False)
    del scratch[: spread_refs(False)]
    out, qkv, lin, query, span, probs, grad, grad_span, back, across, returned = scratch[:11]
    load_sem, store_sem, back_send, back_recv, grad_out = scratch[11:16]
    inputs, attended, query_part, kv_part, out_part = scratch[16:]
    width = line.slots.shape[3]
    pair = 2 * line.tok
    block = chips * pair
    ctx_at = lax.axis_index("ctx")
    planes = lax.axis_size("ctx")
    bfloat = jnp.bfloat16
    loads = [
        pltpu.make_async_copy(src, dst, load_sem.at[at])
        for at, (src, dst) in enumerate(
            (
                (out_hbm, out),
                (span_hbm, span),
                (probs_hbm, probs),
                (lin_hbm, lin),
                (query_hbm, query),
                (qkv_hbm, qkv),
                (inputs_hbm, inputs),
                (attended_hbm, attended),
            )
        )
    ]
    for load in loads:
        load.start()
    greet_all()
    line.gather_begin(own_ref)
    gateup.begin()
    grad_span[...] = jnp.zeros_like(grad_span)
    gains_ref[...] = jnp.zeros_like(gains_ref)
    line.own_copy(own_ref).wait()
    for load in loads[:6]:
        load.wait()

    span_len = WINDOW + pair
    for step in range(chips):
        if step > 0:
            line.gather_step(step)
        chip = line.order(step)
        line.gather_other(chip)
        rows = pl.ds(pl.multiple_of(chip * pair, pair), pair)
        span_rows = pl.ds(pl.multiple_of(chip * pair, pair), span_len)
        grad_out[rows] = dot_nt(line.slots[chip].reshape(pair, width), out[...]).astype(bfloat)
        grad_prob = dot_nt(grad_out[rows], span[1, span_rows])
        prob = probs[rows].astype(jnp.float32)
        inner = jnp.sum(prob * grad_prob, axis=-1, keepdims=True)
        grad_score = (prob * (grad_prob - inner)).astype(bfloat)
        grad_query = dot_nn(grad_score, span[0, span_rows]) * SCORE_SCALE
        grad_lin, grad_gain = rope_norm_back(
            grad_query, lin[rows, :HD], gain_query_ref[...], cos_ref[rows], sin_ref[rows]
        )
        grad[rows, :HD] = grad_lin.astype(bfloat)
        gains_ref[0:1] += grad_gain
        grad_span[0, span_rows] += dot_tn(grad_score, query[rows])
        grad_span[1, span_rows] += dot_tn(probs[rows], grad_out[rows])

    part = WINDOW // 2
    mine, others = line.core * part, (1 - line.core) * part
    back[...] = grad_span[:, pl.ds(pl.multiple_of(others, part), part)].astype(bfloat)
    to_core = remote(
        back, across, back_send.at[0], back_recv.at[0], line.place(line.chip, 1 - line.core)
    )
    to_core.start()
    to_core.wait()
    total = grad_span[:, pl.ds(pl.multiple_of(mine, part), part)]
    back[...] = (total + across[...].astype(jnp.float32)).astype(bfloat)
    to_before = pltpu.make_async_remote_copy(
        src_ref=back,
        dst_ref=returned,
        send_sem=back_send.at[1],
        recv_sem=back_recv.at[1],
        device_id={"ctx": lax.rem(ctx_at + planes - 1, planes)},
        device_id_type=pl.DeviceIdType.MESH,
    )

    @pl.when(ctx_at > 0)
    def _():
        to_before.start()

    down.place_all()
    down.spread_begin()

    @pl.when(ctx_at < planes - 1)
    def _():
        to_before.wait_recv()
        here = pl.ds(pl.multiple_of(block + mine, part), part)
        grad_span[:, here] += returned[...].astype(jnp.float32)

    for step in range(chips):
        chip = line.order(chips - 1 - step)
        rows = pl.ds(pl.multiple_of(chip * pair, pair), pair)
        span_rows = pl.ds(pl.multiple_of(WINDOW + chip * pair, pair), pair)
        grad_lin, grad_gain = rope_norm_back(
            grad_span[0, span_rows], lin[rows, HD:], gain_key_ref[...], cos_ref[rows], sin_ref[rows]
        )
        grad[rows, HD : 2 * HD] = grad_lin.astype(bfloat)
        gains_ref[1:2] += grad_gain
        grad[rows, 2 * HD :] = grad_span[1, span_rows].astype(bfloat)

    wide = 512

    @pl.loop(0, width // wide)
    def _(at):
        cols = pl.ds(pl.multiple_of(at * wide, wide), wide)
        sums = dot_nt(grad[...], qkv[cols]).astype(bfloat)
        line.parts[:, :, :, cols] = sums.reshape(chips, 2, line.tok, wide)

    for step in range(chips):
        line.core_copy(line.order(chips - 1 - step)).start()
    for step in range(chips - 1):
        line.scatter_first(line.order(chips - 1 - step))
    for load in loads[6:]:
        load.wait()
    part_stores = [
        pltpu.make_async_copy(out_part, out_part_hbm, store_sem.at[0]),
        pltpu.make_async_copy(query_part, query_part_hbm, store_sem.at[1]),
        pltpu.make_async_copy(kv_part, kv_part_hbm, store_sem.at[5]),
    ]

    def between(rank):
        if rank == 3:
            for start in range(0, width, wide):
                right = line.slots[:, :, :, start : start + wide].reshape(block, wide)
                out_part[:, start : start + wide] = dot_tn(attended[...], right).astype(bfloat)
            part_stores[0].start()
        if rank == 4:

            @pl.loop(0, width // HD)
            def _(at):
                left = inputs[:, pl.ds(pl.multiple_of(at * HD, HD), HD)]
                query_part[at] = dot_tn(left, grad[:, :HD]).astype(bfloat)
                kv_part[at] = dot_tn(left, grad[:, HD:]).astype(bfloat)

            part_stores[1].start()
            part_stores[2].start()

    gateup.middle()
    down.spread_on()
    line.scatter_rest(result_ref, between)
    gateup.finish()
    stores = [
        pltpu.make_async_copy(gateup.own_rows(half), gateup_kept.at[half], store_sem.at[2 + half])
        for half in (0, 1)
    ]
    down.spread_end()
    stores.append(pltpu.make_async_copy(down.final, down_sum, store_sem.at[4]))
    for store in stores:
        store.start()
    line.gather_end()
    gateup.sum_sent()
    down.spread_sent()

    @pl.when(ctx_at > 0)
    def _():
        to_before.wait_send()

    for store in stores + part_stores:
        store.wait()


def attention_backward(
    own,
    out,
    qkv,
    lin,
    query,
    span,
    probs,
    cosine,
    sine_part,
    gain_query,
    gain_key,
    part_gateup,
    held_down,
    inputs,
    attended,
):
    tok_count, width = own.shape
    members = part_gateup.shape[0]
    chips = members // 2
    block = members * tok_count
    bfloat = jnp.bfloat16
    anywhere = pl.BlockSpec(memory_space=pl.ANY)
    vmem = pl.BlockSpec(memory_space=pltpu.VMEM)
    dma = pltpu.SemaphoreType.DMA
    eighth = part_gateup.shape[1] // 8
    down_shape = (8 * held_down.shape[1], held_down.shape[2])
    outputs = [
        ((tok_count, width), jnp.float32),
        ((members, HD, HD), bfloat),
        ((members, HD, 2 * HD), bfloat),
        ((HD, width), bfloat),
        ((2, HD), jnp.float32),
        ((2, members, eighth, part_gateup.shape[2]), bfloat),
        (down_shape, bfloat),
    ]
    half_span = (2, WINDOW // 2, HD)
    return pl.pallas_call(
        functools.partial(attention_backward_kernel, chips),
        out_shape=[jax.ShapeDtypeStruct(*output) for output in outputs],
        in_specs=[vmem] + [anywhere] * 6 + [vmem] * 4 + [anywhere] * 4,
        out_specs=[vmem, anywhere, anywhere, anywhere, vmem, anywhere, anywhere],
        scratch_shapes=line_scratch(chips, tok_count, width)
        + sum_scratch(part_gateup.shape)
        + spread_scratch(down_shape)
        + [pltpu.VMEM(one.shape, one.dtype) for one in (out, qkv, lin, query, span, probs)]
        + [
            pltpu.VMEM((block, 3 * HD), bfloat),
            pltpu.VMEM(span.shape, jnp.float32),
            pltpu.VMEM(half_span, bfloat),
            pltpu.VMEM(half_span, bfloat),
            pltpu.VMEM(half_span, bfloat),
            dma((8,)),
            dma((6,)),
            dma((2,)),
            dma((2,)),
            pltpu.VMEM((block, HD), bfloat),
            pltpu.VMEM((block, width), bfloat),
            pltpu.VMEM((block, HD), bfloat),
            pltpu.VMEM((members, HD, HD), bfloat),
            pltpu.VMEM((members, HD, 2 * HD), bfloat),
            pltpu.VMEM((HD, width), bfloat),
        ],
        compiler_params=pltpu.CompilerParams(
            collective_id=5, has_side_effects=True, vmem_limit_bytes=KERNEL_VMEM
        ),
        cost_estimate=pl.CostEstimate(
            flops=8 << 30, bytes_accessed=300 << 20, transcendentals=0
        ),
        name="attention_backward",
    )(
        own,
        out,
        qkv,
        lin,
        query,
        span,
        probs,
        cosine,
        sine_part,
        gain_query,
        gain_key,
        part_gateup,
        held_down,
        inputs,
        attended,
    )

def by_heads(
    tokens,
    per_layer,
    cotangent,
    doc_lengths,
    positions,
    w_query,
    w_key,
    w_value,
    w_out,
    laurel_left,
    laurel_right,
    w_gate,
    w_up,
    w_down,
    ple_gate,
    ple_proj,
    attn_in_gain,
    query_gain,
    key_gain,
    attn_out_gain,
    laurel_gain,
    ffn_in_gain,
    ffn_out_gain,
    ple_gain,
):
    bfloat = jnp.bfloat16
    ctx_count = lax.axis_size("ctx")
    fsdp_count = lax.axis_size("fsdp")
    tok_count = tokens.shape[0]
    block_len = tok_count * fsdp_count
    chips = fsdp_count // 2
    rows = w_query.shape[0]
    ff_part = w_gate.shape[1] // fsdp_count
    ctx_at = lax.axis_index("ctx")
    fsdp_at = lax.axis_index("fsdp")

    wide_gains = (attn_in_gain, attn_out_gain, laurel_gain, ffn_in_gain, ffn_out_gain, ple_gain)
    head_starts = fsdp_at * query_gain.shape[0]
    head_parts = [
        lax.dynamic_update_slice_in_dim(jnp.zeros((HD,), jnp.float32), gain, head_starts, 0)
        for gain in (query_gain, key_gain)
    ]
    packed = jnp.concatenate(list(wide_gains) + [positions.astype(jnp.float32)] + head_parts)
    packed = jnp.pad(packed, (0, GAIN_ROWS * 128 - packed.shape[0])).reshape(GAIN_ROWS, 128)
    frequency = jnp.exp(
        jnp.arange(HD // 2, dtype=jnp.float32) * (-2.0 * math.log(ROPE_BASE) / HD)
    )

    out_low = w_out.astype(bfloat)
    down_low = w_down.astype(bfloat)
    def in_halves(weight):
        return jnp.concatenate(jnp.split(weight.astype(bfloat), rows // 128, axis=0), axis=1)

    def in_stacks(weight):
        pieces = weight.astype(bfloat).reshape(weight.shape[0], 128 // weight.shape[0], -1)
        return jnp.transpose(pieces, (1, 0, 2)).reshape(128, -1)

    small = jnp.concatenate(
        [in_halves(ple_gate), in_stacks(ple_proj), in_halves(laurel_left), in_stacks(laurel_right)],
        axis=1,
    )

    inputs = tokens.astype(jnp.float32)
    ple_input = per_layer.astype(jnp.float32)
    (
        projected,
        packed_all,
        cosine,
        sine_part,
        head_gains,
        normed_all,
        qkv_full,
        gateup_full,
        qk_lin,
        query_low,
        span_kv,
        probs,
        attended_low,
        small_all,
    ) = attention_forward(
        tokens,
        packed,
        frequency[None, :],
        doc_lengths,
        w_query,
        w_key,
        w_value,
        w_gate,
        w_up,
        out_low,
        small,
    )
    small_ends = [0]
    for weight in (ple_gate, ple_proj, laurel_left, laurel_right):
        small_ends.append(small_ends[-1] + weight.size // 128)
    small_cols = [small_all[:, :, small_ends[n] : small_ends[n + 1]] for n in range(4)]

    def side_by_side(cols, shape):
        pieces = jnp.split(cols, cols.shape[2] // shape[1], axis=2)
        return jnp.concatenate(pieces, axis=1).reshape(-1, shape[1])

    def stacked(cols, shape):
        pieces = cols.reshape(fsdp_count, -1, shape[0], cols.shape[2])
        return jnp.transpose(pieces, (0, 2, 1, 3)).reshape(-1, shape[1])

    full_pgate = side_by_side(small_cols[0], ple_gate.shape)
    full_pproj = stacked(small_cols[1], ple_proj.shape)
    full_left = side_by_side(small_cols[2], laurel_left.shape)
    full_right = stacked(small_cols[3], laurel_right.shape)
    wide_rows = attn_in_gain.shape[0] // 128
    gain_in, gain_post, gain_laurel, gain_ffin, gain_ffout, gain_ple = (
        packed_all[:, n * wide_rows : (n + 1) * wide_rows].reshape(-1) for n in range(6)
    )
    normed, norm_back = jax.vjp(rms_norm, inputs, gain_in)
    normed_low = normed.astype(bfloat)
    normed_all = normed_all.reshape(block_len, -1)
    col_qkv = qkv_full.reshape(normed_all.shape[1], -1)
    col_gateup = gateup_full.reshape(normed_all.shape[1], -1)
    narrow_low = matmul(normed_low, full_left).astype(bfloat)
    widened = matmul(narrow_low, full_right)
    mixed, mix_back = jax.vjp(mix_piece, inputs, normed, projected, widened, gain_post, gain_laurel)
    ffn_normed, ffn_norm_back = jax.vjp(rms_norm, mixed, gain_ffin)
    down_lin, ffn_all, hidden_low, act_low, slope_low = ffn_forward(
        ffn_normed.astype(bfloat), col_gateup, down_low, chips
    )
    layer_mid, ffn_out_back = jax.vjp(ffn_out_piece, mixed, down_lin, gain_ffout)
    layer_low = layer_mid.astype(bfloat)
    ple_lin = matmul(layer_low, full_pgate)
    ple_mid, ple_back = jax.vjp(ple_act, ple_lin, ple_input)
    ple_low = ple_mid.astype(bfloat)
    ple_wide = matmul(ple_low, full_pproj)
    out_full, final_back = jax.vjp(final_piece, layer_mid, ple_wide, gain_ple)

    grad_layer, grad_pwide, grad_gple = final_back(cotangent.astype(jnp.float32))
    grad_pwide_low = grad_pwide.astype(bfloat)
    part_pproj = matmul_tn(ple_low, grad_pwide_low)
    grad_plemid = matmul_nt(grad_pwide_low, full_pproj)
    grad_plelin, grad_pleinput = ple_back(grad_plemid)
    grad_plelin_low = grad_plelin.astype(bfloat)
    part_pgate = matmul_tn(layer_low, grad_plelin_low)
    grad_layer = grad_layer + matmul_nt(grad_plelin_low, full_pgate)
    grad_mixed, grad_down, grad_gffout = ffn_out_back(grad_layer)
    grad_ffn, part_gateup, held_wdown, held_pgate, held_pproj = ffn_backward(
        grad_down.astype(bfloat),
        col_gateup,
        down_low,
        hidden_low,
        act_low,
        slope_low,
        ffn_all,
        part_pgate.astype(bfloat).reshape(fsdp_count, rows, -1),
        part_pproj.astype(bfloat).reshape(fsdp_count, 128, -1),
        chips,
    )
    part_gateup = part_gateup.reshape(fsdp_count, rows, -1)
    grad_mixed_more, grad_gffin = ffn_norm_back(grad_ffn)
    grad_mixed = grad_mixed + grad_mixed_more
    grad_in_first, grad_normed, grad_proj, grad_lwide, grad_gpost, grad_glaurel = mix_back(
        grad_mixed
    )
    grad_lwide_low = grad_lwide.astype(bfloat)
    part_right = matmul_tn(narrow_low, grad_lwide_low)
    grad_narrow_low = matmul_nt(grad_lwide_low, full_right).astype(bfloat)
    part_left = matmul_tn(normed_low, grad_narrow_low)
    grad_normed = grad_normed + matmul_nt(grad_narrow_low, full_left)

    (
        grad_normed_more,
        part_query,
        part_kv,
        part_wout,
        grad_head_gains,
        held_gateup,
        sum_wdown,
    ) = (
        attention_backward(
            grad_proj.astype(bfloat),
            out_low,
            col_qkv,
            qk_lin,
            query_low,
            span_kv,
            probs,
            cosine,
            sine_part,
            head_gains[0:1],
            head_gains[1:2],
            part_gateup,
            held_wdown,
            normed_all,
            attended_low,
        )
    )
    grad_gquery, grad_gkey = grad_head_gains[0], grad_head_gains[1]
    part_laurel = jnp.concatenate(
        [part.astype(bfloat).reshape(fsdp_count, 128, -1) for part in (part_left, part_right)],
        axis=2,
    )
    grad_normed = grad_normed + grad_normed_more
    grad_in_second, grad_gin = norm_back(grad_normed)
    grad_tokens = grad_in_first + grad_in_second

    grad_gains = [
        grad_gin,
        grad_gpost,
        grad_glaurel,
        grad_gffin,
        grad_gffout,
        grad_gple,
        grad_gquery,
        grad_gkey,
    ]
    gain_parts = jnp.concatenate([g.reshape(fsdp_count, -1) for g in grad_gains], axis=1)
    gain_parts = jnp.pad(gain_parts, ((0, 0), (0, 128 * 128 - gain_parts.shape[1])))
    gain_parts = gain_parts.astype(bfloat).reshape(fsdp_count, 128, 128)

    (
        sum_wgate,
        sum_wup,
        sum_wquery,
        sum_wkey,
        sum_wvalue,
        sum_wout,
        sum_pgate,
        sum_pproj,
        sum_laurel,
        sum_gains,
    ) = gradient_sum(
        [
            Source(held_gateup, summed=True, part=(0, 2), sides=1),
            Source(held_gateup, summed=True, part=(1, 2), sides=1),
            Source(part_query, sides=1),
            Source(part_kv, groups=KV, sides=2),
            Source(part_wout),
            Source(held_pgate, summed=True, groups=1, sides=1),
            Source(held_pproj, summed=True, groups=1, sides=1),
            Source(part_laurel, groups=1, sides=1),
            Source(gain_parts, groups=1),
        ]
    )
    gain_sums = sum_gains.astype(jnp.float32).reshape(-1)
    wide_size, head_size = attn_in_gain.shape[0], query_gain.shape[0]
    wide_sums = gain_sums[: 6 * wide_size].reshape(6, wide_size)
    head_sums = gain_sums[6 * wide_size : 6 * wide_size + 2 * head_size].reshape(2, head_size)
    grad_wgate = sum_wgate.astype(jnp.float32)
    grad_wup = sum_wup.astype(jnp.float32)
    grad_wdown = sum_wdown.astype(jnp.float32)
    grad_wout = sum_wout.astype(jnp.float32)
    grad_wquery = sum_wquery.astype(jnp.float32)
    grad_wkey = sum_wkey.astype(jnp.float32)
    grad_wvalue = sum_wvalue.astype(jnp.float32)
    grad_pgate = sum_pgate.astype(jnp.float32)
    grad_pproj = sum_pproj.astype(jnp.float32).reshape(ple_proj.shape)
    left_part = sum_laurel.shape[1] // 2
    grad_wleft = sum_laurel[:, :left_part].astype(jnp.float32).reshape(laurel_left.shape)
    grad_wright = sum_laurel[:, left_part:].astype(jnp.float32).reshape(laurel_right.shape)
    return (
        out_full.astype(bfloat),
        grad_tokens,
        grad_pleinput,
        grad_wquery,
        grad_wkey,
        grad_wvalue,
        grad_wout,
        grad_wleft,
        grad_wright,
        grad_wgate,
        grad_wup,
        grad_wdown,
        grad_pgate,
        grad_pproj,
        wide_sums[0],
        head_sums[0],
        head_sums[1],
        *(wide_sums[n] for n in range(1, 6)),
    )


def solution(mesh):
    in_specs = (
        P(("ctx", "fsdp"), None),
        P(("ctx", "fsdp"), None),
        P(("ctx", "fsdp"), None),
        P(),
        P(("ctx", "fsdp")),
        P("fsdp", None),
        P("fsdp", None),
        P("fsdp", None),
        P("fsdp", None),
        P("fsdp", None),
        P("fsdp", None),
        P("fsdp", None),
        P("fsdp", None),
        P("fsdp", None),
        P("fsdp", None),
        P("fsdp", None),
        P("fsdp"),
        P("fsdp"),
        P("fsdp"),
        P("fsdp"),
        P("fsdp"),
        P("fsdp"),
        P("fsdp"),
        P("fsdp"),
    )
    out_specs = (
        P(("ctx", "fsdp"), None),
        P(("ctx", "fsdp"), None),
        P(("ctx", "fsdp"), None),
        P("fsdp", None),
        P("fsdp", None),
        P("fsdp", None),
        P("fsdp", None),
        P("fsdp", None),
        P("fsdp", None),
        P("fsdp", None),
        P("fsdp", None),
        P("fsdp", None),
        P("fsdp", None),
        P("fsdp", None),
        P("fsdp"),
        P("fsdp"),
        P("fsdp"),
        P("fsdp"),
        P("fsdp"),
        P("fsdp"),
        P("fsdp"),
        P("fsdp"),
    )
    run = by_heads if mesh.shape["fsdp"] == HQ and mesh.shape["ctx"] == 4 else local
    return jax.shard_map(run, mesh=mesh, in_specs=in_specs, out_specs=out_specs, check_vma=False)
```

```python
import dataclasses
import functools
import math

import jax
import jax.numpy as jnp
from jax import lax
from jax.experimental import pallas as pl
from jax.experimental.pallas import tpu as pltpu
from jax.sharding import PartitionSpec as P

HQ = 8
KV = 2
HD = 256
WINDOW = 1024


EPSILON = 1e-06
NEGATIVE = -1e30
ROPE_BASE = 10000.0
HALF_ROOT = 1.0 / math.sqrt(2.0)
GELU_ROOT = math.sqrt(2.0 / math.pi)
GELU_CUBE = 0.044715
SCORE_SCALE = 1.0 / math.sqrt(HD)
KERNEL_VMEM = 62 << 20


def passed_along(block, axis, distance):
    devices = range(lax.axis_size(axis))
    route = [(i - distance, i) for i in devices if i - distance in devices]
    return lax.ppermute(block, axis, route)


def matmul(left_mat, right_mat):
    return jnp.dot(left_mat, right_mat, preferred_element_type=jnp.float32)


def matmul_tn(left_mat, right_mat):
    return lax.dot_general(
        left_mat, right_mat, (((0,), (0,)), ((), ())), preferred_element_type=jnp.float32
    )


def matmul_nt(left_mat, right_mat):
    return lax.dot_general(
        left_mat, right_mat, (((1,), (1,)), ((), ())), preferred_element_type=jnp.float32
    )


def rms_norm(values, gain_vec):
    return (
        values * lax.rsqrt(jnp.mean(values * values, axis=-1, keepdims=True) + EPSILON) * gain_vec
    )


def rope_tables(positions, width):
    half_width = width // 2
    frequency = jnp.exp(
        jnp.arange(half_width, dtype=jnp.float32) * (-2.0 * math.log(ROPE_BASE) / width)
    )
    angles = positions.astype(jnp.float32)[:, None] * frequency[None, :]
    return (jnp.cos(angles)[:, None, :], jnp.sin(angles)[:, None, :])


def rotate(values, cosine, sine_part):
    half_width = values.shape[-1] // 2
    first_half = values[..., :half_width]
    second_half = values[..., half_width:]
    return jnp.concatenate(
        [
            first_half * cosine - second_half * sine_part,
            second_half * cosine + first_half * sine_part,
        ],
        axis=-1,
    )


def document_ids(doc_lengths, places):
    doc_ends = jnp.cumsum(doc_lengths)
    return jnp.sum((places[:, None] >= doc_ends[None, :-1]).astype(jnp.int32), axis=1)


def query_key(cosine, sine_part, query_lin, key_lin, gain_query, gain_key):
    tok_count = query_lin.shape[0]
    query_rot = rotate(
        rms_norm(query_lin.reshape(tok_count, HQ, HD), gain_query), cosine, sine_part
    )
    key_rot = rotate(rms_norm(key_lin.reshape(tok_count, KV, HD), gain_key), cosine, sine_part)
    return (query_rot, key_rot)


def mix_piece(inputs, normed, projected, widened, gain_post, gain_laurel):
    return (
        inputs + rms_norm(projected, gain_post) + normed + rms_norm(widened, gain_laurel)
    ) * HALF_ROOT


def geglu(gate_lin, up_lin):
    return jax.nn.gelu(gate_lin, approximate=True) * up_lin


def ffn_out_piece(mixed, down_lin, gain_ffout):
    return mixed + rms_norm(down_lin, gain_ffout)


def ple_act(ple_lin, ple_input):
    return jax.nn.gelu(ple_lin, approximate=True) * ple_input


def final_piece(layer_mid, ple_wide, gain_ple):
    return layer_mid + rms_norm(ple_wide, gain_ple)


def visibility(doc_lengths, query_start, key_start, tok_count, span_len):
    query_places = query_start + jnp.arange(tok_count, dtype=jnp.int32)
    key_places = key_start + jnp.arange(span_len, dtype=jnp.int32)
    distance = query_places[:, None] - key_places[None, :]
    query_docs = document_ids(doc_lengths, query_places)
    key_docs = document_ids(doc_lengths, key_places)
    return (
        (distance >= 0)
        & (distance < WINDOW)
        & (key_places[None, :] >= 0)
        & (query_docs[:, None] == key_docs[None, :])
    )


def attend_forward(query_low, span_kv, visible):
    tok_count = query_low.shape[0]
    scale_factor = 1.0 / math.sqrt(HD)
    scores = (
        jnp.einsum("tkgh,skh->kgts", query_low, span_kv[0], preferred_element_type=jnp.float32)
        * scale_factor
    )
    scores = jnp.where(visible, scores, NEGATIVE)
    row_top = jnp.max(scores, axis=-1, keepdims=True)
    shifted = jnp.exp(scores - row_top)
    row_total = jnp.sum(shifted, axis=-1, keepdims=True)
    attn_probs = shifted / row_total
    attended = jnp.einsum(
        "kgts,skh->tkgh",
        attn_probs.astype(jnp.bfloat16),
        span_kv[1],
        preferred_element_type=jnp.float32,
    )
    return (attended.reshape(tok_count, -1), row_top + jnp.log(row_total))


def attend_backward(query_low, span_kv, visible, log_total, grad_out_low):
    scale_factor = 1.0 / math.sqrt(HD)
    scores = (
        jnp.einsum("tkgh,skh->kgts", query_low, span_kv[0], preferred_element_type=jnp.float32)
        * scale_factor
    )
    attn_probs = jnp.where(visible, jnp.exp(jnp.where(visible, scores, NEGATIVE) - log_total), 0.0)
    grad_probs = jnp.einsum(
        "tkgh,skh->kgts", grad_out_low, span_kv[1], preferred_element_type=jnp.float32
    )
    inner_sum = jnp.sum(attn_probs * grad_probs, axis=-1, keepdims=True)
    grad_scores = (attn_probs * (grad_probs - inner_sum)).astype(jnp.bfloat16)
    grad_query = (
        jnp.einsum("kgts,skh->tkgh", grad_scores, span_kv[0], preferred_element_type=jnp.float32)
        * scale_factor
    )
    grad_keys = (
        jnp.einsum("kgts,tkgh->skh", grad_scores, query_low, preferred_element_type=jnp.float32)
        * scale_factor
    )
    grad_values = jnp.einsum(
        "kgts,tkgh->skh",
        attn_probs.astype(jnp.bfloat16),
        grad_out_low,
        preferred_element_type=jnp.float32,
    )
    return (grad_query, jnp.stack([grad_keys, grad_values]))


def settle(act_low, grad_low):
    act_cols = lax.all_to_all(act_low, "fsdp", split_axis=1, concat_axis=0, tiled=True)
    shard_rows = matmul_tn(act_cols, lax.all_gather(grad_low, "fsdp", axis=0, tiled=True))
    return lax.psum(shard_rows.astype(jnp.bfloat16), "ctx").astype(jnp.float32)


def local(
    tokens,
    per_layer,
    cotangent,
    doc_lengths,
    positions,
    w_query,
    w_key,
    w_value,
    w_out,
    laurel_left,
    laurel_right,
    w_gate,
    w_up,
    w_down,
    ple_gate,
    ple_proj,
    attn_in_gain,
    query_gain,
    key_gain,
    attn_out_gain,
    laurel_gain,
    ffn_in_gain,
    ffn_out_gain,
    ple_gain,
):
    bfloat = jnp.bfloat16
    tok_count = tokens.shape[0]
    span_len = WINDOW + tok_count
    groups = HQ // KV
    dev_index = lax.axis_index("ctx") * lax.axis_size("fsdp") + lax.axis_index("fsdp")
    query_start = dev_index * tok_count
    key_start = query_start - WINDOW
    visible = visibility(doc_lengths, query_start, key_start, tok_count, span_len)
    cosine, sine_part = rope_tables(positions, HD)
    gain_in, gain_query, gain_key, gain_post, gain_laurel, gain_ffin, gain_ffout, gain_ple = (
        lax.all_gather(attn_in_gain, "fsdp", axis=0, tiled=True),
        lax.all_gather(query_gain, "fsdp", axis=0, tiled=True),
        lax.all_gather(key_gain, "fsdp", axis=0, tiled=True),
        lax.all_gather(attn_out_gain, "fsdp", axis=0, tiled=True),
        lax.all_gather(laurel_gain, "fsdp", axis=0, tiled=True),
        lax.all_gather(ffn_in_gain, "fsdp", axis=0, tiled=True),
        lax.all_gather(ffn_out_gain, "fsdp", axis=0, tiled=True),
        lax.all_gather(ple_gain, "fsdp", axis=0, tiled=True),
    )
    full_query, full_key, full_value, full_out, full_left, full_right = (
        lax.all_gather(w_query.astype(bfloat), "fsdp", axis=0, tiled=True),
        lax.all_gather(w_key.astype(bfloat), "fsdp", axis=0, tiled=True),
        lax.all_gather(w_value.astype(bfloat), "fsdp", axis=0, tiled=True),
        lax.all_gather(w_out.astype(bfloat), "fsdp", axis=0, tiled=True),
        lax.all_gather(laurel_left.astype(bfloat), "fsdp", axis=0, tiled=True),
        lax.all_gather(laurel_right.astype(bfloat), "fsdp", axis=0, tiled=True),
    )
    inputs = tokens.astype(jnp.float32)
    ple_input = per_layer.astype(jnp.float32)
    normed, norm_back = jax.vjp(rms_norm, inputs, gain_in)
    normed_low = normed.astype(bfloat)
    query_lin = matmul(normed_low, full_query)
    key_lin = matmul(normed_low, full_key)
    value_lin = matmul(normed_low, full_value)
    (query_rot, key_rot), rope_back = jax.vjp(
        functools.partial(query_key, cosine, sine_part), query_lin, key_lin, gain_query, gain_key
    )
    query_low = query_rot.astype(bfloat).reshape(tok_count, KV, groups, HD)
    keys_values = jnp.stack(
        [key_rot.astype(bfloat), value_lin.astype(bfloat).reshape(tok_count, KV, HD)]
    )
    block_kv = lax.all_gather(keys_values, "fsdp", axis=1, tiled=True)
    block_len = block_kv.shape[1]
    before_kv = passed_along(block_kv, "ctx", 1)
    span_offset = block_len + lax.axis_index("fsdp") * tok_count - WINDOW
    span_kv = lax.dynamic_slice_in_dim(
        jnp.concatenate([before_kv, block_kv], axis=1), span_offset, span_len, 1
    )
    attended, log_total = attend_forward(query_low, span_kv, visible)
    attended_low = attended.astype(bfloat)
    projected = matmul(attended_low, full_out)
    narrow_low = matmul(normed_low, full_left).astype(bfloat)
    widened = matmul(narrow_low, full_right)
    mixed, mix_back = jax.vjp(mix_piece, inputs, normed, projected, widened, gain_post, gain_laurel)
    full_gate, full_up, full_down, full_pgate, full_pproj = (
        lax.all_gather(w_gate.astype(bfloat), "fsdp", axis=0, tiled=True),
        lax.all_gather(w_up.astype(bfloat), "fsdp", axis=0, tiled=True),
        lax.all_gather(w_down.astype(bfloat), "fsdp", axis=0, tiled=True),
        lax.all_gather(ple_gate.astype(bfloat), "fsdp", axis=0, tiled=True),
        lax.all_gather(ple_proj.astype(bfloat), "fsdp", axis=0, tiled=True),
    )
    ffn_normed, ffn_norm_back = jax.vjp(rms_norm, mixed, gain_ffin)
    ffn_low = ffn_normed.astype(bfloat)
    gate_lin = matmul(ffn_low, full_gate)
    up_lin = matmul(ffn_low, full_up)
    hidden, geglu_back = jax.vjp(geglu, gate_lin, up_lin)
    hidden_low = hidden.astype(bfloat)
    down_lin = matmul(hidden_low, full_down)
    layer_mid, ffn_out_back = jax.vjp(ffn_out_piece, mixed, down_lin, gain_ffout)
    layer_low = layer_mid.astype(bfloat)
    ple_lin = matmul(layer_low, full_pgate)
    ple_mid, ple_back = jax.vjp(ple_act, ple_lin, ple_input)
    ple_low = ple_mid.astype(bfloat)
    ple_wide = matmul(ple_low, full_pproj)
    out_full, final_back = jax.vjp(final_piece, layer_mid, ple_wide, gain_ple)
    full_gate, full_up, full_down, full_pgate, full_pproj = (
        lax.all_gather(w_gate.astype(bfloat), "fsdp", axis=0, tiled=True),
        lax.all_gather(w_up.astype(bfloat), "fsdp", axis=0, tiled=True),
        lax.all_gather(w_down.astype(bfloat), "fsdp", axis=0, tiled=True),
        lax.all_gather(ple_gate.astype(bfloat), "fsdp", axis=0, tiled=True),
        lax.all_gather(ple_proj.astype(bfloat), "fsdp", axis=0, tiled=True),
    )
    grad_layer, grad_pwide, grad_gple = final_back(cotangent.astype(jnp.float32))
    grad_pwide_low = grad_pwide.astype(bfloat)
    grad_pproj = settle(ple_low, grad_pwide_low)
    grad_plemid = matmul_nt(grad_pwide_low, full_pproj)
    grad_plelin, grad_pleinput = ple_back(grad_plemid)
    grad_plelin_low = grad_plelin.astype(bfloat)
    grad_pgate = settle(layer_low, grad_plelin_low)
    grad_layer = grad_layer + matmul_nt(grad_plelin_low, full_pgate)
    grad_mixed, grad_down, grad_gffout = ffn_out_back(grad_layer)
    grad_down_low = grad_down.astype(bfloat)
    grad_wdown = settle(hidden_low, grad_down_low)
    grad_hidden = matmul_nt(grad_down_low, full_down)
    grad_gate, grad_up = geglu_back(grad_hidden)
    grad_gate_low = grad_gate.astype(bfloat)
    grad_up_low = grad_up.astype(bfloat)
    grad_wgate = settle(ffn_low, grad_gate_low)
    grad_wup = settle(ffn_low, grad_up_low)
    grad_ffn = matmul_nt(grad_gate_low, full_gate) + matmul_nt(grad_up_low, full_up)
    grad_mixed_more, grad_gffin = ffn_norm_back(grad_ffn)
    grad_mixed = grad_mixed + grad_mixed_more
    full_query, full_key, full_value, full_out, full_left, full_right = (
        lax.all_gather(w_query.astype(bfloat), "fsdp", axis=0, tiled=True),
        lax.all_gather(w_key.astype(bfloat), "fsdp", axis=0, tiled=True),
        lax.all_gather(w_value.astype(bfloat), "fsdp", axis=0, tiled=True),
        lax.all_gather(w_out.astype(bfloat), "fsdp", axis=0, tiled=True),
        lax.all_gather(laurel_left.astype(bfloat), "fsdp", axis=0, tiled=True),
        lax.all_gather(laurel_right.astype(bfloat), "fsdp", axis=0, tiled=True),
    )
    grad_in_first, grad_normed, grad_proj, grad_lwide, grad_gpost, grad_glaurel = mix_back(
        grad_mixed
    )
    grad_proj_low = grad_proj.astype(bfloat)
    grad_wout = settle(attended_low, grad_proj_low)
    grad_att_low = matmul_nt(grad_proj_low, full_out).astype(bfloat)
    grad_lwide_low = grad_lwide.astype(bfloat)
    grad_wright = settle(narrow_low, grad_lwide_low)
    grad_narrow_low = matmul_nt(grad_lwide_low, full_right).astype(bfloat)
    grad_wleft = settle(normed_low, grad_narrow_low)
    grad_normed = grad_normed + matmul_nt(grad_narrow_low, full_left)
    grad_query_att, grad_span = attend_backward(
        query_low, span_kv, visible, log_total, grad_att_low.reshape(tok_count, KV, groups, HD)
    )
    whole_grad = jnp.zeros((2, 2 * block_len, KV, HD), jnp.float32)
    whole_grad = lax.dynamic_update_slice_in_dim(whole_grad, grad_span, span_offset, 1)
    returned = passed_along(whole_grad[:, :block_len].astype(jnp.bfloat16), "ctx", -1).astype(
        jnp.float32
    )
    own_grad = lax.psum_scatter(
        (whole_grad[:, block_len:] + returned).astype(jnp.bfloat16),
        "fsdp",
        scatter_dimension=1,
        tiled=True,
    ).astype(jnp.float32)
    grad_qlin, grad_klin, grad_gquery, grad_gkey = rope_back(
        (grad_query_att.reshape(tok_count, HQ, HD), own_grad[0])
    )
    grad_qlin_low = grad_qlin.astype(bfloat)
    grad_klin_low = grad_klin.astype(bfloat)
    grad_vlin_low = own_grad[1].reshape(tok_count, KV * HD).astype(bfloat)
    grad_wquery = settle(normed_low, grad_qlin_low)
    grad_wkey = settle(normed_low, grad_klin_low)
    grad_wvalue = settle(normed_low, grad_vlin_low)
    grad_normed = (
        grad_normed
        + matmul_nt(grad_qlin_low, full_query)
        + matmul_nt(grad_klin_low, full_key)
        + matmul_nt(grad_vlin_low, full_value)
    )
    grad_in_second, grad_gin = norm_back(grad_normed)
    grad_tokens = grad_in_first + grad_in_second
    sum_gin, sum_gquery, sum_gkey, sum_gpost, sum_glaurel, sum_gffin, sum_gffout, sum_gple = (
        lax.psum(
            (
                grad_gin,
                grad_gquery,
                grad_gkey,
                grad_gpost,
                grad_glaurel,
                grad_gffin,
                grad_gffout,
                grad_gple,
            ),
            ("ctx", "fsdp"),
        )
    )
    wide_rows = attn_in_gain.shape[0]
    head_rows = query_gain.shape[0]
    wide_start = lax.axis_index("fsdp") * wide_rows
    head_start = lax.axis_index("fsdp") * head_rows

    def wide_part(full_vec):
        return lax.dynamic_slice_in_dim(full_vec, wide_start, wide_rows, 0)

    def head_part(full_vec):
        return lax.dynamic_slice_in_dim(full_vec, head_start, head_rows, 0)

    return (
        out_full.astype(bfloat),
        grad_tokens,
        grad_pleinput,
        grad_wquery,
        grad_wkey,
        grad_wvalue,
        grad_wout,
        grad_wleft,
        grad_wright,
        grad_wgate,
        grad_wup,
        grad_wdown,
        grad_pgate,
        grad_pproj,
        wide_part(sum_gin),
        head_part(sum_gquery),
        head_part(sum_gkey),
        wide_part(sum_gpost),
        wide_part(sum_glaurel),
        wide_part(sum_gffin),
        wide_part(sum_gffout),
        wide_part(sum_gple),
    )

class Plane:
    def locate(self, columns, rows):
        self.columns = columns
        at = lax.axis_index("ctx")
        self.at_x, self.at_y = at % 2, at // 2
        self.beside = (at + 1 - 2 * (at % 2), (at + 2) % 4)
        self.me = lax.axis_index("fsdp")
        self.members = lax.axis_size("fsdp")
        self.half = rows // 2
        self.quarter = rows // 4
        self.eighth = rows // 8

    def rows(self, ref, start, size):
        start = pl.multiple_of(start, size)
        return ref.at[:, pl.ds(start, size)] if self.columns else ref.at[pl.ds(start, size)]

    def sides(self, half):
        return (self.at_x, self.at_y) if half == 0 else (self.at_y, self.at_x)

    def kept_start(self, half):
        return half * self.half + self.sides(half)[0] * self.quarter

    def given_start(self, half):
        return half * self.half + (1 - self.sides(half)[0]) * self.quarter

    def own_start(self, half):
        return self.kept_start(half) + self.sides(half)[1] * self.eighth

    def copy(self, src, dst, send_sem, recv_sem, half, stage):
        return pltpu.make_async_remote_copy(
            src_ref=src,
            dst_ref=dst,
            send_sem=send_sem.at[half, stage],
            recv_sem=recv_sem.at[half, stage],
            device_id={"ctx": self.beside[(half + stage) % 2]},
            device_id_type=pl.DeviceIdType.MESH,
        )


class Summed(Plane):
    def __init__(self, source, refs, columns):
        self.source = source
        self.kept, self.taken, self.last, self.load_sem, self.sum_send, self.sum_recv = refs
        self.locate(columns, source.shape[-2])

    def load(self, half):
        return pltpu.make_async_copy(
            self.rows(self.source, self.kept_start(half), self.quarter),
            self.kept.at[half],
            self.load_sem.at[half],
        )

    def first(self, half):
        return self.copy(
            self.rows(self.source, self.given_start(half), self.quarter),
            self.taken.at[half],
            self.sum_send,
            self.sum_recv,
            half,
            0,
        )

    def second(self, half):
        other = (1 - self.sides(half)[1]) * self.eighth
        return self.copy(
            self.rows(self.kept.at[half], other, self.eighth),
            self.last.at[half],
            self.sum_send,
            self.sum_recv,
            half,
            1,
        )

    def begin(self):
        for half in (0, 1):
            self.first(half).start()
            self.load(half).start()

    def add(self, half, start, more, more_start):
        step = min(32, self.eighth)
        blocks = self.eighth // step
        layers = self.source.shape[0] if self.columns else 1

        @pl.loop(0, layers * blocks)
        def _(at):
            layer, block = at // blocks, at % blocks
            here = pl.ds(pl.multiple_of(start + block * step, step), step)
            there = pl.ds(pl.multiple_of(more_start + block * step, step), step)
            if self.columns:
                self.kept[half, layer, here] += more[half, layer, there]
            else:
                self.kept[half, here] += more[half, there]

    def middle(self):
        for half in (0, 1):
            self.load(half).wait()
            self.first(half).wait_recv()
            side = self.sides(half)[1]
            other = (1 - side) * self.eighth
            self.add(half, other, self.taken, other)
            self.second(half).start()
            mine = side * self.eighth
            self.add(half, mine, self.taken, mine)

    def finish(self):
        for half in (0, 1):
            self.second(half).wait_recv()
            self.add(half, self.sides(half)[1] * self.eighth, self.last, 0)

    def own_rows(self, half):
        return self.rows(self.kept.at[half], self.sides(half)[1] * self.eighth, self.eighth)

    def held(self, half, member):
        side = self.sides(half)[1] * self.eighth
        return self.kept.at[half, member, pl.ds(pl.multiple_of(side, self.eighth), self.eighth)]

    def sum_sent(self):
        for half in (0, 1):
            self.first(half).wait_send()
            self.second(half).wait_send()


class Held:
    def __init__(self, kept, side=0, sides=1):
        self.kept = kept
        width = kept.shape[-1] // sides
        self.cols = pl.ds(side * width, width)

    def own_rows(self, half):
        return self.kept.at[half]

    def held(self, half, member):
        return self.kept.at[half, member, :, self.cols]


class Spread(Plane):
    def __init__(self, source, refs, columns):
        self.own_rows, self.held = source.own_rows, source.held
        self.final, self.spread_send, self.spread_recv, self.place_sem = refs[:4]
        if columns:
            self.swap_send, self.swap_recv = refs[4:]
        self.locate(columns, self.final.shape[-2])

    def place(self, half):
        return pltpu.make_async_copy(
            self.own_rows(half),
            self.rows(self.final, self.own_start(half), self.eighth),
            self.place_sem.at[half],
        )

    def place_all(self):
        for half in (0, 1):
            self.place(half).start()
        for half in (0, 1):
            self.place(half).wait()

    def swap_place(self, half, member):
        start = pl.multiple_of(self.own_start(half), self.eighth)
        return self.final.at[member, pl.ds(start, self.eighth)]

    def swap_copy(self, half, hop, src_member):
        target = lax.rem(self.me + hop, self.members)
        return remote(
            self.held(half, target),
            self.swap_place(half, src_member),
            self.swap_send.at[hop, half],
            self.swap_recv.at[hop, half],
            target,
        )

    def swap_local(self, half):
        return pltpu.make_async_copy(
            self.held(half, self.me),
            self.swap_place(half, self.me),
            self.place_sem.at[half],
        )

    def swap_begin(self):
        for half in (0, 1):
            for hop in range(1, self.members):
                self.swap_copy(half, hop, self.me).start()
            self.swap_local(half).start()

    def swap_end(self):
        for half in (0, 1):
            for hop in range(1, self.members):
                source = lax.rem(self.me + self.members - hop, self.members)
                self.swap_copy(half, hop, source).wait_recv()
            self.swap_local(half).wait()

    def spread_copy(self, half, stage):
        if stage == 0:
            rows = self.rows(self.final, self.own_start(half), self.eighth)
        else:
            rows = self.rows(self.final, self.kept_start(half), self.quarter)
        return self.copy(rows, rows, self.spread_send, self.spread_recv, half, 1 - stage)

    def spread_wait(self, half, stage):
        side = self.sides(half)[1]
        if stage == 0:
            start = self.kept_start(half) + (1 - side) * self.eighth
            rows = self.rows(self.final, start, self.eighth)
        else:
            rows = self.rows(self.final, self.given_start(half), self.quarter)
        self.copy(rows, rows, self.spread_send, self.spread_recv, half, 1 - stage).wait_recv()

    def spread_begin(self):
        for half in (0, 1):
            self.spread_copy(half, 0).start()

    def spread_on(self):
        for half in (0, 1):
            self.spread_wait(half, 0)
            self.spread_copy(half, 1).start()

    def spread_end(self):
        for half in (0, 1):
            self.spread_wait(half, 1)

    def spread_sent(self, swapped=True):
        for half in (0, 1):
            self.spread_copy(half, 0).wait_send()
            self.spread_copy(half, 1).wait_send()
            if self.columns and swapped:
                for hop in range(1, self.members):
                    self.swap_copy(half, hop, self.me).wait_send()


class GroupSpread(Spread):
    def __init__(self, source, refs):
        self.landing = refs[0]
        super().__init__(source, refs[1:], True)

    def swap_place(self, half, member):
        return self.landing.at[half, member]

    def swap_end(self):
        super().swap_end()
        groups = self.final.shape[0]
        size = self.landing.shape[1] // groups
        for half in (0, 1):
            rows = pl.ds(pl.multiple_of(self.own_start(half), self.eighth), self.eighth)
            for group in range(groups):
                total = self.landing[half, group * size].astype(jnp.float32)
                for member in range(group * size + 1, (group + 1) * size):
                    total = total + self.landing[half, member].astype(jnp.float32)
                self.final[group, rows] = total.astype(jnp.bfloat16)


class Everywhere(Spread):
    def swap_begin(self):
        chips = self.members // 2
        for half in (0, 1):
            own = self.own_rows(half)
            for hop in range(1, chips):
                self.hand_to(half, hop, own, lax.rem(self.me + 2 * hop, self.members)).start()
            self.pass_on(half, self.me // 2, own).start()
            self.swap_local(half).start()

    def hand_to(self, half, hop, own, place):
        return remote(
            own,
            self.swap_place(half, self.me),
            self.swap_send.at[0, hop, half],
            self.swap_recv.at[0, hop, half],
            place,
        )

    def pass_on(self, half, chip, source):
        core = self.me % 2
        return remote(
            source,
            self.swap_place(half, 2 * chip + core),
            self.swap_send.at[1, chip, half],
            self.swap_recv.at[1, chip, half],
            self.me + 1 - 2 * core,
        )

    def swap_on(self):
        chips = self.members // 2
        for hop in range(1, chips):
            sender = lax.rem(self.me + self.members - 2 * hop, self.members)
            for half in (0, 1):
                place = self.swap_place(half, sender)
                remote(
                    place,
                    place,
                    self.swap_send.at[0, hop, half],
                    self.swap_recv.at[0, hop, half],
                    sender,
                ).wait_recv()
                self.pass_on(half, sender // 2, place).start()

    def swap_end(self):
        core = self.me % 2
        for chip in range(self.members // 2):
            for half in (0, 1):
                place = self.swap_place(half, 2 * chip + 1 - core)
                remote(
                    place,
                    place,
                    self.swap_send.at[1, chip, half],
                    self.swap_recv.at[1, chip, half],
                    self.me + 1 - 2 * core,
                ).wait_recv()
        for half in (0, 1):
            self.swap_local(half).wait()

    def spread_sent(self):
        for half in (0, 1):
            self.spread_copy(half, 0).wait_send()
            self.spread_copy(half, 1).wait_send()
        self.swap_sent()

    def swap_sent(self):
        chips = self.members // 2
        for half in (0, 1):
            own = self.own_rows(half)
            for hop in range(1, chips):
                self.hand_to(half, hop, own, lax.rem(self.me + 2 * hop, self.members)).wait_send()
            for chip in range(chips):
                self.pass_on(half, chip, own).wait_send()


def sum_scratch(shape):
    dma = pltpu.SemaphoreType.DMA
    rows, width = shape[-2:]

    def buffer(count):
        return pltpu.VMEM((2,) + shape[:-2] + (count, width), jnp.bfloat16)

    buffers = [buffer(rows // 4), buffer(rows // 4), buffer(rows // 8)]
    return buffers + [dma((2,)), dma((2, 2)), dma((2, 2))]


SUM_REFS = 6


def spread_scratch(shape, members=None):
    dma = pltpu.SemaphoreType.DMA
    scratch = [pltpu.VMEM(shape, jnp.bfloat16), dma((2, 2)), dma((2, 2)), dma((2,))]
    if len(shape) == 3:
        count = members or shape[0]
        scratch += [dma((count, 2)), dma((count, 2))]
    return scratch


def everywhere_scratch(shape):
    dma = pltpu.SemaphoreType.DMA
    chips = shape[0] // 2
    scratch = [pltpu.VMEM(shape, jnp.bfloat16), dma((2, 2)), dma((2, 2)), dma((2,))]
    return scratch + [dma((2, chips, 2)), dma((2, chips, 2))]


def spread_refs(columns):
    return 6 if columns else 4


def gradient_sum_kernel(plan, *refs):
    refs = list(refs)
    count = len(plan)
    sources = refs[:count]
    results_count = sum(max(1, one.sides) for one in plan)
    results = refs[count : count + results_count]
    scratch = refs[count + results_count :]
    store_sem = scratch.pop()

    def take(size):
        taken = scratch[:size]
        del scratch[:size]
        return taken

    sums, spreads, late = [], [], []
    for source, one in zip(sources, plan):
        if one.summed:
            held = Held(source, *one.part)
        else:
            held = Summed(source, take(SUM_REFS), one.columns)
            sums.append(held)
        size = spread_refs(one.columns)
        if one.groups:
            spreads.append(GroupSpread(held, take(size + 1)))
        else:
            spreads.append(Spread(held, take(size), one.columns))
        if not one.summed:
            late.append(spreads[-1])
    early = [spread for spread in spreads if spread not in late]
    greet_all()

    def stores(at):
        final, sides = spreads[at].final, plan[at].sides
        first = sum(max(1, one.sides) for one in plan[:at])
        if sides == 0:
            return [pltpu.make_async_copy(final, results[first], store_sem.at[at, 0, 0])]
        part = final.shape[2] // sides
        return [
            pltpu.make_async_copy(
                final.at[member, :, pl.ds(side * part, part)],
                results[first + side].at[:, pl.ds(member * part, part)],
                store_sem.at[at, side, member],
            )
            for member in range(final.shape[0])
            for side in range(sides)
        ]

    def launch(spread):
        if spread.columns:
            spread.swap_begin()
        else:
            spread.place_all()
            spread.spread_begin()

    for share in sums:
        share.begin()
    for spread in early:
        launch(spread)
    for share in sums:
        share.middle()
    for spread in early[:1]:
        spread.swap_end()
        spread.spread_begin()
    for share, spread in zip(sums, late):
        share.finish()
        launch(spread)
    for spread in early[:1]:
        spread.spread_on()
    for spread in early[1:]:
        spread.swap_end()
        spread.spread_begin()
    for spread in late:
        if spread.columns:
            spread.swap_end()
            spread.spread_begin()
        else:
            spread.spread_on()
    for spread in early[1:]:
        spread.spread_on()
    for spread in late:
        if spread.columns:
            spread.spread_on()
    for at in sorted(range(count), key=lambda one: spreads[one] in early):
        spreads[at].spread_end()
        for store in stores(at):
            store.start()
    for share in sums:
        share.sum_sent()
    for spread in spreads:
        spread.spread_sent()
    for at in range(count):
        for store in stores(at):
            store.wait()


@dataclasses.dataclass
class Source:
    array: jax.Array
    summed: bool = False
    part: tuple = (0, 1)
    groups: int = 0
    sides: int = 0

    @property
    def columns(self):
        return self.array.ndim - self.summed == 3

    @property
    def shape(self):
        shape = self.array.shape
        if self.summed:
            shape = shape[1:-2] + (8 * shape[-2], shape[-1] // self.part[1])
        return shape


def gradient_sum(sources):
    members = lax.axis_size("fsdp")
    anywhere = pl.BlockSpec(memory_space=pl.ANY)
    scratch, results = [], []
    for one in sources:
        shape = one.shape
        if not one.summed:
            scratch += sum_scratch(shape)
        if one.groups:
            landing = (2, members, shape[1] // 8, shape[2])
            scratch.append(pltpu.VMEM(landing, jnp.bfloat16))
            shape = (one.groups,) + shape[1:]
        scratch += spread_scratch(shape, members)
        if one.sides == 0:
            results.append(shape)
        else:
            results += [(shape[1], shape[0] * shape[2] // one.sides)] * one.sides
    return pl.pallas_call(
        functools.partial(gradient_sum_kernel, sources),
        out_shape=[jax.ShapeDtypeStruct(shape, jnp.bfloat16) for shape in results],
        in_specs=[anywhere] * len(sources),
        out_specs=[anywhere] * len(results),
        scratch_shapes=scratch + [pltpu.SemaphoreType.DMA((len(sources), 2, members))],
        compiler_params=pltpu.CompilerParams(
            collective_id=3, has_side_effects=True, vmem_limit_bytes=KERNEL_VMEM
        ),
        cost_estimate=pl.CostEstimate(flops=0, bytes_accessed=300 << 20, transcendentals=0),
        name="gradient_sum",
    )(*(one.array for one in sources))

def remote(src, dst, send_sem, recv_sem, place):
    return pltpu.make_async_remote_copy(
        src_ref=src,
        dst_ref=dst,
        send_sem=send_sem,
        recv_sem=recv_sem,
        device_id={"fsdp": place},
        device_id_type=pl.DeviceIdType.MESH,
    )


def dot_nn(left_mat, right_mat):
    return jnp.dot(left_mat, right_mat, preferred_element_type=jnp.float32)


def dot_nt(left_mat, right_mat):
    return lax.dot_general(
        left_mat, right_mat, (((1,), (1,)), ((), ())), preferred_element_type=jnp.float32
    )


def dot_tn(left_mat, right_mat):
    return lax.dot_general(
        left_mat, right_mat, (((0,), (0,)), ((), ())), preferred_element_type=jnp.float32
    )


def greet_all():
    sem = pltpu.get_barrier_semaphore()
    members, planes = lax.axis_size("fsdp"), lax.axis_size("ctx")
    mesh_id = pl.DeviceIdType.MESH
    for hop in range(1, planes):
        other = lax.rem(lax.axis_index("ctx") + hop, planes)
        pl.semaphore_signal(sem, inc=1, device_id={"ctx": other}, device_id_type=mesh_id)
    for hop in range(1, members):
        other = lax.rem(lax.axis_index("fsdp") + hop, members)
        pl.semaphore_signal(sem, inc=1, device_id={"fsdp": other}, device_id_type=mesh_id)
    pl.semaphore_wait(sem, members + planes - 2)


PIECES = 4


def line_scratch(chips, tok_count, width):
    dma = pltpu.SemaphoreType.DMA
    shard = (tok_count, width)
    return [
        pltpu.VMEM((chips, 2) + shard, jnp.bfloat16),
        dma((chips, 2)),
        dma((chips, 3)),
        dma,
        pltpu.VMEM((chips, 2) + shard, jnp.bfloat16),
        pltpu.VMEM((chips,) + shard, jnp.bfloat16),
        pltpu.VMEM((chips,) + shard, jnp.bfloat16),
        pltpu.VMEM((chips,) + shard, jnp.bfloat16),
        dma((chips,)),
        dma((chips,)),
        dma((chips, PIECES)),
        dma((chips, PIECES)),
        dma((chips, PIECES)),
    ]


LINE_REFS = 13


class Line:
    def __init__(self, chips, refs):
        (
            self.slots,
            self.slot_recv,
            self.slot_send,
            self.own_sem,
            self.parts,
            self.from_core,
            self.from_left,
            self.from_right,
            self.core_send,
            self.core_recv,
            self.flow_send,
            self.left_recv,
            self.right_recv,
        ) = refs
        self.chips = chips
        me = lax.axis_index("fsdp")
        self.chip = me // 2
        self.core = me % 2
        self.tok = self.slots.shape[2]
        self.piece = self.tok // PIECES

    def place(self, chip, core):
        return chip * 2 + core

    def order(self, step):
        picked = 0
        for chip in range(self.chips):
            near = sorted(range(self.chips), key=lambda other: (abs(other - chip), other))
            picked = picked + jnp.where(self.chip == chip, near[step], 0)
        return picked

    def slot_copy(self, src, chip, way):
        place = (
            self.place(self.chip + 1, self.core),
            self.place(self.chip - 1, self.core),
            self.place(self.chip, 1 - self.core),
        )[way]
        return remote(
            src,
            self.slots.at[chip, self.core],
            self.slot_send.at[chip, way],
            self.slot_recv.at[chip, self.core],
            place,
        )

    def own_copy(self, own_ref):
        return pltpu.make_async_copy(own_ref, self.slots.at[self.chip, self.core], self.own_sem)

    def gather_begin(self, own_ref):
        @pl.when(self.chip < self.chips - 1)
        def _():
            self.slot_copy(own_ref, self.chip, 0).start()

        @pl.when(self.chip > 0)
        def _():
            self.slot_copy(own_ref, self.chip, 1).start()

        self.slot_copy(own_ref, self.chip, 2).start()
        self.own_copy(own_ref).start()

    def gather_step(self, distance):
        for chip, there, way, onward in (
            (self.chip - distance, self.chip >= distance, 0, self.chip < self.chips - 1),
            (self.chip + distance, self.chip + distance < self.chips, 1, self.chip > 0),
        ):

            @pl.when(there)
            def _(chip=chip, way=way, onward=onward):
                src = self.slots.at[chip, self.core]
                self.slot_copy(src, chip, way).wait_recv()

                @pl.when(onward)
                def _():
                    self.slot_copy(src, chip, way).start()

                self.slot_copy(src, chip, 2).start()

    def gather_other(self, chip):
        dst = self.slots.at[chip, 1 - self.core]
        remote(
            dst,
            dst,
            self.slot_send.at[chip, 2],
            self.slot_recv.at[chip, 1 - self.core],
            self.place(self.chip, 1 - self.core),
        ).wait_recv()

    def gather_end(self):
        for chip in range(self.chips):
            src = self.slots.at[chip, self.core]

            @pl.when((self.chip >= chip) & (self.chip < self.chips - 1))
            def _(src=src, chip=chip):
                self.slot_copy(src, chip, 0).wait_send()

            @pl.when((self.chip <= chip) & (self.chip > 0))
            def _(src=src, chip=chip):
                self.slot_copy(src, chip, 1).wait_send()

            self.slot_copy(src, chip, 2).wait_send()

    def core_copy(self, chip):
        return remote(
            self.parts.at[chip, 1 - self.core],
            self.from_core.at[chip],
            self.core_send.at[chip],
            self.core_recv.at[chip],
            self.place(self.chip, 1 - self.core),
        )

    def flow_copy(self, chip, piece, right):
        rows = pl.ds(piece * self.piece, self.piece)
        return remote(
            self.parts.at[chip, self.core, rows],
            (self.from_left if right else self.from_right).at[chip, rows],
            self.flow_send.at[chip, piece],
            (self.left_recv if right else self.right_recv).at[chip, piece],
            self.place(self.chip + (1 if right else -1), self.core),
        )

    def flow(self, chip, right, incoming):
        self.core_copy(chip).wait_recv()

        @pl.loop(0, PIECES)
        def _(piece):
            rows = pl.ds(pl.multiple_of(piece * self.piece, self.piece), self.piece)
            total = self.parts[chip, self.core, rows].astype(jnp.float32)
            total = total + self.from_core[chip, rows].astype(jnp.float32)
            if incoming:
                self.flow_copy(chip, piece, right).wait_recv()
                source = self.from_left if right else self.from_right
                total = total + source[chip, rows].astype(jnp.float32)
            self.parts[chip, self.core, rows] = total.astype(jnp.bfloat16)
            self.flow_copy(chip, piece, right).start()

    def scatter_first(self, chip):
        @pl.when((self.chip == 0) & (chip > 0))
        def _():
            self.flow(chip, True, False)

        @pl.when((self.chip == self.chips - 1) & (chip < self.chips - 1))
        def _():
            self.flow(chip, False, False)

    def scatter_rest(self, result_ref, between=None):
        for rank in range(3, 2 * self.chips - 2):
            right = rank - self.chip

            @pl.when((self.chip > 0) & (right > self.chip) & (right < self.chips))
            def _(right=right):
                self.flow(right, True, True)

            left = 2 * (self.chips - 1) - self.chip - rank

            @pl.when((self.chip < self.chips - 1) & (left < self.chip) & (left >= 0))
            def _(left=left):
                self.flow(left, False, True)

            if between is not None:
                between(rank)

        own = self.chip
        self.core_copy(own).wait_recv()

        @pl.loop(0, PIECES)
        def _(piece):
            rows = pl.ds(pl.multiple_of(piece * self.piece, self.piece), self.piece)
            total = self.parts[own, self.core, rows].astype(jnp.float32)
            total = total + self.from_core[own, rows].astype(jnp.float32)
            result_ref[rows] = total

        @pl.when(own > 0)
        def _():
            @pl.loop(0, PIECES)
            def _(piece):
                rows = pl.ds(pl.multiple_of(piece * self.piece, self.piece), self.piece)
                self.flow_copy(own, piece, True).wait_recv()
                result_ref[rows] += self.from_left[own, rows].astype(jnp.float32)

        @pl.when(own < self.chips - 1)
        def _():
            @pl.loop(0, PIECES)
            def _(piece):
                rows = pl.ds(pl.multiple_of(piece * self.piece, self.piece), self.piece)
                self.flow_copy(own, piece, False).wait_recv()
                result_ref[rows] += self.from_right[own, rows].astype(jnp.float32)

        for chip in range(self.chips):
            self.core_copy(chip).wait_send()

            @pl.when(self.chip != chip)
            def _(chip=chip):
                for piece in range(PIECES):
                    self.flow_copy(chip, piece, True).wait_send()


def ffn_forward_kernel(
    chips,
    own_ref,
    gateup_hbm,
    down_hbm,
    ple_held,
    result_ref,
    all_hbm,
    hidden_hbm,
    act_hbm,
    slope_hbm,
    ple_hbm,
    down_low,
    *scratch,
):
    line = Line(chips, scratch[:LINE_REFS])
    gateup, down, hidden, act, slope, load_sems, store_sems = scratch[LINE_REFS : LINE_REFS + 7]
    down_wide = scratch[LINE_REFS + 7]
    ple = Spread(Held(ple_held), scratch[LINE_REFS + 8 :], True)
    ff_part = down.shape[0]
    width = down.shape[1]
    pair = 2 * line.tok
    load_gateup = pltpu.make_async_copy(gateup_hbm, gateup, load_sems.at[0])
    load_down = pltpu.make_async_copy(down_hbm, down_wide, load_sems.at[1])
    store_down = pltpu.make_async_copy(down, down_low, load_sems.at[3])
    load_gateup.start()
    load_down.start()
    greet_all()
    line.gather_begin(own_ref)
    ple.place_all()
    ple.spread_begin()
    line.own_copy(own_ref).wait()
    store_ple = pltpu.make_async_copy(ple.final, ple_hbm, load_sems.at[2])

    def stores(chip):
        rows = pl.ds(pl.multiple_of(chip * pair, pair), pair)
        return [
            pltpu.make_async_copy(line.slots.at[chip], all_hbm.at[chip], store_sems.at[chip, 0]),
            pltpu.make_async_copy(hidden.at[rows], hidden_hbm.at[rows], store_sems.at[chip, 1]),
            pltpu.make_async_copy(act.at[rows], act_hbm.at[rows], store_sems.at[chip, 2]),
            pltpu.make_async_copy(slope.at[rows], slope_hbm.at[rows], store_sems.at[chip, 3]),
        ]

    tile = 256
    for step in range(chips):
        if step > 0:
            line.gather_step(step)
        chip = line.order(step)
        line.gather_other(chip)
        if step == 0:
            load_gateup.wait()
            load_down.wait()
            down[...] = down_wide[...].astype(jnp.bfloat16)
            store_down.start()
        rows = pl.ds(pl.multiple_of(chip * pair, pair), pair)

        @pl.loop(0, ff_part // tile)
        def _(at, chip=chip, rows=rows):
            inputs = line.slots[chip].reshape(pair, width)
            gate_cols = pl.ds(pl.multiple_of(at * tile, tile), tile)
            up_cols = pl.ds(pl.multiple_of(ff_part + at * tile, tile), tile)
            gate = dot_nn(inputs, gateup[:, gate_cols])
            up = dot_nn(inputs, gateup[:, up_cols])
            square = gate * gate
            bent = jnp.tanh(GELU_ROOT * gate * (1.0 + GELU_CUBE * square))
            half = 0.5 + 0.5 * bent
            activated = gate * half
            rise = half + 0.5 * gate * (1.0 - bent * bent) * (
                GELU_ROOT * (1.0 + 3.0 * GELU_CUBE * square)
            )
            hidden[rows, gate_cols] = (activated * up).astype(jnp.bfloat16)
            act[rows, gate_cols] = activated.astype(jnp.bfloat16)
            slope[rows, gate_cols] = (rise * up).astype(jnp.bfloat16)

        for copy in stores(chip):
            copy.start()

        wide = 512

        @pl.loop(0, width // wide)
        def _(at, chip=chip, rows=rows):
            cols = pl.ds(pl.multiple_of(at * wide, wide), wide)
            sums = dot_nn(hidden[rows, :], down[:, cols]).astype(jnp.bfloat16)
            line.parts[chip, :, :, cols] = sums.reshape(2, line.tok, wide)

        line.core_copy(chip).start()
        line.scatter_first(chip)
    ple.spread_on()
    line.scatter_rest(result_ref)
    ple.spread_end()
    store_ple.start()
    line.gather_end()
    ple.spread_sent(False)
    store_ple.wait()
    store_down.wait()
    for chip in range(chips):
        for copy in stores(chip):
            copy.wait()


def ffn_forward(own, gateup, down, ple, chips):
    tok_count, width = own.shape
    ff_part = down.shape[0]
    block = 2 * chips * tok_count
    bfloat = jnp.bfloat16
    anywhere = pl.BlockSpec(memory_space=pl.ANY)
    vmem = pl.BlockSpec(memory_space=pltpu.VMEM)
    part = jax.ShapeDtypeStruct((block, ff_part), bfloat)
    ple_shape = (ple.shape[1], 8 * ple.shape[2], ple.shape[3])
    result, gathered, hidden, act, slope, ple_all, down_low = pl.pallas_call(
        functools.partial(ffn_forward_kernel, chips),
        out_shape=[
            jax.ShapeDtypeStruct((tok_count, width), jnp.float32),
            jax.ShapeDtypeStruct((chips, 2, tok_count, width), bfloat),
            part,
            part,
            part,
            jax.ShapeDtypeStruct(ple_shape, bfloat),
            jax.ShapeDtypeStruct(down.shape, bfloat),
        ],
        in_specs=[vmem, anywhere, anywhere, anywhere],
        out_specs=[vmem] + [anywhere] * 6,
        scratch_shapes=line_scratch(chips, tok_count, width)
        + [
            pltpu.VMEM(gateup.shape, bfloat),
            pltpu.VMEM(down.shape, bfloat),
            pltpu.VMEM((block, ff_part), bfloat),
            pltpu.VMEM((block, ff_part), bfloat),
            pltpu.VMEM((block, ff_part), bfloat),
            pltpu.SemaphoreType.DMA((4,)),
            pltpu.SemaphoreType.DMA((chips, 4)),
            pltpu.VMEM(down.shape, down.dtype),
        ]
        + spread_scratch(ple_shape),
        compiler_params=pltpu.CompilerParams(
            collective_id=1, has_side_effects=True, vmem_limit_bytes=KERNEL_VMEM
        ),
        cost_estimate=pl.CostEstimate(
            flops=6 * block * width * ff_part,
            bytes_accessed=40 << 20,
            transcendentals=block * ff_part,
        ),
        name="ffn_forward",
    )(own, gateup, down, ple)
    return result, gathered.reshape(block, width), hidden, act, slope, ple_all, down_low


def ffn_backward_kernel(
    chips,
    own_ref,
    gateup_hbm,
    down_hbm,
    hidden_hbm,
    act_hbm,
    slope_hbm,
    inputs_hbm,
    pgate_hbm,
    pproj_hbm,
    result_ref,
    part_hbm,
    down_kept,
    pgate_kept,
    pproj_kept,
    *scratch,
):
    line = Line(chips, scratch[:LINE_REFS])
    scratch = scratch[LINE_REFS:]
    gateup, down, hidden, act, slope, inputs, grad, part_down, staged = scratch[:9]
    load_sems, store_sems, kept_sems = scratch[9:12]
    share = Summed(part_down, scratch[12 : 12 + SUM_REFS], False)
    small = [
        Summed(pgate_hbm, scratch[12 + SUM_REFS : 12 + 2 * SUM_REFS], True),
        Summed(pproj_hbm, scratch[12 + 2 * SUM_REFS :], True),
    ]
    ff_part = down.shape[0]
    width = down.shape[1]
    pair = 2 * line.tok
    loads = [
        pltpu.make_async_copy(src, dst, load_sems.at[at])
        for at, (src, dst) in enumerate(
            (
                (down_hbm, down),
                (act_hbm, act),
                (slope_hbm, slope),
                (gateup_hbm, gateup),
                (hidden_hbm, hidden),
                (inputs_hbm, inputs),
            )
        )
    ]
    for load in loads:
        load.start()
    greet_all()
    line.gather_begin(own_ref)
    for one in small:
        one.begin()
    line.own_copy(own_ref).wait()

    tile = 256
    wide = 512
    for step in range(chips):
        if step > 0:
            line.gather_step(step)
        chip = line.order(step)
        line.gather_other(chip)
        if step == 0:
            for load in loads[:4]:
                load.wait()
        rows = pl.ds(pl.multiple_of(chip * pair, pair), pair)

        @pl.loop(0, ff_part // tile)
        def _(at, chip=chip, rows=rows):
            grads = line.slots[chip].reshape(pair, width)
            gate_cols = pl.ds(pl.multiple_of(at * tile, tile), tile)
            up_cols = pl.ds(pl.multiple_of(ff_part + at * tile, tile), tile)
            grad_hidden = dot_nt(grads, down[gate_cols, :])
            grad[rows, gate_cols] = (
                grad_hidden * slope[rows, gate_cols].astype(jnp.float32)
            ).astype(jnp.bfloat16)
            grad[rows, up_cols] = (grad_hidden * act[rows, gate_cols].astype(jnp.float32)).astype(
                jnp.bfloat16
            )

        @pl.loop(0, width // wide)
        def _(at, chip=chip, rows=rows):
            cols = pl.ds(pl.multiple_of(at * wide, wide), wide)
            sums = dot_nt(grad[rows, :], gateup[cols, :]).astype(jnp.bfloat16)
            line.parts[chip, :, :, cols] = sums.reshape(2, line.tok, wide)

        line.core_copy(chip).start()
        line.scatter_first(chip)
    for one in small:
        one.middle()
    for load in loads[4:]:
        load.wait()

    block = chips * pair

    def down_grads():
        @pl.loop(0, ff_part // tile)
        def _(at):
            rows = pl.ds(pl.multiple_of(at * tile, tile), tile)
            left = hidden[:, rows]
            for start in range(0, width, wide):
                right = line.slots[:, :, :, start : start + wide].reshape(block, wide)
                part_down[rows, start : start + wide] = dot_tn(left, right).astype(jnp.bfloat16)

    def part_store(at):
        slot = at % 2
        return pltpu.make_async_copy(
            staged.at[slot], part_hbm.at[at], store_sems.at[slot]
        )

    def gateup_grads(first, last):
        @pl.loop(first, last)
        def _(at):
            cols = pl.ds(pl.multiple_of(at * tile, tile), tile)

            @pl.when(at >= 2)
            def _():
                part_store(at - 2).wait()

            left = inputs[:, cols]
            for start in range(0, 2 * ff_part, wide):
                staged[at % 2, :, start : start + wide] = dot_tn(
                    left, grad[:, start : start + wide]
                ).astype(jnp.bfloat16)
            part_store(at).start()

    tiles = width // tile
    done = [0]

    def between(rank):
        upto = min(tiles, done[0] + 2)
        gateup_grads(done[0], upto)
        done[0] = upto

    down_grads()
    share.begin()
    for one in small:
        one.finish()
    line.scatter_rest(result_ref, between)
    share.middle()
    gateup_grads(done[0], tiles)
    share.finish()
    stores = [
        pltpu.make_async_copy(one.own_rows(half), kept.at[half], kept_sems.at[at, half])
        for at, (one, kept) in enumerate(
            ((share, down_kept), (small[0], pgate_kept), (small[1], pproj_kept))
        )
        for half in (0, 1)
    ]
    for store in stores:
        store.start()
    line.gather_end()
    for one in [share] + small:
        one.sum_sent()
    for at in (tiles - 2, tiles - 1):
        part_store(at).wait()
    for store in stores:
        store.wait()


def ffn_backward(own, gateup, down, hidden, act, slope, inputs, pgate, pproj, chips):
    tok_count, width = own.shape
    ff_part = down.shape[0]
    block = 2 * chips * tok_count
    bfloat = jnp.bfloat16
    anywhere = pl.BlockSpec(memory_space=pl.ANY)
    vmem = pl.BlockSpec(memory_space=pltpu.VMEM)
    dma = pltpu.SemaphoreType.DMA
    tile = 256
    held = (gateup, down, hidden, act, slope, inputs)
    return pl.pallas_call(
        functools.partial(ffn_backward_kernel, chips),
        out_shape=[
            jax.ShapeDtypeStruct((tok_count, width), jnp.float32),
            jax.ShapeDtypeStruct((width // tile, tile, 2 * ff_part), bfloat),
            jax.ShapeDtypeStruct((2, ff_part // 8, width), bfloat),
        ]
        + [
            jax.ShapeDtypeStruct((2, one.shape[0], one.shape[1] // 8, one.shape[2]), bfloat)
            for one in (pgate, pproj)
        ],
        in_specs=[vmem] + [anywhere] * 8,
        out_specs=[vmem] + [anywhere] * 4,
        scratch_shapes=line_scratch(chips, tok_count, width)
        + [pltpu.VMEM(one.shape, bfloat) for one in held]
        + [
            pltpu.VMEM((block, 2 * ff_part), bfloat),
            pltpu.VMEM(down.shape, bfloat),
            pltpu.VMEM((2, tile, 2 * ff_part), bfloat),
            dma((6,)),
            dma((2,)),
            dma((3, 2)),
        ]
        + sum_scratch(down.shape)
        + sum_scratch(pgate.shape)
        + sum_scratch(pproj.shape),
        compiler_params=pltpu.CompilerParams(
            collective_id=2, has_side_effects=True, vmem_limit_bytes=KERNEL_VMEM
        ),
        cost_estimate=pl.CostEstimate(
            flops=12 * block * width * ff_part, bytes_accessed=40 << 20, transcendentals=0
        ),
        name="ffn_backward",
    )(own, *held, pgate, pproj)

def rope_norm(lin, gain, cosine, sine_part):
    scale = lax.rsqrt(jnp.mean(lin * lin, axis=-1, keepdims=True) + EPSILON)
    scaled = lin * scale * gain
    first, second = scaled[:, : HD // 2], scaled[:, HD // 2 :]
    return jnp.concatenate(
        [first * cosine - second * sine_part, second * cosine + first * sine_part], axis=-1
    )


class RowHeld:
    def __init__(self, kept, part):
        self.kept, self.part = kept, part

    def own_rows(self, half):
        return self.kept.at[half]

    def held(self, half, member):
        cols = pl.ds(pl.multiple_of(member * self.part, self.part), self.part)
        return self.kept.at[half, :, cols]


class SameHeld:
    def __init__(self, shard, spread_rows):
        self.shard, self.spread_rows = shard, spread_rows

    def own_rows(self, half):
        start, size = self.spread_rows(half)
        return self.shard.at[pl.ds(pl.multiple_of(start, size), size)]

    def held(self, half, member):
        return self.own_rows(half)


GAIN_ROWS = 24
POSITION_ROW = 12
QUERY_ROW = 13
KEY_ROW = 15


def attention_forward_kernel(
    chips,
    tokens_ref,
    packed_ref,
    frequency_ref,
    lengths_ref,
    query_weight,
    key_weight,
    value_weight,
    gate_weight,
    up_weight,
    out_hbm,
    small_hbm,
    ple_hbm,
    result_ref,
    packed_all,
    cos_ref,
    sin_ref,
    head_gains_ref,
    all_hbm,
    qkv_hbm,
    gateup_hbm,
    lin_hbm,
    query_hbm,
    span_hbm,
    probs_hbm,
    attended_hbm,
    small_all,
    ple_held,
    *scratch,
):
    scratch = list(scratch)
    line = Line(chips, scratch[:LINE_REFS])
    del scratch[:LINE_REFS]
    qkv_kept, gate_kept, up_kept = scratch[:3]
    wide_rows, narrow_rows, row_sem = scratch[3:6]
    own_ref, gains_send, gains_recv, query_docs, key_docs = scratch[6:11]
    del scratch[:11]
    ff_part = gate_kept.shape[2] // (2 * chips)
    spreads = []
    for held in (Held(qkv_kept), RowHeld(gate_kept, ff_part), RowHeld(up_kept, ff_part)):
        spreads.append(Spread(held, scratch[: spread_refs(True)], True))
        del scratch[: spread_refs(True)]
    qkv, gate, up = spreads
    small_held = SameHeld(small_hbm, lambda half: (small.own_start(half), small.eighth))
    small = Everywhere(small_held, scratch[: spread_refs(True)], True)
    del scratch[: spread_refs(True)]
    ple_source = SameHeld(ple_hbm, lambda half: (ple.own_start(half), ple.eighth))
    ple = Everywhere(ple_source, scratch[: spread_refs(True)], True)
    del scratch[: spread_refs(True)]
    out, lin, query, span, probs, attended = scratch[:6]
    load_sem, store_sem, span_send, span_recv = scratch[6:]
    width = line.slots.shape[3]
    pair = 2 * line.tok
    block = chips * pair
    members = 2 * chips
    ctx_at = lax.axis_index("ctx")
    planes = lax.axis_size("ctx")
    me = lax.axis_index("fsdp")
    bfloat = jnp.bfloat16

    def row_load(weight, buffer, at):
        return [
            pltpu.make_async_copy(
                weight.at[pl.ds(pl.multiple_of(qkv.own_start(half), qkv.eighth), qkv.eighth)],
                buffer.at[half],
                row_sem.at[at, half],
            )
            for half in (0, 1)
        ]

    query_rows = row_load(query_weight, wide_rows.at[0, :, :, pl.ds(0, HQ * HD)], 0)
    key_rows = row_load(key_weight, narrow_rows.at[0], 1)
    value_rows = row_load(value_weight, narrow_rows.at[1], 2)
    gate_rows = row_load(gate_weight, wide_rows.at[1], 3)
    up_rows = row_load(up_weight, wide_rows.at[0], 4)
    for load in query_rows + key_rows + value_rows + gate_rows:
        load.start()
    load_out = pltpu.make_async_copy(out_hbm, out, load_sem)
    load_out.start()
    greet_all()

    def gains_copy(hop, source):
        return remote(
            packed_ref,
            packed_all.at[source],
            gains_send.at[hop],
            gains_recv.at[hop],
            lax.rem(me + hop, members),
        )

    for hop in range(1, members):
        gains_copy(hop, me).start()
    packed_all[me] = packed_ref[...]

    for load in query_rows + key_rows + value_rows:
        load.wait()
    for half in (0, 1):
        for member in range(members):
            head = member * KV // members
            qkv_kept[half, member, :, :HD] = wide_rows[
                0, half, :, member * HD : (member + 1) * HD
            ].astype(bfloat)
            for side in (0, 1):
                qkv_kept[half, member, :, (1 + side) * HD : (2 + side) * HD] = narrow_rows[
                    side, half, :, head * HD : (head + 1) * HD
                ].astype(bfloat)
    qkv.swap_begin()
    for load in up_rows:
        load.start()
    for hop in range(1, members):
        gains_copy(hop, lax.rem(me + members - hop, members)).wait_recv()

    inputs = tokens_ref[...].astype(jnp.float32)
    scale = lax.rsqrt(jnp.mean(inputs * inputs, axis=-1, keepdims=True) + EPSILON)
    gain = jnp.concatenate(
        [packed_all[member, row : row + 1] for member in range(members) for row in (0, 1)], axis=1
    )
    own_ref[...] = (inputs * scale * gain).astype(bfloat)
    line.gather_begin(own_ref)

    for load in gate_rows + up_rows:
        load.wait()
    gate_kept[...] = wide_rows[1].astype(bfloat)
    up_kept[...] = wide_rows[0].astype(bfloat)
    for at, row in ((0, QUERY_ROW), (1, KEY_ROW)):
        total = packed_all[0, row : row + 2]
        for member in range(1, members):
            total = total + packed_all[member, row : row + 2]
        head_gains_ref[at : at + 1] = jnp.concatenate([total[0:1], total[1:2]], axis=1)
    gain_query, gain_key = head_gains_ref[0:1], head_gains_ref[1:2]

    line.gather_step(1)
    qkv.swap_end()
    qkv.spread_begin()

    places = ctx_at * block + lax.broadcasted_iota(jnp.int32, (block, 1), 0)
    spots = ctx_at * block - WINDOW + lax.broadcasted_iota(jnp.int32, (1, WINDOW + block), 1)
    doc_end = 0
    query_doc = jnp.zeros(places.shape, jnp.int32)
    key_doc = jnp.where(spots >= 0, 0, -1)
    for doc in range(lengths_ref.shape[0] - 1):
        doc_end = doc_end + lengths_ref[doc]
        query_doc = query_doc + jnp.where(places >= doc_end, 1, 0)
        key_doc = key_doc + jnp.where(spots >= doc_end, 1, 0)
    query_docs[...] = query_doc
    key_docs[...] = key_doc
    positions = jnp.concatenate(
        [packed_all[member, POSITION_ROW : POSITION_ROW + 1] for member in range(members)], axis=0
    )
    columns = jnp.transpose(positions)
    for member in range(members):
        angle = columns[:, member : member + 1] * frequency_ref[...]
        token_rows = pl.ds(member * line.tok, line.tok)
        cos_ref[token_rows] = jnp.cos(angle)
        sin_ref[token_rows] = jnp.sin(angle)

    line.gather_step(2)
    small.swap_begin()
    gate.swap_begin()
    qkv.spread_on()
    for distance in range(3, chips):
        line.gather_step(distance)
    up.swap_begin()
    ple.swap_begin()
    line.own_copy(own_ref).wait()
    for chip in range(chips):
        line.gather_other(chip)
    qkv.spread_end()
    stores = [
        pltpu.make_async_copy(line.slots, all_hbm, store_sem.at[0]),
        pltpu.make_async_copy(qkv.final, qkv_hbm, store_sem.at[1]),
        pltpu.make_async_copy(lin, lin_hbm, store_sem.at[2]),
        pltpu.make_async_copy(query, query_hbm, store_sem.at[3]),
        pltpu.make_async_copy(span, span_hbm, store_sem.at[4]),
        pltpu.make_async_copy(probs, probs_hbm, store_sem.at[5]),
        pltpu.make_async_copy(attended, attended_hbm, store_sem.at[6]),
        pltpu.make_async_copy(
            gate.final, gateup_hbm.at[:, :, pl.ds(0, ff_part)], store_sem.at[7]
        ),
        pltpu.make_async_copy(
            up.final, gateup_hbm.at[:, :, pl.ds(ff_part, ff_part)], store_sem.at[8]
        ),
        pltpu.make_async_copy(small.final, small_all, store_sem.at[9]),
    ] + [
        pltpu.make_async_copy(
            ple.rows(ple.final, ple.own_start(half), ple.eighth),
            ple_held.at[half],
            store_sem.at[10 + half],
        )
        for half in (0, 1)
    ]
    stores[0].start()
    stores[1].start()

    @pl.loop(0, chips)
    def _(chip):
        rows = pl.ds(pl.multiple_of(chip * pair, pair), pair)
        span_rows = pl.ds(pl.multiple_of(WINDOW + chip * pair, pair), pair)
        inputs = line.slots[chip].reshape(pair, width)
        weights = qkv.final[...].reshape(width, 3 * HD)
        key_lin = dot_nn(inputs, weights[:, HD : 2 * HD])
        lin[rows, HD : 2 * HD] = key_lin
        span[0, span_rows] = rope_norm(
            key_lin, gain_key, cos_ref[rows], sin_ref[rows]
        ).astype(bfloat)
        span[1, span_rows] = dot_nn(inputs, weights[:, 2 * HD :]).astype(bfloat)

    part = WINDOW // 2

    def span_copy(start, to_start, way, device):
        return pltpu.make_async_remote_copy(
            src_ref=span.at[:, pl.ds(pl.multiple_of(start, part), part)],
            dst_ref=span.at[:, pl.ds(pl.multiple_of(to_start, part), part)],
            send_sem=span_send.at[way],
            recv_sem=span_recv.at[way],
            device_id=device,
            device_id_type=pl.DeviceIdType.MESH,
        )

    mine = line.core * part
    others = (1 - line.core) * part
    onward = span_copy(block + mine, mine, 0, {"ctx": lax.rem(ctx_at + 1, planes)})
    across = span_copy(mine, mine, 1, {"fsdp": line.place(line.chip, 1 - line.core)})
    arrived = span_copy(others, others, 1, {"fsdp": line.place(line.chip, 1 - line.core)})

    @pl.when(ctx_at < planes - 1)
    def _():
        onward.start()

    @pl.when(ctx_at == 0)
    def _():
        span[:, pl.ds(0, WINDOW)] = jnp.zeros((2, WINDOW, HD), bfloat)

    @pl.loop(0, chips)
    def _(chip):
        rows = pl.ds(pl.multiple_of(chip * pair, pair), pair)
        inputs = line.slots[chip].reshape(pair, width)
        weights = qkv.final[...].reshape(width, 3 * HD)
        query_lin = dot_nn(inputs, weights[:, :HD])
        lin[rows, :HD] = query_lin
        rotated = rope_norm(query_lin, gain_query, cos_ref[rows], sin_ref[rows])
        query[rows] = (rotated.astype(bfloat).astype(jnp.float32) * SCORE_SCALE).astype(bfloat)

    @pl.when(ctx_at > 0)
    def _():
        onward.wait_recv()
        across.start()
        arrived.wait_recv()

    for store in stores[2:5]:
        store.start()
    load_out.wait()
    small.swap_on()

    span_len = WINDOW + pair
    for step in range(chips):
        chip = line.order(chips - 1 - step)
        rows = pl.ds(pl.multiple_of(chip * pair, pair), pair)
        span_rows = pl.ds(pl.multiple_of(chip * pair, pair), span_len)
        scores = dot_nt(query[rows], span[0, span_rows])
        distance = (
            WINDOW
            + lax.broadcasted_iota(jnp.int32, (pair, span_len), 0)
            - lax.broadcasted_iota(jnp.int32, (pair, span_len), 1)
        )
        visible = (
            (distance >= 0)
            & (distance < WINDOW)
            & (query_docs[rows] == key_docs[:, span_rows])
        )
        scores = jnp.where(visible, scores, NEGATIVE)
        shifted = jnp.exp(scores - jnp.max(scores, axis=-1, keepdims=True))
        prob = (shifted / jnp.sum(shifted, axis=-1, keepdims=True)).astype(bfloat)
        probs[rows] = prob
        attended[rows] = dot_nn(prob, span[1, span_rows]).astype(bfloat)

        wide = 512

        @pl.loop(0, width // wide)
        def _(at, chip=chip, rows=rows):
            cols = pl.ds(pl.multiple_of(at * wide, wide), wide)
            sums = dot_nn(attended[rows], out[:, cols]).astype(bfloat)
            line.parts[chip, :, :, cols] = sums.reshape(2, line.tok, wide)

        line.core_copy(chip).start()
        line.scatter_first(chip)
        if step == 0:
            gate.swap_end()
            gate.spread_begin()
            small.swap_end()
            small.spread_begin()
    for store in stores[5:7]:
        store.start()
    gate.spread_on()

    def between(rank):
        if rank == 3:
            up.swap_end()
            up.spread_begin()
            small.spread_on()
            ple.swap_on()
        if rank == 2 * chips - 3:
            up.spread_on()

    line.scatter_rest(result_ref, between)
    ple.swap_end()
    for store in stores[10:]:
        store.start()
    gate.spread_end()
    stores[7].start()
    up.spread_end()
    stores[8].start()
    small.spread_end()
    stores[9].start()
    line.gather_end()
    for hop in range(1, members):
        gains_copy(hop, me).wait_send()
    for spread in spreads + [small]:
        spread.spread_sent()
    ple.swap_sent()

    @pl.when(ctx_at < planes - 1)
    def _():
        onward.wait_send()

    @pl.when(ctx_at > 0)
    def _():
        across.wait_send()

    for store in stores:
        store.wait()


def attention_forward(
    tokens,
    packed,
    frequency,
    lengths,
    query_weight,
    key_weight,
    value_weight,
    gate,
    up,
    out,
    small,
    ple,
):
    tok_count, width = tokens.shape
    rows = query_weight.shape[0]
    members = width // rows
    chips = members // 2
    block = members * tok_count
    span_len = WINDOW + block
    ff_part = gate.shape[1] // members
    bfloat = jnp.bfloat16
    anywhere = pl.BlockSpec(memory_space=pl.ANY)
    vmem = pl.BlockSpec(memory_space=pltpu.VMEM)
    dma = pltpu.SemaphoreType.DMA
    kept = [
        ((block, 2 * HD), jnp.float32),
        ((block, HD), bfloat),
        ((2, span_len, HD), bfloat),
        ((block, WINDOW + 2 * tok_count), bfloat),
        ((block, HD), bfloat),
    ]
    outputs = [
        ((tok_count, width), jnp.float32),
        ((members,) + packed.shape, jnp.float32),
        ((block, HD // 2), jnp.float32),
        ((block, HD // 2), jnp.float32),
        ((2, HD), jnp.float32),
        ((chips, 2, tok_count, width), bfloat),
        ((members, rows, 3 * HD), bfloat),
        ((members, rows, 2 * ff_part), bfloat),
    ] + kept
    outputs.append(((members,) + small.shape, bfloat))
    outputs.append(((2, members, ple.shape[0] // 8, ple.shape[1]), bfloat))
    return pl.pallas_call(
        functools.partial(attention_forward_kernel, chips),
        out_shape=[jax.ShapeDtypeStruct(*output) for output in outputs],
        in_specs=[vmem] * 3 + [pl.BlockSpec(memory_space=pltpu.SMEM)] + [anywhere] * 8,
        out_specs=[vmem] * 5 + [anywhere] * 10,
        scratch_shapes=line_scratch(chips, tok_count, width)
        + [
            pltpu.VMEM((2, members, rows // 8, 3 * HD), bfloat),
            pltpu.VMEM((2, rows // 8, gate.shape[1]), bfloat),
            pltpu.VMEM((2, rows // 8, gate.shape[1]), bfloat),
            pltpu.VMEM((2, 2, rows // 8, gate.shape[1]), jnp.float32),
            pltpu.VMEM((2, 2, rows // 8, KV * HD), jnp.float32),
            dma((5, 2)),
            pltpu.VMEM((tok_count, width), bfloat),
            dma((members,)),
            dma((members,)),
            pltpu.VMEM((block, 1), jnp.int32),
            pltpu.VMEM((1, span_len), jnp.int32),
        ]
        + spread_scratch((members, rows, 3 * HD))
        + spread_scratch((members, rows, ff_part))
        + spread_scratch((members, rows, ff_part))
        + everywhere_scratch((members,) + small.shape)
        + everywhere_scratch((members,) + ple.shape)
        + [pltpu.VMEM(out.shape, bfloat)]
        + [pltpu.VMEM(*one) for one in kept]
        + [dma, dma((12,)), dma((2,)), dma((2,))],
        compiler_params=pltpu.CompilerParams(
            collective_id=4, has_side_effects=True, vmem_limit_bytes=KERNEL_VMEM
        ),
        cost_estimate=pl.CostEstimate(
            flops=8 << 30, bytes_accessed=300 << 20, transcendentals=block * 1280
        ),
        name="attention_forward",
    )(
        tokens,
        packed,
        frequency,
        lengths,
        query_weight,
        key_weight,
        value_weight,
        gate,
        up,
        out,
        small,
        ple,
    )

def rope_norm_back(grad, lin, gain, cosine, sine_part):
    first, second = grad[:, : HD // 2], grad[:, HD // 2 :]
    turned = jnp.concatenate(
        [first * cosine + second * sine_part, second * cosine - first * sine_part], axis=-1
    )
    scale = lax.rsqrt(jnp.mean(lin * lin, axis=-1, keepdims=True) + EPSILON)
    scaled = turned * gain
    along = jnp.mean(lin * scaled, axis=-1, keepdims=True)
    grad_lin = scale * scaled - lin * (scale * scale * scale * along)
    return grad_lin, jnp.sum(lin * scale * turned, axis=0, keepdims=True)


def attention_backward_kernel(
    chips,
    own_ref,
    out_hbm,
    qkv_hbm,
    lin_hbm,
    query_hbm,
    span_hbm,
    probs_hbm,
    cos_ref,
    sin_ref,
    gain_query_ref,
    gain_key_ref,
    gateup_hbm,
    down_kept,
    inputs_hbm,
    attended_hbm,
    result_ref,
    query_part_hbm,
    kv_part_hbm,
    out_part_hbm,
    gains_ref,
    gateup_kept,
    down_sum,
    *scratch,
):
    scratch = list(scratch)
    line = Line(chips, scratch[:LINE_REFS])
    del scratch[:LINE_REFS]
    gateup = Summed(gateup_hbm, scratch[:SUM_REFS], True)
    del scratch[:SUM_REFS]
    down = Spread(Held(down_kept), scratch[: spread_refs(False)], False)
    del scratch[: spread_refs(False)]
    out, qkv, lin, query, span, probs, grad, grad_span, back, across, returned = scratch[:11]
    load_sem, store_sem, back_send, back_recv, grad_out = scratch[11:16]
    inputs, attended, query_part, kv_part, out_part = scratch[16:]
    width = line.slots.shape[3]
    pair = 2 * line.tok
    block = chips * pair
    ctx_at = lax.axis_index("ctx")
    planes = lax.axis_size("ctx")
    bfloat = jnp.bfloat16
    loads = [
        pltpu.make_async_copy(src, dst, load_sem.at[at])
        for at, (src, dst) in enumerate(
            (
                (out_hbm, out),
                (span_hbm, span),
                (probs_hbm, probs),
                (lin_hbm, lin),
                (query_hbm, query),
                (qkv_hbm, qkv),
                (inputs_hbm, inputs),
                (attended_hbm, attended),
            )
        )
    ]
    for load in loads:
        load.start()
    greet_all()
    line.gather_begin(own_ref)
    gateup.begin()
    grad_span[...] = jnp.zeros_like(grad_span)
    gains_ref[...] = jnp.zeros_like(gains_ref)
    line.own_copy(own_ref).wait()
    for load in loads[:6]:
        load.wait()

    span_len = WINDOW + pair
    for step in range(chips):
        if step > 0:
            line.gather_step(step)
        chip = line.order(step)
        line.gather_other(chip)
        rows = pl.ds(pl.multiple_of(chip * pair, pair), pair)
        span_rows = pl.ds(pl.multiple_of(chip * pair, pair), span_len)
        grad_out[rows] = dot_nt(line.slots[chip].reshape(pair, width), out[...]).astype(bfloat)
        grad_prob = dot_nt(grad_out[rows], span[1, span_rows])
        prob = probs[rows].astype(jnp.float32)
        inner = jnp.sum(prob * grad_prob, axis=-1, keepdims=True)
        grad_score = (prob * (grad_prob - inner)).astype(bfloat)
        grad_query = dot_nn(grad_score, span[0, span_rows]) * SCORE_SCALE
        grad_lin, grad_gain = rope_norm_back(
            grad_query, lin[rows, :HD], gain_query_ref[...], cos_ref[rows], sin_ref[rows]
        )
        grad[rows, :HD] = grad_lin.astype(bfloat)
        gains_ref[0:1] += grad_gain
        grad_span[0, span_rows] += dot_tn(grad_score, query[rows])
        grad_span[1, span_rows] += dot_tn(probs[rows], grad_out[rows])

    part = WINDOW // 2
    mine, others = line.core * part, (1 - line.core) * part
    back[...] = grad_span[:, pl.ds(pl.multiple_of(others, part), part)].astype(bfloat)
    to_core = remote(
        back, across, back_send.at[0], back_recv.at[0], line.place(line.chip, 1 - line.core)
    )
    to_core.start()
    to_core.wait()
    total = grad_span[:, pl.ds(pl.multiple_of(mine, part), part)]
    back[...] = (total + across[...].astype(jnp.float32)).astype(bfloat)
    to_before = pltpu.make_async_remote_copy(
        src_ref=back,
        dst_ref=returned,
        send_sem=back_send.at[1],
        recv_sem=back_recv.at[1],
        device_id={"ctx": lax.rem(ctx_at + planes - 1, planes)},
        device_id_type=pl.DeviceIdType.MESH,
    )

    @pl.when(ctx_at > 0)
    def _():
        to_before.start()

    down.place_all()
    down.spread_begin()

    @pl.when(ctx_at < planes - 1)
    def _():
        to_before.wait_recv()
        here = pl.ds(pl.multiple_of(block + mine, part), part)
        grad_span[:, here] += returned[...].astype(jnp.float32)

    for step in range(chips):
        chip = line.order(chips - 1 - step)
        rows = pl.ds(pl.multiple_of(chip * pair, pair), pair)
        span_rows = pl.ds(pl.multiple_of(WINDOW + chip * pair, pair), pair)
        grad_lin, grad_gain = rope_norm_back(
            grad_span[0, span_rows], lin[rows, HD:], gain_key_ref[...], cos_ref[rows], sin_ref[rows]
        )
        grad[rows, HD : 2 * HD] = grad_lin.astype(bfloat)
        gains_ref[1:2] += grad_gain
        grad[rows, 2 * HD :] = grad_span[1, span_rows].astype(bfloat)

    wide = 512

    @pl.loop(0, width // wide)
    def _(at):
        cols = pl.ds(pl.multiple_of(at * wide, wide), wide)
        sums = dot_nt(grad[...], qkv[cols]).astype(bfloat)
        line.parts[:, :, :, cols] = sums.reshape(chips, 2, line.tok, wide)

    for step in range(chips):
        line.core_copy(line.order(chips - 1 - step)).start()
    for step in range(chips - 1):
        line.scatter_first(line.order(chips - 1 - step))
    for load in loads[6:]:
        load.wait()
    part_stores = [
        pltpu.make_async_copy(out_part, out_part_hbm, store_sem.at[0]),
        pltpu.make_async_copy(query_part, query_part_hbm, store_sem.at[1]),
        pltpu.make_async_copy(kv_part, kv_part_hbm, store_sem.at[5]),
    ]

    def between(rank):
        if rank == 3:
            for start in range(0, width, wide):
                right = line.slots[:, :, :, start : start + wide].reshape(block, wide)
                out_part[:, start : start + wide] = dot_tn(attended[...], right).astype(bfloat)
            part_stores[0].start()
        if rank == 4:

            @pl.loop(0, width // HD)
            def _(at):
                left = inputs[:, pl.ds(pl.multiple_of(at * HD, HD), HD)]
                query_part[at] = dot_tn(left, grad[:, :HD]).astype(bfloat)
                kv_part[at] = dot_tn(left, grad[:, HD:]).astype(bfloat)

            part_stores[1].start()
            part_stores[2].start()

    gateup.middle()
    down.spread_on()
    line.scatter_rest(result_ref, between)
    gateup.finish()
    stores = [
        pltpu.make_async_copy(gateup.own_rows(half), gateup_kept.at[half], store_sem.at[2 + half])
        for half in (0, 1)
    ]
    down.spread_end()
    stores.append(pltpu.make_async_copy(down.final, down_sum, store_sem.at[4]))
    for store in stores:
        store.start()
    line.gather_end()
    gateup.sum_sent()
    down.spread_sent()

    @pl.when(ctx_at > 0)
    def _():
        to_before.wait_send()

    for store in stores + part_stores:
        store.wait()


def attention_backward(
    own,
    out,
    qkv,
    lin,
    query,
    span,
    probs,
    cosine,
    sine_part,
    gain_query,
    gain_key,
    part_gateup,
    held_down,
    inputs,
    attended,
):
    tok_count, width = own.shape
    members = part_gateup.shape[0]
    chips = members // 2
    block = members * tok_count
    bfloat = jnp.bfloat16
    anywhere = pl.BlockSpec(memory_space=pl.ANY)
    vmem = pl.BlockSpec(memory_space=pltpu.VMEM)
    dma = pltpu.SemaphoreType.DMA
    eighth = part_gateup.shape[1] // 8
    down_shape = (8 * held_down.shape[1], held_down.shape[2])
    outputs = [
        ((tok_count, width), jnp.float32),
        ((members, HD, HD), bfloat),
        ((members, HD, 2 * HD), bfloat),
        ((HD, width), bfloat),
        ((2, HD), jnp.float32),
        ((2, members, eighth, part_gateup.shape[2]), bfloat),
        (down_shape, bfloat),
    ]
    half_span = (2, WINDOW // 2, HD)
    return pl.pallas_call(
        functools.partial(attention_backward_kernel, chips),
        out_shape=[jax.ShapeDtypeStruct(*output) for output in outputs],
        in_specs=[vmem] + [anywhere] * 6 + [vmem] * 4 + [anywhere] * 4,
        out_specs=[vmem, anywhere, anywhere, anywhere, vmem, anywhere, anywhere],
        scratch_shapes=line_scratch(chips, tok_count, width)
        + sum_scratch(part_gateup.shape)
        + spread_scratch(down_shape)
        + [pltpu.VMEM(one.shape, one.dtype) for one in (out, qkv, lin, query, span, probs)]
        + [
            pltpu.VMEM((block, 3 * HD), bfloat),
            pltpu.VMEM(span.shape, jnp.float32),
            pltpu.VMEM(half_span, bfloat),
            pltpu.VMEM(half_span, bfloat),
            pltpu.VMEM(half_span, bfloat),
            dma((8,)),
            dma((6,)),
            dma((2,)),
            dma((2,)),
            pltpu.VMEM((block, HD), bfloat),
            pltpu.VMEM((block, width), bfloat),
            pltpu.VMEM((block, HD), bfloat),
            pltpu.VMEM((members, HD, HD), bfloat),
            pltpu.VMEM((members, HD, 2 * HD), bfloat),
            pltpu.VMEM((HD, width), bfloat),
        ],
        compiler_params=pltpu.CompilerParams(
            collective_id=5, has_side_effects=True, vmem_limit_bytes=KERNEL_VMEM
        ),
        cost_estimate=pl.CostEstimate(
            flops=8 << 30, bytes_accessed=300 << 20, transcendentals=0
        ),
        name="attention_backward",
    )(
        own,
        out,
        qkv,
        lin,
        query,
        span,
        probs,
        cosine,
        sine_part,
        gain_query,
        gain_key,
        part_gateup,
        held_down,
        inputs,
        attended,
    )

def by_heads(
    tokens,
    per_layer,
    cotangent,
    doc_lengths,
    positions,
    w_query,
    w_key,
    w_value,
    w_out,
    laurel_left,
    laurel_right,
    w_gate,
    w_up,
    w_down,
    ple_gate,
    ple_proj,
    attn_in_gain,
    query_gain,
    key_gain,
    attn_out_gain,
    laurel_gain,
    ffn_in_gain,
    ffn_out_gain,
    ple_gain,
):
    bfloat = jnp.bfloat16
    ctx_count = lax.axis_size("ctx")
    fsdp_count = lax.axis_size("fsdp")
    tok_count = tokens.shape[0]
    block_len = tok_count * fsdp_count
    chips = fsdp_count // 2
    rows = w_query.shape[0]
    ff_part = w_gate.shape[1] // fsdp_count
    ctx_at = lax.axis_index("ctx")
    fsdp_at = lax.axis_index("fsdp")

    wide_gains = (attn_in_gain, attn_out_gain, laurel_gain, ffn_in_gain, ffn_out_gain, ple_gain)
    turn = jnp.arange(HD, dtype=jnp.int32) // query_gain.shape[0]
    head_parts = [
        jnp.where(turn == fsdp_at, jnp.tile(gain, fsdp_count), 0.0)
        for gain in (query_gain, key_gain)
    ]
    packed = jnp.zeros((GAIN_ROWS * 128,), jnp.float32)
    at = 0
    for part in list(wide_gains) + [positions.astype(jnp.float32)] + head_parts:
        packed = packed + jnp.pad(part, (at, packed.shape[0] - at - part.shape[0]))
        at += part.shape[0]
    packed = packed.reshape(GAIN_ROWS, 128)
    frequency = jnp.exp(
        jnp.arange(HD // 2, dtype=jnp.float32) * (-2.0 * math.log(ROPE_BASE) / HD)
    )

    out_low = w_out.astype(bfloat)
    def in_halves(weight):
        return jnp.concatenate(jnp.split(weight.astype(bfloat), rows // 128, axis=0), axis=1)

    def in_stacks(weight):
        pieces = weight.astype(bfloat).reshape(weight.shape[0], 128 // weight.shape[0], -1)
        return jnp.transpose(pieces, (1, 0, 2)).reshape(128, -1)

    small = jnp.concatenate([in_halves(laurel_left), in_stacks(laurel_right)], axis=1)
    ple_small = jnp.concatenate([in_halves(ple_gate), in_stacks(ple_proj)], axis=1)

    inputs = tokens.astype(jnp.float32)
    ple_input = per_layer.astype(jnp.float32)
    (
        projected,
        packed_all,
        cosine,
        sine_part,
        head_gains,
        normed_all,
        qkv_full,
        gateup_full,
        qk_lin,
        query_low,
        span_kv,
        probs,
        attended_low,
        small_all,
        ple_held,
    ) = attention_forward(
        tokens,
        packed,
        frequency[None, :],
        doc_lengths,
        w_query,
        w_key,
        w_value,
        w_gate,
        w_up,
        out_low,
        small,
        ple_small,
    )
    def side_by_side(cols, shape):
        pieces = jnp.split(cols, cols.shape[2] // shape[1], axis=2)
        return jnp.concatenate(pieces, axis=1).reshape(-1, shape[1])

    def stacked(cols, shape):
        pieces = cols.reshape(fsdp_count, -1, shape[0], cols.shape[2])
        return jnp.transpose(pieces, (0, 2, 1, 3)).reshape(-1, shape[1])

    left_size = laurel_left.size // 128
    full_left = side_by_side(small_all[:, :, :left_size], laurel_left.shape)
    full_right = stacked(small_all[:, :, left_size:], laurel_right.shape)
    wide_rows = attn_in_gain.shape[0] // 128
    gain_in, gain_post, gain_laurel, gain_ffin, gain_ffout, gain_ple = (
        packed_all[:, n * wide_rows : (n + 1) * wide_rows].reshape(-1) for n in range(6)
    )
    normed, norm_back = jax.vjp(rms_norm, inputs, gain_in)
    normed_low = normed.astype(bfloat)
    normed_all = normed_all.reshape(block_len, -1)
    col_qkv = qkv_full.reshape(normed_all.shape[1], -1)
    col_gateup = gateup_full.reshape(normed_all.shape[1], -1)
    narrow_low = matmul(normed_low, full_left).astype(bfloat)
    widened = matmul(narrow_low, full_right)
    mixed, mix_back = jax.vjp(mix_piece, inputs, normed, projected, widened, gain_post, gain_laurel)
    ffn_normed, ffn_norm_back = jax.vjp(rms_norm, mixed, gain_ffin)
    down_lin, ffn_all, hidden_low, act_low, slope_low, ple_all, down_low = ffn_forward(
        ffn_normed.astype(bfloat), col_gateup, w_down, ple_held, chips
    )
    pgate_size = ple_gate.size // 128
    full_pgate = side_by_side(ple_all[:, :, :pgate_size], ple_gate.shape)
    full_pproj = stacked(ple_all[:, :, pgate_size:], ple_proj.shape)
    layer_mid, ffn_out_back = jax.vjp(ffn_out_piece, mixed, down_lin, gain_ffout)
    layer_low = layer_mid.astype(bfloat)
    ple_lin = matmul(layer_low, full_pgate)
    ple_mid, ple_back = jax.vjp(ple_act, ple_lin, ple_input)
    ple_low = ple_mid.astype(bfloat)
    ple_wide = matmul(ple_low, full_pproj)
    out_full, final_back = jax.vjp(final_piece, layer_mid, ple_wide, gain_ple)

    grad_layer, grad_pwide, grad_gple = final_back(cotangent.astype(jnp.float32))
    grad_pwide_low = grad_pwide.astype(bfloat)
    part_pproj = matmul_tn(ple_low, grad_pwide_low)
    grad_plemid = matmul_nt(grad_pwide_low, full_pproj)
    grad_plelin, grad_pleinput = ple_back(grad_plemid)
    grad_plelin_low = grad_plelin.astype(bfloat)
    part_pgate = matmul_tn(layer_low, grad_plelin_low)
    grad_layer = grad_layer + matmul_nt(grad_plelin_low, full_pgate)
    grad_mixed, grad_down, grad_gffout = ffn_out_back(grad_layer)
    grad_ffn, part_gateup, held_wdown, held_pgate, held_pproj = ffn_backward(
        grad_down.astype(bfloat),
        col_gateup,
        down_low,
        hidden_low,
        act_low,
        slope_low,
        ffn_all,
        part_pgate.astype(bfloat).reshape(fsdp_count, rows, -1),
        part_pproj.astype(bfloat).reshape(fsdp_count, 128, -1),
        chips,
    )
    part_gateup = part_gateup.reshape(fsdp_count, rows, -1)
    grad_mixed_more, grad_gffin = ffn_norm_back(grad_ffn)
    grad_mixed = grad_mixed + grad_mixed_more
    grad_in_first, grad_normed, grad_proj, grad_lwide, grad_gpost, grad_glaurel = mix_back(
        grad_mixed
    )
    grad_lwide_low = grad_lwide.astype(bfloat)
    part_right = matmul_tn(narrow_low, grad_lwide_low)
    grad_narrow_low = matmul_nt(grad_lwide_low, full_right).astype(bfloat)
    part_left = matmul_tn(normed_low, grad_narrow_low)
    grad_normed = grad_normed + matmul_nt(grad_narrow_low, full_left)

    (
        grad_normed_more,
        part_query,
        part_kv,
        part_wout,
        grad_head_gains,
        held_gateup,
        sum_wdown,
    ) = (
        attention_backward(
            grad_proj.astype(bfloat),
            out_low,
            col_qkv,
            qk_lin,
            query_low,
            span_kv,
            probs,
            cosine,
            sine_part,
            head_gains[0:1],
            head_gains[1:2],
            part_gateup,
            held_wdown,
            normed_all,
            attended_low,
        )
    )
    grad_gquery, grad_gkey = grad_head_gains[0], grad_head_gains[1]
    part_laurel = jnp.concatenate(
        [part.astype(bfloat).reshape(fsdp_count, 128, -1) for part in (part_left, part_right)],
        axis=2,
    )
    grad_normed = grad_normed + grad_normed_more
    grad_in_second, grad_gin = norm_back(grad_normed)
    grad_tokens = grad_in_first + grad_in_second

    grad_gains = [
        grad_gin,
        grad_gpost,
        grad_glaurel,
        grad_gffin,
        grad_gffout,
        grad_gple,
        grad_gquery,
        grad_gkey,
    ]
    gain_parts = jnp.concatenate([g.reshape(fsdp_count, -1) for g in grad_gains], axis=1)
    gain_parts = jnp.pad(gain_parts, ((0, 0), (0, 128 * 128 - gain_parts.shape[1])))
    gain_parts = gain_parts.astype(bfloat).reshape(fsdp_count, 128, 128)

    (
        sum_wgate,
        sum_wup,
        sum_wquery,
        sum_wkey,
        sum_wvalue,
        sum_wout,
        sum_pgate,
        sum_pproj,
        sum_laurel,
        sum_gains,
    ) = gradient_sum(
        [
            Source(held_gateup, summed=True, part=(0, 2), sides=1),
            Source(held_gateup, summed=True, part=(1, 2), sides=1),
            Source(part_query, sides=1),
            Source(part_kv, groups=KV, sides=2),
            Source(part_wout),
            Source(held_pgate, summed=True, groups=1, sides=1),
            Source(held_pproj, summed=True, groups=1, sides=1),
            Source(part_laurel, groups=1, sides=1),
            Source(gain_parts, groups=1),
        ]
    )
    gain_sums = sum_gains.astype(jnp.float32).reshape(-1)
    wide_size, head_size = attn_in_gain.shape[0], query_gain.shape[0]
    wide_sums = gain_sums[: 6 * wide_size].reshape(6, wide_size)
    head_sums = gain_sums[6 * wide_size : 6 * wide_size + 2 * head_size].reshape(2, head_size)
    grad_wgate = sum_wgate.astype(jnp.float32)
    grad_wup = sum_wup.astype(jnp.float32)
    grad_wdown = sum_wdown.astype(jnp.float32)
    grad_wout = sum_wout.astype(jnp.float32)
    grad_wquery = sum_wquery.astype(jnp.float32)
    grad_wkey = sum_wkey.astype(jnp.float32)
    grad_wvalue = sum_wvalue.astype(jnp.float32)
    grad_pgate = sum_pgate.astype(jnp.float32)
    grad_pproj = sum_pproj.astype(jnp.float32).reshape(ple_proj.shape)
    left_part = sum_laurel.shape[1] // 2
    grad_wleft = sum_laurel[:, :left_part].astype(jnp.float32).reshape(laurel_left.shape)
    grad_wright = sum_laurel[:, left_part:].astype(jnp.float32).reshape(laurel_right.shape)
    return (
        out_full.astype(bfloat),
        grad_tokens,
        grad_pleinput,
        grad_wquery,
        grad_wkey,
        grad_wvalue,
        grad_wout,
        grad_wleft,
        grad_wright,
        grad_wgate,
        grad_wup,
        grad_wdown,
        grad_pgate,
        grad_pproj,
        wide_sums[0],
        head_sums[0],
        head_sums[1],
        *(wide_sums[n] for n in range(1, 6)),
    )


def solution(mesh):
    in_specs = (
        P(("ctx", "fsdp"), None),
        P(("ctx", "fsdp"), None),
        P(("ctx", "fsdp"), None),
        P(),
        P(("ctx", "fsdp")),
        P("fsdp", None),
        P("fsdp", None),
        P("fsdp", None),
        P("fsdp", None),
        P("fsdp", None),
        P("fsdp", None),
        P("fsdp", None),
        P("fsdp", None),
        P("fsdp", None),
        P("fsdp", None),
        P("fsdp", None),
        P("fsdp"),
        P("fsdp"),
        P("fsdp"),
        P("fsdp"),
        P("fsdp"),
        P("fsdp"),
        P("fsdp"),
        P("fsdp"),
    )
    out_specs = (
        P(("ctx", "fsdp"), None),
        P(("ctx", "fsdp"), None),
        P(("ctx", "fsdp"), None),
        P("fsdp", None),
        P("fsdp", None),
        P("fsdp", None),
        P("fsdp", None),
        P("fsdp", None),
        P("fsdp", None),
        P("fsdp", None),
        P("fsdp", None),
        P("fsdp", None),
        P("fsdp", None),
        P("fsdp", None),
        P("fsdp"),
        P("fsdp"),
        P("fsdp"),
        P("fsdp"),
        P("fsdp"),
        P("fsdp"),
        P("fsdp"),
        P("fsdp"),
    )
    run = by_heads if mesh.shape["fsdp"] == HQ and mesh.shape["ctx"] == 4 else local
    return jax.shard_map(run, mesh=mesh, in_specs=in_specs, out_specs=out_specs, check_vma=False)
```

```python
import dataclasses
import functools
import math

import jax
import jax.numpy as jnp
from jax import lax
from jax.experimental import pallas as pl
from jax.experimental.pallas import tpu as pltpu
from jax.sharding import PartitionSpec as P

HQ = 8
KV = 2
HD = 256
WINDOW = 1024


EPSILON = 1e-06
NEGATIVE = -1e30
ROPE_BASE = 10000.0
HALF_ROOT = 1.0 / math.sqrt(2.0)
GELU_ROOT = math.sqrt(2.0 / math.pi)
GELU_CUBE = 0.044715
SCORE_SCALE = 1.0 / math.sqrt(HD)
KERNEL_VMEM = 62 << 20


def passed_along(block, axis, distance):
    devices = range(lax.axis_size(axis))
    route = [(i - distance, i) for i in devices if i - distance in devices]
    return lax.ppermute(block, axis, route)


def matmul(left_mat, right_mat):
    return jnp.dot(left_mat, right_mat, preferred_element_type=jnp.float32)


def matmul_tn(left_mat, right_mat):
    return lax.dot_general(
        left_mat, right_mat, (((0,), (0,)), ((), ())), preferred_element_type=jnp.float32
    )


def matmul_nt(left_mat, right_mat):
    return lax.dot_general(
        left_mat, right_mat, (((1,), (1,)), ((), ())), preferred_element_type=jnp.float32
    )


def rms_norm(values, gain_vec):
    return (
        values * lax.rsqrt(jnp.mean(values * values, axis=-1, keepdims=True) + EPSILON) * gain_vec
    )


def rope_tables(positions, width):
    half_width = width // 2
    frequency = jnp.exp(
        jnp.arange(half_width, dtype=jnp.float32) * (-2.0 * math.log(ROPE_BASE) / width)
    )
    angles = positions.astype(jnp.float32)[:, None] * frequency[None, :]
    return (jnp.cos(angles)[:, None, :], jnp.sin(angles)[:, None, :])


def rotate(values, cosine, sine_part):
    half_width = values.shape[-1] // 2
    first_half = values[..., :half_width]
    second_half = values[..., half_width:]
    return jnp.concatenate(
        [
            first_half * cosine - second_half * sine_part,
            second_half * cosine + first_half * sine_part,
        ],
        axis=-1,
    )


def document_ids(doc_lengths, places):
    doc_ends = jnp.cumsum(doc_lengths)
    return jnp.sum((places[:, None] >= doc_ends[None, :-1]).astype(jnp.int32), axis=1)


def query_key(cosine, sine_part, query_lin, key_lin, gain_query, gain_key):
    tok_count = query_lin.shape[0]
    query_rot = rotate(
        rms_norm(query_lin.reshape(tok_count, HQ, HD), gain_query), cosine, sine_part
    )
    key_rot = rotate(rms_norm(key_lin.reshape(tok_count, KV, HD), gain_key), cosine, sine_part)
    return (query_rot, key_rot)


def mix_piece(inputs, normed, projected, widened, gain_post, gain_laurel):
    return (
        inputs + rms_norm(projected, gain_post) + normed + rms_norm(widened, gain_laurel)
    ) * HALF_ROOT


def geglu(gate_lin, up_lin):
    return jax.nn.gelu(gate_lin, approximate=True) * up_lin


def ffn_out_piece(mixed, down_lin, gain_ffout):
    return mixed + rms_norm(down_lin, gain_ffout)


def ple_act(ple_lin, ple_input):
    return jax.nn.gelu(ple_lin, approximate=True) * ple_input


def final_piece(layer_mid, ple_wide, gain_ple):
    return layer_mid + rms_norm(ple_wide, gain_ple)


def visibility(doc_lengths, query_start, key_start, tok_count, span_len):
    query_places = query_start + jnp.arange(tok_count, dtype=jnp.int32)
    key_places = key_start + jnp.arange(span_len, dtype=jnp.int32)
    distance = query_places[:, None] - key_places[None, :]
    query_docs = document_ids(doc_lengths, query_places)
    key_docs = document_ids(doc_lengths, key_places)
    return (
        (distance >= 0)
        & (distance < WINDOW)
        & (key_places[None, :] >= 0)
        & (query_docs[:, None] == key_docs[None, :])
    )


def attend_forward(query_low, span_kv, visible):
    tok_count = query_low.shape[0]
    scale_factor = 1.0 / math.sqrt(HD)
    scores = (
        jnp.einsum("tkgh,skh->kgts", query_low, span_kv[0], preferred_element_type=jnp.float32)
        * scale_factor
    )
    scores = jnp.where(visible, scores, NEGATIVE)
    row_top = jnp.max(scores, axis=-1, keepdims=True)
    shifted = jnp.exp(scores - row_top)
    row_total = jnp.sum(shifted, axis=-1, keepdims=True)
    attn_probs = shifted / row_total
    attended = jnp.einsum(
        "kgts,skh->tkgh",
        attn_probs.astype(jnp.bfloat16),
        span_kv[1],
        preferred_element_type=jnp.float32,
    )
    return (attended.reshape(tok_count, -1), row_top + jnp.log(row_total))


def attend_backward(query_low, span_kv, visible, log_total, grad_out_low):
    scale_factor = 1.0 / math.sqrt(HD)
    scores = (
        jnp.einsum("tkgh,skh->kgts", query_low, span_kv[0], preferred_element_type=jnp.float32)
        * scale_factor
    )
    attn_probs = jnp.where(visible, jnp.exp(jnp.where(visible, scores, NEGATIVE) - log_total), 0.0)
    grad_probs = jnp.einsum(
        "tkgh,skh->kgts", grad_out_low, span_kv[1], preferred_element_type=jnp.float32
    )
    inner_sum = jnp.sum(attn_probs * grad_probs, axis=-1, keepdims=True)
    grad_scores = (attn_probs * (grad_probs - inner_sum)).astype(jnp.bfloat16)
    grad_query = (
        jnp.einsum("kgts,skh->tkgh", grad_scores, span_kv[0], preferred_element_type=jnp.float32)
        * scale_factor
    )
    grad_keys = (
        jnp.einsum("kgts,tkgh->skh", grad_scores, query_low, preferred_element_type=jnp.float32)
        * scale_factor
    )
    grad_values = jnp.einsum(
        "kgts,tkgh->skh",
        attn_probs.astype(jnp.bfloat16),
        grad_out_low,
        preferred_element_type=jnp.float32,
    )
    return (grad_query, jnp.stack([grad_keys, grad_values]))


def settle(act_low, grad_low):
    act_cols = lax.all_to_all(act_low, "fsdp", split_axis=1, concat_axis=0, tiled=True)
    shard_rows = matmul_tn(act_cols, lax.all_gather(grad_low, "fsdp", axis=0, tiled=True))
    return lax.psum(shard_rows.astype(jnp.bfloat16), "ctx").astype(jnp.float32)


def local(
    tokens,
    per_layer,
    cotangent,
    doc_lengths,
    positions,
    w_query,
    w_key,
    w_value,
    w_out,
    laurel_left,
    laurel_right,
    w_gate,
    w_up,
    w_down,
    ple_gate,
    ple_proj,
    attn_in_gain,
    query_gain,
    key_gain,
    attn_out_gain,
    laurel_gain,
    ffn_in_gain,
    ffn_out_gain,
    ple_gain,
):
    bfloat = jnp.bfloat16
    tok_count = tokens.shape[0]
    span_len = WINDOW + tok_count
    groups = HQ // KV
    dev_index = lax.axis_index("ctx") * lax.axis_size("fsdp") + lax.axis_index("fsdp")
    query_start = dev_index * tok_count
    key_start = query_start - WINDOW
    visible = visibility(doc_lengths, query_start, key_start, tok_count, span_len)
    cosine, sine_part = rope_tables(positions, HD)
    gain_in, gain_query, gain_key, gain_post, gain_laurel, gain_ffin, gain_ffout, gain_ple = (
        lax.all_gather(attn_in_gain, "fsdp", axis=0, tiled=True),
        lax.all_gather(query_gain, "fsdp", axis=0, tiled=True),
        lax.all_gather(key_gain, "fsdp", axis=0, tiled=True),
        lax.all_gather(attn_out_gain, "fsdp", axis=0, tiled=True),
        lax.all_gather(laurel_gain, "fsdp", axis=0, tiled=True),
        lax.all_gather(ffn_in_gain, "fsdp", axis=0, tiled=True),
        lax.all_gather(ffn_out_gain, "fsdp", axis=0, tiled=True),
        lax.all_gather(ple_gain, "fsdp", axis=0, tiled=True),
    )
    full_query, full_key, full_value, full_out, full_left, full_right = (
        lax.all_gather(w_query.astype(bfloat), "fsdp", axis=0, tiled=True),
        lax.all_gather(w_key.astype(bfloat), "fsdp", axis=0, tiled=True),
        lax.all_gather(w_value.astype(bfloat), "fsdp", axis=0, tiled=True),
        lax.all_gather(w_out.astype(bfloat), "fsdp", axis=0, tiled=True),
        lax.all_gather(laurel_left.astype(bfloat), "fsdp", axis=0, tiled=True),
        lax.all_gather(laurel_right.astype(bfloat), "fsdp", axis=0, tiled=True),
    )
    inputs = tokens.astype(jnp.float32)
    ple_input = per_layer.astype(jnp.float32)
    normed, norm_back = jax.vjp(rms_norm, inputs, gain_in)
    normed_low = normed.astype(bfloat)
    query_lin = matmul(normed_low, full_query)
    key_lin = matmul(normed_low, full_key)
    value_lin = matmul(normed_low, full_value)
    (query_rot, key_rot), rope_back = jax.vjp(
        functools.partial(query_key, cosine, sine_part), query_lin, key_lin, gain_query, gain_key
    )
    query_low = query_rot.astype(bfloat).reshape(tok_count, KV, groups, HD)
    keys_values = jnp.stack(
        [key_rot.astype(bfloat), value_lin.astype(bfloat).reshape(tok_count, KV, HD)]
    )
    block_kv = lax.all_gather(keys_values, "fsdp", axis=1, tiled=True)
    block_len = block_kv.shape[1]
    before_kv = passed_along(block_kv, "ctx", 1)
    span_offset = block_len + lax.axis_index("fsdp") * tok_count - WINDOW
    span_kv = lax.dynamic_slice_in_dim(
        jnp.concatenate([before_kv, block_kv], axis=1), span_offset, span_len, 1
    )
    attended, log_total = attend_forward(query_low, span_kv, visible)
    attended_low = attended.astype(bfloat)
    projected = matmul(attended_low, full_out)
    narrow_low = matmul(normed_low, full_left).astype(bfloat)
    widened = matmul(narrow_low, full_right)
    mixed, mix_back = jax.vjp(mix_piece, inputs, normed, projected, widened, gain_post, gain_laurel)
    full_gate, full_up, full_down, full_pgate, full_pproj = (
        lax.all_gather(w_gate.astype(bfloat), "fsdp", axis=0, tiled=True),
        lax.all_gather(w_up.astype(bfloat), "fsdp", axis=0, tiled=True),
        lax.all_gather(w_down.astype(bfloat), "fsdp", axis=0, tiled=True),
        lax.all_gather(ple_gate.astype(bfloat), "fsdp", axis=0, tiled=True),
        lax.all_gather(ple_proj.astype(bfloat), "fsdp", axis=0, tiled=True),
    )
    ffn_normed, ffn_norm_back = jax.vjp(rms_norm, mixed, gain_ffin)
    ffn_low = ffn_normed.astype(bfloat)
    gate_lin = matmul(ffn_low, full_gate)
    up_lin = matmul(ffn_low, full_up)
    hidden, geglu_back = jax.vjp(geglu, gate_lin, up_lin)
    hidden_low = hidden.astype(bfloat)
    down_lin = matmul(hidden_low, full_down)
    layer_mid, ffn_out_back = jax.vjp(ffn_out_piece, mixed, down_lin, gain_ffout)
    layer_low = layer_mid.astype(bfloat)
    ple_lin = matmul(layer_low, full_pgate)
    ple_mid, ple_back = jax.vjp(ple_act, ple_lin, ple_input)
    ple_low = ple_mid.astype(bfloat)
    ple_wide = matmul(ple_low, full_pproj)
    out_full, final_back = jax.vjp(final_piece, layer_mid, ple_wide, gain_ple)
    full_gate, full_up, full_down, full_pgate, full_pproj = (
        lax.all_gather(w_gate.astype(bfloat), "fsdp", axis=0, tiled=True),
        lax.all_gather(w_up.astype(bfloat), "fsdp", axis=0, tiled=True),
        lax.all_gather(w_down.astype(bfloat), "fsdp", axis=0, tiled=True),
        lax.all_gather(ple_gate.astype(bfloat), "fsdp", axis=0, tiled=True),
        lax.all_gather(ple_proj.astype(bfloat), "fsdp", axis=0, tiled=True),
    )
    grad_layer, grad_pwide, grad_gple = final_back(cotangent.astype(jnp.float32))
    grad_pwide_low = grad_pwide.astype(bfloat)
    grad_pproj = settle(ple_low, grad_pwide_low)
    grad_plemid = matmul_nt(grad_pwide_low, full_pproj)
    grad_plelin, grad_pleinput = ple_back(grad_plemid)
    grad_plelin_low = grad_plelin.astype(bfloat)
    grad_pgate = settle(layer_low, grad_plelin_low)
    grad_layer = grad_layer + matmul_nt(grad_plelin_low, full_pgate)
    grad_mixed, grad_down, grad_gffout = ffn_out_back(grad_layer)
    grad_down_low = grad_down.astype(bfloat)
    grad_wdown = settle(hidden_low, grad_down_low)
    grad_hidden = matmul_nt(grad_down_low, full_down)
    grad_gate, grad_up = geglu_back(grad_hidden)
    grad_gate_low = grad_gate.astype(bfloat)
    grad_up_low = grad_up.astype(bfloat)
    grad_wgate = settle(ffn_low, grad_gate_low)
    grad_wup = settle(ffn_low, grad_up_low)
    grad_ffn = matmul_nt(grad_gate_low, full_gate) + matmul_nt(grad_up_low, full_up)
    grad_mixed_more, grad_gffin = ffn_norm_back(grad_ffn)
    grad_mixed = grad_mixed + grad_mixed_more
    full_query, full_key, full_value, full_out, full_left, full_right = (
        lax.all_gather(w_query.astype(bfloat), "fsdp", axis=0, tiled=True),
        lax.all_gather(w_key.astype(bfloat), "fsdp", axis=0, tiled=True),
        lax.all_gather(w_value.astype(bfloat), "fsdp", axis=0, tiled=True),
        lax.all_gather(w_out.astype(bfloat), "fsdp", axis=0, tiled=True),
        lax.all_gather(laurel_left.astype(bfloat), "fsdp", axis=0, tiled=True),
        lax.all_gather(laurel_right.astype(bfloat), "fsdp", axis=0, tiled=True),
    )
    grad_in_first, grad_normed, grad_proj, grad_lwide, grad_gpost, grad_glaurel = mix_back(
        grad_mixed
    )
    grad_proj_low = grad_proj.astype(bfloat)
    grad_wout = settle(attended_low, grad_proj_low)
    grad_att_low = matmul_nt(grad_proj_low, full_out).astype(bfloat)
    grad_lwide_low = grad_lwide.astype(bfloat)
    grad_wright = settle(narrow_low, grad_lwide_low)
    grad_narrow_low = matmul_nt(grad_lwide_low, full_right).astype(bfloat)
    grad_wleft = settle(normed_low, grad_narrow_low)
    grad_normed = grad_normed + matmul_nt(grad_narrow_low, full_left)
    grad_query_att, grad_span = attend_backward(
        query_low, span_kv, visible, log_total, grad_att_low.reshape(tok_count, KV, groups, HD)
    )
    whole_grad = jnp.zeros((2, 2 * block_len, KV, HD), jnp.float32)
    whole_grad = lax.dynamic_update_slice_in_dim(whole_grad, grad_span, span_offset, 1)
    returned = passed_along(whole_grad[:, :block_len].astype(jnp.bfloat16), "ctx", -1).astype(
        jnp.float32
    )
    own_grad = lax.psum_scatter(
        (whole_grad[:, block_len:] + returned).astype(jnp.bfloat16),
        "fsdp",
        scatter_dimension=1,
        tiled=True,
    ).astype(jnp.float32)
    grad_qlin, grad_klin, grad_gquery, grad_gkey = rope_back(
        (grad_query_att.reshape(tok_count, HQ, HD), own_grad[0])
    )
    grad_qlin_low = grad_qlin.astype(bfloat)
    grad_klin_low = grad_klin.astype(bfloat)
    grad_vlin_low = own_grad[1].reshape(tok_count, KV * HD).astype(bfloat)
    grad_wquery = settle(normed_low, grad_qlin_low)
    grad_wkey = settle(normed_low, grad_klin_low)
    grad_wvalue = settle(normed_low, grad_vlin_low)
    grad_normed = (
        grad_normed
        + matmul_nt(grad_qlin_low, full_query)
        + matmul_nt(grad_klin_low, full_key)
        + matmul_nt(grad_vlin_low, full_value)
    )
    grad_in_second, grad_gin = norm_back(grad_normed)
    grad_tokens = grad_in_first + grad_in_second
    sum_gin, sum_gquery, sum_gkey, sum_gpost, sum_glaurel, sum_gffin, sum_gffout, sum_gple = (
        lax.psum(
            (
                grad_gin,
                grad_gquery,
                grad_gkey,
                grad_gpost,
                grad_glaurel,
                grad_gffin,
                grad_gffout,
                grad_gple,
            ),
            ("ctx", "fsdp"),
        )
    )
    wide_rows = attn_in_gain.shape[0]
    head_rows = query_gain.shape[0]
    wide_start = lax.axis_index("fsdp") * wide_rows
    head_start = lax.axis_index("fsdp") * head_rows

    def wide_part(full_vec):
        return lax.dynamic_slice_in_dim(full_vec, wide_start, wide_rows, 0)

    def head_part(full_vec):
        return lax.dynamic_slice_in_dim(full_vec, head_start, head_rows, 0)

    return (
        out_full.astype(bfloat),
        grad_tokens,
        grad_pleinput,
        grad_wquery,
        grad_wkey,
        grad_wvalue,
        grad_wout,
        grad_wleft,
        grad_wright,
        grad_wgate,
        grad_wup,
        grad_wdown,
        grad_pgate,
        grad_pproj,
        wide_part(sum_gin),
        head_part(sum_gquery),
        head_part(sum_gkey),
        wide_part(sum_gpost),
        wide_part(sum_glaurel),
        wide_part(sum_gffin),
        wide_part(sum_gffout),
        wide_part(sum_gple),
    )

class Plane:
    def locate(self, columns, rows):
        self.columns = columns
        at = lax.axis_index("ctx")
        self.at_x, self.at_y = at % 2, at // 2
        self.beside = (at + 1 - 2 * (at % 2), (at + 2) % 4)
        self.me = lax.axis_index("fsdp")
        self.members = lax.axis_size("fsdp")
        self.half = rows // 2
        self.quarter = rows // 4
        self.eighth = rows // 8

    def rows(self, ref, start, size):
        start = pl.multiple_of(start, size)
        return ref.at[:, pl.ds(start, size)] if self.columns else ref.at[pl.ds(start, size)]

    def sides(self, half):
        return (self.at_x, self.at_y) if half == 0 else (self.at_y, self.at_x)

    def kept_start(self, half):
        return half * self.half + self.sides(half)[0] * self.quarter

    def given_start(self, half):
        return half * self.half + (1 - self.sides(half)[0]) * self.quarter

    def own_start(self, half):
        return self.kept_start(half) + self.sides(half)[1] * self.eighth

    def copy(self, src, dst, send_sem, recv_sem, half, stage):
        return pltpu.make_async_remote_copy(
            src_ref=src,
            dst_ref=dst,
            send_sem=send_sem.at[half, stage],
            recv_sem=recv_sem.at[half, stage],
            device_id={"ctx": self.beside[(half + stage) % 2]},
            device_id_type=pl.DeviceIdType.MESH,
        )


class Summed(Plane):
    def __init__(self, source, refs, columns):
        self.source = source
        self.kept, self.taken, self.last, self.load_sem, self.sum_send, self.sum_recv = refs
        self.locate(columns, source.shape[-2])

    def load(self, half):
        return pltpu.make_async_copy(
            self.rows(self.source, self.kept_start(half), self.quarter),
            self.kept.at[half],
            self.load_sem.at[half],
        )

    def first(self, half):
        return self.copy(
            self.rows(self.source, self.given_start(half), self.quarter),
            self.taken.at[half],
            self.sum_send,
            self.sum_recv,
            half,
            0,
        )

    def second(self, half):
        other = (1 - self.sides(half)[1]) * self.eighth
        return self.copy(
            self.rows(self.kept.at[half], other, self.eighth),
            self.last.at[half],
            self.sum_send,
            self.sum_recv,
            half,
            1,
        )

    def begin(self):
        for half in (0, 1):
            self.first(half).start()
            self.load(half).start()

    def add(self, half, start, more, more_start):
        step = min(32, self.eighth)
        blocks = self.eighth // step
        layers = self.source.shape[0] if self.columns else 1

        @pl.loop(0, layers * blocks)
        def _(at):
            layer, block = at // blocks, at % blocks
            here = pl.ds(pl.multiple_of(start + block * step, step), step)
            there = pl.ds(pl.multiple_of(more_start + block * step, step), step)
            if self.columns:
                self.kept[half, layer, here] += more[half, layer, there]
            else:
                self.kept[half, here] += more[half, there]

    def middle(self):
        for half in (0, 1):
            self.load(half).wait()
            self.first(half).wait_recv()
            side = self.sides(half)[1]
            other = (1 - side) * self.eighth
            self.add(half, other, self.taken, other)
            self.second(half).start()
            mine = side * self.eighth
            self.add(half, mine, self.taken, mine)

    def finish(self):
        for half in (0, 1):
            self.second(half).wait_recv()
            self.add(half, self.sides(half)[1] * self.eighth, self.last, 0)

    def own_rows(self, half):
        return self.rows(self.kept.at[half], self.sides(half)[1] * self.eighth, self.eighth)

    def held(self, half, member):
        side = self.sides(half)[1] * self.eighth
        return self.kept.at[half, member, pl.ds(pl.multiple_of(side, self.eighth), self.eighth)]

    def sum_sent(self):
        for half in (0, 1):
            self.first(half).wait_send()
            self.second(half).wait_send()


class Held:
    def __init__(self, kept, side=0, sides=1):
        self.kept = kept
        width = kept.shape[-1] // sides
        self.cols = pl.ds(side * width, width)

    def own_rows(self, half):
        return self.kept.at[half]

    def held(self, half, member):
        return self.kept.at[half, member, :, self.cols]


class Spread(Plane):
    def __init__(self, source, refs, columns):
        self.own_rows, self.held = source.own_rows, source.held
        self.final, self.spread_send, self.spread_recv, self.place_sem = refs[:4]
        if columns:
            self.swap_send, self.swap_recv = refs[4:]
        self.locate(columns, self.final.shape[-2])

    def place(self, half):
        return pltpu.make_async_copy(
            self.own_rows(half),
            self.rows(self.final, self.own_start(half), self.eighth),
            self.place_sem.at[half],
        )

    def place_all(self):
        for half in (0, 1):
            self.place(half).start()
        for half in (0, 1):
            self.place(half).wait()

    def swap_place(self, half, member):
        start = pl.multiple_of(self.own_start(half), self.eighth)
        return self.final.at[member, pl.ds(start, self.eighth)]

    def swap_copy(self, half, hop, src_member):
        target = lax.rem(self.me + hop, self.members)
        return remote(
            self.held(half, target),
            self.swap_place(half, src_member),
            self.swap_send.at[hop, half],
            self.swap_recv.at[hop, half],
            target,
        )

    def swap_local(self, half):
        return pltpu.make_async_copy(
            self.held(half, self.me),
            self.swap_place(half, self.me),
            self.place_sem.at[half],
        )

    def swap_begin(self):
        for half in (0, 1):
            for hop in range(1, self.members):
                self.swap_copy(half, hop, self.me).start()
            self.swap_local(half).start()

    def swap_end(self):
        for half in (0, 1):
            for hop in range(1, self.members):
                source = lax.rem(self.me + self.members - hop, self.members)
                self.swap_copy(half, hop, source).wait_recv()
            self.swap_local(half).wait()

    def spread_copy(self, half, stage):
        if stage == 0:
            rows = self.rows(self.final, self.own_start(half), self.eighth)
        else:
            rows = self.rows(self.final, self.kept_start(half), self.quarter)
        return self.copy(rows, rows, self.spread_send, self.spread_recv, half, 1 - stage)

    def spread_wait(self, half, stage):
        side = self.sides(half)[1]
        if stage == 0:
            start = self.kept_start(half) + (1 - side) * self.eighth
            rows = self.rows(self.final, start, self.eighth)
        else:
            rows = self.rows(self.final, self.given_start(half), self.quarter)
        self.copy(rows, rows, self.spread_send, self.spread_recv, half, 1 - stage).wait_recv()

    def spread_begin(self):
        for half in (0, 1):
            self.spread_copy(half, 0).start()

    def spread_on(self):
        for half in (0, 1):
            self.spread_wait(half, 0)
            self.spread_copy(half, 1).start()

    def spread_end(self):
        for half in (0, 1):
            self.spread_wait(half, 1)

    def spread_sent(self, swapped=True):
        for half in (0, 1):
            self.spread_copy(half, 0).wait_send()
            self.spread_copy(half, 1).wait_send()
            if self.columns and swapped:
                for hop in range(1, self.members):
                    self.swap_copy(half, hop, self.me).wait_send()


class GroupSpread(Spread):
    def __init__(self, source, refs):
        self.landing = refs[0]
        super().__init__(source, refs[1:], True)

    def swap_place(self, half, member):
        return self.landing.at[half, member]

    def swap_end(self):
        super().swap_end()
        groups = self.final.shape[0]
        size = self.landing.shape[1] // groups
        for half in (0, 1):
            rows = pl.ds(pl.multiple_of(self.own_start(half), self.eighth), self.eighth)
            for group in range(groups):
                total = self.landing[half, group * size].astype(jnp.float32)
                for member in range(group * size + 1, (group + 1) * size):
                    total = total + self.landing[half, member].astype(jnp.float32)
                self.final[group, rows] = total.astype(jnp.bfloat16)


class PairSpread(Spread):
    def __init__(self, source, refs):
        self.landing = refs[0]
        super().__init__(source, refs[1:], True)
        self.chips = self.members // 2
        self.chip, self.core = self.me // 2, self.me % 2

    def to_member(self, half, at):
        return remote(
            self.held(half, at),
            self.landing.at[half, self.chip],
            self.swap_send.at[at, half],
            self.swap_recv.at[self.chip, half],
            self.core * self.chips + at,
        )

    def from_chip(self, half, chip):
        place = self.landing.at[half, chip]
        return remote(
            place,
            place,
            self.swap_send.at[chip, half],
            self.swap_recv.at[chip, half],
            lax.rem(self.me + 1, self.members),
        )

    def swap_local(self, half):
        return pltpu.make_async_copy(
            self.held(half, self.me - self.core * self.chips),
            self.landing.at[half, self.chip],
            self.place_sem.at[half],
        )

    def swap_begin(self):
        for half in (0, 1):
            for at in range(self.chips):
                mine = self.core * self.chips + at == self.me
                pl.when(mine)(self.swap_local(half).start)
                pl.when(jnp.logical_not(mine))(self.to_member(half, at).start)

    def swap_end(self):
        groups = self.final.shape[0]
        size = self.chips // groups
        for half in (0, 1):
            for chip in range(self.chips):
                mine = 2 * chip + self.me // self.chips == self.me
                pl.when(mine)(self.swap_local(half).wait)
                pl.when(jnp.logical_not(mine))(self.from_chip(half, chip).wait_recv)
            rows = pl.ds(pl.multiple_of(self.own_start(half), self.eighth), self.eighth)
            for group in range(groups):
                total = self.landing[half, group * size].astype(jnp.float32)
                for chip in range(group * size + 1, (group + 1) * size):
                    total = total + self.landing[half, chip].astype(jnp.float32)
                self.final[group, rows] = total.astype(jnp.bfloat16)

    def spread_sent(self):
        for half in (0, 1):
            self.spread_copy(half, 0).wait_send()
            self.spread_copy(half, 1).wait_send()
            for at in range(self.chips):
                mine = self.core * self.chips + at == self.me
                pl.when(jnp.logical_not(mine))(self.to_member(half, at).wait_send)


class Everywhere(Spread):
    def swap_begin(self):
        chips = self.members // 2
        for half in (0, 1):
            own = self.own_rows(half)
            for hop in range(1, chips):
                self.hand_to(half, hop, own, lax.rem(self.me + 2 * hop, self.members)).start()
            self.pass_on(half, self.me // 2, own).start()
            self.swap_local(half).start()

    def hand_to(self, half, hop, own, place):
        return remote(
            own,
            self.swap_place(half, self.me),
            self.swap_send.at[0, hop, half],
            self.swap_recv.at[0, hop, half],
            place,
        )

    def pass_on(self, half, chip, source):
        core = self.me % 2
        return remote(
            source,
            self.swap_place(half, 2 * chip + core),
            self.swap_send.at[1, chip, half],
            self.swap_recv.at[1, chip, half],
            self.me + 1 - 2 * core,
        )

    def swap_on(self):
        chips = self.members // 2
        for hop in range(1, chips):
            sender = lax.rem(self.me + self.members - 2 * hop, self.members)
            for half in (0, 1):
                place = self.swap_place(half, sender)
                remote(
                    place,
                    place,
                    self.swap_send.at[0, hop, half],
                    self.swap_recv.at[0, hop, half],
                    sender,
                ).wait_recv()
                self.pass_on(half, sender // 2, place).start()

    def swap_end(self):
        core = self.me % 2
        for chip in range(self.members // 2):
            for half in (0, 1):
                place = self.swap_place(half, 2 * chip + 1 - core)
                remote(
                    place,
                    place,
                    self.swap_send.at[1, chip, half],
                    self.swap_recv.at[1, chip, half],
                    self.me + 1 - 2 * core,
                ).wait_recv()
        for half in (0, 1):
            self.swap_local(half).wait()

    def spread_sent(self):
        for half in (0, 1):
            self.spread_copy(half, 0).wait_send()
            self.spread_copy(half, 1).wait_send()
        self.swap_sent()

    def swap_sent(self):
        chips = self.members // 2
        for half in (0, 1):
            own = self.own_rows(half)
            for hop in range(1, chips):
                self.hand_to(half, hop, own, lax.rem(self.me + 2 * hop, self.members)).wait_send()
            for chip in range(chips):
                self.pass_on(half, chip, own).wait_send()


def sum_scratch(shape):
    dma = pltpu.SemaphoreType.DMA
    rows, width = shape[-2:]

    def buffer(count):
        return pltpu.VMEM((2,) + shape[:-2] + (count, width), jnp.bfloat16)

    buffers = [buffer(rows // 4), buffer(rows // 4), buffer(rows // 8)]
    return buffers + [dma((2,)), dma((2, 2)), dma((2, 2))]


SUM_REFS = 6


def spread_scratch(shape, members=None):
    dma = pltpu.SemaphoreType.DMA
    scratch = [pltpu.VMEM(shape, jnp.bfloat16), dma((2, 2)), dma((2, 2)), dma((2,))]
    if len(shape) == 3:
        count = members or shape[0]
        scratch += [dma((count, 2)), dma((count, 2))]
    return scratch


def everywhere_scratch(shape):
    dma = pltpu.SemaphoreType.DMA
    chips = shape[0] // 2
    scratch = [pltpu.VMEM(shape, jnp.bfloat16), dma((2, 2)), dma((2, 2)), dma((2,))]
    return scratch + [dma((2, chips, 2)), dma((2, chips, 2))]


def spread_refs(columns):
    return 6 if columns else 4


def gradient_sum_kernel(plan, *refs):
    refs = list(refs)
    count = len(plan)
    sources = refs[:count]
    results_count = sum(max(1, one.sides) for one in plan)
    results = refs[count : count + results_count]
    scratch = refs[count + results_count :]
    store_sem = scratch.pop()

    def take(size):
        taken = scratch[:size]
        del scratch[:size]
        return taken

    sums, spreads, late = [], [], []
    for source, one in zip(sources, plan):
        if one.summed:
            held = Held(source, *one.part)
        else:
            held = Summed(source, take(SUM_REFS), one.columns)
            sums.append(held)
        size = spread_refs(one.columns)
        if one.groups:
            kind = PairSpread if one.paired else GroupSpread
            spreads.append(kind(held, take(size + 1)))
        else:
            spreads.append(Spread(held, take(size), one.columns))
        if not one.summed:
            late.append(spreads[-1])
    early = [spread for spread in spreads if spread not in late]
    greet_all()

    def stores(at):
        final, sides = spreads[at].final, plan[at].sides
        first = sum(max(1, one.sides) for one in plan[:at])
        if sides == 0:
            return [pltpu.make_async_copy(final, results[first], store_sem.at[at, 0, 0])]
        part = final.shape[2] // sides
        return [
            pltpu.make_async_copy(
                final.at[member, :, pl.ds(side * part, part)],
                results[first + side].at[:, pl.ds(member * part, part)],
                store_sem.at[at, side, member],
            )
            for member in range(final.shape[0])
            for side in range(sides)
        ]

    def launch(spread):
        if spread.columns:
            spread.swap_begin()
        else:
            spread.place_all()
            spread.spread_begin()

    for share in sums:
        share.begin()
    for spread in early:
        launch(spread)
    for share in sums:
        share.middle()
    for spread in early[:1]:
        spread.swap_end()
        spread.spread_begin()
    for share, spread in zip(sums, late):
        share.finish()
        launch(spread)
    for spread in early[:1]:
        spread.spread_on()
    for spread in early[1:]:
        spread.swap_end()
        spread.spread_begin()
    for spread in late:
        if spread.columns:
            spread.swap_end()
            spread.spread_begin()
        else:
            spread.spread_on()
    for spread in early[1:]:
        spread.spread_on()
    for spread in late:
        if spread.columns:
            spread.spread_on()
    for at in sorted(range(count), key=lambda one: spreads[one] in early):
        spreads[at].spread_end()
        for store in stores(at):
            store.start()
    for share in sums:
        share.sum_sent()
    for spread in spreads:
        spread.spread_sent()
    for at in range(count):
        for store in stores(at):
            store.wait()


@dataclasses.dataclass
class Source:
    array: jax.Array
    summed: bool = False
    part: tuple = (0, 1)
    groups: int = 0
    paired: bool = False
    sides: int = 0

    @property
    def columns(self):
        return self.array.ndim - self.summed == 3

    @property
    def shape(self):
        shape = self.array.shape
        if self.summed:
            shape = shape[1:-2] + (8 * shape[-2], shape[-1] // self.part[1])
        return shape


def gradient_sum(sources):
    members = lax.axis_size("fsdp")
    anywhere = pl.BlockSpec(memory_space=pl.ANY)
    scratch, results = [], []
    for one in sources:
        shape = one.shape
        if not one.summed:
            scratch += sum_scratch(shape)
        if one.groups:
            landing = (2, shape[0] if one.paired else members, shape[1] // 8, shape[2])
            scratch.append(pltpu.VMEM(landing, jnp.bfloat16))
            shape = (one.groups,) + shape[1:]
        scratch += spread_scratch(shape, members)
        if one.sides == 0:
            results.append(shape)
        else:
            results += [(shape[1], shape[0] * shape[2] // one.sides)] * one.sides
    return pl.pallas_call(
        functools.partial(gradient_sum_kernel, sources),
        out_shape=[jax.ShapeDtypeStruct(shape, jnp.bfloat16) for shape in results],
        in_specs=[anywhere] * len(sources),
        out_specs=[anywhere] * len(results),
        scratch_shapes=scratch + [pltpu.SemaphoreType.DMA((len(sources), 2, members))],
        compiler_params=pltpu.CompilerParams(
            collective_id=3, has_side_effects=True, vmem_limit_bytes=KERNEL_VMEM
        ),
        cost_estimate=pl.CostEstimate(flops=0, bytes_accessed=300 << 20, transcendentals=0),
        name="gradient_sum",
    )(*(one.array for one in sources))

def remote(src, dst, send_sem, recv_sem, place):
    return pltpu.make_async_remote_copy(
        src_ref=src,
        dst_ref=dst,
        send_sem=send_sem,
        recv_sem=recv_sem,
        device_id={"fsdp": place},
        device_id_type=pl.DeviceIdType.MESH,
    )


def dot_nn(left_mat, right_mat):
    return jnp.dot(left_mat, right_mat, preferred_element_type=jnp.float32)


def dot_nt(left_mat, right_mat):
    return lax.dot_general(
        left_mat, right_mat, (((1,), (1,)), ((), ())), preferred_element_type=jnp.float32
    )


def dot_tn(left_mat, right_mat):
    return lax.dot_general(
        left_mat, right_mat, (((0,), (0,)), ((), ())), preferred_element_type=jnp.float32
    )


def greet_all():
    sem = pltpu.get_barrier_semaphore()
    members, planes = lax.axis_size("fsdp"), lax.axis_size("ctx")
    mesh_id = pl.DeviceIdType.MESH
    for hop in range(1, planes):
        other = lax.rem(lax.axis_index("ctx") + hop, planes)
        pl.semaphore_signal(sem, inc=1, device_id={"ctx": other}, device_id_type=mesh_id)
    for hop in range(1, members):
        other = lax.rem(lax.axis_index("fsdp") + hop, members)
        pl.semaphore_signal(sem, inc=1, device_id={"fsdp": other}, device_id_type=mesh_id)
    pl.semaphore_wait(sem, members + planes - 2)


PIECES = 4


def line_scratch(chips, tok_count, width):
    dma = pltpu.SemaphoreType.DMA
    shard = (tok_count, width)
    return [
        pltpu.VMEM((chips, 2) + shard, jnp.bfloat16),
        dma((chips, 2)),
        dma((chips, 3)),
        dma,
        pltpu.VMEM((chips, 2) + shard, jnp.bfloat16),
        pltpu.VMEM((chips,) + shard, jnp.bfloat16),
        pltpu.VMEM((chips,) + shard, jnp.bfloat16),
        pltpu.VMEM((chips,) + shard, jnp.bfloat16),
        dma((chips,)),
        dma((chips,)),
        dma((chips, PIECES)),
        dma((chips, PIECES)),
        dma((chips, PIECES)),
    ]


LINE_REFS = 13


class Line:
    def __init__(self, chips, refs):
        (
            self.slots,
            self.slot_recv,
            self.slot_send,
            self.own_sem,
            self.parts,
            self.from_core,
            self.from_left,
            self.from_right,
            self.core_send,
            self.core_recv,
            self.flow_send,
            self.left_recv,
            self.right_recv,
        ) = refs
        self.chips = chips
        me = lax.axis_index("fsdp")
        self.chip = me // 2
        self.core = me % 2
        self.tok = self.slots.shape[2]
        self.piece = self.tok // PIECES

    def place(self, chip, core):
        return chip * 2 + core

    def order(self, step):
        picked = 0
        for chip in range(self.chips):
            near = sorted(range(self.chips), key=lambda other: (abs(other - chip), other))
            picked = picked + jnp.where(self.chip == chip, near[step], 0)
        return picked

    def slot_copy(self, src, chip, way):
        place = (
            self.place(self.chip + 1, self.core),
            self.place(self.chip - 1, self.core),
            self.place(self.chip, 1 - self.core),
        )[way]
        return remote(
            src,
            self.slots.at[chip, self.core],
            self.slot_send.at[chip, way],
            self.slot_recv.at[chip, self.core],
            place,
        )

    def own_copy(self, own_ref):
        return pltpu.make_async_copy(own_ref, self.slots.at[self.chip, self.core], self.own_sem)

    def gather_begin(self, own_ref):
        @pl.when(self.chip < self.chips - 1)
        def _():
            self.slot_copy(own_ref, self.chip, 0).start()

        @pl.when(self.chip > 0)
        def _():
            self.slot_copy(own_ref, self.chip, 1).start()

        self.slot_copy(own_ref, self.chip, 2).start()
        self.own_copy(own_ref).start()

    def gather_step(self, distance):
        for chip, there, way, onward in (
            (self.chip - distance, self.chip >= distance, 0, self.chip < self.chips - 1),
            (self.chip + distance, self.chip + distance < self.chips, 1, self.chip > 0),
        ):

            @pl.when(there)
            def _(chip=chip, way=way, onward=onward):
                src = self.slots.at[chip, self.core]
                self.slot_copy(src, chip, way).wait_recv()

                @pl.when(onward)
                def _():
                    self.slot_copy(src, chip, way).start()

                self.slot_copy(src, chip, 2).start()

    def gather_other(self, chip):
        dst = self.slots.at[chip, 1 - self.core]
        remote(
            dst,
            dst,
            self.slot_send.at[chip, 2],
            self.slot_recv.at[chip, 1 - self.core],
            self.place(self.chip, 1 - self.core),
        ).wait_recv()

    def gather_end(self):
        for chip in range(self.chips):
            src = self.slots.at[chip, self.core]

            @pl.when((self.chip >= chip) & (self.chip < self.chips - 1))
            def _(src=src, chip=chip):
                self.slot_copy(src, chip, 0).wait_send()

            @pl.when((self.chip <= chip) & (self.chip > 0))
            def _(src=src, chip=chip):
                self.slot_copy(src, chip, 1).wait_send()

            self.slot_copy(src, chip, 2).wait_send()

    def core_copy(self, chip):
        return remote(
            self.parts.at[chip, 1 - self.core],
            self.from_core.at[chip],
            self.core_send.at[chip],
            self.core_recv.at[chip],
            self.place(self.chip, 1 - self.core),
        )

    def flow_copy(self, chip, piece, right):
        rows = pl.ds(piece * self.piece, self.piece)
        return remote(
            self.parts.at[chip, self.core, rows],
            (self.from_left if right else self.from_right).at[chip, rows],
            self.flow_send.at[chip, piece],
            (self.left_recv if right else self.right_recv).at[chip, piece],
            self.place(self.chip + (1 if right else -1), self.core),
        )

    def flow(self, chip, right, incoming):
        self.core_copy(chip).wait_recv()

        @pl.loop(0, PIECES)
        def _(piece):
            rows = pl.ds(pl.multiple_of(piece * self.piece, self.piece), self.piece)
            total = self.parts[chip, self.core, rows].astype(jnp.float32)
            total = total + self.from_core[chip, rows].astype(jnp.float32)
            if incoming:
                self.flow_copy(chip, piece, right).wait_recv()
                source = self.from_left if right else self.from_right
                total = total + source[chip, rows].astype(jnp.float32)
            self.parts[chip, self.core, rows] = total.astype(jnp.bfloat16)
            self.flow_copy(chip, piece, right).start()

    def scatter_first(self, chip):
        @pl.when((self.chip == 0) & (chip > 0))
        def _():
            self.flow(chip, True, False)

        @pl.when((self.chip == self.chips - 1) & (chip < self.chips - 1))
        def _():
            self.flow(chip, False, False)

    def scatter_rest(self, result_ref, between=None):
        for rank in range(3, 2 * self.chips - 2):
            right = rank - self.chip

            @pl.when((self.chip > 0) & (right > self.chip) & (right < self.chips))
            def _(right=right):
                self.flow(right, True, True)

            left = 2 * (self.chips - 1) - self.chip - rank

            @pl.when((self.chip < self.chips - 1) & (left < self.chip) & (left >= 0))
            def _(left=left):
                self.flow(left, False, True)

            if between is not None:
                between(rank)

        own = self.chip
        self.core_copy(own).wait_recv()

        @pl.loop(0, PIECES)
        def _(piece):
            rows = pl.ds(pl.multiple_of(piece * self.piece, self.piece), self.piece)
            total = self.parts[own, self.core, rows].astype(jnp.float32)
            total = total + self.from_core[own, rows].astype(jnp.float32)
            result_ref[rows] = total

        @pl.when(own > 0)
        def _():
            @pl.loop(0, PIECES)
            def _(piece):
                rows = pl.ds(pl.multiple_of(piece * self.piece, self.piece), self.piece)
                self.flow_copy(own, piece, True).wait_recv()
                result_ref[rows] += self.from_left[own, rows].astype(jnp.float32)

        @pl.when(own < self.chips - 1)
        def _():
            @pl.loop(0, PIECES)
            def _(piece):
                rows = pl.ds(pl.multiple_of(piece * self.piece, self.piece), self.piece)
                self.flow_copy(own, piece, False).wait_recv()
                result_ref[rows] += self.from_right[own, rows].astype(jnp.float32)

        for chip in range(self.chips):
            self.core_copy(chip).wait_send()

            @pl.when(self.chip != chip)
            def _(chip=chip):
                for piece in range(PIECES):
                    self.flow_copy(chip, piece, True).wait_send()


def ffn_forward_kernel(
    chips,
    own_ref,
    gateup_hbm,
    down_hbm,
    ple_held,
    result_ref,
    all_hbm,
    hidden_hbm,
    act_hbm,
    slope_hbm,
    ple_hbm,
    down_low,
    *scratch,
):
    line = Line(chips, scratch[:LINE_REFS])
    gateup, down, hidden, act, slope, load_sems, store_sems = scratch[LINE_REFS : LINE_REFS + 7]
    down_wide = scratch[LINE_REFS + 7]
    ple = Spread(Held(ple_held), scratch[LINE_REFS + 8 :], True)
    ff_part = down.shape[0]
    width = down.shape[1]
    pair = 2 * line.tok
    load_gateup = pltpu.make_async_copy(gateup_hbm, gateup, load_sems.at[0])
    load_down = pltpu.make_async_copy(down_hbm, down_wide, load_sems.at[1])
    store_down = pltpu.make_async_copy(down, down_low, load_sems.at[3])
    load_gateup.start()
    load_down.start()
    greet_all()
    line.gather_begin(own_ref)
    ple.place_all()
    ple.spread_begin()
    line.own_copy(own_ref).wait()
    store_ple = pltpu.make_async_copy(ple.final, ple_hbm, load_sems.at[2])

    def stores(chip):
        rows = pl.ds(pl.multiple_of(chip * pair, pair), pair)
        return [
            pltpu.make_async_copy(line.slots.at[chip], all_hbm.at[chip], store_sems.at[chip, 0]),
            pltpu.make_async_copy(hidden.at[rows], hidden_hbm.at[rows], store_sems.at[chip, 1]),
            pltpu.make_async_copy(act.at[rows], act_hbm.at[rows], store_sems.at[chip, 2]),
            pltpu.make_async_copy(slope.at[rows], slope_hbm.at[rows], store_sems.at[chip, 3]),
        ]

    tile = 256
    for step in range(chips):
        if step > 0:
            line.gather_step(step)
        chip = line.order(step)
        line.gather_other(chip)
        if step == 0:
            load_gateup.wait()
            load_down.wait()
            down[...] = down_wide[...].astype(jnp.bfloat16)
            store_down.start()
        rows = pl.ds(pl.multiple_of(chip * pair, pair), pair)

        @pl.loop(0, ff_part // tile)
        def _(at, chip=chip, rows=rows):
            inputs = line.slots[chip].reshape(pair, width)
            gate_cols = pl.ds(pl.multiple_of(at * tile, tile), tile)
            up_cols = pl.ds(pl.multiple_of(ff_part + at * tile, tile), tile)
            gate = dot_nn(inputs, gateup[:, gate_cols])
            up = dot_nn(inputs, gateup[:, up_cols])
            square = gate * gate
            bent = jnp.tanh(GELU_ROOT * gate * (1.0 + GELU_CUBE * square))
            half = 0.5 + 0.5 * bent
            activated = gate * half
            rise = half + 0.5 * gate * (1.0 - bent * bent) * (
                GELU_ROOT * (1.0 + 3.0 * GELU_CUBE * square)
            )
            hidden[rows, gate_cols] = (activated * up).astype(jnp.bfloat16)
            act[rows, gate_cols] = activated.astype(jnp.bfloat16)
            slope[rows, gate_cols] = (rise * up).astype(jnp.bfloat16)

        for copy in stores(chip):
            copy.start()

        wide = 512

        @pl.loop(0, width // wide)
        def _(at, chip=chip, rows=rows):
            cols = pl.ds(pl.multiple_of(at * wide, wide), wide)
            sums = dot_nn(hidden[rows, :], down[:, cols]).astype(jnp.bfloat16)
            line.parts[chip, :, :, cols] = sums.reshape(2, line.tok, wide)

        line.core_copy(chip).start()
        line.scatter_first(chip)
    ple.spread_on()
    line.scatter_rest(result_ref)
    ple.spread_end()
    store_ple.start()
    line.gather_end()
    ple.spread_sent(False)
    store_ple.wait()
    store_down.wait()
    for chip in range(chips):
        for copy in stores(chip):
            copy.wait()


def ffn_forward(own, gateup, down, ple, chips):
    tok_count, width = own.shape
    ff_part = down.shape[0]
    block = 2 * chips * tok_count
    bfloat = jnp.bfloat16
    anywhere = pl.BlockSpec(memory_space=pl.ANY)
    vmem = pl.BlockSpec(memory_space=pltpu.VMEM)
    part = jax.ShapeDtypeStruct((block, ff_part), bfloat)
    ple_shape = (ple.shape[1], 8 * ple.shape[2], ple.shape[3])
    result, gathered, hidden, act, slope, ple_all, down_low = pl.pallas_call(
        functools.partial(ffn_forward_kernel, chips),
        out_shape=[
            jax.ShapeDtypeStruct((tok_count, width), jnp.float32),
            jax.ShapeDtypeStruct((chips, 2, tok_count, width), bfloat),
            part,
            part,
            part,
            jax.ShapeDtypeStruct(ple_shape, bfloat),
            jax.ShapeDtypeStruct(down.shape, bfloat),
        ],
        in_specs=[vmem, anywhere, anywhere, anywhere],
        out_specs=[vmem] + [anywhere] * 6,
        scratch_shapes=line_scratch(chips, tok_count, width)
        + [
            pltpu.VMEM(gateup.shape, bfloat),
            pltpu.VMEM(down.shape, bfloat),
            pltpu.VMEM((block, ff_part), bfloat),
            pltpu.VMEM((block, ff_part), bfloat),
            pltpu.VMEM((block, ff_part), bfloat),
            pltpu.SemaphoreType.DMA((4,)),
            pltpu.SemaphoreType.DMA((chips, 4)),
            pltpu.VMEM(down.shape, down.dtype),
        ]
        + spread_scratch(ple_shape),
        compiler_params=pltpu.CompilerParams(
            collective_id=1, has_side_effects=True, vmem_limit_bytes=KERNEL_VMEM
        ),
        cost_estimate=pl.CostEstimate(
            flops=6 * block * width * ff_part,
            bytes_accessed=40 << 20,
            transcendentals=block * ff_part,
        ),
        name="ffn_forward",
    )(own, gateup, down, ple)
    return result, gathered.reshape(block, width), hidden, act, slope, ple_all, down_low


def ffn_backward_kernel(
    chips,
    own_ref,
    gateup_hbm,
    down_hbm,
    hidden_hbm,
    act_hbm,
    slope_hbm,
    inputs_hbm,
    pgate_hbm,
    pproj_hbm,
    result_ref,
    part_hbm,
    down_kept,
    pgate_kept,
    pproj_kept,
    *scratch,
):
    line = Line(chips, scratch[:LINE_REFS])
    scratch = scratch[LINE_REFS:]
    gateup, down, hidden, act, slope, inputs, grad, part_down, staged = scratch[:9]
    load_sems, store_sems, kept_sems = scratch[9:12]
    share = Summed(part_down, scratch[12 : 12 + SUM_REFS], False)
    small = [
        Summed(pgate_hbm, scratch[12 + SUM_REFS : 12 + 2 * SUM_REFS], True),
        Summed(pproj_hbm, scratch[12 + 2 * SUM_REFS :], True),
    ]
    ff_part = down.shape[0]
    width = down.shape[1]
    pair = 2 * line.tok
    loads = [
        pltpu.make_async_copy(src, dst, load_sems.at[at])
        for at, (src, dst) in enumerate(
            (
                (down_hbm, down),
                (act_hbm, act),
                (slope_hbm, slope),
                (gateup_hbm, gateup),
                (hidden_hbm, hidden),
                (inputs_hbm, inputs),
            )
        )
    ]
    for load in loads:
        load.start()
    greet_all()
    line.gather_begin(own_ref)
    for one in small:
        one.begin()
    line.own_copy(own_ref).wait()

    tile = 256
    wide = 512
    for step in range(chips):
        if step > 0:
            line.gather_step(step)
        chip = line.order(step)
        line.gather_other(chip)
        if step == 0:
            for load in loads[:4]:
                load.wait()
        rows = pl.ds(pl.multiple_of(chip * pair, pair), pair)

        @pl.loop(0, ff_part // tile)
        def _(at, chip=chip, rows=rows):
            grads = line.slots[chip].reshape(pair, width)
            gate_cols = pl.ds(pl.multiple_of(at * tile, tile), tile)
            up_cols = pl.ds(pl.multiple_of(ff_part + at * tile, tile), tile)
            grad_hidden = dot_nt(grads, down[gate_cols, :])
            grad[rows, gate_cols] = (
                grad_hidden * slope[rows, gate_cols].astype(jnp.float32)
            ).astype(jnp.bfloat16)
            grad[rows, up_cols] = (grad_hidden * act[rows, gate_cols].astype(jnp.float32)).astype(
                jnp.bfloat16
            )

        @pl.loop(0, width // wide)
        def _(at, chip=chip, rows=rows):
            cols = pl.ds(pl.multiple_of(at * wide, wide), wide)
            sums = dot_nt(grad[rows, :], gateup[cols, :]).astype(jnp.bfloat16)
            line.parts[chip, :, :, cols] = sums.reshape(2, line.tok, wide)

        line.core_copy(chip).start()
        line.scatter_first(chip)
    for one in small:
        one.middle()
    for load in loads[4:]:
        load.wait()

    block = chips * pair

    def down_grads():
        @pl.loop(0, ff_part // tile)
        def _(at):
            rows = pl.ds(pl.multiple_of(at * tile, tile), tile)
            left = hidden[:, rows]
            for start in range(0, width, wide):
                right = line.slots[:, :, :, start : start + wide].reshape(block, wide)
                part_down[rows, start : start + wide] = dot_tn(left, right).astype(jnp.bfloat16)

    def part_store(at):
        slot = at % 2
        return pltpu.make_async_copy(
            staged.at[slot], part_hbm.at[at], store_sems.at[slot]
        )

    def gateup_grads(first, last):
        @pl.loop(first, last)
        def _(at):
            cols = pl.ds(pl.multiple_of(at * tile, tile), tile)

            @pl.when(at >= 2)
            def _():
                part_store(at - 2).wait()

            left = inputs[:, cols]
            for start in range(0, 2 * ff_part, wide):
                staged[at % 2, :, start : start + wide] = dot_tn(
                    left, grad[:, start : start + wide]
                ).astype(jnp.bfloat16)
            part_store(at).start()

    tiles = width // tile
    done = [0]

    def between(rank):
        upto = min(tiles, done[0] + 2)
        gateup_grads(done[0], upto)
        done[0] = upto

    down_grads()
    share.begin()
    for one in small:
        one.finish()
    line.scatter_rest(result_ref, between)
    share.middle()
    gateup_grads(done[0], tiles)
    share.finish()
    stores = [
        pltpu.make_async_copy(one.own_rows(half), kept.at[half], kept_sems.at[at, half])
        for at, (one, kept) in enumerate(
            ((share, down_kept), (small[0], pgate_kept), (small[1], pproj_kept))
        )
        for half in (0, 1)
    ]
    for store in stores:
        store.start()
    line.gather_end()
    for one in [share] + small:
        one.sum_sent()
    for at in (tiles - 2, tiles - 1):
        part_store(at).wait()
    for store in stores:
        store.wait()


def ffn_backward(own, gateup, down, hidden, act, slope, inputs, pgate, pproj, chips):
    tok_count, width = own.shape
    ff_part = down.shape[0]
    block = 2 * chips * tok_count
    bfloat = jnp.bfloat16
    anywhere = pl.BlockSpec(memory_space=pl.ANY)
    vmem = pl.BlockSpec(memory_space=pltpu.VMEM)
    dma = pltpu.SemaphoreType.DMA
    tile = 256
    held = (gateup, down, hidden, act, slope, inputs)
    return pl.pallas_call(
        functools.partial(ffn_backward_kernel, chips),
        out_shape=[
            jax.ShapeDtypeStruct((tok_count, width), jnp.float32),
            jax.ShapeDtypeStruct((width // tile, tile, 2 * ff_part), bfloat),
            jax.ShapeDtypeStruct((2, ff_part // 8, width), bfloat),
        ]
        + [
            jax.ShapeDtypeStruct((2, one.shape[0], one.shape[1] // 8, one.shape[2]), bfloat)
            for one in (pgate, pproj)
        ],
        in_specs=[vmem] + [anywhere] * 8,
        out_specs=[vmem] + [anywhere] * 4,
        scratch_shapes=line_scratch(chips, tok_count, width)
        + [pltpu.VMEM(one.shape, bfloat) for one in held]
        + [
            pltpu.VMEM((block, 2 * ff_part), bfloat),
            pltpu.VMEM(down.shape, bfloat),
            pltpu.VMEM((2, tile, 2 * ff_part), bfloat),
            dma((6,)),
            dma((2,)),
            dma((3, 2)),
        ]
        + sum_scratch(down.shape)
        + sum_scratch(pgate.shape)
        + sum_scratch(pproj.shape),
        compiler_params=pltpu.CompilerParams(
            collective_id=2, has_side_effects=True, vmem_limit_bytes=KERNEL_VMEM
        ),
        cost_estimate=pl.CostEstimate(
            flops=12 * block * width * ff_part, bytes_accessed=40 << 20, transcendentals=0
        ),
        name="ffn_backward",
    )(own, *held, pgate, pproj)

def rope_norm(lin, gain, cosine, sine_part):
    scale = lax.rsqrt(jnp.mean(lin * lin, axis=-1, keepdims=True) + EPSILON)
    scaled = lin * scale * gain
    first, second = scaled[:, : HD // 2], scaled[:, HD // 2 :]
    return jnp.concatenate(
        [first * cosine - second * sine_part, second * cosine + first * sine_part], axis=-1
    )


class RowHeld:
    def __init__(self, kept, part):
        self.kept, self.part = kept, part

    def own_rows(self, half):
        return self.kept.at[half]

    def held(self, half, member):
        cols = pl.ds(pl.multiple_of(member * self.part, self.part), self.part)
        return self.kept.at[half, :, cols]


class SameHeld:
    def __init__(self, shard, spread_rows):
        self.shard, self.spread_rows = shard, spread_rows

    def own_rows(self, half):
        start, size = self.spread_rows(half)
        return self.shard.at[pl.ds(pl.multiple_of(start, size), size)]

    def held(self, half, member):
        return self.own_rows(half)


GAIN_ROWS = 24
POSITION_ROW = 12
QUERY_ROW = 13
KEY_ROW = 15


def attention_forward_kernel(
    chips,
    tokens_ref,
    packed_ref,
    frequency_ref,
    lengths_ref,
    query_weight,
    key_weight,
    value_weight,
    gate_weight,
    up_weight,
    out_hbm,
    small_hbm,
    ple_hbm,
    result_ref,
    packed_all,
    cos_ref,
    sin_ref,
    head_gains_ref,
    all_hbm,
    qkv_hbm,
    gateup_hbm,
    lin_hbm,
    query_hbm,
    span_hbm,
    probs_hbm,
    attended_hbm,
    small_all,
    ple_held,
    *scratch,
):
    scratch = list(scratch)
    line = Line(chips, scratch[:LINE_REFS])
    del scratch[:LINE_REFS]
    qkv_kept, gate_kept, up_kept = scratch[:3]
    wide_rows, narrow_rows, row_sem = scratch[3:6]
    own_ref, gains_send, gains_recv, query_docs, key_docs = scratch[6:11]
    del scratch[:11]
    ff_part = gate_kept.shape[2] // (2 * chips)
    spreads = []
    for held in (Held(qkv_kept), RowHeld(gate_kept, ff_part), RowHeld(up_kept, ff_part)):
        spreads.append(Spread(held, scratch[: spread_refs(True)], True))
        del scratch[: spread_refs(True)]
    qkv, gate, up = spreads
    small_held = SameHeld(small_hbm, lambda half: (small.own_start(half), small.eighth))
    small = Everywhere(small_held, scratch[: spread_refs(True)], True)
    del scratch[: spread_refs(True)]
    ple_source = SameHeld(ple_hbm, lambda half: (ple.own_start(half), ple.eighth))
    ple = Everywhere(ple_source, scratch[: spread_refs(True)], True)
    del scratch[: spread_refs(True)]
    out, lin, query, span, probs, attended = scratch[:6]
    load_sem, store_sem, span_send, span_recv = scratch[6:]
    width = line.slots.shape[3]
    pair = 2 * line.tok
    block = chips * pair
    members = 2 * chips
    ctx_at = lax.axis_index("ctx")
    planes = lax.axis_size("ctx")
    me = lax.axis_index("fsdp")
    bfloat = jnp.bfloat16

    def row_load(weight, buffer, at):
        return [
            pltpu.make_async_copy(
                weight.at[pl.ds(pl.multiple_of(qkv.own_start(half), qkv.eighth), qkv.eighth)],
                buffer.at[half],
                row_sem.at[at, half],
            )
            for half in (0, 1)
        ]

    query_rows = row_load(query_weight, wide_rows.at[0, :, :, pl.ds(0, HQ * HD)], 0)
    key_rows = row_load(key_weight, narrow_rows.at[0], 1)
    value_rows = row_load(value_weight, narrow_rows.at[1], 2)
    gate_rows = row_load(gate_weight, wide_rows.at[1], 3)
    up_rows = row_load(up_weight, wide_rows.at[0], 4)
    for load in query_rows + key_rows + value_rows + gate_rows:
        load.start()
    load_out = pltpu.make_async_copy(out_hbm, out, load_sem)
    load_out.start()
    greet_all()

    def gains_copy(hop, source):
        return remote(
            packed_ref,
            packed_all.at[source],
            gains_send.at[hop],
            gains_recv.at[hop],
            lax.rem(me + hop, members),
        )

    for hop in range(1, members):
        gains_copy(hop, me).start()
    packed_all[me] = packed_ref[...]

    for load in query_rows + key_rows + value_rows:
        load.wait()
    for half in (0, 1):
        for member in range(members):
            head = member * KV // members
            qkv_kept[half, member, :, :HD] = wide_rows[
                0, half, :, member * HD : (member + 1) * HD
            ].astype(bfloat)
            for side in (0, 1):
                qkv_kept[half, member, :, (1 + side) * HD : (2 + side) * HD] = narrow_rows[
                    side, half, :, head * HD : (head + 1) * HD
                ].astype(bfloat)
    qkv.swap_begin()
    for load in up_rows:
        load.start()
    for hop in range(1, members):
        gains_copy(hop, lax.rem(me + members - hop, members)).wait_recv()

    inputs = tokens_ref[...].astype(jnp.float32)
    scale = lax.rsqrt(jnp.mean(inputs * inputs, axis=-1, keepdims=True) + EPSILON)
    gain = jnp.concatenate(
        [packed_all[member, row : row + 1] for member in range(members) for row in (0, 1)], axis=1
    )
    own_ref[...] = (inputs * scale * gain).astype(bfloat)
    line.gather_begin(own_ref)

    for load in gate_rows + up_rows:
        load.wait()
    gate_kept[...] = wide_rows[1].astype(bfloat)
    up_kept[...] = wide_rows[0].astype(bfloat)
    for at, row in ((0, QUERY_ROW), (1, KEY_ROW)):
        total = packed_all[0, row : row + 2]
        for member in range(1, members):
            total = total + packed_all[member, row : row + 2]
        head_gains_ref[at : at + 1] = jnp.concatenate([total[0:1], total[1:2]], axis=1)
    gain_query, gain_key = head_gains_ref[0:1], head_gains_ref[1:2]

    line.gather_step(1)
    qkv.swap_end()
    qkv.spread_begin()

    places = ctx_at * block + lax.broadcasted_iota(jnp.int32, (block, 1), 0)
    spots = ctx_at * block - WINDOW + lax.broadcasted_iota(jnp.int32, (1, WINDOW + block), 1)
    doc_end = 0
    query_doc = jnp.zeros(places.shape, jnp.int32)
    key_doc = jnp.where(spots >= 0, 0, -1)
    for doc in range(lengths_ref.shape[0] - 1):
        doc_end = doc_end + lengths_ref[doc]
        query_doc = query_doc + jnp.where(places >= doc_end, 1, 0)
        key_doc = key_doc + jnp.where(spots >= doc_end, 1, 0)
    query_docs[...] = query_doc
    key_docs[...] = key_doc
    positions = jnp.concatenate(
        [packed_all[member, POSITION_ROW : POSITION_ROW + 1] for member in range(members)], axis=0
    )
    columns = jnp.transpose(positions)
    for member in range(members):
        angle = columns[:, member : member + 1] * frequency_ref[...]
        token_rows = pl.ds(member * line.tok, line.tok)
        cos_ref[token_rows] = jnp.cos(angle)
        sin_ref[token_rows] = jnp.sin(angle)

    line.gather_step(2)
    small.swap_begin()
    gate.swap_begin()
    qkv.spread_on()
    for distance in range(3, chips):
        line.gather_step(distance)
    up.swap_begin()
    ple.swap_begin()
    line.own_copy(own_ref).wait()
    for chip in range(chips):
        line.gather_other(chip)
    qkv.spread_end()
    stores = [
        pltpu.make_async_copy(line.slots, all_hbm, store_sem.at[0]),
        pltpu.make_async_copy(qkv.final, qkv_hbm, store_sem.at[1]),
        pltpu.make_async_copy(lin, lin_hbm, store_sem.at[2]),
        pltpu.make_async_copy(query, query_hbm, store_sem.at[3]),
        pltpu.make_async_copy(span, span_hbm, store_sem.at[4]),
        pltpu.make_async_copy(probs, probs_hbm, store_sem.at[5]),
        pltpu.make_async_copy(attended, attended_hbm, store_sem.at[6]),
        pltpu.make_async_copy(
            gate.final, gateup_hbm.at[:, :, pl.ds(0, ff_part)], store_sem.at[7]
        ),
        pltpu.make_async_copy(
            up.final, gateup_hbm.at[:, :, pl.ds(ff_part, ff_part)], store_sem.at[8]
        ),
        pltpu.make_async_copy(small.final, small_all, store_sem.at[9]),
    ] + [
        pltpu.make_async_copy(
            ple.rows(ple.final, ple.own_start(half), ple.eighth),
            ple_held.at[half],
            store_sem.at[10 + half],
        )
        for half in (0, 1)
    ]
    stores[0].start()
    stores[1].start()

    @pl.loop(0, chips)
    def _(chip):
        rows = pl.ds(pl.multiple_of(chip * pair, pair), pair)
        span_rows = pl.ds(pl.multiple_of(WINDOW + chip * pair, pair), pair)
        inputs = line.slots[chip].reshape(pair, width)
        weights = qkv.final[...].reshape(width, 3 * HD)
        key_lin = dot_nn(inputs, weights[:, HD : 2 * HD])
        lin[rows, HD : 2 * HD] = key_lin
        span[0, span_rows] = rope_norm(
            key_lin, gain_key, cos_ref[rows], sin_ref[rows]
        ).astype(bfloat)
        span[1, span_rows] = dot_nn(inputs, weights[:, 2 * HD :]).astype(bfloat)

    part = WINDOW // 2

    def span_copy(start, to_start, way, device):
        return pltpu.make_async_remote_copy(
            src_ref=span.at[:, pl.ds(pl.multiple_of(start, part), part)],
            dst_ref=span.at[:, pl.ds(pl.multiple_of(to_start, part), part)],
            send_sem=span_send.at[way],
            recv_sem=span_recv.at[way],
            device_id=device,
            device_id_type=pl.DeviceIdType.MESH,
        )

    mine = line.core * part
    others = (1 - line.core) * part
    onward = span_copy(block + mine, mine, 0, {"ctx": lax.rem(ctx_at + 1, planes)})
    across = span_copy(mine, mine, 1, {"fsdp": line.place(line.chip, 1 - line.core)})
    arrived = span_copy(others, others, 1, {"fsdp": line.place(line.chip, 1 - line.core)})

    @pl.when(ctx_at < planes - 1)
    def _():
        onward.start()

    @pl.when(ctx_at == 0)
    def _():
        span[:, pl.ds(0, WINDOW)] = jnp.zeros((2, WINDOW, HD), bfloat)

    @pl.loop(0, chips)
    def _(chip):
        rows = pl.ds(pl.multiple_of(chip * pair, pair), pair)
        inputs = line.slots[chip].reshape(pair, width)
        weights = qkv.final[...].reshape(width, 3 * HD)
        query_lin = dot_nn(inputs, weights[:, :HD])
        lin[rows, :HD] = query_lin
        rotated = rope_norm(query_lin, gain_query, cos_ref[rows], sin_ref[rows])
        query[rows] = (rotated.astype(bfloat).astype(jnp.float32) * SCORE_SCALE).astype(bfloat)

    @pl.when(ctx_at > 0)
    def _():
        onward.wait_recv()
        across.start()
        arrived.wait_recv()

    for store in stores[2:5]:
        store.start()
    load_out.wait()
    small.swap_on()

    span_len = WINDOW + pair
    for step in range(chips):
        chip = line.order(chips - 1 - step)
        rows = pl.ds(pl.multiple_of(chip * pair, pair), pair)
        span_rows = pl.ds(pl.multiple_of(chip * pair, pair), span_len)
        scores = dot_nt(query[rows], span[0, span_rows])
        distance = (
            WINDOW
            + lax.broadcasted_iota(jnp.int32, (pair, span_len), 0)
            - lax.broadcasted_iota(jnp.int32, (pair, span_len), 1)
        )
        visible = (
            (distance >= 0)
            & (distance < WINDOW)
            & (query_docs[rows] == key_docs[:, span_rows])
        )
        scores = jnp.where(visible, scores, NEGATIVE)
        shifted = jnp.exp(scores - jnp.max(scores, axis=-1, keepdims=True))
        prob = (shifted / jnp.sum(shifted, axis=-1, keepdims=True)).astype(bfloat)
        probs[rows] = prob
        attended[rows] = dot_nn(prob, span[1, span_rows]).astype(bfloat)

        wide = 512

        @pl.loop(0, width // wide)
        def _(at, chip=chip, rows=rows):
            cols = pl.ds(pl.multiple_of(at * wide, wide), wide)
            sums = dot_nn(attended[rows], out[:, cols]).astype(bfloat)
            line.parts[chip, :, :, cols] = sums.reshape(2, line.tok, wide)

        line.core_copy(chip).start()
        line.scatter_first(chip)
        if step == 0:
            gate.swap_end()
            gate.spread_begin()
            small.swap_end()
            small.spread_begin()
    for store in stores[5:7]:
        store.start()
    gate.spread_on()

    def between(rank):
        if rank == 3:
            up.swap_end()
            up.spread_begin()
            small.spread_on()
            ple.swap_on()
        if rank == 2 * chips - 3:
            up.spread_on()

    line.scatter_rest(result_ref, between)
    ple.swap_end()
    for store in stores[10:]:
        store.start()
    gate.spread_end()
    stores[7].start()
    up.spread_end()
    stores[8].start()
    small.spread_end()
    stores[9].start()
    line.gather_end()
    for hop in range(1, members):
        gains_copy(hop, me).wait_send()
    for spread in spreads + [small]:
        spread.spread_sent()
    ple.swap_sent()

    @pl.when(ctx_at < planes - 1)
    def _():
        onward.wait_send()

    @pl.when(ctx_at > 0)
    def _():
        across.wait_send()

    for store in stores:
        store.wait()


def attention_forward(
    tokens,
    packed,
    frequency,
    lengths,
    query_weight,
    key_weight,
    value_weight,
    gate,
    up,
    out,
    small,
    ple,
):
    tok_count, width = tokens.shape
    rows = query_weight.shape[0]
    members = width // rows
    chips = members // 2
    block = members * tok_count
    span_len = WINDOW + block
    ff_part = gate.shape[1] // members
    bfloat = jnp.bfloat16
    anywhere = pl.BlockSpec(memory_space=pl.ANY)
    vmem = pl.BlockSpec(memory_space=pltpu.VMEM)
    dma = pltpu.SemaphoreType.DMA
    kept = [
        ((block, 2 * HD), jnp.float32),
        ((block, HD), bfloat),
        ((2, span_len, HD), bfloat),
        ((block, WINDOW + 2 * tok_count), bfloat),
        ((block, HD), bfloat),
    ]
    outputs = [
        ((tok_count, width), jnp.float32),
        ((members,) + packed.shape, jnp.float32),
        ((block, HD // 2), jnp.float32),
        ((block, HD // 2), jnp.float32),
        ((2, HD), jnp.float32),
        ((chips, 2, tok_count, width), bfloat),
        ((members, rows, 3 * HD), bfloat),
        ((members, rows, 2 * ff_part), bfloat),
    ] + kept
    outputs.append(((members,) + small.shape, bfloat))
    outputs.append(((2, members, ple.shape[0] // 8, ple.shape[1]), bfloat))
    return pl.pallas_call(
        functools.partial(attention_forward_kernel, chips),
        out_shape=[jax.ShapeDtypeStruct(*output) for output in outputs],
        in_specs=[vmem] * 3 + [pl.BlockSpec(memory_space=pltpu.SMEM)] + [anywhere] * 8,
        out_specs=[vmem] * 5 + [anywhere] * 10,
        scratch_shapes=line_scratch(chips, tok_count, width)
        + [
            pltpu.VMEM((2, members, rows // 8, 3 * HD), bfloat),
            pltpu.VMEM((2, rows // 8, gate.shape[1]), bfloat),
            pltpu.VMEM((2, rows // 8, gate.shape[1]), bfloat),
            pltpu.VMEM((2, 2, rows // 8, gate.shape[1]), jnp.float32),
            pltpu.VMEM((2, 2, rows // 8, KV * HD), jnp.float32),
            dma((5, 2)),
            pltpu.VMEM((tok_count, width), bfloat),
            dma((members,)),
            dma((members,)),
            pltpu.VMEM((block, 1), jnp.int32),
            pltpu.VMEM((1, span_len), jnp.int32),
        ]
        + spread_scratch((members, rows, 3 * HD))
        + spread_scratch((members, rows, ff_part))
        + spread_scratch((members, rows, ff_part))
        + everywhere_scratch((members,) + small.shape)
        + everywhere_scratch((members,) + ple.shape)
        + [pltpu.VMEM(out.shape, bfloat)]
        + [pltpu.VMEM(*one) for one in kept]
        + [dma, dma((12,)), dma((2,)), dma((2,))],
        compiler_params=pltpu.CompilerParams(
            collective_id=4, has_side_effects=True, vmem_limit_bytes=KERNEL_VMEM
        ),
        cost_estimate=pl.CostEstimate(
            flops=8 << 30, bytes_accessed=300 << 20, transcendentals=block * 1280
        ),
        name="attention_forward",
    )(
        tokens,
        packed,
        frequency,
        lengths,
        query_weight,
        key_weight,
        value_weight,
        gate,
        up,
        out,
        small,
        ple,
    )

def rope_norm_back(grad, lin, gain, cosine, sine_part):
    first, second = grad[:, : HD // 2], grad[:, HD // 2 :]
    turned = jnp.concatenate(
        [first * cosine + second * sine_part, second * cosine - first * sine_part], axis=-1
    )
    scale = lax.rsqrt(jnp.mean(lin * lin, axis=-1, keepdims=True) + EPSILON)
    scaled = turned * gain
    along = jnp.mean(lin * scaled, axis=-1, keepdims=True)
    grad_lin = scale * scaled - lin * (scale * scale * scale * along)
    return grad_lin, jnp.sum(lin * scale * turned, axis=0, keepdims=True)


def attention_backward_kernel(
    chips,
    own_ref,
    out_hbm,
    qkv_hbm,
    lin_hbm,
    query_hbm,
    span_hbm,
    probs_hbm,
    cos_ref,
    sin_ref,
    gain_query_ref,
    gain_key_ref,
    gateup_hbm,
    down_kept,
    inputs_hbm,
    attended_hbm,
    result_ref,
    query_part_hbm,
    kv_part_hbm,
    out_part_hbm,
    gains_ref,
    gateup_kept,
    down_sum,
    *scratch,
):
    scratch = list(scratch)
    line = Line(chips, scratch[:LINE_REFS])
    del scratch[:LINE_REFS]
    gateup = Summed(gateup_hbm, scratch[:SUM_REFS], True)
    del scratch[:SUM_REFS]
    down = Spread(Held(down_kept), scratch[: spread_refs(False)], False)
    del scratch[: spread_refs(False)]
    out, qkv, lin, query, span, probs, grad, grad_span, back, across, returned = scratch[:11]
    load_sem, store_sem, back_send, back_recv, grad_out = scratch[11:16]
    inputs, attended, query_part, kv_part, out_part, pair_send, pair_recv = scratch[16:]
    width = line.slots.shape[3]
    pair = 2 * line.tok
    block = chips * pair
    ctx_at = lax.axis_index("ctx")
    planes = lax.axis_size("ctx")
    bfloat = jnp.bfloat16
    loads = [
        pltpu.make_async_copy(src, dst, load_sem.at[at])
        for at, (src, dst) in enumerate(
            (
                (out_hbm, out),
                (span_hbm, span),
                (probs_hbm, probs),
                (lin_hbm, lin),
                (query_hbm, query),
                (qkv_hbm, qkv),
                (inputs_hbm, inputs),
                (attended_hbm, attended),
            )
        )
    ]
    for load in loads:
        load.start()
    greet_all()
    line.gather_begin(own_ref)
    gateup.begin()
    grad_span[...] = jnp.zeros_like(grad_span)
    gains_ref[...] = jnp.zeros_like(gains_ref)
    line.own_copy(own_ref).wait()
    for load in loads[:6]:
        load.wait()

    span_len = WINDOW + pair
    for step in range(chips):
        if step > 0:
            line.gather_step(step)
        chip = line.order(step)
        line.gather_other(chip)
        rows = pl.ds(pl.multiple_of(chip * pair, pair), pair)
        span_rows = pl.ds(pl.multiple_of(chip * pair, pair), span_len)
        grad_out[rows] = dot_nt(line.slots[chip].reshape(pair, width), out[...]).astype(bfloat)
        grad_prob = dot_nt(grad_out[rows], span[1, span_rows])
        prob = probs[rows].astype(jnp.float32)
        inner = jnp.sum(prob * grad_prob, axis=-1, keepdims=True)
        grad_score = (prob * (grad_prob - inner)).astype(bfloat)
        grad_query = dot_nn(grad_score, span[0, span_rows]) * SCORE_SCALE
        grad_lin, grad_gain = rope_norm_back(
            grad_query, lin[rows, :HD], gain_query_ref[...], cos_ref[rows], sin_ref[rows]
        )
        grad[rows, :HD] = grad_lin.astype(bfloat)
        gains_ref[0:1] += grad_gain
        grad_span[0, span_rows] += dot_tn(grad_score, query[rows])
        grad_span[1, span_rows] += dot_tn(probs[rows], grad_out[rows])

    part = WINDOW // 2
    mine, others = line.core * part, (1 - line.core) * part
    back[...] = grad_span[:, pl.ds(pl.multiple_of(others, part), part)].astype(bfloat)
    to_core = remote(
        back, across, back_send.at[0], back_recv.at[0], line.place(line.chip, 1 - line.core)
    )
    to_core.start()
    to_core.wait()
    total = grad_span[:, pl.ds(pl.multiple_of(mine, part), part)]
    back[...] = (total + across[...].astype(jnp.float32)).astype(bfloat)
    to_before = pltpu.make_async_remote_copy(
        src_ref=back,
        dst_ref=returned,
        send_sem=back_send.at[1],
        recv_sem=back_recv.at[1],
        device_id={"ctx": lax.rem(ctx_at + planes - 1, planes)},
        device_id_type=pl.DeviceIdType.MESH,
    )

    @pl.when(ctx_at > 0)
    def _():
        to_before.start()

    down.place_all()
    down.spread_begin()

    @pl.when(ctx_at < planes - 1)
    def _():
        to_before.wait_recv()
        here = pl.ds(pl.multiple_of(block + mine, part), part)
        grad_span[:, here] += returned[...].astype(jnp.float32)

    for step in range(chips):
        chip = line.order(chips - 1 - step)
        rows = pl.ds(pl.multiple_of(chip * pair, pair), pair)
        span_rows = pl.ds(pl.multiple_of(WINDOW + chip * pair, pair), pair)
        grad_lin, grad_gain = rope_norm_back(
            grad_span[0, span_rows], lin[rows, HD:], gain_key_ref[...], cos_ref[rows], sin_ref[rows]
        )
        grad[rows, HD : 2 * HD] = grad_lin.astype(bfloat)
        gains_ref[1:2] += grad_gain
        grad[rows, 2 * HD :] = grad_span[1, span_rows].astype(bfloat)

    wide = 512

    @pl.loop(0, width // wide)
    def _(at):
        cols = pl.ds(pl.multiple_of(at * wide, wide), wide)
        sums = dot_nt(grad[...], qkv[cols]).astype(bfloat)
        line.parts[:, :, :, cols] = sums.reshape(chips, 2, line.tok, wide)

    for step in range(chips):
        line.core_copy(line.order(chips - 1 - step)).start()
    for step in range(chips - 1):
        line.scatter_first(line.order(chips - 1 - step))
    for load in loads[6:]:
        load.wait()
    part_stores = [
        pltpu.make_async_copy(out_part, out_part_hbm, store_sem.at[0]),
        pltpu.make_async_copy(query_part, query_part_hbm, store_sem.at[1]),
        pltpu.make_async_copy(
            kv_part.at[pl.ds(line.core * chips, chips)], kv_part_hbm, store_sem.at[5]
        ),
    ]

    def pair_copy(at):
        return remote(
            kv_part.at[(1 - line.core) * chips + at],
            probs.at[pl.ds(at * HD, HD), pl.ds(0, 2 * HD)],
            pair_send.at[at],
            pair_recv.at[at],
            line.place(line.chip, 1 - line.core),
        )

    def between(rank):
        if rank == 3:
            for start in range(0, width, wide):
                right = line.slots[:, :, :, start : start + wide].reshape(block, wide)
                out_part[:, start : start + wide] = dot_tn(attended[...], right).astype(bfloat)
            part_stores[0].start()
        if rank == 4:

            @pl.loop(0, width // HD)
            def _(at):
                left = inputs[:, pl.ds(pl.multiple_of(at * HD, HD), HD)]
                query_part[at] = dot_tn(left, grad[:, :HD]).astype(bfloat)
                kv_part[at] = dot_tn(left, grad[:, HD:]).astype(bfloat)

            part_stores[1].start()
            for at in range(chips):
                pair_copy(at).start()
        if rank == 5:
            for at in range(chips):
                pair_copy(at).wait_recv()
                kv_part[line.core * chips + at] += probs[at * HD : (at + 1) * HD, : 2 * HD]
            part_stores[2].start()

    gateup.middle()
    down.spread_on()
    line.scatter_rest(result_ref, between)
    gateup.finish()
    stores = [
        pltpu.make_async_copy(gateup.own_rows(half), gateup_kept.at[half], store_sem.at[2 + half])
        for half in (0, 1)
    ]
    down.spread_end()
    stores.append(pltpu.make_async_copy(down.final, down_sum, store_sem.at[4]))
    for store in stores:
        store.start()
    line.gather_end()
    gateup.sum_sent()
    down.spread_sent()
    for at in range(chips):
        pair_copy(at).wait_send()

    @pl.when(ctx_at > 0)
    def _():
        to_before.wait_send()

    for store in stores + part_stores:
        store.wait()


def attention_backward(
    own,
    out,
    qkv,
    lin,
    query,
    span,
    probs,
    cosine,
    sine_part,
    gain_query,
    gain_key,
    part_gateup,
    held_down,
    inputs,
    attended,
):
    tok_count, width = own.shape
    members = part_gateup.shape[0]
    chips = members // 2
    block = members * tok_count
    bfloat = jnp.bfloat16
    anywhere = pl.BlockSpec(memory_space=pl.ANY)
    vmem = pl.BlockSpec(memory_space=pltpu.VMEM)
    dma = pltpu.SemaphoreType.DMA
    eighth = part_gateup.shape[1] // 8
    down_shape = (8 * held_down.shape[1], held_down.shape[2])
    outputs = [
        ((tok_count, width), jnp.float32),
        ((members, HD, HD), bfloat),
        ((chips, HD, 2 * HD), bfloat),
        ((HD, width), bfloat),
        ((2, HD), jnp.float32),
        ((2, members, eighth, part_gateup.shape[2]), bfloat),
        (down_shape, bfloat),
    ]
    half_span = (2, WINDOW // 2, HD)
    return pl.pallas_call(
        functools.partial(attention_backward_kernel, chips),
        out_shape=[jax.ShapeDtypeStruct(*output) for output in outputs],
        in_specs=[vmem] + [anywhere] * 6 + [vmem] * 4 + [anywhere] * 4,
        out_specs=[vmem, anywhere, anywhere, anywhere, vmem, anywhere, anywhere],
        scratch_shapes=line_scratch(chips, tok_count, width)
        + sum_scratch(part_gateup.shape)
        + spread_scratch(down_shape)
        + [pltpu.VMEM(one.shape, one.dtype) for one in (out, qkv, lin, query, span, probs)]
        + [
            pltpu.VMEM((block, 3 * HD), bfloat),
            pltpu.VMEM(span.shape, jnp.float32),
            pltpu.VMEM(half_span, bfloat),
            pltpu.VMEM(half_span, bfloat),
            pltpu.VMEM(half_span, bfloat),
            dma((8,)),
            dma((6,)),
            dma((2,)),
            dma((2,)),
            pltpu.VMEM((block, HD), bfloat),
            pltpu.VMEM((block, width), bfloat),
            pltpu.VMEM((block, HD), bfloat),
            pltpu.VMEM((members, HD, HD), bfloat),
            pltpu.VMEM((members, HD, 2 * HD), bfloat),
            pltpu.VMEM((HD, width), bfloat),
            dma((chips,)),
            dma((chips,)),
        ],
        compiler_params=pltpu.CompilerParams(
            collective_id=5, has_side_effects=True, vmem_limit_bytes=KERNEL_VMEM
        ),
        cost_estimate=pl.CostEstimate(
            flops=8 << 30, bytes_accessed=300 << 20, transcendentals=0
        ),
        name="attention_backward",
    )(
        own,
        out,
        qkv,
        lin,
        query,
        span,
        probs,
        cosine,
        sine_part,
        gain_query,
        gain_key,
        part_gateup,
        held_down,
        inputs,
        attended,
    )

def by_heads(
    tokens,
    per_layer,
    cotangent,
    doc_lengths,
    positions,
    w_query,
    w_key,
    w_value,
    w_out,
    laurel_left,
    laurel_right,
    w_gate,
    w_up,
    w_down,
    ple_gate,
    ple_proj,
    attn_in_gain,
    query_gain,
    key_gain,
    attn_out_gain,
    laurel_gain,
    ffn_in_gain,
    ffn_out_gain,
    ple_gain,
):
    bfloat = jnp.bfloat16
    ctx_count = lax.axis_size("ctx")
    fsdp_count = lax.axis_size("fsdp")
    tok_count = tokens.shape[0]
    block_len = tok_count * fsdp_count
    chips = fsdp_count // 2
    rows = w_query.shape[0]
    ff_part = w_gate.shape[1] // fsdp_count
    ctx_at = lax.axis_index("ctx")
    fsdp_at = lax.axis_index("fsdp")

    wide_gains = (attn_in_gain, attn_out_gain, laurel_gain, ffn_in_gain, ffn_out_gain, ple_gain)
    turn = jnp.arange(HD, dtype=jnp.int32) // query_gain.shape[0]
    head_parts = [
        jnp.where(turn == fsdp_at, jnp.tile(gain, fsdp_count), 0.0)
        for gain in (query_gain, key_gain)
    ]
    packed = jnp.zeros((GAIN_ROWS * 128,), jnp.float32)
    at = 0
    for part in list(wide_gains) + [positions.astype(jnp.float32)] + head_parts:
        packed = packed + jnp.pad(part, (at, packed.shape[0] - at - part.shape[0]))
        at += part.shape[0]
    packed = packed.reshape(GAIN_ROWS, 128)
    frequency = jnp.exp(
        jnp.arange(HD // 2, dtype=jnp.float32) * (-2.0 * math.log(ROPE_BASE) / HD)
    )

    out_low = w_out.astype(bfloat)
    def in_halves(weight):
        return jnp.concatenate(jnp.split(weight.astype(bfloat), rows // 128, axis=0), axis=1)

    def in_stacks(weight):
        pieces = weight.astype(bfloat).reshape(weight.shape[0], 128 // weight.shape[0], -1)
        return jnp.transpose(pieces, (1, 0, 2)).reshape(128, -1)

    small = jnp.concatenate([in_halves(laurel_left), in_stacks(laurel_right)], axis=1)
    ple_small = jnp.concatenate([in_halves(ple_gate), in_stacks(ple_proj)], axis=1)

    inputs = tokens.astype(jnp.float32)
    ple_input = per_layer.astype(jnp.float32)
    (
        projected,
        packed_all,
        cosine,
        sine_part,
        head_gains,
        normed_all,
        qkv_full,
        gateup_full,
        qk_lin,
        query_low,
        span_kv,
        probs,
        attended_low,
        small_all,
        ple_held,
    ) = attention_forward(
        tokens,
        packed,
        frequency[None, :],
        doc_lengths,
        w_query,
        w_key,
        w_value,
        w_gate,
        w_up,
        out_low,
        small,
        ple_small,
    )
    def side_by_side(cols, shape):
        pieces = jnp.split(cols, cols.shape[2] // shape[1], axis=2)
        return jnp.concatenate(pieces, axis=1).reshape(-1, shape[1])

    def stacked(cols, shape):
        pieces = cols.reshape(fsdp_count, -1, shape[0], cols.shape[2])
        return jnp.transpose(pieces, (0, 2, 1, 3)).reshape(-1, shape[1])

    left_size = laurel_left.size // 128
    full_left = side_by_side(small_all[:, :, :left_size], laurel_left.shape)
    full_right = stacked(small_all[:, :, left_size:], laurel_right.shape)
    wide_rows = attn_in_gain.shape[0] // 128
    gain_in, gain_post, gain_laurel, gain_ffin, gain_ffout, gain_ple = (
        packed_all[:, n * wide_rows : (n + 1) * wide_rows].reshape(-1) for n in range(6)
    )
    normed, norm_back = jax.vjp(rms_norm, inputs, gain_in)
    normed_low = normed.astype(bfloat)
    normed_all = normed_all.reshape(block_len, -1)
    col_qkv = qkv_full.reshape(normed_all.shape[1], -1)
    col_gateup = gateup_full.reshape(normed_all.shape[1], -1)
    narrow_low = matmul(normed_low, full_left).astype(bfloat)
    widened = matmul(narrow_low, full_right)
    mixed, mix_back = jax.vjp(mix_piece, inputs, normed, projected, widened, gain_post, gain_laurel)
    ffn_normed, ffn_norm_back = jax.vjp(rms_norm, mixed, gain_ffin)
    down_lin, ffn_all, hidden_low, act_low, slope_low, ple_all, down_low = ffn_forward(
        ffn_normed.astype(bfloat), col_gateup, w_down, ple_held, chips
    )
    pgate_size = ple_gate.size // 128
    full_pgate = side_by_side(ple_all[:, :, :pgate_size], ple_gate.shape)
    full_pproj = stacked(ple_all[:, :, pgate_size:], ple_proj.shape)
    layer_mid, ffn_out_back = jax.vjp(ffn_out_piece, mixed, down_lin, gain_ffout)
    layer_low = layer_mid.astype(bfloat)
    ple_lin = matmul(layer_low, full_pgate)
    ple_mid, ple_back = jax.vjp(ple_act, ple_lin, ple_input)
    ple_low = ple_mid.astype(bfloat)
    ple_wide = matmul(ple_low, full_pproj)
    out_full, final_back = jax.vjp(final_piece, layer_mid, ple_wide, gain_ple)

    grad_layer, grad_pwide, grad_gple = final_back(cotangent.astype(jnp.float32))
    grad_pwide_low = grad_pwide.astype(bfloat)
    part_pproj = matmul_tn(ple_low, grad_pwide_low)
    grad_plemid = matmul_nt(grad_pwide_low, full_pproj)
    grad_plelin, grad_pleinput = ple_back(grad_plemid)
    grad_plelin_low = grad_plelin.astype(bfloat)
    part_pgate = matmul_tn(layer_low, grad_plelin_low)
    grad_layer = grad_layer + matmul_nt(grad_plelin_low, full_pgate)
    grad_mixed, grad_down, grad_gffout = ffn_out_back(grad_layer)
    grad_ffn, part_gateup, held_wdown, held_pgate, held_pproj = ffn_backward(
        grad_down.astype(bfloat),
        col_gateup,
        down_low,
        hidden_low,
        act_low,
        slope_low,
        ffn_all,
        part_pgate.astype(bfloat).reshape(fsdp_count, rows, -1),
        part_pproj.astype(bfloat).reshape(fsdp_count, 128, -1),
        chips,
    )
    part_gateup = part_gateup.reshape(fsdp_count, rows, -1)
    grad_mixed_more, grad_gffin = ffn_norm_back(grad_ffn)
    grad_mixed = grad_mixed + grad_mixed_more
    grad_in_first, grad_normed, grad_proj, grad_lwide, grad_gpost, grad_glaurel = mix_back(
        grad_mixed
    )
    grad_lwide_low = grad_lwide.astype(bfloat)
    part_right = matmul_tn(narrow_low, grad_lwide_low)
    grad_narrow_low = matmul_nt(grad_lwide_low, full_right).astype(bfloat)
    part_left = matmul_tn(normed_low, grad_narrow_low)
    grad_normed = grad_normed + matmul_nt(grad_narrow_low, full_left)

    (
        grad_normed_more,
        part_query,
        part_kv,
        part_wout,
        grad_head_gains,
        held_gateup,
        sum_wdown,
    ) = (
        attention_backward(
            grad_proj.astype(bfloat),
            out_low,
            col_qkv,
            qk_lin,
            query_low,
            span_kv,
            probs,
            cosine,
            sine_part,
            head_gains[0:1],
            head_gains[1:2],
            part_gateup,
            held_wdown,
            normed_all,
            attended_low,
        )
    )
    grad_gquery, grad_gkey = grad_head_gains[0], grad_head_gains[1]
    part_laurel = jnp.concatenate(
        [part.astype(bfloat).reshape(fsdp_count, 128, -1) for part in (part_left, part_right)],
        axis=2,
    )
    grad_normed = grad_normed + grad_normed_more
    grad_in_second, grad_gin = norm_back(grad_normed)
    grad_tokens = grad_in_first + grad_in_second

    grad_gains = [
        grad_gin,
        grad_gpost,
        grad_glaurel,
        grad_gffin,
        grad_gffout,
        grad_gple,
        grad_gquery,
        grad_gkey,
    ]
    gain_parts = jnp.concatenate([g.reshape(fsdp_count, -1) for g in grad_gains], axis=1)
    gain_parts = jnp.pad(gain_parts, ((0, 0), (0, 128 * 128 - gain_parts.shape[1])))
    gain_parts = gain_parts.astype(bfloat).reshape(fsdp_count, 128, 128)

    (
        sum_wgate,
        sum_wup,
        sum_wquery,
        sum_wkey,
        sum_wvalue,
        sum_wout,
        sum_pgate,
        sum_pproj,
        sum_laurel,
        sum_gains,
    ) = gradient_sum(
        [
            Source(held_gateup, summed=True, part=(0, 2), sides=1),
            Source(held_gateup, summed=True, part=(1, 2), sides=1),
            Source(part_query, sides=1),
            Source(part_kv, groups=KV, paired=True, sides=2),
            Source(part_wout),
            Source(held_pgate, summed=True, groups=1, sides=1),
            Source(held_pproj, summed=True, groups=1, sides=1),
            Source(part_laurel, groups=1, sides=1),
            Source(gain_parts, groups=1),
        ]
    )
    gain_sums = sum_gains.astype(jnp.float32).reshape(-1)
    wide_size, head_size = attn_in_gain.shape[0], query_gain.shape[0]
    wide_sums = gain_sums[: 6 * wide_size].reshape(6, wide_size)
    head_sums = gain_sums[6 * wide_size : 6 * wide_size + 2 * head_size].reshape(2, head_size)
    grad_wgate = sum_wgate.astype(jnp.float32)
    grad_wup = sum_wup.astype(jnp.float32)
    grad_wdown = sum_wdown.astype(jnp.float32)
    grad_wout = sum_wout.astype(jnp.float32)
    grad_wquery = sum_wquery.astype(jnp.float32)
    grad_wkey = sum_wkey.astype(jnp.float32)
    grad_wvalue = sum_wvalue.astype(jnp.float32)
    grad_pgate = sum_pgate.astype(jnp.float32)
    grad_pproj = sum_pproj.astype(jnp.float32).reshape(ple_proj.shape)
    left_part = sum_laurel.shape[1] // 2
    grad_wleft = sum_laurel[:, :left_part].astype(jnp.float32).reshape(laurel_left.shape)
    grad_wright = sum_laurel[:, left_part:].astype(jnp.float32).reshape(laurel_right.shape)
    return (
        out_full.astype(bfloat),
        grad_tokens,
        grad_pleinput,
        grad_wquery,
        grad_wkey,
        grad_wvalue,
        grad_wout,
        grad_wleft,
        grad_wright,
        grad_wgate,
        grad_wup,
        grad_wdown,
        grad_pgate,
        grad_pproj,
        wide_sums[0],
        head_sums[0],
        head_sums[1],
        *(wide_sums[n] for n in range(1, 6)),
    )


def solution(mesh):
    in_specs = (
        P(("ctx", "fsdp"), None),
        P(("ctx", "fsdp"), None),
        P(("ctx", "fsdp"), None),
        P(),
        P(("ctx", "fsdp")),
        P("fsdp", None),
        P("fsdp", None),
        P("fsdp", None),
        P("fsdp", None),
        P("fsdp", None),
        P("fsdp", None),
        P("fsdp", None),
        P("fsdp", None),
        P("fsdp", None),
        P("fsdp", None),
        P("fsdp", None),
        P("fsdp"),
        P("fsdp"),
        P("fsdp"),
        P("fsdp"),
        P("fsdp"),
        P("fsdp"),
        P("fsdp"),
        P("fsdp"),
    )
    out_specs = (
        P(("ctx", "fsdp"), None),
        P(("ctx", "fsdp"), None),
        P(("ctx", "fsdp"), None),
        P("fsdp", None),
        P("fsdp", None),
        P("fsdp", None),
        P("fsdp", None),
        P("fsdp", None),
        P("fsdp", None),
        P("fsdp", None),
        P("fsdp", None),
        P("fsdp", None),
        P("fsdp", None),
        P("fsdp", None),
        P("fsdp"),
        P("fsdp"),
        P("fsdp"),
        P("fsdp"),
        P("fsdp"),
        P("fsdp"),
        P("fsdp"),
        P("fsdp"),
    )
    run = by_heads if mesh.shape["fsdp"] == HQ and mesh.shape["ctx"] == 4 else local
    return jax.shard_map(run, mesh=mesh, in_specs=in_specs, out_specs=out_specs, check_vma=False)
```

```python
import dataclasses
import functools
import math

import jax
import jax.numpy as jnp
from jax import lax
from jax.experimental import pallas as pl
from jax.experimental.pallas import tpu as pltpu
from jax.sharding import PartitionSpec as P

HQ = 8
KV = 2
HD = 256
WINDOW = 1024


EPSILON = 1e-06
NEGATIVE = -1e30
ROPE_BASE = 10000.0
HALF_ROOT = 1.0 / math.sqrt(2.0)
GELU_ROOT = math.sqrt(2.0 / math.pi)
GELU_CUBE = 0.044715
SCORE_SCALE = 1.0 / math.sqrt(HD)
KERNEL_VMEM = 62 << 20


def passed_along(block, axis, distance):
    devices = range(lax.axis_size(axis))
    route = [(i - distance, i) for i in devices if i - distance in devices]
    return lax.ppermute(block, axis, route)


def matmul(left_mat, right_mat):
    return jnp.dot(left_mat, right_mat, preferred_element_type=jnp.float32)


def matmul_tn(left_mat, right_mat):
    return lax.dot_general(
        left_mat, right_mat, (((0,), (0,)), ((), ())), preferred_element_type=jnp.float32
    )


def matmul_nt(left_mat, right_mat):
    return lax.dot_general(
        left_mat, right_mat, (((1,), (1,)), ((), ())), preferred_element_type=jnp.float32
    )


def rms_norm(values, gain_vec):
    return (
        values * lax.rsqrt(jnp.mean(values * values, axis=-1, keepdims=True) + EPSILON) * gain_vec
    )


def rope_tables(positions, width):
    half_width = width // 2
    frequency = jnp.exp(
        jnp.arange(half_width, dtype=jnp.float32) * (-2.0 * math.log(ROPE_BASE) / width)
    )
    angles = positions.astype(jnp.float32)[:, None] * frequency[None, :]
    return (jnp.cos(angles)[:, None, :], jnp.sin(angles)[:, None, :])


def rotate(values, cosine, sine_part):
    half_width = values.shape[-1] // 2
    first_half = values[..., :half_width]
    second_half = values[..., half_width:]
    return jnp.concatenate(
        [
            first_half * cosine - second_half * sine_part,
            second_half * cosine + first_half * sine_part,
        ],
        axis=-1,
    )


def document_ids(doc_lengths, places):
    doc_ends = jnp.cumsum(doc_lengths)
    return jnp.sum((places[:, None] >= doc_ends[None, :-1]).astype(jnp.int32), axis=1)


def query_key(cosine, sine_part, query_lin, key_lin, gain_query, gain_key):
    tok_count = query_lin.shape[0]
    query_rot = rotate(
        rms_norm(query_lin.reshape(tok_count, HQ, HD), gain_query), cosine, sine_part
    )
    key_rot = rotate(rms_norm(key_lin.reshape(tok_count, KV, HD), gain_key), cosine, sine_part)
    return (query_rot, key_rot)


def mix_piece(inputs, normed, projected, widened, gain_post, gain_laurel):
    return (
        inputs + rms_norm(projected, gain_post) + normed + rms_norm(widened, gain_laurel)
    ) * HALF_ROOT


def geglu(gate_lin, up_lin):
    return jax.nn.gelu(gate_lin, approximate=True) * up_lin


def ffn_out_piece(mixed, down_lin, gain_ffout):
    return mixed + rms_norm(down_lin, gain_ffout)


def ple_act(ple_lin, ple_input):
    return jax.nn.gelu(ple_lin, approximate=True) * ple_input


def final_piece(layer_mid, ple_wide, gain_ple):
    return layer_mid + rms_norm(ple_wide, gain_ple)


def visibility(doc_lengths, query_start, key_start, tok_count, span_len):
    query_places = query_start + jnp.arange(tok_count, dtype=jnp.int32)
    key_places = key_start + jnp.arange(span_len, dtype=jnp.int32)
    distance = query_places[:, None] - key_places[None, :]
    query_docs = document_ids(doc_lengths, query_places)
    key_docs = document_ids(doc_lengths, key_places)
    return (
        (distance >= 0)
        & (distance < WINDOW)
        & (key_places[None, :] >= 0)
        & (query_docs[:, None] == key_docs[None, :])
    )


def attend_forward(query_low, span_kv, visible):
    tok_count = query_low.shape[0]
    scale_factor = 1.0 / math.sqrt(HD)
    scores = (
        jnp.einsum("tkgh,skh->kgts", query_low, span_kv[0], preferred_element_type=jnp.float32)
        * scale_factor
    )
    scores = jnp.where(visible, scores, NEGATIVE)
    row_top = jnp.max(scores, axis=-1, keepdims=True)
    shifted = jnp.exp(scores - row_top)
    row_total = jnp.sum(shifted, axis=-1, keepdims=True)
    attn_probs = shifted / row_total
    attended = jnp.einsum(
        "kgts,skh->tkgh",
        attn_probs.astype(jnp.bfloat16),
        span_kv[1],
        preferred_element_type=jnp.float32,
    )
    return (attended.reshape(tok_count, -1), row_top + jnp.log(row_total))


def attend_backward(query_low, span_kv, visible, log_total, grad_out_low):
    scale_factor = 1.0 / math.sqrt(HD)
    scores = (
        jnp.einsum("tkgh,skh->kgts", query_low, span_kv[0], preferred_element_type=jnp.float32)
        * scale_factor
    )
    attn_probs = jnp.where(visible, jnp.exp(jnp.where(visible, scores, NEGATIVE) - log_total), 0.0)
    grad_probs = jnp.einsum(
        "tkgh,skh->kgts", grad_out_low, span_kv[1], preferred_element_type=jnp.float32
    )
    inner_sum = jnp.sum(attn_probs * grad_probs, axis=-1, keepdims=True)
    grad_scores = (attn_probs * (grad_probs - inner_sum)).astype(jnp.bfloat16)
    grad_query = (
        jnp.einsum("kgts,skh->tkgh", grad_scores, span_kv[0], preferred_element_type=jnp.float32)
        * scale_factor
    )
    grad_keys = (
        jnp.einsum("kgts,tkgh->skh", grad_scores, query_low, preferred_element_type=jnp.float32)
        * scale_factor
    )
    grad_values = jnp.einsum(
        "kgts,tkgh->skh",
        attn_probs.astype(jnp.bfloat16),
        grad_out_low,
        preferred_element_type=jnp.float32,
    )
    return (grad_query, jnp.stack([grad_keys, grad_values]))


def settle(act_low, grad_low):
    act_cols = lax.all_to_all(act_low, "fsdp", split_axis=1, concat_axis=0, tiled=True)
    shard_rows = matmul_tn(act_cols, lax.all_gather(grad_low, "fsdp", axis=0, tiled=True))
    return lax.psum(shard_rows.astype(jnp.bfloat16), "ctx").astype(jnp.float32)


def local(
    tokens,
    per_layer,
    cotangent,
    doc_lengths,
    positions,
    w_query,
    w_key,
    w_value,
    w_out,
    laurel_left,
    laurel_right,
    w_gate,
    w_up,
    w_down,
    ple_gate,
    ple_proj,
    attn_in_gain,
    query_gain,
    key_gain,
    attn_out_gain,
    laurel_gain,
    ffn_in_gain,
    ffn_out_gain,
    ple_gain,
):
    bfloat = jnp.bfloat16
    tok_count = tokens.shape[0]
    span_len = WINDOW + tok_count
    groups = HQ // KV
    dev_index = lax.axis_index("ctx") * lax.axis_size("fsdp") + lax.axis_index("fsdp")
    query_start = dev_index * tok_count
    key_start = query_start - WINDOW
    visible = visibility(doc_lengths, query_start, key_start, tok_count, span_len)
    cosine, sine_part = rope_tables(positions, HD)
    gain_in, gain_query, gain_key, gain_post, gain_laurel, gain_ffin, gain_ffout, gain_ple = (
        lax.all_gather(attn_in_gain, "fsdp", axis=0, tiled=True),
        lax.all_gather(query_gain, "fsdp", axis=0, tiled=True),
        lax.all_gather(key_gain, "fsdp", axis=0, tiled=True),
        lax.all_gather(attn_out_gain, "fsdp", axis=0, tiled=True),
        lax.all_gather(laurel_gain, "fsdp", axis=0, tiled=True),
        lax.all_gather(ffn_in_gain, "fsdp", axis=0, tiled=True),
        lax.all_gather(ffn_out_gain, "fsdp", axis=0, tiled=True),
        lax.all_gather(ple_gain, "fsdp", axis=0, tiled=True),
    )
    full_query, full_key, full_value, full_out, full_left, full_right = (
        lax.all_gather(w_query.astype(bfloat), "fsdp", axis=0, tiled=True),
        lax.all_gather(w_key.astype(bfloat), "fsdp", axis=0, tiled=True),
        lax.all_gather(w_value.astype(bfloat), "fsdp", axis=0, tiled=True),
        lax.all_gather(w_out.astype(bfloat), "fsdp", axis=0, tiled=True),
        lax.all_gather(laurel_left.astype(bfloat), "fsdp", axis=0, tiled=True),
        lax.all_gather(laurel_right.astype(bfloat), "fsdp", axis=0, tiled=True),
    )
    inputs = tokens.astype(jnp.float32)
    ple_input = per_layer.astype(jnp.float32)
    normed, norm_back = jax.vjp(rms_norm, inputs, gain_in)
    normed_low = normed.astype(bfloat)
    query_lin = matmul(normed_low, full_query)
    key_lin = matmul(normed_low, full_key)
    value_lin = matmul(normed_low, full_value)
    (query_rot, key_rot), rope_back = jax.vjp(
        functools.partial(query_key, cosine, sine_part), query_lin, key_lin, gain_query, gain_key
    )
    query_low = query_rot.astype(bfloat).reshape(tok_count, KV, groups, HD)
    keys_values = jnp.stack(
        [key_rot.astype(bfloat), value_lin.astype(bfloat).reshape(tok_count, KV, HD)]
    )
    block_kv = lax.all_gather(keys_values, "fsdp", axis=1, tiled=True)
    block_len = block_kv.shape[1]
    before_kv = passed_along(block_kv, "ctx", 1)
    span_offset = block_len + lax.axis_index("fsdp") * tok_count - WINDOW
    span_kv = lax.dynamic_slice_in_dim(
        jnp.concatenate([before_kv, block_kv], axis=1), span_offset, span_len, 1
    )
    attended, log_total = attend_forward(query_low, span_kv, visible)
    attended_low = attended.astype(bfloat)
    projected = matmul(attended_low, full_out)
    narrow_low = matmul(normed_low, full_left).astype(bfloat)
    widened = matmul(narrow_low, full_right)
    mixed, mix_back = jax.vjp(mix_piece, inputs, normed, projected, widened, gain_post, gain_laurel)
    full_gate, full_up, full_down, full_pgate, full_pproj = (
        lax.all_gather(w_gate.astype(bfloat), "fsdp", axis=0, tiled=True),
        lax.all_gather(w_up.astype(bfloat), "fsdp", axis=0, tiled=True),
        lax.all_gather(w_down.astype(bfloat), "fsdp", axis=0, tiled=True),
        lax.all_gather(ple_gate.astype(bfloat), "fsdp", axis=0, tiled=True),
        lax.all_gather(ple_proj.astype(bfloat), "fsdp", axis=0, tiled=True),
    )
    ffn_normed, ffn_norm_back = jax.vjp(rms_norm, mixed, gain_ffin)
    ffn_low = ffn_normed.astype(bfloat)
    gate_lin = matmul(ffn_low, full_gate)
    up_lin = matmul(ffn_low, full_up)
    hidden, geglu_back = jax.vjp(geglu, gate_lin, up_lin)
    hidden_low = hidden.astype(bfloat)
    down_lin = matmul(hidden_low, full_down)
    layer_mid, ffn_out_back = jax.vjp(ffn_out_piece, mixed, down_lin, gain_ffout)
    layer_low = layer_mid.astype(bfloat)
    ple_lin = matmul(layer_low, full_pgate)
    ple_mid, ple_back = jax.vjp(ple_act, ple_lin, ple_input)
    ple_low = ple_mid.astype(bfloat)
    ple_wide = matmul(ple_low, full_pproj)
    out_full, final_back = jax.vjp(final_piece, layer_mid, ple_wide, gain_ple)
    full_gate, full_up, full_down, full_pgate, full_pproj = (
        lax.all_gather(w_gate.astype(bfloat), "fsdp", axis=0, tiled=True),
        lax.all_gather(w_up.astype(bfloat), "fsdp", axis=0, tiled=True),
        lax.all_gather(w_down.astype(bfloat), "fsdp", axis=0, tiled=True),
        lax.all_gather(ple_gate.astype(bfloat), "fsdp", axis=0, tiled=True),
        lax.all_gather(ple_proj.astype(bfloat), "fsdp", axis=0, tiled=True),
    )
    grad_layer, grad_pwide, grad_gple = final_back(cotangent.astype(jnp.float32))
    grad_pwide_low = grad_pwide.astype(bfloat)
    grad_pproj = settle(ple_low, grad_pwide_low)
    grad_plemid = matmul_nt(grad_pwide_low, full_pproj)
    grad_plelin, grad_pleinput = ple_back(grad_plemid)
    grad_plelin_low = grad_plelin.astype(bfloat)
    grad_pgate = settle(layer_low, grad_plelin_low)
    grad_layer = grad_layer + matmul_nt(grad_plelin_low, full_pgate)
    grad_mixed, grad_down, grad_gffout = ffn_out_back(grad_layer)
    grad_down_low = grad_down.astype(bfloat)
    grad_wdown = settle(hidden_low, grad_down_low)
    grad_hidden = matmul_nt(grad_down_low, full_down)
    grad_gate, grad_up = geglu_back(grad_hidden)
    grad_gate_low = grad_gate.astype(bfloat)
    grad_up_low = grad_up.astype(bfloat)
    grad_wgate = settle(ffn_low, grad_gate_low)
    grad_wup = settle(ffn_low, grad_up_low)
    grad_ffn = matmul_nt(grad_gate_low, full_gate) + matmul_nt(grad_up_low, full_up)
    grad_mixed_more, grad_gffin = ffn_norm_back(grad_ffn)
    grad_mixed = grad_mixed + grad_mixed_more
    full_query, full_key, full_value, full_out, full_left, full_right = (
        lax.all_gather(w_query.astype(bfloat), "fsdp", axis=0, tiled=True),
        lax.all_gather(w_key.astype(bfloat), "fsdp", axis=0, tiled=True),
        lax.all_gather(w_value.astype(bfloat), "fsdp", axis=0, tiled=True),
        lax.all_gather(w_out.astype(bfloat), "fsdp", axis=0, tiled=True),
        lax.all_gather(laurel_left.astype(bfloat), "fsdp", axis=0, tiled=True),
        lax.all_gather(laurel_right.astype(bfloat), "fsdp", axis=0, tiled=True),
    )
    grad_in_first, grad_normed, grad_proj, grad_lwide, grad_gpost, grad_glaurel = mix_back(
        grad_mixed
    )
    grad_proj_low = grad_proj.astype(bfloat)
    grad_wout = settle(attended_low, grad_proj_low)
    grad_att_low = matmul_nt(grad_proj_low, full_out).astype(bfloat)
    grad_lwide_low = grad_lwide.astype(bfloat)
    grad_wright = settle(narrow_low, grad_lwide_low)
    grad_narrow_low = matmul_nt(grad_lwide_low, full_right).astype(bfloat)
    grad_wleft = settle(normed_low, grad_narrow_low)
    grad_normed = grad_normed + matmul_nt(grad_narrow_low, full_left)
    grad_query_att, grad_span = attend_backward(
        query_low, span_kv, visible, log_total, grad_att_low.reshape(tok_count, KV, groups, HD)
    )
    whole_grad = jnp.zeros((2, 2 * block_len, KV, HD), jnp.float32)
    whole_grad = lax.dynamic_update_slice_in_dim(whole_grad, grad_span, span_offset, 1)
    returned = passed_along(whole_grad[:, :block_len].astype(jnp.bfloat16), "ctx", -1).astype(
        jnp.float32
    )
    own_grad = lax.psum_scatter(
        (whole_grad[:, block_len:] + returned).astype(jnp.bfloat16),
        "fsdp",
        scatter_dimension=1,
        tiled=True,
    ).astype(jnp.float32)
    grad_qlin, grad_klin, grad_gquery, grad_gkey = rope_back(
        (grad_query_att.reshape(tok_count, HQ, HD), own_grad[0])
    )
    grad_qlin_low = grad_qlin.astype(bfloat)
    grad_klin_low = grad_klin.astype(bfloat)
    grad_vlin_low = own_grad[1].reshape(tok_count, KV * HD).astype(bfloat)
    grad_wquery = settle(normed_low, grad_qlin_low)
    grad_wkey = settle(normed_low, grad_klin_low)
    grad_wvalue = settle(normed_low, grad_vlin_low)
    grad_normed = (
        grad_normed
        + matmul_nt(grad_qlin_low, full_query)
        + matmul_nt(grad_klin_low, full_key)
        + matmul_nt(grad_vlin_low, full_value)
    )
    grad_in_second, grad_gin = norm_back(grad_normed)
    grad_tokens = grad_in_first + grad_in_second
    sum_gin, sum_gquery, sum_gkey, sum_gpost, sum_glaurel, sum_gffin, sum_gffout, sum_gple = (
        lax.psum(
            (
                grad_gin,
                grad_gquery,
                grad_gkey,
                grad_gpost,
                grad_glaurel,
                grad_gffin,
                grad_gffout,
                grad_gple,
            ),
            ("ctx", "fsdp"),
        )
    )
    wide_rows = attn_in_gain.shape[0]
    head_rows = query_gain.shape[0]
    wide_start = lax.axis_index("fsdp") * wide_rows
    head_start = lax.axis_index("fsdp") * head_rows

    def wide_part(full_vec):
        return lax.dynamic_slice_in_dim(full_vec, wide_start, wide_rows, 0)

    def head_part(full_vec):
        return lax.dynamic_slice_in_dim(full_vec, head_start, head_rows, 0)

    return (
        out_full.astype(bfloat),
        grad_tokens,
        grad_pleinput,
        grad_wquery,
        grad_wkey,
        grad_wvalue,
        grad_wout,
        grad_wleft,
        grad_wright,
        grad_wgate,
        grad_wup,
        grad_wdown,
        grad_pgate,
        grad_pproj,
        wide_part(sum_gin),
        head_part(sum_gquery),
        head_part(sum_gkey),
        wide_part(sum_gpost),
        wide_part(sum_glaurel),
        wide_part(sum_gffin),
        wide_part(sum_gffout),
        wide_part(sum_gple),
    )

class Plane:
    def locate(self, columns, rows):
        self.columns = columns
        at = lax.axis_index("ctx")
        self.at_x, self.at_y = at % 2, at // 2
        self.beside = (at + 1 - 2 * (at % 2), (at + 2) % 4)
        self.me = lax.axis_index("fsdp")
        self.members = lax.axis_size("fsdp")
        self.half = rows // 2
        self.quarter = rows // 4
        self.eighth = rows // 8

    def rows(self, ref, start, size):
        start = pl.multiple_of(start, size)
        return ref.at[:, pl.ds(start, size)] if self.columns else ref.at[pl.ds(start, size)]

    def sides(self, half):
        return (self.at_x, self.at_y) if half == 0 else (self.at_y, self.at_x)

    def kept_start(self, half):
        return half * self.half + self.sides(half)[0] * self.quarter

    def given_start(self, half):
        return half * self.half + (1 - self.sides(half)[0]) * self.quarter

    def own_start(self, half):
        return self.kept_start(half) + self.sides(half)[1] * self.eighth

    def copy(self, src, dst, send_sem, recv_sem, half, stage):
        return pltpu.make_async_remote_copy(
            src_ref=src,
            dst_ref=dst,
            send_sem=send_sem.at[half, stage],
            recv_sem=recv_sem.at[half, stage],
            device_id={"ctx": self.beside[(half + stage) % 2]},
            device_id_type=pl.DeviceIdType.MESH,
        )


class Summed(Plane):
    def __init__(self, source, refs, columns):
        self.source = source
        self.kept, self.taken, self.last, self.load_sem, self.sum_send, self.sum_recv = refs
        self.locate(columns, source.shape[-2])

    def load(self, half):
        return pltpu.make_async_copy(
            self.rows(self.source, self.kept_start(half), self.quarter),
            self.kept.at[half],
            self.load_sem.at[half],
        )

    def first(self, half):
        return self.copy(
            self.rows(self.source, self.given_start(half), self.quarter),
            self.taken.at[half],
            self.sum_send,
            self.sum_recv,
            half,
            0,
        )

    def second(self, half):
        other = (1 - self.sides(half)[1]) * self.eighth
        return self.copy(
            self.rows(self.kept.at[half], other, self.eighth),
            self.last.at[half],
            self.sum_send,
            self.sum_recv,
            half,
            1,
        )

    def begin(self):
        for half in (0, 1):
            self.first(half).start()
            self.load(half).start()

    def add(self, half, start, more, more_start):
        step = min(32, self.eighth)
        blocks = self.eighth // step
        layers = self.source.shape[0] if self.columns else 1

        @pl.loop(0, layers * blocks)
        def _(at):
            layer, block = at // blocks, at % blocks
            here = pl.ds(pl.multiple_of(start + block * step, step), step)
            there = pl.ds(pl.multiple_of(more_start + block * step, step), step)
            if self.columns:
                self.kept[half, layer, here] += more[half, layer, there]
            else:
                self.kept[half, here] += more[half, there]

    def middle(self):
        for half in (0, 1):
            self.load(half).wait()
            self.first(half).wait_recv()
            side = self.sides(half)[1]
            other = (1 - side) * self.eighth
            self.add(half, other, self.taken, other)
            self.second(half).start()
            mine = side * self.eighth
            self.add(half, mine, self.taken, mine)

    def finish(self):
        for half in (0, 1):
            self.second(half).wait_recv()
            self.add(half, self.sides(half)[1] * self.eighth, self.last, 0)

    def own_rows(self, half):
        return self.rows(self.kept.at[half], self.sides(half)[1] * self.eighth, self.eighth)

    def held(self, half, member):
        side = self.sides(half)[1] * self.eighth
        return self.kept.at[half, member, pl.ds(pl.multiple_of(side, self.eighth), self.eighth)]

    def sum_sent(self):
        for half in (0, 1):
            self.first(half).wait_send()
            self.second(half).wait_send()


class Held:
    def __init__(self, kept, side=0, sides=1):
        self.kept = kept
        width = kept.shape[-1] // sides
        self.cols = pl.ds(side * width, width)

    def own_rows(self, half):
        return self.kept.at[half]

    def held(self, half, member):
        return self.kept.at[half, member, :, self.cols]


class Spread(Plane):
    def __init__(self, source, refs, columns):
        self.own_rows, self.held = source.own_rows, source.held
        self.final, self.spread_send, self.spread_recv, self.place_sem = refs[:4]
        if columns:
            self.swap_send, self.swap_recv = refs[4:]
        self.locate(columns, self.final.shape[-2])

    def place(self, half):
        return pltpu.make_async_copy(
            self.own_rows(half),
            self.rows(self.final, self.own_start(half), self.eighth),
            self.place_sem.at[half],
        )

    def place_all(self):
        for half in (0, 1):
            self.place(half).start()
        for half in (0, 1):
            self.place(half).wait()

    def swap_place(self, half, member):
        start = pl.multiple_of(self.own_start(half), self.eighth)
        return self.final.at[member, pl.ds(start, self.eighth)]

    def swap_copy(self, half, hop, src_member):
        target = lax.rem(self.me + hop, self.members)
        return remote(
            self.held(half, target),
            self.swap_place(half, src_member),
            self.swap_send.at[hop, half],
            self.swap_recv.at[hop, half],
            target,
        )

    def swap_local(self, half):
        return pltpu.make_async_copy(
            self.held(half, self.me),
            self.swap_place(half, self.me),
            self.place_sem.at[half],
        )

    def swap_begin(self):
        for half in (0, 1):
            for hop in range(1, self.members):
                self.swap_copy(half, hop, self.me).start()
            self.swap_local(half).start()

    def swap_end(self):
        for half in (0, 1):
            for hop in range(1, self.members):
                source = lax.rem(self.me + self.members - hop, self.members)
                self.swap_copy(half, hop, source).wait_recv()
            self.swap_local(half).wait()

    def spread_copy(self, half, stage):
        if stage == 0:
            rows = self.rows(self.final, self.own_start(half), self.eighth)
        else:
            rows = self.rows(self.final, self.kept_start(half), self.quarter)
        return self.copy(rows, rows, self.spread_send, self.spread_recv, half, 1 - stage)

    def spread_wait(self, half, stage):
        side = self.sides(half)[1]
        if stage == 0:
            start = self.kept_start(half) + (1 - side) * self.eighth
            rows = self.rows(self.final, start, self.eighth)
        else:
            rows = self.rows(self.final, self.given_start(half), self.quarter)
        self.copy(rows, rows, self.spread_send, self.spread_recv, half, 1 - stage).wait_recv()

    def spread_begin(self):
        for half in (0, 1):
            self.spread_copy(half, 0).start()

    def spread_on(self):
        for half in (0, 1):
            self.spread_wait(half, 0)
            self.spread_copy(half, 1).start()

    def spread_end(self):
        for half in (0, 1):
            self.spread_wait(half, 1)

    def spread_sent(self, swapped=True):
        for half in (0, 1):
            self.spread_copy(half, 0).wait_send()
            self.spread_copy(half, 1).wait_send()
            if self.columns and swapped:
                for hop in range(1, self.members):
                    self.swap_copy(half, hop, self.me).wait_send()


class GroupSpread(Spread):
    def __init__(self, source, refs):
        self.landing = refs[0]
        super().__init__(source, refs[1:], True)

    def swap_place(self, half, member):
        return self.landing.at[half, member]

    def swap_end(self):
        super().swap_end()
        groups = self.final.shape[0]
        size = self.landing.shape[1] // groups
        for half in (0, 1):
            rows = pl.ds(pl.multiple_of(self.own_start(half), self.eighth), self.eighth)
            for group in range(groups):
                total = self.landing[half, group * size].astype(jnp.float32)
                for member in range(group * size + 1, (group + 1) * size):
                    total = total + self.landing[half, member].astype(jnp.float32)
                self.final[group, rows] = total.astype(jnp.bfloat16)


class PairSpread(Spread):
    def __init__(self, source, refs):
        self.landing = refs[0]
        super().__init__(source, refs[1:], True)
        self.chips = self.members // 2
        self.chip, self.core = self.me // 2, self.me % 2

    def to_member(self, half, at):
        return remote(
            self.held(half, at),
            self.landing.at[half, self.chip],
            self.swap_send.at[at, half],
            self.swap_recv.at[self.chip, half],
            self.core * self.chips + at,
        )

    def from_chip(self, half, chip):
        place = self.landing.at[half, chip]
        return remote(
            place,
            place,
            self.swap_send.at[chip, half],
            self.swap_recv.at[chip, half],
            lax.rem(self.me + 1, self.members),
        )

    def swap_local(self, half):
        return pltpu.make_async_copy(
            self.held(half, self.me - self.core * self.chips),
            self.landing.at[half, self.chip],
            self.place_sem.at[half],
        )

    def swap_begin(self):
        for half in (0, 1):
            for at in range(self.chips):
                mine = self.core * self.chips + at == self.me
                pl.when(mine)(self.swap_local(half).start)
                pl.when(jnp.logical_not(mine))(self.to_member(half, at).start)

    def swap_end(self):
        groups = self.final.shape[0]
        size = self.chips // groups
        for half in (0, 1):
            for chip in range(self.chips):
                mine = 2 * chip + self.me // self.chips == self.me
                pl.when(mine)(self.swap_local(half).wait)
                pl.when(jnp.logical_not(mine))(self.from_chip(half, chip).wait_recv)
            rows = pl.ds(pl.multiple_of(self.own_start(half), self.eighth), self.eighth)
            for group in range(groups):
                total = self.landing[half, group * size].astype(jnp.float32)
                for chip in range(group * size + 1, (group + 1) * size):
                    total = total + self.landing[half, chip].astype(jnp.float32)
                self.final[group, rows] = total.astype(jnp.bfloat16)

    def spread_sent(self):
        for half in (0, 1):
            self.spread_copy(half, 0).wait_send()
            self.spread_copy(half, 1).wait_send()
            for at in range(self.chips):
                mine = self.core * self.chips + at == self.me
                pl.when(jnp.logical_not(mine))(self.to_member(half, at).wait_send)


class Everywhere(Spread):
    def swap_begin(self):
        chips = self.members // 2
        for half in (0, 1):
            own = self.own_rows(half)
            for hop in range(1, chips):
                self.hand_to(half, hop, own, lax.rem(self.me + 2 * hop, self.members)).start()
            self.pass_on(half, self.me // 2, own).start()
            self.swap_local(half).start()

    def hand_to(self, half, hop, own, place):
        return remote(
            own,
            self.swap_place(half, self.me),
            self.swap_send.at[0, hop, half],
            self.swap_recv.at[0, hop, half],
            place,
        )

    def pass_on(self, half, chip, source):
        core = self.me % 2
        return remote(
            source,
            self.swap_place(half, 2 * chip + core),
            self.swap_send.at[1, chip, half],
            self.swap_recv.at[1, chip, half],
            self.me + 1 - 2 * core,
        )

    def swap_on(self):
        chips = self.members // 2
        for hop in range(1, chips):
            sender = lax.rem(self.me + self.members - 2 * hop, self.members)
            for half in (0, 1):
                place = self.swap_place(half, sender)
                remote(
                    place,
                    place,
                    self.swap_send.at[0, hop, half],
                    self.swap_recv.at[0, hop, half],
                    sender,
                ).wait_recv()
                self.pass_on(half, sender // 2, place).start()

    def swap_end(self):
        core = self.me % 2
        for chip in range(self.members // 2):
            for half in (0, 1):
                place = self.swap_place(half, 2 * chip + 1 - core)
                remote(
                    place,
                    place,
                    self.swap_send.at[1, chip, half],
                    self.swap_recv.at[1, chip, half],
                    self.me + 1 - 2 * core,
                ).wait_recv()
        for half in (0, 1):
            self.swap_local(half).wait()

    def spread_sent(self):
        for half in (0, 1):
            self.spread_copy(half, 0).wait_send()
            self.spread_copy(half, 1).wait_send()
        self.swap_sent()

    def swap_sent(self):
        chips = self.members // 2
        for half in (0, 1):
            own = self.own_rows(half)
            for hop in range(1, chips):
                self.hand_to(half, hop, own, lax.rem(self.me + 2 * hop, self.members)).wait_send()
            for chip in range(chips):
                self.pass_on(half, chip, own).wait_send()


def sum_scratch(shape):
    dma = pltpu.SemaphoreType.DMA
    rows, width = shape[-2:]

    def buffer(count):
        return pltpu.VMEM((2,) + shape[:-2] + (count, width), jnp.bfloat16)

    buffers = [buffer(rows // 4), buffer(rows // 4), buffer(rows // 8)]
    return buffers + [dma((2,)), dma((2, 2)), dma((2, 2))]


SUM_REFS = 6


def spread_scratch(shape, members=None):
    dma = pltpu.SemaphoreType.DMA
    scratch = [pltpu.VMEM(shape, jnp.bfloat16), dma((2, 2)), dma((2, 2)), dma((2,))]
    if len(shape) == 3:
        count = members or shape[0]
        scratch += [dma((count, 2)), dma((count, 2))]
    return scratch


def everywhere_scratch(shape):
    dma = pltpu.SemaphoreType.DMA
    chips = shape[0] // 2
    scratch = [pltpu.VMEM(shape, jnp.bfloat16), dma((2, 2)), dma((2, 2)), dma((2,))]
    return scratch + [dma((2, chips, 2)), dma((2, chips, 2))]


def spread_refs(columns):
    return 6 if columns else 4


def gradient_sum_kernel(plan, *refs):
    refs = list(refs)
    count = len(plan)
    sources = refs[:count]
    results_count = sum(max(1, one.sides) for one in plan)
    results = refs[count : count + results_count]
    scratch = refs[count + results_count :]
    store_sem = scratch.pop()

    def take(size):
        taken = scratch[:size]
        del scratch[:size]
        return taken

    sums, spreads, late = [], [], []
    for source, one in zip(sources, plan):
        if one.summed:
            held = Held(source, *one.part)
        else:
            held = Summed(source, take(SUM_REFS), one.columns)
            sums.append(held)
        size = spread_refs(one.columns)
        if one.groups:
            kind = PairSpread if one.paired else GroupSpread
            spreads.append(kind(held, take(size + 1)))
        else:
            spreads.append(Spread(held, take(size), one.columns))
        if not one.summed:
            late.append(spreads[-1])
    early = [spread for spread in spreads if spread not in late]
    greet_all()

    def stores(at):
        final, sides = spreads[at].final, plan[at].sides
        first = sum(max(1, one.sides) for one in plan[:at])
        if sides == 0:
            return [pltpu.make_async_copy(final, results[first], store_sem.at[at, 0, 0])]
        part = final.shape[2] // sides
        return [
            pltpu.make_async_copy(
                final.at[member, :, pl.ds(side * part, part)],
                results[first + side].at[:, pl.ds(member * part, part)],
                store_sem.at[at, side, member],
            )
            for member in range(final.shape[0])
            for side in range(sides)
        ]

    def launch(spread):
        if spread.columns:
            spread.swap_begin()
        else:
            spread.place_all()
            spread.spread_begin()

    for share in sums:
        share.begin()
    for spread in early:
        launch(spread)
    for share in sums:
        share.middle()
    for spread in early[:1]:
        spread.swap_end()
        spread.spread_begin()
    for share, spread in zip(sums, late):
        share.finish()
        launch(spread)
    for spread in early[:1]:
        spread.spread_on()
    for spread in early[1:]:
        spread.swap_end()
        spread.spread_begin()
    for spread in late:
        if spread.columns:
            spread.swap_end()
            spread.spread_begin()
        else:
            spread.spread_on()
    for spread in early[1:]:
        spread.spread_on()
    for spread in late:
        if spread.columns:
            spread.spread_on()
    for at in sorted(range(count), key=lambda one: spreads[one] in early):
        spreads[at].spread_end()
        for store in stores(at):
            store.start()
    for share in sums:
        share.sum_sent()
    for spread in spreads:
        spread.spread_sent()
    for at in range(count):
        for store in stores(at):
            store.wait()


@dataclasses.dataclass
class Source:
    array: jax.Array
    summed: bool = False
    part: tuple = (0, 1)
    groups: int = 0
    paired: bool = False
    sides: int = 0

    @property
    def columns(self):
        return self.array.ndim - self.summed == 3

    @property
    def shape(self):
        shape = self.array.shape
        if self.summed:
            shape = shape[1:-2] + (8 * shape[-2], shape[-1] // self.part[1])
        return shape


def gradient_sum(sources):
    members = lax.axis_size("fsdp")
    anywhere = pl.BlockSpec(memory_space=pl.ANY)
    scratch, results = [], []
    for one in sources:
        shape = one.shape
        if not one.summed:
            scratch += sum_scratch(shape)
        if one.groups:
            landing = (2, shape[0] if one.paired else members, shape[1] // 8, shape[2])
            scratch.append(pltpu.VMEM(landing, jnp.bfloat16))
            shape = (one.groups,) + shape[1:]
        scratch += spread_scratch(shape, members)
        if one.sides == 0:
            results.append(shape)
        else:
            results += [(shape[1], shape[0] * shape[2] // one.sides)] * one.sides
    return pl.pallas_call(
        functools.partial(gradient_sum_kernel, sources),
        out_shape=[jax.ShapeDtypeStruct(shape, jnp.bfloat16) for shape in results],
        in_specs=[anywhere] * len(sources),
        out_specs=[anywhere] * len(results),
        scratch_shapes=scratch + [pltpu.SemaphoreType.DMA((len(sources), 2, members))],
        compiler_params=pltpu.CompilerParams(
            collective_id=3, has_side_effects=True, vmem_limit_bytes=KERNEL_VMEM
        ),
        cost_estimate=pl.CostEstimate(flops=0, bytes_accessed=300 << 20, transcendentals=0),
        name="gradient_sum",
    )(*(one.array for one in sources))

def remote(src, dst, send_sem, recv_sem, place):
    return pltpu.make_async_remote_copy(
        src_ref=src,
        dst_ref=dst,
        send_sem=send_sem,
        recv_sem=recv_sem,
        device_id={"fsdp": place},
        device_id_type=pl.DeviceIdType.MESH,
    )


def dot_nn(left_mat, right_mat):
    return jnp.dot(left_mat, right_mat, preferred_element_type=jnp.float32)


def dot_nt(left_mat, right_mat):
    return lax.dot_general(
        left_mat, right_mat, (((1,), (1,)), ((), ())), preferred_element_type=jnp.float32
    )


def dot_tn(left_mat, right_mat):
    return lax.dot_general(
        left_mat, right_mat, (((0,), (0,)), ((), ())), preferred_element_type=jnp.float32
    )


def greet_all():
    sem = pltpu.get_barrier_semaphore()
    members, planes = lax.axis_size("fsdp"), lax.axis_size("ctx")
    mesh_id = pl.DeviceIdType.MESH
    for hop in range(1, planes):
        other = lax.rem(lax.axis_index("ctx") + hop, planes)
        pl.semaphore_signal(sem, inc=1, device_id={"ctx": other}, device_id_type=mesh_id)
    for hop in range(1, members):
        other = lax.rem(lax.axis_index("fsdp") + hop, members)
        pl.semaphore_signal(sem, inc=1, device_id={"fsdp": other}, device_id_type=mesh_id)
    pl.semaphore_wait(sem, members + planes - 2)


PIECES = 4


def line_scratch(chips, tok_count, width):
    dma = pltpu.SemaphoreType.DMA
    shard = (tok_count, width)
    return [
        pltpu.VMEM((chips, 2) + shard, jnp.bfloat16),
        dma((chips, 2)),
        dma((chips, 3)),
        dma,
        pltpu.VMEM((chips, 2) + shard, jnp.bfloat16),
        pltpu.VMEM((chips,) + shard, jnp.bfloat16),
        pltpu.VMEM((chips,) + shard, jnp.bfloat16),
        pltpu.VMEM((chips,) + shard, jnp.bfloat16),
        dma((chips,)),
        dma((chips,)),
        dma((chips, PIECES)),
        dma((chips, PIECES)),
        dma((chips, PIECES)),
    ]


LINE_REFS = 13


class Line:
    def __init__(self, chips, refs):
        (
            self.slots,
            self.slot_recv,
            self.slot_send,
            self.own_sem,
            self.parts,
            self.from_core,
            self.from_left,
            self.from_right,
            self.core_send,
            self.core_recv,
            self.flow_send,
            self.left_recv,
            self.right_recv,
        ) = refs
        self.chips = chips
        me = lax.axis_index("fsdp")
        self.chip = me // 2
        self.core = me % 2
        self.tok = self.slots.shape[2]
        self.piece = self.tok // PIECES

    def place(self, chip, core):
        return chip * 2 + core

    def order(self, step):
        picked = 0
        for chip in range(self.chips):
            near = sorted(range(self.chips), key=lambda other: (abs(other - chip), other))
            picked = picked + jnp.where(self.chip == chip, near[step], 0)
        return picked

    def slot_copy(self, src, chip, way):
        place = (
            self.place(self.chip + 1, self.core),
            self.place(self.chip - 1, self.core),
            self.place(self.chip, 1 - self.core),
        )[way]
        return remote(
            src,
            self.slots.at[chip, self.core],
            self.slot_send.at[chip, way],
            self.slot_recv.at[chip, self.core],
            place,
        )

    def own_copy(self, own_ref):
        return pltpu.make_async_copy(own_ref, self.slots.at[self.chip, self.core], self.own_sem)

    def gather_begin(self, own_ref):
        @pl.when(self.chip < self.chips - 1)
        def _():
            self.slot_copy(own_ref, self.chip, 0).start()

        @pl.when(self.chip > 0)
        def _():
            self.slot_copy(own_ref, self.chip, 1).start()

        self.slot_copy(own_ref, self.chip, 2).start()
        self.own_copy(own_ref).start()

    def gather_step(self, distance):
        for chip, there, way, onward in (
            (self.chip - distance, self.chip >= distance, 0, self.chip < self.chips - 1),
            (self.chip + distance, self.chip + distance < self.chips, 1, self.chip > 0),
        ):

            @pl.when(there)
            def _(chip=chip, way=way, onward=onward):
                src = self.slots.at[chip, self.core]
                self.slot_copy(src, chip, way).wait_recv()

                @pl.when(onward)
                def _():
                    self.slot_copy(src, chip, way).start()

                self.slot_copy(src, chip, 2).start()

    def gather_other(self, chip):
        dst = self.slots.at[chip, 1 - self.core]
        remote(
            dst,
            dst,
            self.slot_send.at[chip, 2],
            self.slot_recv.at[chip, 1 - self.core],
            self.place(self.chip, 1 - self.core),
        ).wait_recv()

    def gather_end(self):
        for chip in range(self.chips):
            src = self.slots.at[chip, self.core]

            @pl.when((self.chip >= chip) & (self.chip < self.chips - 1))
            def _(src=src, chip=chip):
                self.slot_copy(src, chip, 0).wait_send()

            @pl.when((self.chip <= chip) & (self.chip > 0))
            def _(src=src, chip=chip):
                self.slot_copy(src, chip, 1).wait_send()

            self.slot_copy(src, chip, 2).wait_send()

    def core_copy(self, chip):
        return remote(
            self.parts.at[chip, 1 - self.core],
            self.from_core.at[chip],
            self.core_send.at[chip],
            self.core_recv.at[chip],
            self.place(self.chip, 1 - self.core),
        )

    def flow_copy(self, chip, piece, right):
        rows = pl.ds(piece * self.piece, self.piece)
        return remote(
            self.parts.at[chip, self.core, rows],
            (self.from_left if right else self.from_right).at[chip, rows],
            self.flow_send.at[chip, piece],
            (self.left_recv if right else self.right_recv).at[chip, piece],
            self.place(self.chip + (1 if right else -1), self.core),
        )

    def flow(self, chip, right, incoming):
        self.core_copy(chip).wait_recv()

        @pl.loop(0, PIECES)
        def _(piece):
            rows = pl.ds(pl.multiple_of(piece * self.piece, self.piece), self.piece)
            total = self.parts[chip, self.core, rows].astype(jnp.float32)
            total = total + self.from_core[chip, rows].astype(jnp.float32)
            if incoming:
                self.flow_copy(chip, piece, right).wait_recv()
                source = self.from_left if right else self.from_right
                total = total + source[chip, rows].astype(jnp.float32)
            self.parts[chip, self.core, rows] = total.astype(jnp.bfloat16)
            self.flow_copy(chip, piece, right).start()

    def scatter_first(self, chip):
        @pl.when((self.chip == 0) & (chip > 0))
        def _():
            self.flow(chip, True, False)

        @pl.when((self.chip == self.chips - 1) & (chip < self.chips - 1))
        def _():
            self.flow(chip, False, False)

    def scatter_rest(self, result_ref, between=None):
        for rank in range(3, 2 * self.chips - 2):
            right = rank - self.chip

            @pl.when((self.chip > 0) & (right > self.chip) & (right < self.chips))
            def _(right=right):
                self.flow(right, True, True)

            left = 2 * (self.chips - 1) - self.chip - rank

            @pl.when((self.chip < self.chips - 1) & (left < self.chip) & (left >= 0))
            def _(left=left):
                self.flow(left, False, True)

            if between is not None:
                between(rank)

        own = self.chip
        self.core_copy(own).wait_recv()

        @pl.loop(0, PIECES)
        def _(piece):
            rows = pl.ds(pl.multiple_of(piece * self.piece, self.piece), self.piece)
            total = self.parts[own, self.core, rows].astype(jnp.float32)
            total = total + self.from_core[own, rows].astype(jnp.float32)
            result_ref[rows] = total

        @pl.when(own > 0)
        def _():
            @pl.loop(0, PIECES)
            def _(piece):
                rows = pl.ds(pl.multiple_of(piece * self.piece, self.piece), self.piece)
                self.flow_copy(own, piece, True).wait_recv()
                result_ref[rows] += self.from_left[own, rows].astype(jnp.float32)

        @pl.when(own < self.chips - 1)
        def _():
            @pl.loop(0, PIECES)
            def _(piece):
                rows = pl.ds(pl.multiple_of(piece * self.piece, self.piece), self.piece)
                self.flow_copy(own, piece, False).wait_recv()
                result_ref[rows] += self.from_right[own, rows].astype(jnp.float32)

        for chip in range(self.chips):
            self.core_copy(chip).wait_send()

            @pl.when(self.chip != chip)
            def _(chip=chip):
                for piece in range(PIECES):
                    self.flow_copy(chip, piece, True).wait_send()


def ffn_forward_kernel(
    chips,
    own_ref,
    gateup_hbm,
    down_hbm,
    ple_held,
    result_ref,
    all_hbm,
    hidden_hbm,
    act_hbm,
    slope_hbm,
    ple_hbm,
    down_low,
    *scratch,
):
    line = Line(chips, scratch[:LINE_REFS])
    gateup, down, hidden, act, slope, load_sems, store_sems = scratch[LINE_REFS : LINE_REFS + 7]
    down_wide = scratch[LINE_REFS + 7]
    ple = Spread(Held(ple_held), scratch[LINE_REFS + 8 :], True)
    ff_part = down.shape[0]
    width = down.shape[1]
    pair = 2 * line.tok
    load_gateup = pltpu.make_async_copy(gateup_hbm, gateup, load_sems.at[0])
    load_down = pltpu.make_async_copy(down_hbm, down_wide, load_sems.at[1])
    store_down = pltpu.make_async_copy(down, down_low, load_sems.at[3])
    load_gateup.start()
    load_down.start()
    greet_all()
    line.gather_begin(own_ref)
    ple.place_all()
    ple.spread_begin()
    line.own_copy(own_ref).wait()
    store_ple = pltpu.make_async_copy(ple.final, ple_hbm, load_sems.at[2])

    def stores(chip):
        rows = pl.ds(pl.multiple_of(chip * pair, pair), pair)
        return [
            pltpu.make_async_copy(line.slots.at[chip], all_hbm.at[chip], store_sems.at[chip, 0]),
            pltpu.make_async_copy(hidden.at[rows], hidden_hbm.at[rows], store_sems.at[chip, 1]),
            pltpu.make_async_copy(act.at[rows], act_hbm.at[rows], store_sems.at[chip, 2]),
            pltpu.make_async_copy(slope.at[rows], slope_hbm.at[rows], store_sems.at[chip, 3]),
        ]

    tile = 256
    for step in range(chips):
        if step > 0:
            line.gather_step(step)
        chip = line.order(step)
        line.gather_other(chip)
        if step == 0:
            load_gateup.wait()
            load_down.wait()
            down[...] = down_wide[...].astype(jnp.bfloat16)
            store_down.start()
        rows = pl.ds(pl.multiple_of(chip * pair, pair), pair)

        @pl.loop(0, ff_part // tile)
        def _(at, chip=chip, rows=rows):
            inputs = line.slots[chip].reshape(pair, width)
            gate_cols = pl.ds(pl.multiple_of(at * tile, tile), tile)
            up_cols = pl.ds(pl.multiple_of(ff_part + at * tile, tile), tile)
            gate = dot_nn(inputs, gateup[:, gate_cols])
            up = dot_nn(inputs, gateup[:, up_cols])
            square = gate * gate
            bent = jnp.tanh(GELU_ROOT * gate * (1.0 + GELU_CUBE * square))
            half = 0.5 + 0.5 * bent
            activated = gate * half
            rise = half + 0.5 * gate * (1.0 - bent * bent) * (
                GELU_ROOT * (1.0 + 3.0 * GELU_CUBE * square)
            )
            hidden[rows, gate_cols] = (activated * up).astype(jnp.bfloat16)
            act[rows, gate_cols] = activated.astype(jnp.bfloat16)
            slope[rows, gate_cols] = (rise * up).astype(jnp.bfloat16)

        for copy in stores(chip):
            copy.start()

        wide = 512

        @pl.loop(0, width // wide)
        def _(at, chip=chip, rows=rows):
            cols = pl.ds(pl.multiple_of(at * wide, wide), wide)
            sums = dot_nn(hidden[rows, :], down[:, cols]).astype(jnp.bfloat16)
            line.parts[chip, :, :, cols] = sums.reshape(2, line.tok, wide)

        line.core_copy(chip).start()
        line.scatter_first(chip)
    ple.spread_on()
    line.scatter_rest(result_ref)
    ple.spread_end()
    store_ple.start()
    line.gather_end()
    ple.spread_sent(False)
    store_ple.wait()
    store_down.wait()
    for chip in range(chips):
        for copy in stores(chip):
            copy.wait()


def ffn_forward(own, gateup, down, ple, chips):
    tok_count, width = own.shape
    ff_part = down.shape[0]
    block = 2 * chips * tok_count
    bfloat = jnp.bfloat16
    anywhere = pl.BlockSpec(memory_space=pl.ANY)
    vmem = pl.BlockSpec(memory_space=pltpu.VMEM)
    part = jax.ShapeDtypeStruct((block, ff_part), bfloat)
    ple_shape = (ple.shape[1], 8 * ple.shape[2], ple.shape[3])
    result, gathered, hidden, act, slope, ple_all, down_low = pl.pallas_call(
        functools.partial(ffn_forward_kernel, chips),
        out_shape=[
            jax.ShapeDtypeStruct((tok_count, width), jnp.float32),
            jax.ShapeDtypeStruct((chips, 2, tok_count, width), bfloat),
            part,
            part,
            part,
            jax.ShapeDtypeStruct(ple_shape, bfloat),
            jax.ShapeDtypeStruct(down.shape, bfloat),
        ],
        in_specs=[vmem, anywhere, anywhere, anywhere],
        out_specs=[vmem] + [anywhere] * 6,
        scratch_shapes=line_scratch(chips, tok_count, width)
        + [
            pltpu.VMEM(gateup.shape, bfloat),
            pltpu.VMEM(down.shape, bfloat),
            pltpu.VMEM((block, ff_part), bfloat),
            pltpu.VMEM((block, ff_part), bfloat),
            pltpu.VMEM((block, ff_part), bfloat),
            pltpu.SemaphoreType.DMA((4,)),
            pltpu.SemaphoreType.DMA((chips, 4)),
            pltpu.VMEM(down.shape, down.dtype),
        ]
        + spread_scratch(ple_shape),
        compiler_params=pltpu.CompilerParams(
            collective_id=1, has_side_effects=True, vmem_limit_bytes=KERNEL_VMEM
        ),
        cost_estimate=pl.CostEstimate(
            flops=6 * block * width * ff_part,
            bytes_accessed=40 << 20,
            transcendentals=block * ff_part,
        ),
        name="ffn_forward",
    )(own, gateup, down, ple)
    return result, gathered.reshape(block, width), hidden, act, slope, ple_all, down_low


def ffn_backward_kernel(
    chips,
    own_ref,
    gateup_hbm,
    down_hbm,
    hidden_hbm,
    act_hbm,
    slope_hbm,
    inputs_hbm,
    pgate_hbm,
    pproj_hbm,
    result_ref,
    part_hbm,
    down_kept,
    pgate_kept,
    pproj_kept,
    *scratch,
):
    line = Line(chips, scratch[:LINE_REFS])
    scratch = scratch[LINE_REFS:]
    gateup, down, hidden, act, slope, inputs, grad, part_down, staged = scratch[:9]
    load_sems, store_sems, kept_sems = scratch[9:12]
    share = Summed(part_down, scratch[12 : 12 + SUM_REFS], False)
    small = [
        Summed(pgate_hbm, scratch[12 + SUM_REFS : 12 + 2 * SUM_REFS], True),
        Summed(pproj_hbm, scratch[12 + 2 * SUM_REFS :], True),
    ]
    ff_part = down.shape[0]
    width = down.shape[1]
    pair = 2 * line.tok
    loads = [
        pltpu.make_async_copy(src, dst, load_sems.at[at])
        for at, (src, dst) in enumerate(
            (
                (down_hbm, down),
                (act_hbm, act),
                (slope_hbm, slope),
                (gateup_hbm, gateup),
                (hidden_hbm, hidden),
                (inputs_hbm, inputs),
            )
        )
    ]
    for load in loads:
        load.start()
    greet_all()
    line.gather_begin(own_ref)
    for one in small:
        one.begin()
    line.own_copy(own_ref).wait()

    tile = 256
    wide = 512
    for step in range(chips):
        if step > 0:
            line.gather_step(step)
        chip = line.order(step)
        line.gather_other(chip)
        if step == 0:
            for load in loads[:4]:
                load.wait()
        rows = pl.ds(pl.multiple_of(chip * pair, pair), pair)

        @pl.loop(0, ff_part // tile)
        def _(at, chip=chip, rows=rows):
            grads = line.slots[chip].reshape(pair, width)
            gate_cols = pl.ds(pl.multiple_of(at * tile, tile), tile)
            up_cols = pl.ds(pl.multiple_of(ff_part + at * tile, tile), tile)
            grad_hidden = dot_nt(grads, down[gate_cols, :])
            grad[rows, gate_cols] = (
                grad_hidden * slope[rows, gate_cols].astype(jnp.float32)
            ).astype(jnp.bfloat16)
            grad[rows, up_cols] = (grad_hidden * act[rows, gate_cols].astype(jnp.float32)).astype(
                jnp.bfloat16
            )

        @pl.loop(0, width // wide)
        def _(at, chip=chip, rows=rows):
            cols = pl.ds(pl.multiple_of(at * wide, wide), wide)
            sums = dot_nt(grad[rows, :], gateup[cols, :]).astype(jnp.bfloat16)
            line.parts[chip, :, :, cols] = sums.reshape(2, line.tok, wide)

        line.core_copy(chip).start()
        line.scatter_first(chip)
    for one in small:
        one.middle()
    for load in loads[4:]:
        load.wait()

    block = chips * pair

    def down_grads():
        @pl.loop(0, ff_part // tile)
        def _(at):
            rows = pl.ds(pl.multiple_of(at * tile, tile), tile)
            left = hidden[:, rows]
            for start in range(0, width, wide):
                right = line.slots[:, :, :, start : start + wide].reshape(block, wide)
                part_down[rows, start : start + wide] = dot_tn(left, right).astype(jnp.bfloat16)

    def part_store(at):
        slot = at % 2
        return pltpu.make_async_copy(
            staged.at[slot], part_hbm.at[at], store_sems.at[slot]
        )

    def gateup_grads(first, last):
        @pl.loop(first, last)
        def _(at):
            cols = pl.ds(pl.multiple_of(at * tile, tile), tile)

            @pl.when(at >= 2)
            def _():
                part_store(at - 2).wait()

            left = inputs[:, cols]
            for start in range(0, 2 * ff_part, wide):
                staged[at % 2, :, start : start + wide] = dot_tn(
                    left, grad[:, start : start + wide]
                ).astype(jnp.bfloat16)
            part_store(at).start()

    tiles = width // tile
    done = [0]

    def between(rank):
        upto = min(tiles, done[0] + 2)
        gateup_grads(done[0], upto)
        done[0] = upto

    down_grads()
    share.begin()
    for one in small:
        one.finish()
    line.scatter_rest(result_ref, between)
    share.middle()
    gateup_grads(done[0], tiles)
    share.finish()
    stores = [
        pltpu.make_async_copy(one.own_rows(half), kept.at[half], kept_sems.at[at, half])
        for at, (one, kept) in enumerate(
            ((share, down_kept), (small[0], pgate_kept), (small[1], pproj_kept))
        )
        for half in (0, 1)
    ]
    for store in stores:
        store.start()
    line.gather_end()
    for one in [share] + small:
        one.sum_sent()
    for at in (tiles - 2, tiles - 1):
        part_store(at).wait()
    for store in stores:
        store.wait()


def ffn_backward(own, gateup, down, hidden, act, slope, inputs, pgate, pproj, chips):
    tok_count, width = own.shape
    ff_part = down.shape[0]
    block = 2 * chips * tok_count
    bfloat = jnp.bfloat16
    anywhere = pl.BlockSpec(memory_space=pl.ANY)
    vmem = pl.BlockSpec(memory_space=pltpu.VMEM)
    dma = pltpu.SemaphoreType.DMA
    tile = 256
    held = (gateup, down, hidden, act, slope, inputs)
    return pl.pallas_call(
        functools.partial(ffn_backward_kernel, chips),
        out_shape=[
            jax.ShapeDtypeStruct((tok_count, width), jnp.float32),
            jax.ShapeDtypeStruct((width // tile, tile, 2 * ff_part), bfloat),
            jax.ShapeDtypeStruct((2, ff_part // 8, width), bfloat),
        ]
        + [
            jax.ShapeDtypeStruct((2, one.shape[0], one.shape[1] // 8, one.shape[2]), bfloat)
            for one in (pgate, pproj)
        ],
        in_specs=[vmem] + [anywhere] * 8,
        out_specs=[vmem] + [anywhere] * 4,
        scratch_shapes=line_scratch(chips, tok_count, width)
        + [pltpu.VMEM(one.shape, bfloat) for one in held]
        + [
            pltpu.VMEM((block, 2 * ff_part), bfloat),
            pltpu.VMEM(down.shape, bfloat),
            pltpu.VMEM((2, tile, 2 * ff_part), bfloat),
            dma((6,)),
            dma((2,)),
            dma((3, 2)),
        ]
        + sum_scratch(down.shape)
        + sum_scratch(pgate.shape)
        + sum_scratch(pproj.shape),
        compiler_params=pltpu.CompilerParams(
            collective_id=2, has_side_effects=True, vmem_limit_bytes=KERNEL_VMEM
        ),
        cost_estimate=pl.CostEstimate(
            flops=12 * block * width * ff_part, bytes_accessed=40 << 20, transcendentals=0
        ),
        name="ffn_backward",
    )(own, *held, pgate, pproj)

def rope_norm(lin, gain, cosine, sine_part):
    scale = lax.rsqrt(jnp.mean(lin * lin, axis=-1, keepdims=True) + EPSILON)
    scaled = lin * scale * gain
    first, second = scaled[:, : HD // 2], scaled[:, HD // 2 :]
    return jnp.concatenate(
        [first * cosine - second * sine_part, second * cosine + first * sine_part], axis=-1
    )


class RowHeld:
    def __init__(self, kept, part):
        self.kept, self.part = kept, part

    def own_rows(self, half):
        return self.kept.at[half]

    def held(self, half, member):
        cols = pl.ds(pl.multiple_of(member * self.part, self.part), self.part)
        return self.kept.at[half, :, cols]


class SameHeld:
    def __init__(self, shard, spread_rows):
        self.shard, self.spread_rows = shard, spread_rows

    def own_rows(self, half):
        start, size = self.spread_rows(half)
        return self.shard.at[pl.ds(pl.multiple_of(start, size), size)]

    def held(self, half, member):
        return self.own_rows(half)


GAIN_ROWS = 24
POSITION_ROW = 12
QUERY_ROW = 13
KEY_ROW = 15


def attention_forward_kernel(
    chips,
    tokens_ref,
    packed_ref,
    frequency_ref,
    lengths_ref,
    query_weight,
    key_weight,
    value_weight,
    gate_weight,
    up_weight,
    out_hbm,
    small_hbm,
    ple_hbm,
    result_ref,
    packed_all,
    cos_ref,
    sin_ref,
    head_gains_ref,
    all_hbm,
    qkv_hbm,
    gateup_hbm,
    lin_hbm,
    query_hbm,
    span_hbm,
    probs_hbm,
    attended_hbm,
    small_all,
    ple_held,
    *scratch,
):
    scratch = list(scratch)
    line = Line(chips, scratch[:LINE_REFS])
    del scratch[:LINE_REFS]
    qkv_kept, gate_kept, up_kept = scratch[:3]
    wide_rows, narrow_rows, row_sem = scratch[3:6]
    own_ref, gains_send, gains_recv, query_docs, key_docs = scratch[6:11]
    del scratch[:11]
    ff_part = gate_kept.shape[2] // (2 * chips)
    spreads = []
    for held in (Held(qkv_kept), RowHeld(gate_kept, ff_part), RowHeld(up_kept, ff_part)):
        spreads.append(Spread(held, scratch[: spread_refs(True)], True))
        del scratch[: spread_refs(True)]
    qkv, gate, up = spreads
    small_held = SameHeld(small_hbm, lambda half: (small.own_start(half), small.eighth))
    small = Everywhere(small_held, scratch[: spread_refs(True)], True)
    del scratch[: spread_refs(True)]
    ple_source = SameHeld(ple_hbm, lambda half: (ple.own_start(half), ple.eighth))
    ple = Everywhere(ple_source, scratch[: spread_refs(True)], True)
    del scratch[: spread_refs(True)]
    out, lin, query, span, probs, attended = scratch[:6]
    load_sem, store_sem, span_send, span_recv = scratch[6:]
    width = line.slots.shape[3]
    pair = 2 * line.tok
    block = chips * pair
    members = 2 * chips
    ctx_at = lax.axis_index("ctx")
    planes = lax.axis_size("ctx")
    me = lax.axis_index("fsdp")
    bfloat = jnp.bfloat16

    def row_load(weight, buffer, at):
        return [
            pltpu.make_async_copy(
                weight.at[pl.ds(pl.multiple_of(qkv.own_start(half), qkv.eighth), qkv.eighth)],
                buffer.at[half],
                row_sem.at[at, half],
            )
            for half in (0, 1)
        ]

    query_rows = row_load(query_weight, wide_rows.at[0, :, :, pl.ds(0, HQ * HD)], 0)
    key_rows = row_load(key_weight, narrow_rows.at[0], 1)
    value_rows = row_load(value_weight, narrow_rows.at[1], 2)
    gate_rows = row_load(gate_weight, wide_rows.at[1], 3)
    up_rows = row_load(up_weight, wide_rows.at[0], 4)
    for load in query_rows + key_rows + value_rows + gate_rows:
        load.start()
    load_out = pltpu.make_async_copy(out_hbm, out, load_sem)
    load_out.start()
    greet_all()

    def gains_copy(hop, source):
        return remote(
            packed_ref,
            packed_all.at[source],
            gains_send.at[hop],
            gains_recv.at[hop],
            lax.rem(me + hop, members),
        )

    for hop in range(1, members):
        gains_copy(hop, me).start()
    packed_all[me] = packed_ref[...]

    for load in query_rows + key_rows + value_rows:
        load.wait()
    for half in (0, 1):
        for member in range(members):
            head = member * KV // members
            qkv_kept[half, member, :, :HD] = wide_rows[
                0, half, :, member * HD : (member + 1) * HD
            ].astype(bfloat)
            for side in (0, 1):
                qkv_kept[half, member, :, (1 + side) * HD : (2 + side) * HD] = narrow_rows[
                    side, half, :, head * HD : (head + 1) * HD
                ].astype(bfloat)
    qkv.swap_begin()
    for load in up_rows:
        load.start()
    for hop in range(1, members):
        gains_copy(hop, lax.rem(me + members - hop, members)).wait_recv()

    inputs = tokens_ref[...].astype(jnp.float32)
    scale = lax.rsqrt(jnp.mean(inputs * inputs, axis=-1, keepdims=True) + EPSILON)
    gain = jnp.concatenate(
        [packed_all[member, row : row + 1] for member in range(members) for row in (0, 1)], axis=1
    )
    own_ref[...] = (inputs * scale * gain).astype(bfloat)
    line.gather_begin(own_ref)

    for load in gate_rows + up_rows:
        load.wait()
    gate_kept[...] = wide_rows[1].astype(bfloat)
    up_kept[...] = wide_rows[0].astype(bfloat)
    for at, row in ((0, QUERY_ROW), (1, KEY_ROW)):
        total = packed_all[0, row : row + 2]
        for member in range(1, members):
            total = total + packed_all[member, row : row + 2]
        head_gains_ref[at : at + 1] = jnp.concatenate([total[0:1], total[1:2]], axis=1)
    gain_query, gain_key = head_gains_ref[0:1], head_gains_ref[1:2]

    line.gather_step(1)
    qkv.swap_end()
    qkv.spread_begin()

    places = ctx_at * block + lax.broadcasted_iota(jnp.int32, (block, 1), 0)
    spots = ctx_at * block - WINDOW + lax.broadcasted_iota(jnp.int32, (1, WINDOW + block), 1)
    doc_end = 0
    query_doc = jnp.zeros(places.shape, jnp.int32)
    key_doc = jnp.where(spots >= 0, 0, -1)
    for doc in range(lengths_ref.shape[0] - 1):
        doc_end = doc_end + lengths_ref[doc]
        query_doc = query_doc + jnp.where(places >= doc_end, 1, 0)
        key_doc = key_doc + jnp.where(spots >= doc_end, 1, 0)
    query_docs[...] = query_doc
    key_docs[...] = key_doc
    positions = jnp.concatenate(
        [packed_all[member, POSITION_ROW : POSITION_ROW + 1] for member in range(members)], axis=0
    )
    columns = jnp.transpose(positions)
    for member in range(members):
        angle = columns[:, member : member + 1] * frequency_ref[...]
        token_rows = pl.ds(member * line.tok, line.tok)
        cos_ref[token_rows] = jnp.cos(angle)
        sin_ref[token_rows] = jnp.sin(angle)

    line.gather_step(2)
    small.swap_begin()
    gate.swap_begin()
    qkv.spread_on()
    for distance in range(3, chips):
        line.gather_step(distance)
    up.swap_begin()
    ple.swap_begin()
    line.own_copy(own_ref).wait()
    for chip in range(chips):
        line.gather_other(chip)
    qkv.spread_end()
    stores = [
        pltpu.make_async_copy(line.slots, all_hbm, store_sem.at[0]),
        pltpu.make_async_copy(qkv.final, qkv_hbm, store_sem.at[1]),
        pltpu.make_async_copy(lin, lin_hbm, store_sem.at[2]),
        pltpu.make_async_copy(query, query_hbm, store_sem.at[3]),
        pltpu.make_async_copy(span, span_hbm, store_sem.at[4]),
        pltpu.make_async_copy(probs, probs_hbm, store_sem.at[5]),
        pltpu.make_async_copy(attended, attended_hbm, store_sem.at[6]),
        pltpu.make_async_copy(
            gate.final, gateup_hbm.at[:, :, pl.ds(0, ff_part)], store_sem.at[7]
        ),
        pltpu.make_async_copy(
            up.final, gateup_hbm.at[:, :, pl.ds(ff_part, ff_part)], store_sem.at[8]
        ),
        pltpu.make_async_copy(small.final, small_all, store_sem.at[9]),
    ] + [
        pltpu.make_async_copy(
            ple.rows(ple.final, ple.own_start(half), ple.eighth),
            ple_held.at[half],
            store_sem.at[10 + half],
        )
        for half in (0, 1)
    ]
    stores[0].start()
    stores[1].start()

    @pl.loop(0, chips)
    def _(chip):
        rows = pl.ds(pl.multiple_of(chip * pair, pair), pair)
        span_rows = pl.ds(pl.multiple_of(WINDOW + chip * pair, pair), pair)
        inputs = line.slots[chip].reshape(pair, width)
        weights = qkv.final[...].reshape(width, 3 * HD)
        key_lin = dot_nn(inputs, weights[:, HD : 2 * HD])
        lin[rows, HD : 2 * HD] = key_lin
        span[0, span_rows] = rope_norm(
            key_lin, gain_key, cos_ref[rows], sin_ref[rows]
        ).astype(bfloat)
        span[1, span_rows] = dot_nn(inputs, weights[:, 2 * HD :]).astype(bfloat)

    part = WINDOW // 2

    def span_copy(start, to_start, way, device):
        return pltpu.make_async_remote_copy(
            src_ref=span.at[:, pl.ds(pl.multiple_of(start, part), part)],
            dst_ref=span.at[:, pl.ds(pl.multiple_of(to_start, part), part)],
            send_sem=span_send.at[way],
            recv_sem=span_recv.at[way],
            device_id=device,
            device_id_type=pl.DeviceIdType.MESH,
        )

    mine = line.core * part
    others = (1 - line.core) * part
    onward = span_copy(block + mine, mine, 0, {"ctx": lax.rem(ctx_at + 1, planes)})
    across = span_copy(mine, mine, 1, {"fsdp": line.place(line.chip, 1 - line.core)})
    arrived = span_copy(others, others, 1, {"fsdp": line.place(line.chip, 1 - line.core)})

    @pl.when(ctx_at < planes - 1)
    def _():
        onward.start()

    @pl.when(ctx_at == 0)
    def _():
        span[:, pl.ds(0, WINDOW)] = jnp.zeros((2, WINDOW, HD), bfloat)

    @pl.loop(0, chips)
    def _(chip):
        rows = pl.ds(pl.multiple_of(chip * pair, pair), pair)
        inputs = line.slots[chip].reshape(pair, width)
        weights = qkv.final[...].reshape(width, 3 * HD)
        query_lin = dot_nn(inputs, weights[:, :HD])
        lin[rows, :HD] = query_lin
        rotated = rope_norm(query_lin, gain_query, cos_ref[rows], sin_ref[rows])
        query[rows] = (rotated.astype(bfloat).astype(jnp.float32) * SCORE_SCALE).astype(bfloat)

    @pl.when(ctx_at > 0)
    def _():
        onward.wait_recv()
        across.start()
        arrived.wait_recv()

    for store in stores[2:5]:
        store.start()
    load_out.wait()
    small.swap_on()

    span_len = WINDOW + pair
    for step in range(chips):
        chip = line.order(chips - 1 - step)
        rows = pl.ds(pl.multiple_of(chip * pair, pair), pair)
        span_rows = pl.ds(pl.multiple_of(chip * pair, pair), span_len)
        scores = dot_nt(query[rows], span[0, span_rows])
        distance = (
            WINDOW
            + lax.broadcasted_iota(jnp.int32, (pair, span_len), 0)
            - lax.broadcasted_iota(jnp.int32, (pair, span_len), 1)
        )
        visible = (
            (distance >= 0)
            & (distance < WINDOW)
            & (query_docs[rows] == key_docs[:, span_rows])
        )
        scores = jnp.where(visible, scores, NEGATIVE)
        shifted = jnp.exp(scores - jnp.max(scores, axis=-1, keepdims=True))
        prob = (shifted / jnp.sum(shifted, axis=-1, keepdims=True)).astype(bfloat)
        probs[rows] = prob
        attended[rows] = dot_nn(prob, span[1, span_rows]).astype(bfloat)

        wide = 512

        @pl.loop(0, width // wide)
        def _(at, chip=chip, rows=rows):
            cols = pl.ds(pl.multiple_of(at * wide, wide), wide)
            sums = dot_nn(attended[rows], out[:, cols]).astype(bfloat)
            line.parts[chip, :, :, cols] = sums.reshape(2, line.tok, wide)

        line.core_copy(chip).start()
        line.scatter_first(chip)
        if step == 0:
            gate.swap_end()
            gate.spread_begin()
            small.swap_end()
            small.spread_begin()
    for store in stores[5:7]:
        store.start()
    gate.spread_on()

    def between(rank):
        if rank == 3:
            up.swap_end()
            up.spread_begin()
            small.spread_on()
            ple.swap_on()
        if rank == 2 * chips - 4:
            up.spread_on()

    line.scatter_rest(result_ref, between)
    ple.swap_end()
    for store in stores[10:]:
        store.start()
    gate.spread_end()
    stores[7].start()
    up.spread_end()
    stores[8].start()
    small.spread_end()
    stores[9].start()
    line.gather_end()
    for hop in range(1, members):
        gains_copy(hop, me).wait_send()
    for spread in spreads + [small]:
        spread.spread_sent()
    ple.swap_sent()

    @pl.when(ctx_at < planes - 1)
    def _():
        onward.wait_send()

    @pl.when(ctx_at > 0)
    def _():
        across.wait_send()

    for store in stores:
        store.wait()


def attention_forward(
    tokens,
    packed,
    frequency,
    lengths,
    query_weight,
    key_weight,
    value_weight,
    gate,
    up,
    out,
    small,
    ple,
):
    tok_count, width = tokens.shape
    rows = query_weight.shape[0]
    members = width // rows
    chips = members // 2
    block = members * tok_count
    span_len = WINDOW + block
    ff_part = gate.shape[1] // members
    bfloat = jnp.bfloat16
    anywhere = pl.BlockSpec(memory_space=pl.ANY)
    vmem = pl.BlockSpec(memory_space=pltpu.VMEM)
    dma = pltpu.SemaphoreType.DMA
    kept = [
        ((block, 2 * HD), jnp.float32),
        ((block, HD), bfloat),
        ((2, span_len, HD), bfloat),
        ((block, WINDOW + 2 * tok_count), bfloat),
        ((block, HD), bfloat),
    ]
    outputs = [
        ((tok_count, width), jnp.float32),
        ((members,) + packed.shape, jnp.float32),
        ((block, HD // 2), jnp.float32),
        ((block, HD // 2), jnp.float32),
        ((2, HD), jnp.float32),
        ((chips, 2, tok_count, width), bfloat),
        ((members, rows, 3 * HD), bfloat),
        ((members, rows, 2 * ff_part), bfloat),
    ] + kept
    outputs.append(((members,) + small.shape, bfloat))
    outputs.append(((2, members, ple.shape[0] // 8, ple.shape[1]), bfloat))
    return pl.pallas_call(
        functools.partial(attention_forward_kernel, chips),
        out_shape=[jax.ShapeDtypeStruct(*output) for output in outputs],
        in_specs=[vmem] * 3 + [pl.BlockSpec(memory_space=pltpu.SMEM)] + [anywhere] * 8,
        out_specs=[vmem] * 5 + [anywhere] * 10,
        scratch_shapes=line_scratch(chips, tok_count, width)
        + [
            pltpu.VMEM((2, members, rows // 8, 3 * HD), bfloat),
            pltpu.VMEM((2, rows // 8, gate.shape[1]), bfloat),
            pltpu.VMEM((2, rows // 8, gate.shape[1]), bfloat),
            pltpu.VMEM((2, 2, rows // 8, gate.shape[1]), jnp.float32),
            pltpu.VMEM((2, 2, rows // 8, KV * HD), jnp.float32),
            dma((5, 2)),
            pltpu.VMEM((tok_count, width), bfloat),
            dma((members,)),
            dma((members,)),
            pltpu.VMEM((block, 1), jnp.int32),
            pltpu.VMEM((1, span_len), jnp.int32),
        ]
        + spread_scratch((members, rows, 3 * HD))
        + spread_scratch((members, rows, ff_part))
        + spread_scratch((members, rows, ff_part))
        + everywhere_scratch((members,) + small.shape)
        + everywhere_scratch((members,) + ple.shape)
        + [pltpu.VMEM(out.shape, bfloat)]
        + [pltpu.VMEM(*one) for one in kept]
        + [dma, dma((12,)), dma((2,)), dma((2,))],
        compiler_params=pltpu.CompilerParams(
            collective_id=4, has_side_effects=True, vmem_limit_bytes=KERNEL_VMEM
        ),
        cost_estimate=pl.CostEstimate(
            flops=8 << 30, bytes_accessed=300 << 20, transcendentals=block * 1280
        ),
        name="attention_forward",
    )(
        tokens,
        packed,
        frequency,
        lengths,
        query_weight,
        key_weight,
        value_weight,
        gate,
        up,
        out,
        small,
        ple,
    )

def rope_norm_back(grad, lin, gain, cosine, sine_part):
    first, second = grad[:, : HD // 2], grad[:, HD // 2 :]
    turned = jnp.concatenate(
        [first * cosine + second * sine_part, second * cosine - first * sine_part], axis=-1
    )
    scale = lax.rsqrt(jnp.mean(lin * lin, axis=-1, keepdims=True) + EPSILON)
    scaled = turned * gain
    along = jnp.mean(lin * scaled, axis=-1, keepdims=True)
    grad_lin = scale * scaled - lin * (scale * scale * scale * along)
    return grad_lin, jnp.sum(lin * scale * turned, axis=0, keepdims=True)


def attention_backward_kernel(
    chips,
    own_ref,
    out_hbm,
    qkv_hbm,
    lin_hbm,
    query_hbm,
    span_hbm,
    probs_hbm,
    cos_ref,
    sin_ref,
    gain_query_ref,
    gain_key_ref,
    gateup_hbm,
    down_kept,
    inputs_hbm,
    attended_hbm,
    result_ref,
    query_part_hbm,
    kv_part_hbm,
    out_part_hbm,
    gains_ref,
    gateup_kept,
    down_sum,
    *scratch,
):
    scratch = list(scratch)
    line = Line(chips, scratch[:LINE_REFS])
    del scratch[:LINE_REFS]
    gateup = Summed(gateup_hbm, scratch[:SUM_REFS], True)
    del scratch[:SUM_REFS]
    down = Spread(Held(down_kept), scratch[: spread_refs(False)], False)
    del scratch[: spread_refs(False)]
    out, qkv, lin, query, span, probs, grad, grad_span, back, across, returned = scratch[:11]
    load_sem, store_sem, back_send, back_recv, grad_out = scratch[11:16]
    inputs, attended, query_part, kv_part, out_part, pair_send, pair_recv = scratch[16:]
    width = line.slots.shape[3]
    pair = 2 * line.tok
    block = chips * pair
    ctx_at = lax.axis_index("ctx")
    planes = lax.axis_size("ctx")
    bfloat = jnp.bfloat16
    loads = [
        pltpu.make_async_copy(src, dst, load_sem.at[at])
        for at, (src, dst) in enumerate(
            (
                (out_hbm, out),
                (span_hbm, span),
                (probs_hbm, probs),
                (lin_hbm, lin),
                (query_hbm, query),
                (qkv_hbm, qkv),
                (inputs_hbm, inputs),
                (attended_hbm, attended),
            )
        )
    ]
    for load in loads:
        load.start()
    greet_all()
    line.gather_begin(own_ref)
    gateup.begin()
    grad_span[...] = jnp.zeros_like(grad_span)
    gains_ref[...] = jnp.zeros_like(gains_ref)
    line.own_copy(own_ref).wait()
    for load in loads[:6]:
        load.wait()

    span_len = WINDOW + pair
    for step in range(chips):
        if step > 0:
            line.gather_step(step)
        chip = line.order(step)
        line.gather_other(chip)
        rows = pl.ds(pl.multiple_of(chip * pair, pair), pair)
        span_rows = pl.ds(pl.multiple_of(chip * pair, pair), span_len)
        grad_out[rows] = dot_nt(line.slots[chip].reshape(pair, width), out[...]).astype(bfloat)
        grad_prob = dot_nt(grad_out[rows], span[1, span_rows])
        prob = probs[rows].astype(jnp.float32)
        inner = jnp.sum(prob * grad_prob, axis=-1, keepdims=True)
        grad_score = (prob * (grad_prob - inner)).astype(bfloat)
        grad_query = dot_nn(grad_score, span[0, span_rows]) * SCORE_SCALE
        grad_lin, grad_gain = rope_norm_back(
            grad_query, lin[rows, :HD], gain_query_ref[...], cos_ref[rows], sin_ref[rows]
        )
        grad[rows, :HD] = grad_lin.astype(bfloat)
        gains_ref[0:1] += grad_gain
        grad_span[0, span_rows] += dot_tn(grad_score, query[rows])
        grad_span[1, span_rows] += dot_tn(probs[rows], grad_out[rows])

    part = WINDOW // 2
    mine, others = line.core * part, (1 - line.core) * part
    back[...] = grad_span[:, pl.ds(pl.multiple_of(others, part), part)].astype(bfloat)
    to_core = remote(
        back, across, back_send.at[0], back_recv.at[0], line.place(line.chip, 1 - line.core)
    )
    to_core.start()
    to_core.wait()
    total = grad_span[:, pl.ds(pl.multiple_of(mine, part), part)]
    back[...] = (total + across[...].astype(jnp.float32)).astype(bfloat)
    to_before = pltpu.make_async_remote_copy(
        src_ref=back,
        dst_ref=returned,
        send_sem=back_send.at[1],
        recv_sem=back_recv.at[1],
        device_id={"ctx": lax.rem(ctx_at + planes - 1, planes)},
        device_id_type=pl.DeviceIdType.MESH,
    )

    @pl.when(ctx_at > 0)
    def _():
        to_before.start()

    down.place_all()
    down.spread_begin()

    @pl.when(ctx_at < planes - 1)
    def _():
        to_before.wait_recv()
        here = pl.ds(pl.multiple_of(block + mine, part), part)
        grad_span[:, here] += returned[...].astype(jnp.float32)

    for step in range(chips):
        chip = line.order(chips - 1 - step)
        rows = pl.ds(pl.multiple_of(chip * pair, pair), pair)
        span_rows = pl.ds(pl.multiple_of(WINDOW + chip * pair, pair), pair)
        grad_lin, grad_gain = rope_norm_back(
            grad_span[0, span_rows], lin[rows, HD:], gain_key_ref[...], cos_ref[rows], sin_ref[rows]
        )
        grad[rows, HD : 2 * HD] = grad_lin.astype(bfloat)
        gains_ref[1:2] += grad_gain
        grad[rows, 2 * HD :] = grad_span[1, span_rows].astype(bfloat)

    wide = 512

    @pl.loop(0, width // wide)
    def _(at):
        cols = pl.ds(pl.multiple_of(at * wide, wide), wide)
        sums = dot_nt(grad[...], qkv[cols]).astype(bfloat)
        line.parts[:, :, :, cols] = sums.reshape(chips, 2, line.tok, wide)

    for step in range(chips):
        line.core_copy(line.order(chips - 1 - step)).start()
    for step in range(chips - 1):
        line.scatter_first(line.order(chips - 1 - step))
    for load in loads[6:]:
        load.wait()
    part_stores = [
        pltpu.make_async_copy(out_part, out_part_hbm, store_sem.at[0]),
        pltpu.make_async_copy(query_part, query_part_hbm, store_sem.at[1]),
        pltpu.make_async_copy(
            kv_part.at[pl.ds(line.core * chips, chips)], kv_part_hbm, store_sem.at[5]
        ),
    ]

    def pair_copy(at):
        return remote(
            kv_part.at[(1 - line.core) * chips + at],
            probs.at[pl.ds(at * HD, HD), pl.ds(0, 2 * HD)],
            pair_send.at[at],
            pair_recv.at[at],
            line.place(line.chip, 1 - line.core),
        )

    def between(rank):
        if rank == 3:
            for start in range(0, width, wide):
                right = line.slots[:, :, :, start : start + wide].reshape(block, wide)
                out_part[:, start : start + wide] = dot_tn(attended[...], right).astype(bfloat)
            part_stores[0].start()
        if rank == 4:

            @pl.loop(0, width // HD)
            def _(at):
                left = inputs[:, pl.ds(pl.multiple_of(at * HD, HD), HD)]
                query_part[at] = dot_tn(left, grad[:, :HD]).astype(bfloat)
                kv_part[at] = dot_tn(left, grad[:, HD:]).astype(bfloat)

            part_stores[1].start()
            for at in range(chips):
                pair_copy(at).start()
        if rank == 5:
            for at in range(chips):
                pair_copy(at).wait_recv()
                kv_part[line.core * chips + at] += probs[at * HD : (at + 1) * HD, : 2 * HD]
            part_stores[2].start()

    gateup.middle()
    down.spread_on()
    line.scatter_rest(result_ref, between)
    gateup.finish()
    stores = [
        pltpu.make_async_copy(gateup.own_rows(half), gateup_kept.at[half], store_sem.at[2 + half])
        for half in (0, 1)
    ]
    down.spread_end()
    stores.append(pltpu.make_async_copy(down.final, down_sum, store_sem.at[4]))
    for store in stores:
        store.start()
    line.gather_end()
    gateup.sum_sent()
    down.spread_sent()
    for at in range(chips):
        pair_copy(at).wait_send()

    @pl.when(ctx_at > 0)
    def _():
        to_before.wait_send()

    for store in stores + part_stores:
        store.wait()


def attention_backward(
    own,
    out,
    qkv,
    lin,
    query,
    span,
    probs,
    cosine,
    sine_part,
    gain_query,
    gain_key,
    part_gateup,
    held_down,
    inputs,
    attended,
):
    tok_count, width = own.shape
    members = part_gateup.shape[0]
    chips = members // 2
    block = members * tok_count
    bfloat = jnp.bfloat16
    anywhere = pl.BlockSpec(memory_space=pl.ANY)
    vmem = pl.BlockSpec(memory_space=pltpu.VMEM)
    dma = pltpu.SemaphoreType.DMA
    eighth = part_gateup.shape[1] // 8
    down_shape = (8 * held_down.shape[1], held_down.shape[2])
    outputs = [
        ((tok_count, width), jnp.float32),
        ((members, HD, HD), bfloat),
        ((chips, HD, 2 * HD), bfloat),
        ((HD, width), bfloat),
        ((2, HD), jnp.float32),
        ((2, members, eighth, part_gateup.shape[2]), bfloat),
        (down_shape, bfloat),
    ]
    half_span = (2, WINDOW // 2, HD)
    return pl.pallas_call(
        functools.partial(attention_backward_kernel, chips),
        out_shape=[jax.ShapeDtypeStruct(*output) for output in outputs],
        in_specs=[vmem] + [anywhere] * 6 + [vmem] * 4 + [anywhere] * 4,
        out_specs=[vmem, anywhere, anywhere, anywhere, vmem, anywhere, anywhere],
        scratch_shapes=line_scratch(chips, tok_count, width)
        + sum_scratch(part_gateup.shape)
        + spread_scratch(down_shape)
        + [pltpu.VMEM(one.shape, one.dtype) for one in (out, qkv, lin, query, span, probs)]
        + [
            pltpu.VMEM((block, 3 * HD), bfloat),
            pltpu.VMEM(span.shape, jnp.float32),
            pltpu.VMEM(half_span, bfloat),
            pltpu.VMEM(half_span, bfloat),
            pltpu.VMEM(half_span, bfloat),
            dma((8,)),
            dma((6,)),
            dma((2,)),
            dma((2,)),
            pltpu.VMEM((block, HD), bfloat),
            pltpu.VMEM((block, width), bfloat),
            pltpu.VMEM((block, HD), bfloat),
            pltpu.VMEM((members, HD, HD), bfloat),
            pltpu.VMEM((members, HD, 2 * HD), bfloat),
            pltpu.VMEM((HD, width), bfloat),
            dma((chips,)),
            dma((chips,)),
        ],
        compiler_params=pltpu.CompilerParams(
            collective_id=5, has_side_effects=True, vmem_limit_bytes=KERNEL_VMEM
        ),
        cost_estimate=pl.CostEstimate(
            flops=8 << 30, bytes_accessed=300 << 20, transcendentals=0
        ),
        name="attention_backward",
    )(
        own,
        out,
        qkv,
        lin,
        query,
        span,
        probs,
        cosine,
        sine_part,
        gain_query,
        gain_key,
        part_gateup,
        held_down,
        inputs,
        attended,
    )

def by_heads(
    tokens,
    per_layer,
    cotangent,
    doc_lengths,
    positions,
    w_query,
    w_key,
    w_value,
    w_out,
    laurel_left,
    laurel_right,
    w_gate,
    w_up,
    w_down,
    ple_gate,
    ple_proj,
    attn_in_gain,
    query_gain,
    key_gain,
    attn_out_gain,
    laurel_gain,
    ffn_in_gain,
    ffn_out_gain,
    ple_gain,
):
    bfloat = jnp.bfloat16
    ctx_count = lax.axis_size("ctx")
    fsdp_count = lax.axis_size("fsdp")
    tok_count = tokens.shape[0]
    block_len = tok_count * fsdp_count
    chips = fsdp_count // 2
    rows = w_query.shape[0]
    ff_part = w_gate.shape[1] // fsdp_count
    ctx_at = lax.axis_index("ctx")
    fsdp_at = lax.axis_index("fsdp")

    wide_gains = (attn_in_gain, attn_out_gain, laurel_gain, ffn_in_gain, ffn_out_gain, ple_gain)
    turn = jnp.arange(HD, dtype=jnp.int32) // query_gain.shape[0]
    head_parts = [
        jnp.where(turn == fsdp_at, jnp.tile(gain, fsdp_count), 0.0)
        for gain in (query_gain, key_gain)
    ]
    packed = jnp.zeros((GAIN_ROWS * 128,), jnp.float32)
    at = 0
    for part in list(wide_gains) + [positions.astype(jnp.float32)] + head_parts:
        packed = packed + jnp.pad(part, (at, packed.shape[0] - at - part.shape[0]))
        at += part.shape[0]
    packed = packed.reshape(GAIN_ROWS, 128)
    frequency = jnp.exp(
        jnp.arange(HD // 2, dtype=jnp.float32) * (-2.0 * math.log(ROPE_BASE) / HD)
    )

    out_low = w_out.astype(bfloat)
    def in_halves(weight):
        return jnp.concatenate(jnp.split(weight.astype(bfloat), rows // 128, axis=0), axis=1)

    def in_stacks(weight):
        pieces = weight.astype(bfloat).reshape(weight.shape[0], 128 // weight.shape[0], -1)
        return jnp.transpose(pieces, (1, 0, 2)).reshape(128, -1)

    small = jnp.concatenate([in_halves(laurel_left), in_stacks(laurel_right)], axis=1)
    ple_small = jnp.concatenate([in_halves(ple_gate), in_stacks(ple_proj)], axis=1)

    inputs = tokens.astype(jnp.float32)
    ple_input = per_layer.astype(jnp.float32)
    (
        projected,
        packed_all,
        cosine,
        sine_part,
        head_gains,
        normed_all,
        qkv_full,
        gateup_full,
        qk_lin,
        query_low,
        span_kv,
        probs,
        attended_low,
        small_all,
        ple_held,
    ) = attention_forward(
        tokens,
        packed,
        frequency[None, :],
        doc_lengths,
        w_query,
        w_key,
        w_value,
        w_gate,
        w_up,
        out_low,
        small,
        ple_small,
    )
    def side_by_side(cols, shape):
        pieces = jnp.split(cols, cols.shape[2] // shape[1], axis=2)
        return jnp.concatenate(pieces, axis=1).reshape(-1, shape[1])

    def stacked(cols, shape):
        pieces = cols.reshape(fsdp_count, -1, shape[0], cols.shape[2])
        return jnp.transpose(pieces, (0, 2, 1, 3)).reshape(-1, shape[1])

    left_size = laurel_left.size // 128
    full_left = side_by_side(small_all[:, :, :left_size], laurel_left.shape)
    full_right = stacked(small_all[:, :, left_size:], laurel_right.shape)
    wide_rows = attn_in_gain.shape[0] // 128
    gain_in, gain_post, gain_laurel, gain_ffin, gain_ffout, gain_ple = (
        packed_all[:, n * wide_rows : (n + 1) * wide_rows].reshape(-1) for n in range(6)
    )
    normed, norm_back = jax.vjp(rms_norm, inputs, gain_in)
    normed_low = normed.astype(bfloat)
    normed_all = normed_all.reshape(block_len, -1)
    col_qkv = qkv_full.reshape(normed_all.shape[1], -1)
    col_gateup = gateup_full.reshape(normed_all.shape[1], -1)
    narrow_low = matmul(normed_low, full_left).astype(bfloat)
    widened = matmul(narrow_low, full_right)
    mixed, mix_back = jax.vjp(mix_piece, inputs, normed, projected, widened, gain_post, gain_laurel)
    ffn_normed, ffn_norm_back = jax.vjp(rms_norm, mixed, gain_ffin)
    down_lin, ffn_all, hidden_low, act_low, slope_low, ple_all, down_low = ffn_forward(
        ffn_normed.astype(bfloat), col_gateup, w_down, ple_held, chips
    )
    pgate_size = ple_gate.size // 128
    full_pgate = side_by_side(ple_all[:, :, :pgate_size], ple_gate.shape)
    full_pproj = stacked(ple_all[:, :, pgate_size:], ple_proj.shape)
    layer_mid, ffn_out_back = jax.vjp(ffn_out_piece, mixed, down_lin, gain_ffout)
    layer_low = layer_mid.astype(bfloat)
    ple_lin = matmul(layer_low, full_pgate)
    ple_mid, ple_back = jax.vjp(ple_act, ple_lin, ple_input)
    ple_low = ple_mid.astype(bfloat)
    ple_wide = matmul(ple_low, full_pproj)
    out_full, final_back = jax.vjp(final_piece, layer_mid, ple_wide, gain_ple)

    grad_layer, grad_pwide, grad_gple = final_back(cotangent.astype(jnp.float32))
    grad_pwide_low = grad_pwide.astype(bfloat)
    part_pproj = matmul_tn(ple_low, grad_pwide_low)
    grad_plemid = matmul_nt(grad_pwide_low, full_pproj)
    grad_plelin, grad_pleinput = ple_back(grad_plemid)
    grad_plelin_low = grad_plelin.astype(bfloat)
    part_pgate = matmul_tn(layer_low, grad_plelin_low)
    grad_layer = grad_layer + matmul_nt(grad_plelin_low, full_pgate)
    grad_mixed, grad_down, grad_gffout = ffn_out_back(grad_layer)
    grad_ffn, part_gateup, held_wdown, held_pgate, held_pproj = ffn_backward(
        grad_down.astype(bfloat),
        col_gateup,
        down_low,
        hidden_low,
        act_low,
        slope_low,
        ffn_all,
        part_pgate.astype(bfloat).reshape(fsdp_count, rows, -1),
        part_pproj.astype(bfloat).reshape(fsdp_count, 128, -1),
        chips,
    )
    part_gateup = part_gateup.reshape(fsdp_count, rows, -1)
    grad_mixed_more, grad_gffin = ffn_norm_back(grad_ffn)
    grad_mixed = grad_mixed + grad_mixed_more
    grad_in_first, grad_normed, grad_proj, grad_lwide, grad_gpost, grad_glaurel = mix_back(
        grad_mixed
    )
    grad_lwide_low = grad_lwide.astype(bfloat)
    part_right = matmul_tn(narrow_low, grad_lwide_low)
    grad_narrow_low = matmul_nt(grad_lwide_low, full_right).astype(bfloat)
    part_left = matmul_tn(normed_low, grad_narrow_low)
    grad_normed = grad_normed + matmul_nt(grad_narrow_low, full_left)

    (
        grad_normed_more,
        part_query,
        part_kv,
        part_wout,
        grad_head_gains,
        held_gateup,
        sum_wdown,
    ) = (
        attention_backward(
            grad_proj.astype(bfloat),
            out_low,
            col_qkv,
            qk_lin,
            query_low,
            span_kv,
            probs,
            cosine,
            sine_part,
            head_gains[0:1],
            head_gains[1:2],
            part_gateup,
            held_wdown,
            normed_all,
            attended_low,
        )
    )
    grad_gquery, grad_gkey = grad_head_gains[0], grad_head_gains[1]
    part_laurel = jnp.concatenate(
        [part.astype(bfloat).reshape(fsdp_count, 128, -1) for part in (part_left, part_right)],
        axis=2,
    )
    grad_normed = grad_normed + grad_normed_more
    grad_in_second, grad_gin = norm_back(grad_normed)
    grad_tokens = grad_in_first + grad_in_second

    grad_gains = [
        grad_gin,
        grad_gpost,
        grad_glaurel,
        grad_gffin,
        grad_gffout,
        grad_gple,
        grad_gquery,
        grad_gkey,
    ]
    gain_parts = jnp.concatenate([g.reshape(fsdp_count, -1) for g in grad_gains], axis=1)
    gain_parts = jnp.pad(gain_parts, ((0, 0), (0, 128 * 128 - gain_parts.shape[1])))
    gain_parts = gain_parts.astype(bfloat).reshape(fsdp_count, 128, 128)

    (
        sum_wgate,
        sum_wup,
        sum_wquery,
        sum_wkey,
        sum_wvalue,
        sum_wout,
        sum_pgate,
        sum_pproj,
        sum_laurel,
        sum_gains,
    ) = gradient_sum(
        [
            Source(held_gateup, summed=True, part=(0, 2), sides=1),
            Source(held_gateup, summed=True, part=(1, 2), sides=1),
            Source(part_query, sides=1),
            Source(part_kv, groups=KV, paired=True, sides=2),
            Source(part_wout),
            Source(held_pgate, summed=True, groups=1, sides=1),
            Source(held_pproj, summed=True, groups=1, sides=1),
            Source(part_laurel, groups=1, sides=1),
            Source(gain_parts, groups=1),
        ]
    )
    gain_sums = sum_gains.astype(jnp.float32).reshape(-1)
    wide_size, head_size = attn_in_gain.shape[0], query_gain.shape[0]
    wide_sums = gain_sums[: 6 * wide_size].reshape(6, wide_size)
    head_sums = gain_sums[6 * wide_size : 6 * wide_size + 2 * head_size].reshape(2, head_size)
    grad_wgate = sum_wgate.astype(jnp.float32)
    grad_wup = sum_wup.astype(jnp.float32)
    grad_wdown = sum_wdown.astype(jnp.float32)
    grad_wout = sum_wout.astype(jnp.float32)
    grad_wquery = sum_wquery.astype(jnp.float32)
    grad_wkey = sum_wkey.astype(jnp.float32)
    grad_wvalue = sum_wvalue.astype(jnp.float32)
    grad_pgate = sum_pgate.astype(jnp.float32)
    grad_pproj = sum_pproj.astype(jnp.float32).reshape(ple_proj.shape)
    left_part = sum_laurel.shape[1] // 2
    grad_wleft = sum_laurel[:, :left_part].astype(jnp.float32).reshape(laurel_left.shape)
    grad_wright = sum_laurel[:, left_part:].astype(jnp.float32).reshape(laurel_right.shape)
    return (
        out_full.astype(bfloat),
        grad_tokens,
        grad_pleinput,
        grad_wquery,
        grad_wkey,
        grad_wvalue,
        grad_wout,
        grad_wleft,
        grad_wright,
        grad_wgate,
        grad_wup,
        grad_wdown,
        grad_pgate,
        grad_pproj,
        wide_sums[0],
        head_sums[0],
        head_sums[1],
        *(wide_sums[n] for n in range(1, 6)),
    )


def solution(mesh):
    in_specs = (
        P(("ctx", "fsdp"), None),
        P(("ctx", "fsdp"), None),
        P(("ctx", "fsdp"), None),
        P(),
        P(("ctx", "fsdp")),
        P("fsdp", None),
        P("fsdp", None),
        P("fsdp", None),
        P("fsdp", None),
        P("fsdp", None),
        P("fsdp", None),
        P("fsdp", None),
        P("fsdp", None),
        P("fsdp", None),
        P("fsdp", None),
        P("fsdp", None),
        P("fsdp"),
        P("fsdp"),
        P("fsdp"),
        P("fsdp"),
        P("fsdp"),
        P("fsdp"),
        P("fsdp"),
        P("fsdp"),
    )
    out_specs = (
        P(("ctx", "fsdp"), None),
        P(("ctx", "fsdp"), None),
        P(("ctx", "fsdp"), None),
        P("fsdp", None),
        P("fsdp", None),
        P("fsdp", None),
        P("fsdp", None),
        P("fsdp", None),
        P("fsdp", None),
        P("fsdp", None),
        P("fsdp", None),
        P("fsdp", None),
        P("fsdp", None),
        P("fsdp", None),
        P("fsdp"),
        P("fsdp"),
        P("fsdp"),
        P("fsdp"),
        P("fsdp"),
        P("fsdp"),
        P("fsdp"),
        P("fsdp"),
    )
    run = by_heads if mesh.shape["fsdp"] == HQ and mesh.shape["ctx"] == 4 else local
    return jax.shard_map(run, mesh=mesh, in_specs=in_specs, out_specs=out_specs, check_vma=False)
```
